32 devices in a mesh: dom: 8 (over z, y), orb: 4 (over x, core).
Axes of the slice: x: 2, y: 2, z: 4, core: 2. Of those that a mesh axis runs over, the one named last changes fastest.
Arguments:
- orbitals: bfloat16 [18816, 1024], P('dom', 'orb'), may hold values from -6 to 6
- potential: float32 [18816], P('dom'), may hold values from 0.5 to 2
- cell_hamiltonian: bfloat16 [64, 343, 343], P('dom'), may hold values from -2 to 2, as said below
- connectivity: int32 [64, 343], P('dom'), may hold values from 0 to 2400, as said below
- face_nodes: int32 [392], P('dom'), may hold values from 0 to 2351, as said below
Outputs:
- residual: float32 [18816, 1024], P(('dom', 'orb'))
- projected: bfloat16 [1024, 1024], replicated
The draws below stay inside these ranges and needn't reach their ends.
Inputs may be any that keep to these rules, and one draw needn't show every extreme that they name: `connectivity`: cell c of a domain is its c-th layer of cells; each row lists the cell's 343 nodes in the domain's local numbering, where a number 2352 + p stands for entry p of the next domain's face_nodes list. Every local node of a domain belongs to some cell of it, and neighbouring cells of a domain share a face of 49 nodes. `face_nodes`: each domain's 49 entries are distinct local node numbers of that domain: the nodes that the previous domain's last cell shares with it, in the order of that cell's numbers 2352 + p. `cell_hamiltonian`: each cell's matrix is symmetric.
All inputs are finite; a program needn't handle non-finite values.
Results may differ from the reference program's by a relative error of at most 0.0096.
Values may be sent and summed in bfloat16 or wider, within the bound.
No kernel may reach another device: no remote copies, remote signals or barrier semaphores. Data moves between devices by JAX's collectives and lax.ppermute only.
A program may use at most 64 MiB of HBM per device.

```python
import math
import jax
import jax.numpy as jnp
from jax import lax

ORDER = 6
NPC = 343
FACE = 49
KZ = 8
NODE_DEV = 2352
ORBITALS = 1024
DEGREE = 4
CELLS = 64
NODES = 18816


def swap_values(perm, first, second):
    return jnp.where(perm == first, second, jnp.where(perm == second, first, perm)).astype(jnp.int32)


def domain_perm(sub):
    raw = jax.random.permutation(sub, NODE_DEV).astype(jnp.int32)
    raw = swap_values(raw, raw[0], NODE_DEV - 1)
    raw = swap_values(raw, raw[1], 0)
    return raw


def mesh_tables(key):
    domains = CELLS // KZ
    keys = jax.random.split(jax.random.fold_in(key, 7), domains)
    perms = jax.vmap(domain_perm)(keys).astype(jnp.int32)
    cell = jnp.arange(KZ, dtype=jnp.int32)
    local = jnp.arange(NPC, dtype=jnp.int32)
    layer = ORDER * cell[:, None] + (local // FACE)[None, :]
    position = (local % FACE)[None, :] + 0 * layer
    natural = jnp.minimum(layer * FACE + position, NODE_DEV - 1)
    owned = jnp.take(perms, natural.reshape(-1), axis=1).reshape(domains, KZ, NPC)
    ghost = jnp.broadcast_to(NODE_DEV + position, (domains, KZ, NPC))
    top = jnp.broadcast_to(layer >= ORDER * KZ, (domains, KZ, NPC))
    conn = jnp.where(top, ghost, owned).astype(jnp.int32)
    faces = perms[:, :FACE]
    return (conn.reshape(CELLS, NPC), faces.reshape(-1).astype(jnp.int32))


def draw_connectivity(key, part):
    return mesh_tables(key)[0]


def draw_face_nodes(key, part):
    return mesh_tables(key)[1]


def draw_cell_hamiltonian(key, part):
    raw = jax.random.normal(jax.random.fold_in(key, 11), (CELLS, NPC, NPC), jnp.float32)
    sym = (raw + jnp.swapaxes(raw, 1, 2)) * (0.02 / 1.4142135)
    sym = jnp.clip(sym, -0.15, 0.15) + 0.3 * jnp.eye(NPC, dtype=jnp.float32)[None, :, :]
    return sym.astype(jnp.bfloat16)


def strengthened(values, stream_key, source, target, blocks, factor):
    def block_of(dim):
        return (jnp.arange(values.shape[dim]) // (values.shape[dim] // blocks)).reshape((-1,) + (1,) * (values.ndim - 1 - dim))

    near = jax.random.permutation(stream_key, blocks)[block_of(target)]
    other_side = (block_of(target) + blocks // 2) % blocks
    return jnp.where((block_of(source) == near) | (block_of(source) == other_side), factor * values, values)


def steps_of(stream_key, dims, shards, smallest, largest):
    loudness = 1.0
    for axis_at, parts in shards:
        heights = jax.random.uniform(jax.random.fold_in(jax.random.fold_in(stream_key, 6), axis_at), (parts,), jnp.float32, smallest / len(shards), largest / len(shards))
        loudness = loudness * jnp.repeat(jnp.exp(heights), dims[axis_at] // parts).reshape((-1,) + (1,) * (len(dims) - 1 - axis_at))
    return loudness


def gaussian_with(key, shape, deviation, limit, cuts, heavy, kind=jnp.bfloat16):
    entries = deviation * jax.random.normal(key, shape, jnp.float32)
    if cuts:
        entries = entries * steps_of(key, shape, cuts, -0.22, 0.18)
    return jnp.clip(strengthened(entries, jax.random.fold_in(key, 3), *heavy), -limit, limit).astype(kind)


def setup_inputs(seed: int = 0) -> dict:
    key_list = jax.random.split(jax.random.key(seed), 6)
    return {
        "orbitals": gaussian_with(key_list[0], (NODES, ORBITALS), 1.0, 6.0, ((0, 8), (1, 4)), (0, 1, 8, 2.0)),
        "potential": jnp.clip(jnp.exp(math.log(2.0) - 1.3862944 * jax.random.uniform(key_list[1], (NODES,), jnp.float32) ** steps_of(key_list[1], (NODES,), ((0, 8),), -0.2, 0.2)), 0.5, 2.0),
        "cell_hamiltonian": draw_cell_hamiltonian(jax.random.fold_in(key_list[5], 71), 0),
        "connectivity": draw_connectivity(jax.random.fold_in(key_list[5], 71), 0),
        "face_nodes": draw_face_nodes(jax.random.fold_in(key_list[5], 71), 0),
    }


filter_center = 1.5
filter_half = 2.0


def reference(orbitals, potential, cell_hamiltonian, connectivity, face_nodes):
    domains = CELLS // KZ
    owner = (jnp.arange(CELLS, dtype=jnp.int32) // KZ)[:, None]
    faces = face_nodes.reshape(domains, FACE)
    following = jnp.minimum(owner + 1, domains - 1)
    ghost_slot = jnp.clip(connectivity - NODE_DEV, 0, FACE - 1)
    ghost_node = faces[following, ghost_slot]
    remote = jnp.where(owner + 1 < domains, (owner + 1) * NODE_DEV + ghost_node, NODES)
    global_index = jnp.where(connectivity >= NODE_DEV, remote, owner * NODE_DEV + connectivity).astype(jnp.int32)
    cell_index = global_index.reshape(domains, KZ, NPC)
    matrices = cell_hamiltonian.reshape(domains, KZ, NPC, NPC)

    def apply_hamiltonian(values):
        padded = jnp.concatenate([values, jnp.zeros((1, ORBITALS), values.dtype)], axis=0)

        def add_domain(running, item):
            index, mats = item
            gathered = padded[index].astype(jnp.float32)
            products = jnp.einsum("kij,kjo->kio", mats.astype(jnp.float32), gathered)
            return running.at[index].add(products), None

        running, unused = lax.scan(add_domain, jnp.zeros((NODES + 1, ORBITALS), jnp.float32), (cell_index, matrices))
        return running[:NODES] + potential[:, None] * values.astype(jnp.float32)

    previous = orbitals
    image = apply_hamiltonian(previous)
    current = ((image - filter_center * previous.astype(jnp.float32)) / filter_half).astype(jnp.bfloat16)
    for step in range(DEGREE - 1):
        image = apply_hamiltonian(current)
        following_iter = (2.0 * (image - filter_center * current.astype(jnp.float32)) / filter_half - previous.astype(jnp.float32)).astype(jnp.bfloat16)
        previous, current = current, following_iter
    image = apply_hamiltonian(current).astype(jnp.bfloat16)
    projected = (jnp.dot(current.T, image, preferred_element_type=jnp.float32) / NODES).astype(jnp.bfloat16)
    residual = image.astype(jnp.float32) - jnp.dot(current, projected, preferred_element_type=jnp.float32)
    return residual, projected
```

```python
import functools

import jax
import jax.numpy as jnp
from jax import lax
from jax.experimental import pallas as pl
from jax.experimental.pallas import tpu as pltpu
from jax.sharding import PartitionSpec as P

DEGREE = 4
CENTER = 1.5
HALF = 2.0
F32 = jnp.float32
BF16 = jnp.bfloat16
VMEM_LIMIT = 50 * 1024 * 1024


def up16(n):
    return (n + 15) // 16 * 16


def iota(shape, dim):
    return lax.broadcasted_iota(jnp.int32, shape, dim).astype(F32)


def to_col(row, rows):
    n = row.shape[1]
    return jnp.sum(jnp.where(iota((rows, n), 0) == iota((rows, n), 1), row, 0.0), axis=1, keepdims=True)


def to_row(col):
    n = col.shape[0]
    return jnp.sum(jnp.where(iota((n, n), 0) == iota((n, n), 1), col, 0.0), axis=0, keepdims=True)


def params():
    return pltpu.CompilerParams(vmem_limit_bytes=VMEM_LIMIT)


def face_kernel(face_ref, x_ref, pot_ref, fv_ref, fp_ref):
    rows = fv_ref.shape[0]
    nodes = x_ref.shape[0]
    col = to_col(face_ref[...].astype(F32) + 1.0, rows) - 1.0
    hit = col == iota((rows, nodes), 1)
    fv_ref[...] = jnp.dot(hit.astype(BF16), x_ref[...], preferred_element_type=F32).astype(BF16)
    fp_ref[...] = jnp.sum(jnp.where(hit, pot_ref[...], 0.0), axis=1, keepdims=True)


def order_kernel(fp, ip, conn_ref, face_ref, h_ref, x_ref, pot_ref, hcan_ref, v_ref, potc_ref, node_ref):
    cells, npc = conn_ref.shape
    nodes = x_ref.shape[0]
    face = face_ref.shape[1]
    stride = fp + ip
    cp = stride + fp
    c = pl.program_id(0)
    last = cells - 1
    row = conn_ref[pl.ds(c, 1), :].astype(F32)
    row_n = conn_ref[pl.ds(jnp.minimum(c + 1, last), 1), :].astype(F32)
    row_p = conn_ref[pl.ds(jnp.maximum(c - 1, 0), 1), :].astype(F32)
    col, col_n, col_p = to_col(row, npc), to_col(row_n, npc), to_col(row_p, npc)
    less = jnp.where(col < row, 1.0, 0.0).astype(BF16)
    shared_n = jnp.max(jnp.where(col_n == row, 1.0, 0.0), axis=0, keepdims=True)
    shared_p = jnp.max(jnp.where(col_p == row, 1.0, 0.0), axis=0, keepdims=True)
    fcol = to_col(face_ref[...].astype(F32), face)
    fhit = fcol == row
    on_face = jnp.max(jnp.where(fhit, 1.0, 0.0), axis=0, keepdims=True)
    face_slot = jnp.sum(jnp.where(fhit, iota((face, npc), 0), 0.0), axis=0, keepdims=True)
    first_f = jnp.where(c == 0, 1.0, 0.0)
    last_f = jnp.where(c == last, 1.0, 0.0)
    ghost = jnp.where(row >= float(nodes), 1.0, 0.0)
    top = last_f * ghost + (1.0 - last_f) * shared_n
    bot = first_f * on_face + (1.0 - first_f) * shared_p
    mid = 1.0 - top - bot
    ri = lax.broadcasted_iota(jnp.int32, (8, npc), 0)
    flags = jnp.where(ri == 0, top, jnp.where(ri == 1, bot, jnp.where(ri == 2, mid, 0.0)))
    ranks = jnp.dot(flags.astype(BF16), less, preferred_element_type=F32)
    bot_slot = first_f * face_slot + (1.0 - first_f) * ranks[1:2]
    slot = jnp.where(top > 0.5, ranks[0:1] + float(stride), jnp.where(bot > 0.5, bot_slot, ranks[2:3] + float(fp)))
    perm = iota((cp, npc), 0) == slot
    perm_b = jnp.where(perm, 1.0, 0.0).astype(BF16)
    half = jnp.dot(perm_b, h_ref[0], preferred_element_type=F32).astype(BF16)
    hcan_ref[0] = lax.dot_general(half, perm_b, (((1,), (1,)), ((), ())), preferred_element_type=F32).astype(BF16)
    node = jnp.sum(jnp.where(perm, row + 1.0, 0.0), axis=1, keepdims=True) - 1.0
    node = node[:stride]
    node_ref[0] = to_row(node)
    hit = node == iota((stride, nodes), 1)
    v_ref[...] = jnp.dot(jnp.where(hit, 1.0, 0.0).astype(BF16), x_ref[...], preferred_element_type=F32).astype(BF16)
    potc_ref[...] = jnp.sum(jnp.where(hit, pot_ref[...], 0.0), axis=1, keepdims=True)


def advance(image, now, before):
    if before is None:
        return (image - CENTER * now) / HALF
    return 2.0 * (image - CENTER * now) / HALF - before


def edge_kernel(step, fp, *refs):
    if step == 0:
        last_ref, ghost_ref, yb_ref, yt_ref, hb_ref, ht_ref, yf_ref, pb_ref, pt_ref = refs
        yf_ref[:fp] = yb_ref[:fp]
        yf_ref[fp:] = ghost_ref[...]
    else:
        if step == 1:
            last_ref, sb_ref, st_ref, rb_ref, rt_ref, now_ref, potf_ref, *refs = refs
            before = None
        else:
            last_ref, sb_ref, st_ref, rb_ref, rt_ref, now_ref, potf_ref, before_ref, *refs = refs
            before = before_ref[...].astype(F32)
        yb_ref, yt_ref, hb_ref, ht_ref, yf_ref, pb_ref, pt_ref = refs
        now = now_ref[...].astype(F32)
        total = jnp.concatenate([sb_ref[...] + rb_ref[...], st_ref[...] + rt_ref[...]], axis=0)
        value = advance(total + potf_ref[...] * now, now, before)
        dead = (lax.broadcasted_iota(jnp.int32, value.shape, 0) >= fp) & (last_ref[0] == 1)
        yf_ref[...] = jnp.where(dead, 0.0, value).astype(BF16)
    low, high = yf_ref[:fp], yf_ref[fp:]
    pb_ref[...] = jnp.dot(
        hb_ref[0], jnp.concatenate([low, yb_ref[fp:]], axis=0), preferred_element_type=F32
    )
    pt_ref[...] = jnp.dot(
        ht_ref[0], jnp.concatenate([yt_ref[...], high], axis=0), preferred_element_type=F32
    )


def bulk_kernel(step, fp, *refs):
    if step == 0 or step == DEGREE:
        y_ref, yf_ref, h_ref, pot_ref, out_ref = refs
    else:
        y_ref, yf_ref, h_ref, pot_ref, before_ref, out_ref = refs
    cells, cp = h_ref.shape[:2]
    stride = cp - fp
    carry = None
    for c in range(cells):
        if c == 0:
            v = jnp.concatenate([yf_ref[:fp], y_ref[fp:cp]], axis=0)
        elif c == cells - 1:
            v = jnp.concatenate([y_ref[c * stride :], yf_ref[fp:]], axis=0)
        else:
            v = y_ref[c * stride : c * stride + cp]
        prod = jnp.dot(h_ref[c], v, preferred_element_type=F32)
        if c == 0:
            rows, lo = prod[fp:stride], fp
            out_ref[:fp] = jnp.zeros((fp, out_ref.shape[1]), BF16)
        else:
            rows, lo = jnp.concatenate([prod[:fp] + carry, prod[fp:stride]], axis=0), 0
        carry = prod[stride:]
        at = slice(c * stride + lo, (c + 1) * stride)
        now = v[lo:stride].astype(F32)
        image = rows + pot_ref[at] * now
        if step == DEGREE:
            out_ref[at] = image.astype(BF16)
        else:
            before = None if step == 0 else before_ref[at].astype(F32)
            out_ref[at] = advance(image, now, before).astype(BF16)


def back_kernel(fp, node_ref, y_ref, low_ref, out_ref):
    rows = out_ref.shape[1]
    want = (lax.broadcasted_iota(jnp.int32, (rows, 1), 0) + pl.program_id(0) * rows).astype(F32)
    hit = jnp.where(want == node_ref[...], 1.0, 0.0).astype(BF16)
    out = jnp.dot(hit, y_ref[...], preferred_element_type=F32)
    out = out + jnp.dot(hit[:, :fp], low_ref[...], preferred_element_type=F32)
    out_ref[0] = out.astype(BF16)


def back_image_kernel(fp, node_ref, y_ref, sb_ref, rb_ref, now_ref, pot_ref, out_ref):
    rows = out_ref.shape[1]
    low = (sb_ref[...] + rb_ref[...] + pot_ref[...] * now_ref[...].astype(F32)).astype(BF16)
    want = (lax.broadcasted_iota(jnp.int32, (rows, 1), 0) + pl.program_id(0) * rows).astype(F32)
    hit = jnp.where(want == node_ref[...], 1.0, 0.0).astype(BF16)
    out = jnp.dot(hit, y_ref[...], preferred_element_type=F32)
    out = out + jnp.dot(hit[:, :fp], low, preferred_element_type=F32)
    out_ref[0] = out.astype(BF16)


def gram_kernel(scale, x_ref, y_ref, out_ref, rows_ref):
    parts, _, width = y_ref.shape

    @pl.when(pl.program_id(0) == 0)
    def _():
        for j in range(parts):
            rows_ref[:, j * width : (j + 1) * width] = y_ref[j]

    out_ref[0] = (
        lax.dot_general(x_ref[0], rows_ref[...], (((0,), (0,)), ((), ())), preferred_element_type=F32) * scale
    ).astype(BF16)


def residual_kernel(x_ref, y_ref, p_ref, out_ref):
    parts, _, width = x_ref.shape
    x = jnp.concatenate([x_ref[j] for j in range(parts)], axis=1)
    y = jnp.concatenate([y_ref[j] for j in range(parts)], axis=1)
    out_ref[...] = y.astype(F32) - jnp.dot(x, p_ref[...], preferred_element_type=F32)


def full(shape):
    return pl.BlockSpec(shape, lambda i: (0,) * len(shape))


def swap(block, axis, bit):
    return lax.ppermute(block, axis, [(i, i ^ bit) for i in range(lax.axis_size(axis))])


def shift(block, axis, distance):
    n = lax.axis_size(axis)
    return lax.ppermute(block, axis, [(i, i + distance) for i in range(n) if 0 <= i + distance < n])


def body(orbitals, potential, cell_hamiltonian, connectivity, face_nodes):
    nodes, width = orbitals.shape
    cells, npc = connectivity.shape
    face = face_nodes.shape[0]
    fp, ip = up16(face), up16(npc - 2 * face)
    fp = (fp + 63) // 64 * 64
    stride = fp + ip
    cp = stride + fp
    total = cells * stride
    orb, dom = lax.axis_size("orb"), lax.axis_size("dom")
    d = lax.axis_index("dom")
    o = lax.axis_index("orb")
    sds = jax.ShapeDtypeStruct
    pot_row = potential.reshape(1, nodes)
    face_row = face_nodes.reshape(1, face)

    fv, fpot = pl.pallas_call(
        face_kernel,
        out_shape=(sds((fp, width), BF16), sds((fp, 1), F32)),
        compiler_params=params(),
    )(face_row, orbitals, pot_row)
    ghost = shift(fv, "dom", -1)
    ghost_pot = shift(fpot, "dom", -1)

    hcan, y, pot, node = pl.pallas_call(
        functools.partial(order_kernel, fp, ip),
        grid=(cells,),
        in_specs=[
            full((cells, npc)),
            full((1, face)),
            pl.BlockSpec((1, npc, npc), lambda c: (c, 0, 0)),
            full((nodes, width)),
            full((1, nodes)),
        ],
        out_specs=[
            pl.BlockSpec((1, cp, cp), lambda c: (c, 0, 0)),
            pl.BlockSpec((stride, width), lambda c: (c, 0)),
            pl.BlockSpec((stride, 1), lambda c: (c, 0)),
            pl.BlockSpec((1, 1, stride), lambda c: (c, 0, 0)),
        ],
        out_shape=[
            sds((cells, cp, cp), BF16),
            sds((total, width), BF16),
            sds((total, 1), F32),
            sds((cells, 1, stride), F32),
        ],
        compiler_params=params(),
        cost_estimate=pl.CostEstimate(flops=4 * total * nodes * width, bytes_accessed=8 << 20, transcendentals=0),
    )(connectivity, face_row, cell_hamiltonian, orbitals, pot_row)
    node_row = node.reshape(1, total)
    potf = jnp.concatenate([pot[:fp], ghost_pot], axis=0)
    is_last = (d == dom - 1).astype(jnp.int32).reshape(1)

    smem = pl.BlockSpec(memory_space=pltpu.SMEM)
    small = lambda: full((fp, width))
    end_specs = [
        pl.BlockSpec((cp, width), lambda i: (0, 0)),
        pl.BlockSpec((stride, width), lambda i: (cells - 1, 0)),
        pl.BlockSpec((1, fp, cp), lambda i: (0, 0, 0)),
        pl.BlockSpec((1, fp, cp), lambda i: (cells - 1, stride // fp, 0)),
    ]
    edge_out = dict(
        grid=(1,),
        out_specs=[full((2 * fp, width)), small(), small()],
        out_shape=[sds((2 * fp, width), BF16), sds((fp, width), F32), sds((fp, width), F32)],
        compiler_params=params(),
        cost_estimate=pl.CostEstimate(flops=4 * fp * cp * width, bytes_accessed=1 << 20, transcendentals=0),
    )
    bulk_cost = pl.CostEstimate(flops=2 * cells * cp * cp * width, bytes_accessed=6 << 20, transcendentals=0)

    before = yf_before = None
    yf = sums = None
    for step in range(DEGREE + 1):
        ends = [y, y, hcan, hcan]
        if step == 0:
            yf, sb, st = pl.pallas_call(
                functools.partial(edge_kernel, step, fp), in_specs=[smem, small()] + end_specs, **edge_out
            )(is_last, ghost, *ends)
        else:
            args = [sb, st, rb, rt, yf, potf] + ([yf_before] if step > 1 else [])
            specs = [small()] * 4 + [full((2 * fp, width)), full((2 * fp, 1))]
            specs += [full((2 * fp, width))] if step > 1 else []
            yf_new, sb, st = pl.pallas_call(
                functools.partial(edge_kernel, step, fp), in_specs=[smem] + specs + end_specs, **edge_out
            )(is_last, *args, *ends)
            yf_before, yf = yf, yf_new
        rb = shift(st, "dom", 1)
        if step < DEGREE:
            rt = shift(sb, "dom", -1)
        extra = [] if step in (0, DEGREE) else [before]
        out = pl.pallas_call(
            functools.partial(bulk_kernel, step, fp),
            out_shape=sds((total, width), BF16),
            compiler_params=params(),
            cost_estimate=bulk_cost,
        )(y, yf, hcan, pot, *extra)
        if step < DEGREE:
            before, y = y, out
    image = out

    back = dict(
        grid=(orb,),
        out_specs=pl.BlockSpec((1, nodes // orb, width), lambda i: (i, 0, 0)),
        out_shape=sds((orb, nodes // orb, width), BF16),
        compiler_params=params(),
        cost_estimate=pl.CostEstimate(flops=2 * total * nodes * width, bytes_accessed=4 << 20, transcendentals=0),
    )
    x_cols = pl.pallas_call(
        functools.partial(back_kernel, fp), in_specs=[full((1, total)), full((total, width)), small()], **back
    )(node_row, y, yf[:fp])
    x_rows = lax.all_to_all(x_cols, "orb", split_axis=0, concat_axis=0, tiled=True)
    i_cols = pl.pallas_call(
        functools.partial(back_image_kernel, fp),
        in_specs=[full((1, total)), full((total, width)), small(), small(), small(), full((fp, 1))],
        **back,
    )(node_row, image, sb, rb, yf[:fp], pot[:fp])
    i_rows = lax.all_to_all(i_cols, "orb", split_axis=0, concat_axis=0, tiled=True)

    rows = nodes // orb
    cols = orb * width
    share = pl.pallas_call(
        functools.partial(gram_kernel, 1.0 / (nodes * dom)),
        grid=(orb,),
        in_specs=[pl.BlockSpec((1, rows, width), lambda i: (i, 0, 0)), full((orb, rows, width))],
        out_specs=pl.BlockSpec((1, width, cols), lambda i: (i, 0, 0)),
        out_shape=sds((orb, width, cols), BF16),
        scratch_shapes=[pltpu.VMEM((rows, cols), BF16)],
        compiler_params=params(),
    )(x_rows, i_rows)

    hops = []
    for axis, me, size in (("orb", o, orb), ("dom", d, dom)):
        if axis == "dom":
            share = share.reshape(dom, width // dom, cols)
        bit = 1
        while bit < size:
            share = share.reshape((share.shape[0] // 2, 2) + share.shape[1:])
            mine = (me // bit) % 2
            keep = lax.dynamic_index_in_dim(share, mine, 1, keepdims=False)
            give = lax.dynamic_index_in_dim(share, 1 - mine, 1, keepdims=False)
            got = swap(give, axis, bit)
            share = (keep.astype(F32) + got.astype(F32)).astype(BF16)
            hops.append((axis, bit, mine))
            bit *= 2
    for axis, bit, mine in reversed(hops):
        if axis == "orb" and share.shape[0] == dom and bit * 2 == orb:
            share = share.reshape(1, width, cols)
        got = swap(share, axis, bit)
        share = jnp.where(mine == 0, jnp.stack([share, got], axis=1), jnp.stack([got, share], axis=1))
        share = share.reshape((share.shape[0] * 2,) + share.shape[2:])
    projected = share.reshape(cols, cols)

    residual = pl.pallas_call(
        residual_kernel, out_shape=sds((rows, cols), F32), compiler_params=params()
    )(x_rows, i_rows, projected)
    return (residual, projected)


def solution(mesh):
    return jax.shard_map(
        body,
        mesh=mesh,
        in_specs=(P("dom", "orb"), P("dom"), P("dom", None, None), P("dom", None), P("dom")),
        out_specs=(P(("dom", "orb"), None), P()),
        check_vma=False,
    )
```

```python
import functools

import jax
import jax.numpy as jnp
from jax import lax
from jax.experimental import pallas as pl
from jax.experimental.pallas import tpu as pltpu
from jax.sharding import PartitionSpec as P

DEGREE = 4
CENTER = 1.5
HALF = 2.0
F32 = jnp.float32
BF16 = jnp.bfloat16
VMEM_LIMIT = 50 * 1024 * 1024


def up16(n):
    return (n + 15) // 16 * 16


def iota(shape, dim):
    return lax.broadcasted_iota(jnp.int32, shape, dim).astype(F32)


def to_col(row, rows):
    n = row.shape[1]
    return jnp.sum(jnp.where(iota((rows, n), 0) == iota((rows, n), 1), row, 0.0), axis=1, keepdims=True)


def to_row(col):
    n = col.shape[0]
    return jnp.sum(jnp.where(iota((n, n), 0) == iota((n, n), 1), col, 0.0), axis=0, keepdims=True)


def params():
    return pltpu.CompilerParams(vmem_limit_bytes=VMEM_LIMIT)


def face_kernel(face_ref, x_ref, pot_ref, fv_ref, fp_ref):
    rows = fv_ref.shape[0]
    nodes = x_ref.shape[0]
    col = to_col(face_ref[...].astype(F32) + 1.0, rows) - 1.0
    hit = col == iota((rows, nodes), 1)
    fv_ref[...] = jnp.dot(hit.astype(BF16), x_ref[...], preferred_element_type=F32).astype(BF16)
    fp_ref[...] = jnp.sum(jnp.where(hit, pot_ref[...], 0.0), axis=1, keepdims=True)


def order_kernel(fp, ip, conn_ref, face_ref, h_ref, x_ref, pot_ref, hcan_ref, v_ref, potc_ref, node_ref):
    cells, npc = conn_ref.shape
    nodes = x_ref.shape[0]
    face = face_ref.shape[1]
    stride = fp + ip
    cp = stride + fp
    c = pl.program_id(0)
    last = cells - 1
    row = conn_ref[pl.ds(c, 1), :].astype(F32)
    row_n = conn_ref[pl.ds(jnp.minimum(c + 1, last), 1), :].astype(F32)
    row_p = conn_ref[pl.ds(jnp.maximum(c - 1, 0), 1), :].astype(F32)
    col, col_n, col_p = to_col(row, npc), to_col(row_n, npc), to_col(row_p, npc)
    less = jnp.where(col < row, 1.0, 0.0).astype(BF16)
    shared_n = jnp.max(jnp.where(col_n == row, 1.0, 0.0), axis=0, keepdims=True)
    shared_p = jnp.max(jnp.where(col_p == row, 1.0, 0.0), axis=0, keepdims=True)
    fcol = to_col(face_ref[...].astype(F32), face)
    fhit = fcol == row
    on_face = jnp.max(jnp.where(fhit, 1.0, 0.0), axis=0, keepdims=True)
    face_slot = jnp.sum(jnp.where(fhit, iota((face, npc), 0), 0.0), axis=0, keepdims=True)
    first_f = jnp.where(c == 0, 1.0, 0.0)
    last_f = jnp.where(c == last, 1.0, 0.0)
    ghost = jnp.where(row >= float(nodes), 1.0, 0.0)
    top = last_f * ghost + (1.0 - last_f) * shared_n
    bot = first_f * on_face + (1.0 - first_f) * shared_p
    mid = 1.0 - top - bot
    ri = lax.broadcasted_iota(jnp.int32, (8, npc), 0)
    flags = jnp.where(ri == 0, top, jnp.where(ri == 1, bot, jnp.where(ri == 2, mid, 0.0)))
    ranks = jnp.dot(flags.astype(BF16), less, preferred_element_type=F32)
    bot_slot = first_f * face_slot + (1.0 - first_f) * ranks[1:2]
    slot = jnp.where(top > 0.5, ranks[0:1] + float(stride), jnp.where(bot > 0.5, bot_slot, ranks[2:3] + float(fp)))
    perm = iota((cp, npc), 0) == slot
    perm_b = jnp.where(perm, 1.0, 0.0).astype(BF16)
    half = jnp.dot(perm_b, h_ref[0], preferred_element_type=F32).astype(BF16)
    hcan_ref[0] = lax.dot_general(half, perm_b, (((1,), (1,)), ((), ())), preferred_element_type=F32).astype(BF16)
    node = jnp.sum(jnp.where(perm, row + 1.0, 0.0), axis=1, keepdims=True) - 1.0
    node = node[:stride]
    node_ref[0] = to_row(node)
    hit = node == iota((stride, nodes), 1)
    v_ref[...] = jnp.dot(jnp.where(hit, 1.0, 0.0).astype(BF16), x_ref[...], preferred_element_type=F32).astype(BF16)
    potc_ref[...] = jnp.sum(jnp.where(hit, pot_ref[...], 0.0), axis=1, keepdims=True)


def advance(image, now, before):
    if before is None:
        return (image - CENTER * now) / HALF
    return 2.0 * (image - CENTER * now) / HALF - before


def split(a):
    high = a.astype(BF16)
    return high, (a - high.astype(F32)).astype(BF16)


def mul(a, b):
    return jnp.dot(a, b, preferred_element_type=F32)


def mul_r(a, b):
    high, low = split(b)
    return mul(a, high) + mul(a, low)


def sweep(h_ref, y_ref, fp, emit):
    cells, cp = h_ref.shape[:2]
    stride = cp - fp
    carry = None
    for c in range(cells):
        prod = mul(h_ref[c], y_ref[c * stride : c * stride + cp])
        rows = prod[:stride]
        if c > 0:
            rows = jnp.concatenate([rows[:fp] + carry, rows[fp:]], axis=0)
        carry = prod[stride:]
        emit(c, rows)
    return carry


def response(hc, hn, potc, fp, upper):
    cp = hc.shape[0]
    stride = cp - fp
    if upper:
        f, r, s, g = slice(stride, cp), slice(0, stride), slice(0, fp), slice(stride, cp)
        rest = slice(0, stride)
    else:
        f, r, s, g = slice(0, fp), slice(fp, cp), slice(stride - fp, stride), slice(0, fp)
        rest = slice(fp, cp)
    gain = 2.0 / HALF
    out = [hc[f, f].astype(F32)]
    one = gain * hc[r, f].astype(F32)
    out.append(mul_r(hc[f, r], one))

    def pad_next(face_rows):
        zero = jnp.zeros((stride, fp), F32)
        return jnp.concatenate([zero, face_rows] if upper else [face_rows, zero], axis=0)

    def near(value, next_value):
        got = mul_r(hc[r, r], value) + (potc - CENTER) * value
        add = mul_r(hn[g, :], next_value)
        if upper:
            return jnp.concatenate([got[:fp] + add, got[fp:]], axis=0)
        return jnp.concatenate([got[: stride - fp], got[stride - fp :] + add], axis=0)

    two = gain * near(one, pad_next(one[s]))
    out.append(mul_r(hc[f, r], two))
    two_next = gain * mul_r(hn, pad_next(one[s]))
    if upper:
        two_next = jnp.concatenate([two_next[:stride], two[s]], axis=0)
    else:
        two_next = jnp.concatenate([two[s], two_next[fp:]], axis=0)
    three = gain * near(two, two_next) - one
    out.append(mul_r(hc[f, r], three))
    return out


def store_matrices(mats, out_ref, at, fp, width):
    for part in range(2):
        for j, m in enumerate(mats):
            block, lane = divmod((part * len(mats) + j) * fp, width)
            out_ref[at + block, :, lane : lane + fp] = split(m)[part]


def load_matrices(ref, at, count, fp, width):
    out = []
    for j in range(count):
        pieces = []
        for part in range(2):
            block, lane = divmod((part * count + j) * fp, width)
            pieces.append(ref[at + block, :, lane : lane + fp].astype(F32))
        out.append(pieces[0] + pieces[1])
    return out


def free_kernel(fp, v_ref, ghost_ref, h_ref, pot_ref, first_ref, own_ref, up_ref, down_ref, a_ref, b_ref):
    cells, cp = h_ref.shape[:2]
    stride = cp - fp
    total = cells * stride
    width = v_ref.shape[1]
    a_ref[:total] = v_ref[...]
    a_ref[total:] = ghost_ref[...]
    b_ref[total:] = jnp.zeros((fp, width), BF16)

    def keep(k, low, high):
        own_ref[0, k] = low
        own_ref[1, k] = high
        down_ref[k] = low.astype(BF16)
        up_ref[k] = high.astype(BF16)

    now_ref, other_ref = a_ref, b_ref
    for k in range(DEGREE):
        ends = {}

        def emit(c, rows, k=k, now_ref=now_ref, other_ref=other_ref, ends=ends):
            at = slice(c * stride, (c + 1) * stride)
            if c == 0:
                ends["low"] = rows[:fp]
            now = now_ref[at].astype(F32)
            before = None if k == 0 else other_ref[at].astype(F32)
            if k == 1:
                before = v_ref[at].astype(F32)
            value = advance(rows + pot_ref[at] * now, now, before).astype(BF16)
            if c == 0:
                value = jnp.concatenate([jnp.zeros((fp, width), BF16), value[fp:]], axis=0)
            if k == 0:
                first_ref[at] = value
            other_ref[at] = value

        high = sweep(h_ref, now_ref, fp, emit)
        keep(k, ends["low"], high)
        if k == 0:
            a_ref[total:] = jnp.zeros((fp, width), BF16)
        now_ref, other_ref = other_ref, now_ref
    keep(DEGREE, mul(h_ref[0, :fp], now_ref[:cp]), mul(h_ref[cells - 1, stride:], now_ref[total - stride :]))
    low = response(h_ref[0], h_ref[1], pot_ref[fp:cp], fp, False)
    high = response(h_ref[cells - 1], h_ref[cells - 2], pot_ref[total - stride :], fp, True)
    store_matrices(low, down_ref, DEGREE + 1, fp, width)
    store_matrices(high, up_ref, DEGREE + 1, fp, width)
    count = len(low)
    for side, mats in enumerate((low, high)):
        for j, m in enumerate(mats):
            own_ref_at = (DEGREE + 1) * 0
            block, lane = divmod(j * fp, width)
            own_ref[side, DEGREE + 1 + block + own_ref_at, :, lane : lane + fp] = m


def forced_kernel(fp, dead_ref, v_ref, ghost_ref, first_ref, own_ref, fromleft_ref, fromright_ref, h_ref, pot_ref, potg_ref, x_ref, image_ref, a_ref, b_ref, c_ref):
    cells, cp = h_ref.shape[:2]
    stride = cp - fp
    total = cells * stride
    width = v_ref.shape[1]
    histories = []
    last_image = None
    for side, (got_ref, pot, start) in enumerate(
        ((fromleft_ref, pot_ref[:fp], v_ref[:fp]), (fromright_ref, potg_ref[...], ghost_ref[...]))
    ):
        mats = load_matrices(got_ref, DEGREE + 1, DEGREE, fp, width)
        for j in range(DEGREE):
            block, lane = divmod(j * fp, width)
            mats[j] = mats[j] + own_ref[side, DEGREE + 1 + block, :, lane : lane + fp]
        mats = [split(m) for m in mats]
        values = [start]
        for k in range(DEGREE + 1 if side == 0 else DEGREE):
            h = own_ref[side, k] + got_ref[k].astype(F32)
            for m in range(1, k + 1):
                h = h + mul(mats[k - m][0], values[m]) + mul(mats[k - m][1], values[m])
            now = values[k].astype(F32)
            h = h + pot * now
            if k == DEGREE:
                last_image = h
                break
            value = advance(h, now, None if k == 0 else values[k - 1].astype(F32))
            if side == 1:
                value = jnp.where(dead_ref[0] == 1, 0.0, value)
            values.append(value.astype(BF16))
        histories.append(values)
    low, high = histories
    a_ref[:fp] = low[1]
    a_ref[fp:total] = first_ref[fp:]
    a_ref[total:] = high[1]
    refs = [None, a_ref, b_ref, c_ref, a_ref]
    for k in range(1, DEGREE + 1):
        now_ref = refs[k]

        def emit(c, rows, k=k, now_ref=now_ref):
            at = slice(c * stride, (c + 1) * stride)
            now = now_ref[at].astype(F32)
            image = rows + pot_ref[at] * now
            if k == DEGREE:
                out = image.astype(BF16)
                if c == 0:
                    out = jnp.concatenate([last_image.astype(BF16), out[fp:]], axis=0)
                image_ref[at] = out
                return
            before = (v_ref if k == 1 else refs[k - 1])[at].astype(F32)
            value = advance(image, now, before).astype(BF16)
            if c == 0:
                value = jnp.concatenate([low[k + 1], value[fp:]], axis=0)
            refs[k + 1][at] = value
            if k + 1 == DEGREE:
                x_ref[at] = value

        sweep(h_ref, now_ref, fp, emit)
        if k < DEGREE:
            refs[k + 1][total:] = high[k + 1]


def back_kernel(node_ref, y_ref, out_ref):
    rows = out_ref.shape[1]
    want = (lax.broadcasted_iota(jnp.int32, (rows, 1), 0) + pl.program_id(0) * rows).astype(F32)
    hit = jnp.where(want == node_ref[...], 1.0, 0.0).astype(BF16)
    out_ref[0] = mul(hit, y_ref[...]).astype(BF16)


def gram_kernel(scale, x_ref, y_ref, out_ref, rows_ref):
    parts, _, width = y_ref.shape

    @pl.when(pl.program_id(0) == 0)
    def _():
        for j in range(parts):
            rows_ref[:, j * width : (j + 1) * width] = y_ref[j]

    out_ref[0] = (
        lax.dot_general(x_ref[0], rows_ref[...], (((0,), (0,)), ((), ())), preferred_element_type=F32) * scale
    )


def residual_kernel(x_ref, y_ref, p_ref, out_ref):
    parts, _, width = x_ref.shape
    x = jnp.concatenate([x_ref[j] for j in range(parts)], axis=1)
    y = jnp.concatenate([y_ref[j] for j in range(parts)], axis=1)
    out_ref[...] = y.astype(F32) - jnp.dot(x, p_ref[...], preferred_element_type=F32)


def full(shape):
    return pl.BlockSpec(shape, lambda i: (0,) * len(shape))


def swap(block, axis, bit):
    return lax.ppermute(block, axis, [(i, i ^ bit) for i in range(lax.axis_size(axis))])


def shift(block, axis, distance):
    n = lax.axis_size(axis)
    return lax.ppermute(block, axis, [(i, i + distance) for i in range(n) if 0 <= i + distance < n])


def body(orbitals, potential, cell_hamiltonian, connectivity, face_nodes):
    nodes, width = orbitals.shape
    cells, npc = connectivity.shape
    face = face_nodes.shape[0]
    fp, ip = up16(face), up16(npc - 2 * face)
    fp = (fp + 63) // 64 * 64
    stride = fp + ip
    cp = stride + fp
    total = cells * stride
    orb, dom = lax.axis_size("orb"), lax.axis_size("dom")
    d = lax.axis_index("dom")
    o = lax.axis_index("orb")
    sds = jax.ShapeDtypeStruct
    pot_row = potential.reshape(1, nodes)
    face_row = face_nodes.reshape(1, face)

    fv, fpot = pl.pallas_call(
        face_kernel,
        out_shape=(sds((fp, width), BF16), sds((fp, 1), F32)),
        compiler_params=params(),
    )(face_row, orbitals, pot_row)
    ghost = shift(fv, "dom", -1)
    ghost_pot = shift(fpot, "dom", -1)

    hcan, y, pot, node = pl.pallas_call(
        functools.partial(order_kernel, fp, ip),
        grid=(cells,),
        in_specs=[
            full((cells, npc)),
            full((1, face)),
            pl.BlockSpec((1, npc, npc), lambda c: (c, 0, 0)),
            full((nodes, width)),
            full((1, nodes)),
        ],
        out_specs=[
            pl.BlockSpec((1, cp, cp), lambda c: (c, 0, 0)),
            pl.BlockSpec((stride, width), lambda c: (c, 0)),
            pl.BlockSpec((stride, 1), lambda c: (c, 0)),
            pl.BlockSpec((1, 1, stride), lambda c: (c, 0, 0)),
        ],
        out_shape=[
            sds((cells, cp, cp), BF16),
            sds((total, width), BF16),
            sds((total, 1), F32),
            sds((cells, 1, stride), F32),
        ],
        compiler_params=params(),
        cost_estimate=pl.CostEstimate(flops=4 * total * nodes * width, bytes_accessed=8 << 20, transcendentals=0),
    )(connectivity, face_row, cell_hamiltonian, orbitals, pot_row)
    node_row = node.reshape(1, total)
    dead = (d == dom - 1).astype(jnp.int32).reshape(1)

    extra = -(-DEGREE * fp // width)
    sent = DEGREE + 1 + -(-2 * DEGREE * fp // width)
    ext = pltpu.VMEM((total + fp, width), BF16)
    cost = pl.CostEstimate(
        flops=2 * DEGREE * cells * cp * cp * width, bytes_accessed=8 << 20, transcendentals=0
    )
    first, own, up, down = pl.pallas_call(
        functools.partial(free_kernel, fp),
        out_shape=[
            sds((total, width), BF16),
            sds((2, DEGREE + 1 + extra, fp, width), F32),
            sds((sent, fp, width), BF16),
            sds((sent, fp, width), BF16),
        ],
        scratch_shapes=[ext, ext],
        compiler_params=params(),
        cost_estimate=cost,
    )(y, ghost, hcan, pot)
    from_left = shift(up, "dom", 1)
    from_right = shift(down, "dom", -1)
    vmem = pl.BlockSpec(memory_space=pltpu.VMEM)
    x_own, image = pl.pallas_call(
        functools.partial(forced_kernel, fp),
        in_specs=[pl.BlockSpec(memory_space=pltpu.SMEM)] + [vmem] * 9,
        out_shape=[sds((total, width), BF16)] * 2,
        scratch_shapes=[ext, ext, ext],
        compiler_params=params(),
        cost_estimate=cost,
    )(dead, y, ghost, first, own, from_left, from_right, hcan, pot, ghost_pot)

    back = pl.pallas_call(
        back_kernel,
        grid=(orb,),
        in_specs=[full((1, total)), full((total, width))],
        out_specs=pl.BlockSpec((1, nodes // orb, width), lambda i: (i, 0, 0)),
        out_shape=sds((orb, nodes // orb, width), BF16),
        compiler_params=params(),
        cost_estimate=pl.CostEstimate(flops=2 * total * nodes * width, bytes_accessed=4 << 20, transcendentals=0),
    )
    x_rows = lax.all_to_all(back(node_row, x_own), "orb", split_axis=0, concat_axis=0, tiled=True)
    i_rows = lax.all_to_all(back(node_row, image), "orb", split_axis=0, concat_axis=0, tiled=True)

    rows = nodes // orb
    cols = orb * width
    share = pl.pallas_call(
        functools.partial(gram_kernel, 1.0 / (nodes * dom)),
        grid=(orb,),
        in_specs=[pl.BlockSpec((1, rows, width), lambda i: (i, 0, 0)), full((orb, rows, width))],
        out_specs=pl.BlockSpec((1, width, cols), lambda i: (i, 0, 0)),
        out_shape=sds((orb, width, cols), F32),
        scratch_shapes=[pltpu.VMEM((rows, cols), BF16)],
        compiler_params=params(),
    )(x_rows, i_rows)

    hops = []
    for axis, me, size in (("orb", o, orb), ("dom", d, dom)):
        if axis == "dom":
            share = share.reshape(dom, width // dom, cols)
        bit = 1
        while bit < size:
            share = share.reshape((share.shape[0] // 2, 2) + share.shape[1:])
            mine = (me // bit) % 2
            keep = lax.dynamic_index_in_dim(share, mine, 1, keepdims=False)
            give = lax.dynamic_index_in_dim(share, 1 - mine, 1, keepdims=False)
            got = swap(give.astype(BF16), axis, bit)
            share = keep + got.astype(F32)
            hops.append((axis, bit, mine))
            bit *= 2
    share = share.astype(BF16)
    for axis, bit, mine in reversed(hops):
        if axis == "orb" and share.shape[0] == dom and bit * 2 == orb:
            share = share.reshape(1, width, cols)
        got = swap(share, axis, bit)
        share = jnp.where(mine == 0, jnp.stack([share, got], axis=1), jnp.stack([got, share], axis=1))
        share = share.reshape((share.shape[0] * 2,) + share.shape[2:])
    projected = share.reshape(cols, cols)

    residual = pl.pallas_call(
        residual_kernel, out_shape=sds((rows, cols), F32), compiler_params=params()
    )(x_rows, i_rows, projected)
    return (residual, projected)


def solution(mesh):
    return jax.shard_map(
        body,
        mesh=mesh,
        in_specs=(P("dom", "orb"), P("dom"), P("dom", None, None), P("dom", None), P("dom")),
        out_specs=(P(("dom", "orb"), None), P()),
        check_vma=False,
    )
```

```python
import functools

import jax
import jax.numpy as jnp
from jax import lax
from jax.experimental import pallas as pl
from jax.experimental.pallas import tpu as pltpu
from jax.sharding import PartitionSpec as P

DEGREE = 4
CENTER = 1.5
HALF = 2.0
F32 = jnp.float32
BF16 = jnp.bfloat16
VMEM_LIMIT = 50 * 1024 * 1024


def up16(n):
    return (n + 15) // 16 * 16


def iota(shape, dim):
    return lax.broadcasted_iota(jnp.int32, shape, dim).astype(F32)


def to_col(row, rows):
    n = row.shape[1]
    return jnp.sum(jnp.where(iota((rows, n), 0) == iota((rows, n), 1), row, 0.0), axis=1, keepdims=True)


def to_row(col):
    n = col.shape[0]
    return jnp.sum(jnp.where(iota((n, n), 0) == iota((n, n), 1), col, 0.0), axis=0, keepdims=True)


def params():
    return pltpu.CompilerParams(vmem_limit_bytes=VMEM_LIMIT)


def face_kernel(face_ref, x_ref, pot_ref, fv_ref, fp_ref):
    rows = fv_ref.shape[0]
    nodes = x_ref.shape[0]
    col = to_col(face_ref[...].astype(F32) + 1.0, rows) - 1.0
    hit = col == iota((rows, nodes), 1)
    fv_ref[...] = jnp.dot(hit.astype(BF16), x_ref[...], preferred_element_type=F32).astype(BF16)
    fp_ref[...] = jnp.sum(jnp.where(hit, pot_ref[...], 0.0), axis=1, keepdims=True)


def order_kernel(fp, ip, conn_ref, face_ref, h_ref, x_ref, pot_ref, hcan_ref, v_ref, potc_ref, node_ref):
    cells, npc = conn_ref.shape
    nodes = x_ref.shape[0]
    face = face_ref.shape[1]
    stride = fp + ip
    cp = stride + fp
    c = pl.program_id(0)
    last = cells - 1
    row = conn_ref[pl.ds(c, 1), :].astype(F32)
    row_n = conn_ref[pl.ds(jnp.minimum(c + 1, last), 1), :].astype(F32)
    row_p = conn_ref[pl.ds(jnp.maximum(c - 1, 0), 1), :].astype(F32)
    col, col_n, col_p = to_col(row, npc), to_col(row_n, npc), to_col(row_p, npc)
    less = jnp.where(col < row, 1.0, 0.0).astype(BF16)
    shared_n = jnp.max(jnp.where(col_n == row, 1.0, 0.0), axis=0, keepdims=True)
    shared_p = jnp.max(jnp.where(col_p == row, 1.0, 0.0), axis=0, keepdims=True)
    fcol = to_col(face_ref[...].astype(F32), face)
    fhit = fcol == row
    on_face = jnp.max(jnp.where(fhit, 1.0, 0.0), axis=0, keepdims=True)
    face_slot = jnp.sum(jnp.where(fhit, iota((face, npc), 0), 0.0), axis=0, keepdims=True)
    first_f = jnp.where(c == 0, 1.0, 0.0)
    last_f = jnp.where(c == last, 1.0, 0.0)
    ghost = jnp.where(row >= float(nodes), 1.0, 0.0)
    top = last_f * ghost + (1.0 - last_f) * shared_n
    bot = first_f * on_face + (1.0 - first_f) * shared_p
    mid = 1.0 - top - bot
    ri = lax.broadcasted_iota(jnp.int32, (8, npc), 0)
    flags = jnp.where(ri == 0, top, jnp.where(ri == 1, bot, jnp.where(ri == 2, mid, 0.0)))
    ranks = jnp.dot(flags.astype(BF16), less, preferred_element_type=F32)
    bot_slot = first_f * face_slot + (1.0 - first_f) * ranks[1:2]
    slot = jnp.where(top > 0.5, ranks[0:1] + float(stride), jnp.where(bot > 0.5, bot_slot, ranks[2:3] + float(fp)))
    perm = iota((cp, npc), 0) == slot
    perm_b = jnp.where(perm, 1.0, 0.0).astype(BF16)
    half = jnp.dot(perm_b, h_ref[0], preferred_element_type=F32).astype(BF16)
    hcan_ref[0] = lax.dot_general(half, perm_b, (((1,), (1,)), ((), ())), preferred_element_type=F32).astype(BF16)
    node = jnp.sum(jnp.where(perm, row + 1.0, 0.0), axis=1, keepdims=True) - 1.0
    node = node[:stride]
    node_ref[0] = to_row(node)
    hit = node == iota((stride, nodes), 1)
    v_ref[...] = jnp.dot(jnp.where(hit, 1.0, 0.0).astype(BF16), x_ref[...], preferred_element_type=F32).astype(BF16)
    potc_ref[...] = jnp.sum(jnp.where(hit, pot_ref[...], 0.0), axis=1, keepdims=True)


def advance(image, now, before):
    if before is None:
        return (image - CENTER * now) / HALF
    return 2.0 * (image - CENTER * now) / HALF - before


def split(a):
    high = a.astype(BF16)
    return high, (a - high.astype(F32)).astype(BF16)


def mul(a, b):
    return jnp.dot(a, b, preferred_element_type=F32)


def mul_r(a, b):
    high, low = split(b)
    return mul(a, high) + mul(a, low)


def sweep(h_ref, y_ref, fp, emit):
    cells, cp = h_ref.shape[:2]
    stride = cp - fp
    carry = None
    for c in range(cells):
        prod = mul(h_ref[c], y_ref[c * stride : c * stride + cp])
        rows = prod[:stride]
        if c > 0:
            rows = jnp.concatenate([rows[:fp] + carry, rows[fp:]], axis=0)
        emit(c, rows, prod[:fp], carry)
        carry = prod[stride:]
    return carry


def response(hc, hn, potc, fp, upper):
    cp = hc.shape[0]
    stride = cp - fp
    if upper:
        f, r, s, g = slice(stride, cp), slice(0, stride), slice(0, fp), slice(stride, cp)
        rest = slice(0, stride)
    else:
        f, r, s, g = slice(0, fp), slice(fp, cp), slice(stride - fp, stride), slice(0, fp)
        rest = slice(fp, cp)
    gain = 2.0 / HALF
    out = [hc[f, f].astype(F32)]
    one = gain * hc[r, f].astype(F32)
    out.append(mul_r(hc[f, r], one))

    def pad_next(face_rows):
        zero = jnp.zeros((stride, fp), F32)
        return jnp.concatenate([zero, face_rows] if upper else [face_rows, zero], axis=0)

    def near(value, next_value):
        got = mul_r(hc[r, r], value) + (potc - CENTER) * value
        add = mul_r(hn[g, :], next_value)
        if upper:
            return jnp.concatenate([got[:fp] + add, got[fp:]], axis=0)
        return jnp.concatenate([got[: stride - fp], got[stride - fp :] + add], axis=0)

    two = gain * near(one, pad_next(one[s]))
    out.append(mul_r(hc[f, r], two))
    two_next = gain * mul_r(hn, pad_next(one[s]))
    if upper:
        two_next = jnp.concatenate([two_next[:stride], two[s]], axis=0)
    else:
        two_next = jnp.concatenate([two[s], two_next[fp:]], axis=0)
    three = gain * near(two, two_next) - one
    out.append(mul_r(hc[f, r], three))
    return out


def store_matrices(mats, out_ref, at, fp, width):
    for part in range(2):
        for j, m in enumerate(mats):
            block, lane = divmod((part * len(mats) + j) * fp, width)
            out_ref[at + block, :, lane : lane + fp] = split(m)[part]


def load_matrices(ref, at, count, fp, width):
    out = []
    for j in range(count):
        pieces = []
        for part in range(2):
            block, lane = divmod((part * count + j) * fp, width)
            pieces.append(ref[at + block, :, lane : lane + fp].astype(F32))
        out.append(pieces[0] + pieces[1])
    return out


def free_kernel(fp, v_ref, ghost_ref, h_ref, pot_ref, first_ref, own_ref, up_ref, down_ref, a_ref, b_ref):
    cells, cp = h_ref.shape[:2]
    stride = cp - fp
    total = cells * stride
    width = v_ref.shape[1]
    a_ref[:total] = v_ref[...]
    a_ref[total:] = ghost_ref[...]
    b_ref[total:] = jnp.zeros((fp, width), BF16)

    def keep(k, low, high):
        own_ref[0, k] = low
        own_ref[1, k] = high
        down_ref[k] = low.astype(BF16)
        up_ref[k] = high.astype(BF16)

    now_ref, other_ref = a_ref, b_ref
    for k in range(DEGREE):
        ends = {}

        def emit(c, rows, lower, carry, k=k, now_ref=now_ref, other_ref=other_ref, ends=ends):
            at = slice(c * stride, (c + 1) * stride)
            if c == 0:
                ends["low"] = rows[:fp]
            now = now_ref[at].astype(F32)
            before = None if k == 0 else other_ref[at].astype(F32)
            if k == 1:
                before = v_ref[at].astype(F32)
            value = advance(rows + pot_ref[at] * now, now, before).astype(BF16)
            if c == 0:
                value = jnp.concatenate([jnp.zeros((fp, width), BF16), value[fp:]], axis=0)
            if k == 0:
                first_ref[at] = value
            other_ref[at] = value

        high = sweep(h_ref, now_ref, fp, emit)
        keep(k, ends["low"], high)
        if k == 0:
            a_ref[total:] = jnp.zeros((fp, width), BF16)
        now_ref, other_ref = other_ref, now_ref
    keep(DEGREE, mul(h_ref[0, :fp], now_ref[:cp]), mul(h_ref[cells - 1, stride:], now_ref[total - stride :]))
    low = response(h_ref[0], h_ref[1], pot_ref[fp:cp], fp, False)
    high = response(h_ref[cells - 1], h_ref[cells - 2], pot_ref[total - stride :], fp, True)
    store_matrices(low, down_ref, DEGREE + 1, fp, width)
    store_matrices(high, up_ref, DEGREE + 1, fp, width)
    count = len(low)
    for side, mats in enumerate((low, high)):
        for j, m in enumerate(mats):
            own_ref_at = (DEGREE + 1) * 0
            block, lane = divmod(j * fp, width)
            own_ref[side, DEGREE + 1 + block + own_ref_at, :, lane : lane + fp] = m


def forced_kernel(fp, dead_ref, v_ref, ghost_ref, first_ref, own_ref, fromleft_ref, fromright_ref, h_ref, pot_ref, potg_ref, x_ref, image_ref, w_ref, a_ref, b_ref, c_ref):
    cells, cp = h_ref.shape[:2]
    stride = cp - fp
    total = cells * stride
    width = v_ref.shape[1]
    half = cells // 2
    histories = []
    last_image = None
    for side, (got_ref, pot, start) in enumerate(
        ((fromleft_ref, pot_ref[:fp], v_ref[:fp]), (fromright_ref, potg_ref[...], ghost_ref[...]))
    ):
        mats = load_matrices(got_ref, DEGREE + 1, DEGREE, fp, width)
        for j in range(DEGREE):
            block, lane = divmod(j * fp, width)
            mats[j] = mats[j] + own_ref[side, DEGREE + 1 + block, :, lane : lane + fp]
        mats = [split(m) for m in mats]
        values = [start]
        for k in range(DEGREE + 1 if side == 0 else DEGREE):
            h = own_ref[side, k] + got_ref[k].astype(F32)
            for m in range(1, k + 1):
                h = h + mul(mats[k - m][0], values[m]) + mul(mats[k - m][1], values[m])
            now = values[k].astype(F32)
            h = h + pot * now
            if k == DEGREE:
                last_image = h
                break
            value = advance(h, now, None if k == 0 else values[k - 1].astype(F32))
            if side == 1:
                value = jnp.where(dead_ref[0] == 1, 0.0, value)
            values.append(value.astype(BF16))
        histories.append(values)
    low, high = histories
    a_ref[:fp] = low[1]
    a_ref[fp:total] = first_ref[fp:]
    a_ref[total:] = high[1]
    refs = [None, a_ref, b_ref, c_ref, a_ref]
    for k in range(1, DEGREE + 1):
        now_ref = refs[k]

        def emit(c, rows, lower, carry, k=k, now_ref=now_ref):
            at = slice(c * stride, (c + 1) * stride)
            now = now_ref[at].astype(F32)
            image = rows + pot_ref[at] * now
            if k == DEGREE:
                out = image.astype(BF16)
                part, at_w = divmod(c, half)
                w_ref[part, at_w * stride : (at_w + 1) * stride] = out
                if c == half:
                    w_ref[0, half * stride :] = carry.astype(BF16)
                    w_ref[1, :fp] = (lower + pot_ref[c * stride : c * stride + fp] * now[:fp]).astype(BF16)
                if c == 0:
                    out = jnp.concatenate([last_image.astype(BF16), out[fp:]], axis=0)
                image_ref[at] = out
                return
            before = (v_ref if k == 1 else refs[k - 1])[at].astype(F32)
            value = advance(image, now, before).astype(BF16)
            if c == 0:
                value = jnp.concatenate([low[k + 1], value[fp:]], axis=0)
            refs[k + 1][at] = value
            if k + 1 == DEGREE:
                x_ref[at] = value

        end = sweep(h_ref, now_ref, fp, emit)
        if k < DEGREE:
            refs[k + 1][total:] = high[k + 1]
        else:
            w_ref[1, half * stride :] = end.astype(BF16)
    x_ref[total:] = high[DEGREE]


def back_kernel(node_ref, y_ref, out_ref):
    rows = out_ref.shape[1]
    want = (lax.broadcasted_iota(jnp.int32, (rows, 1), 0) + pl.program_id(0) * rows).astype(F32)
    hit = jnp.where(want == node_ref[...], 1.0, 0.0).astype(BF16)
    out_ref[0] = mul(hit, y_ref[...]).astype(BF16)


def gram_kernel(scale, x_ref, y_ref, out_ref, rows_ref):
    parts, _, width = y_ref.shape

    @pl.when(pl.program_id(0) == 0)
    def _():
        for j in range(parts):
            rows_ref[:, j * width : (j + 1) * width] = y_ref[j]

    out_ref[0] = (
        lax.dot_general(x_ref[0], rows_ref[...], (((0,), (0,)), ((), ())), preferred_element_type=F32) * scale
    )


def residual_kernel(x_ref, y_ref, p_ref, out_ref):
    parts, _, width = x_ref.shape
    x = jnp.concatenate([x_ref[j] for j in range(parts)], axis=1)
    y = jnp.concatenate([y_ref[j] for j in range(parts)], axis=1)
    out_ref[...] = y.astype(F32) - jnp.dot(x, p_ref[...], preferred_element_type=F32)


def full(shape):
    return pl.BlockSpec(shape, lambda i: (0,) * len(shape))


def swap(block, axis, bit):
    return lax.ppermute(block, axis, [(i, i ^ bit) for i in range(lax.axis_size(axis))])


def shift(block, axis, distance):
    n = lax.axis_size(axis)
    return lax.ppermute(block, axis, [(i, i + distance) for i in range(n) if 0 <= i + distance < n])


def tmul(a, b):
    return lax.dot_general(a, b, (((0,), (0,)), ((), ())), preferred_element_type=F32)


def near_gram_kernel(scale, core_ref, x_ref, w_ref, other_ref, out_ref):
    slab, width = w_ref.shape[1:]
    at = (slice(0, slab), slice(x_ref.shape[0] - slab, x_ref.shape[0]))
    own = [x_ref[a] for a in at]
    out_ref[:width] = (tmul(own[0], w_ref[0]) + tmul(own[1], w_ref[1])) * scale
    half = width // 2

    @pl.when(core_ref[0] == 0)
    def _():
        out_ref[width:] = sum(tmul(own[i][:, :half], other_ref[i]) for i in range(2)) * scale

    @pl.when(core_ref[0] == 1)
    def _():
        out_ref[width:] = sum(tmul(other_ref[i, :, half:], own[i]) for i in range(2)) * scale


def far_gram_kernel(scale, place_ref, w_ref, other_ref, far_ref, near_ref, out_ref):
    width = w_ref.shape[2]
    near = near_ref.shape[0]
    side, core = place_ref[0], place_ref[1]
    out_ref[:near] = near_ref[...]
    far = far_ref[...]
    mine = pl.multiple_of(near + core * width, width // 2)
    other = pl.multiple_of(near + (1 - core) * width, width // 2)
    out_ref[pl.ds(mine, width)] = tmul(w_ref[side], far) * scale
    out_ref[pl.ds(other, width)] = tmul(other_ref[side], far) * scale


def paired_residual_kernel(place_ref, q0_ref, q1_ref, q2_ref, q3_ref, x_ref, y_ref, out_ref, p_ref, q_ref):
    parts, _, width = x_ref.shape
    half = width // 2
    for k, ref in enumerate((q0_ref, q1_ref, q2_ref, q3_ref)):
        q_ref[k] = ref[...]
    me = place_ref[0]
    eye = (lax.broadcasted_iota(jnp.int32, (width, width), 0) == lax.broadcasted_iota(jnp.int32, (width, width), 1)).astype(
        F32
    ).astype(BF16)

    def turned(a):
        return lax.dot_general(eye, a, (((1,), (1,)), ((), ())), preferred_element_type=F32)

    def piece(i, lo, hi):
        return q_ref[jnp.bitwise_xor(me, i), lo:hi]

    def put(i, j, value):
        p_ref[i * width : (i + 1) * width, j * width : (j + 1) * width] = value

    near = width + half
    for i in range(parts):
        put(i, i, piece(i, 0, width))
    for i in range(0, parts, 2):
        block = jnp.concatenate([piece(i, width, near), piece(i + 1, width, near)], axis=0)
        put(i, i + 1, block)
        put(i + 1, i, turned(block).astype(BF16))
    for i in (0, 1):
        for j in (2, 3):
            one = piece(j ^ 2, near + i * width, near + (i + 1) * width)
            two = piece(i ^ 2, near + (j - 2) * width, near + (j - 1) * width)
            block = (one.astype(F32) + turned(two)).astype(BF16)
            put(i, j, block)
            put(j, i, turned(block).astype(BF16))
    x = jnp.concatenate([x_ref[j] for j in range(parts)], axis=1)
    for j in range(parts):
        at = slice(j * width, (j + 1) * width)
        out_ref[:, at] = y_ref[j].astype(F32) - mul(x, p_ref[:, at])


def paired_tail(x_own, w_own, x_cols, i_cols, o, d, dom, nodes):
    slab, width = w_own.shape[1:]
    orb, rows = x_cols.shape[:2]
    side, core = o // 2, o % 2
    scale = 1.0 / (nodes * dom)
    sds = jax.ShapeDtypeStruct
    smem = pl.BlockSpec(memory_space=pltpu.SMEM)
    vmem = pl.BlockSpec(memory_space=pltpu.VMEM)
    start = (1 - side) * (x_own.shape[0] - slab)
    far = swap(lax.dynamic_slice_in_dim(x_own, start, slab, 0), "orb", 2)
    w_other = swap(w_own, "orb", 1)
    near_rows = width + width // 2
    near = pl.pallas_call(
        functools.partial(near_gram_kernel, scale),
        in_specs=[smem] + [vmem] * 3,
        out_shape=sds((near_rows, width), F32),
        compiler_params=params(),
        cost_estimate=pl.CostEstimate(flops=12 * slab * width * width, bytes_accessed=4 << 20, transcendentals=0),
    )(core.reshape(1), x_own, w_own, w_other)
    x_cols, i_cols, far = lax.optimization_barrier((x_cols, i_cols, far))
    x_rows = lax.all_to_all(x_cols, "orb", split_axis=0, concat_axis=0, tiled=True)
    i_rows = lax.all_to_all(i_cols, "orb", split_axis=0, concat_axis=0, tiled=True)
    share = pl.pallas_call(
        functools.partial(far_gram_kernel, scale),
        in_specs=[smem] + [vmem] * 4,
        out_shape=sds((near_rows + 2 * width, width), F32),
        compiler_params=params(),
        cost_estimate=pl.CostEstimate(flops=8 * slab * width * width, bytes_accessed=4 << 20, transcendentals=0),
    )(jnp.stack([side, core]), w_own, w_other, far, near)

    bits = []
    bit = 1
    while bit < dom:
        mine = (d // bit) % 2
        share = share.reshape(2, share.shape[0] // 2, width)
        keep = lax.dynamic_index_in_dim(share, mine, 0, keepdims=False)
        give = lax.dynamic_index_in_dim(share, 1 - mine, 0, keepdims=False)
        share = keep + swap(give.astype(BF16), "dom", bit).astype(F32)
        bits.append((bit, mine))
        bit *= 2
    share = share.astype(BF16)
    for bit, mine in reversed(bits):
        got = swap(share, "dom", bit)
        share = jnp.where(mine == 0, jnp.concatenate([share, got], axis=0), jnp.concatenate([got, share], axis=0))
    q2 = swap(share, "orb", 2)
    q1 = swap(share, "orb", 1)
    q3 = swap(q2, "orb", 1)
    cols = orb * width
    return pl.pallas_call(
        paired_residual_kernel,
        in_specs=[smem] + [vmem] * 6,
        out_shape=(sds((rows, cols), F32), sds((cols, cols), BF16)),
        scratch_shapes=[pltpu.VMEM((orb,) + share.shape, BF16)],
        compiler_params=params(),
    )(o.reshape(1), share, q1, q2, q3, x_rows, i_rows)


def body(orbitals, potential, cell_hamiltonian, connectivity, face_nodes):
    nodes, width = orbitals.shape
    cells, npc = connectivity.shape
    face = face_nodes.shape[0]
    fp, ip = up16(face), up16(npc - 2 * face)
    fp = (fp + 63) // 64 * 64
    stride = fp + ip
    cp = stride + fp
    total = cells * stride
    orb, dom = lax.axis_size("orb"), lax.axis_size("dom")
    d = lax.axis_index("dom")
    o = lax.axis_index("orb")
    sds = jax.ShapeDtypeStruct
    pot_row = potential.reshape(1, nodes)
    face_row = face_nodes.reshape(1, face)

    fv, fpot = pl.pallas_call(
        face_kernel,
        out_shape=(sds((fp, width), BF16), sds((fp, 1), F32)),
        compiler_params=params(),
    )(face_row, orbitals, pot_row)
    ghost = shift(fv, "dom", -1)
    ghost_pot = shift(fpot, "dom", -1)

    hcan, y, pot, node = pl.pallas_call(
        functools.partial(order_kernel, fp, ip),
        grid=(cells,),
        in_specs=[
            full((cells, npc)),
            full((1, face)),
            pl.BlockSpec((1, npc, npc), lambda c: (c, 0, 0)),
            full((nodes, width)),
            full((1, nodes)),
        ],
        out_specs=[
            pl.BlockSpec((1, cp, cp), lambda c: (c, 0, 0)),
            pl.BlockSpec((stride, width), lambda c: (c, 0)),
            pl.BlockSpec((stride, 1), lambda c: (c, 0)),
            pl.BlockSpec((1, 1, stride), lambda c: (c, 0, 0)),
        ],
        out_shape=[
            sds((cells, cp, cp), BF16),
            sds((total, width), BF16),
            sds((total, 1), F32),
            sds((cells, 1, stride), F32),
        ],
        compiler_params=params(),
        cost_estimate=pl.CostEstimate(flops=4 * total * nodes * width, bytes_accessed=8 << 20, transcendentals=0),
    )(connectivity, face_row, cell_hamiltonian, orbitals, pot_row)
    node_row = node.reshape(1, total)
    dead = (d == dom - 1).astype(jnp.int32).reshape(1)

    extra = -(-DEGREE * fp // width)
    sent = DEGREE + 1 + -(-2 * DEGREE * fp // width)
    ext = pltpu.VMEM((total + fp, width), BF16)
    cost = pl.CostEstimate(
        flops=2 * DEGREE * cells * cp * cp * width, bytes_accessed=8 << 20, transcendentals=0
    )
    first, own, up, down = pl.pallas_call(
        functools.partial(free_kernel, fp),
        out_shape=[
            sds((total, width), BF16),
            sds((2, DEGREE + 1 + extra, fp, width), F32),
            sds((sent, fp, width), BF16),
            sds((sent, fp, width), BF16),
        ],
        scratch_shapes=[ext, ext],
        compiler_params=params(),
        cost_estimate=cost,
    )(y, ghost, hcan, pot)
    from_left = shift(up, "dom", 1)
    from_right = shift(down, "dom", -1)
    vmem = pl.BlockSpec(memory_space=pltpu.VMEM)
    slab = cells // 2 * stride + fp
    x_own, image, w_own = pl.pallas_call(
        functools.partial(forced_kernel, fp),
        in_specs=[pl.BlockSpec(memory_space=pltpu.SMEM)] + [vmem] * 9,
        out_shape=[sds((total + fp, width), BF16), sds((total, width), BF16), sds((2, slab, width), BF16)],
        scratch_shapes=[ext, ext, ext],
        compiler_params=params(),
        cost_estimate=cost,
    )(dead, y, ghost, first, own, from_left, from_right, hcan, pot, ghost_pot)

    back = pl.pallas_call(
        back_kernel,
        grid=(orb,),
        in_specs=[full((1, total)), full((total, width))],
        out_specs=pl.BlockSpec((1, nodes // orb, width), lambda i: (i, 0, 0)),
        out_shape=sds((orb, nodes // orb, width), BF16),
        compiler_params=params(),
        cost_estimate=pl.CostEstimate(flops=2 * total * nodes * width, bytes_accessed=4 << 20, transcendentals=0),
    )
    x_cols, i_cols = back(node_row, x_own), back(node_row, image)
    if orb == 4 and dom % 8 == 0:
        return paired_tail(x_own, w_own, x_cols, i_cols, o, d, dom, nodes)
    x_rows = lax.all_to_all(x_cols, "orb", split_axis=0, concat_axis=0, tiled=True)
    i_rows = lax.all_to_all(i_cols, "orb", split_axis=0, concat_axis=0, tiled=True)

    rows = nodes // orb
    cols = orb * width
    share = pl.pallas_call(
        functools.partial(gram_kernel, 1.0 / (nodes * dom)),
        grid=(orb,),
        in_specs=[pl.BlockSpec((1, rows, width), lambda i: (i, 0, 0)), full((orb, rows, width))],
        out_specs=pl.BlockSpec((1, width, cols), lambda i: (i, 0, 0)),
        out_shape=sds((orb, width, cols), F32),
        scratch_shapes=[pltpu.VMEM((rows, cols), BF16)],
        compiler_params=params(),
    )(x_rows, i_rows)

    hops = []
    for axis, me, size in (("orb", o, orb), ("dom", d, dom)):
        if axis == "dom":
            share = share.reshape(dom, width // dom, cols)
        bit = 1
        while bit < size:
            share = share.reshape((share.shape[0] // 2, 2) + share.shape[1:])
            mine = (me // bit) % 2
            keep = lax.dynamic_index_in_dim(share, mine, 1, keepdims=False)
            give = lax.dynamic_index_in_dim(share, 1 - mine, 1, keepdims=False)
            got = swap(give.astype(BF16), axis, bit)
            share = keep + got.astype(F32)
            hops.append((axis, bit, mine))
            bit *= 2
    share = share.astype(BF16)
    for axis, bit, mine in reversed(hops):
        if axis == "orb" and share.shape[0] == dom and bit * 2 == orb:
            share = share.reshape(1, width, cols)
        got = swap(share, axis, bit)
        share = jnp.where(mine == 0, jnp.stack([share, got], axis=1), jnp.stack([got, share], axis=1))
        share = share.reshape((share.shape[0] * 2,) + share.shape[2:])
    projected = share.reshape(cols, cols)

    residual = pl.pallas_call(
        residual_kernel, out_shape=sds((rows, cols), F32), compiler_params=params()
    )(x_rows, i_rows, projected)
    return (residual, projected)


def solution(mesh):
    return jax.shard_map(
        body,
        mesh=mesh,
        in_specs=(P("dom", "orb"), P("dom"), P("dom", None, None), P("dom", None), P("dom")),
        out_specs=(P(("dom", "orb"), None), P()),
        check_vma=False,
    )
```

```python
import functools

import jax
import jax.numpy as jnp
from jax import lax
from jax.experimental import pallas as pl
from jax.experimental.pallas import tpu as pltpu
from jax.sharding import PartitionSpec as P

DEGREE = 4
CENTER = 1.5
HALF = 2.0
F32 = jnp.float32
BF16 = jnp.bfloat16
VMEM_LIMIT = 50 * 1024 * 1024


def up16(n):
    return (n + 15) // 16 * 16


def iota(shape, dim):
    return lax.broadcasted_iota(jnp.int32, shape, dim).astype(F32)


def to_col(row, rows):
    n = row.shape[1]
    return jnp.sum(jnp.where(iota((rows, n), 0) == iota((rows, n), 1), row, 0.0), axis=1, keepdims=True)


def to_row(col):
    n = col.shape[0]
    return jnp.sum(jnp.where(iota((n, n), 0) == iota((n, n), 1), col, 0.0), axis=0, keepdims=True)


def params():
    return pltpu.CompilerParams(vmem_limit_bytes=VMEM_LIMIT)


def thirds(a):
    one = a.astype(BF16)
    rest = a - one.astype(F32)
    two = rest.astype(BF16)
    return one, two, (rest - two.astype(F32)).astype(BF16)


def face_kernel(face_ref, x_ref, pot_ref, out_ref):
    width = x_ref.shape[1]
    fp = out_ref.shape[0] - 16
    nodes = x_ref.shape[0]
    col = to_col(face_ref[...].astype(F32) + 1.0, fp) - 1.0
    hit = jnp.where(col == iota((fp, nodes), 1), 1.0, 0.0).astype(BF16)
    out_ref[:fp] = mul(hit, x_ref[...]).astype(BF16)
    ri = lax.broadcasted_iota(jnp.int32, (16, nodes), 0)
    parts = [p.astype(F32) for p in thirds(pot_ref[...])]
    rows = jnp.where(ri == 0, parts[0], jnp.where(ri == 1, parts[1], jnp.where(ri == 2, parts[2], 0.0))).astype(BF16)
    got = lax.dot_general(rows, hit, (((1,), (1,)), ((), ())), preferred_element_type=F32).astype(BF16)
    if width > fp:
        got = jnp.concatenate([got, jnp.zeros((16, width - fp), BF16)], axis=1)
    out_ref[fp:] = got


def turn(a, b):
    return lax.dot_general(a, b, (((1,), (1,)), ((), ())), preferred_element_type=F32)


def halves(a):
    high = jnp.floor(a * (1.0 / 64.0))
    return high.astype(BF16), (a - 64.0 * high).astype(BF16)


def flat(mask):
    return jnp.where(mask, 1.0, 0.0).astype(BF16)


def order(fp, ip, conn_ref, face_ref, h_ref, x_ref, pot_ref, hcan_ref, v_ref, potc_ref, node_ref):
    cells, npc = conn_ref.shape
    nodes = x_ref.shape[0]
    face = face_ref.shape[1]
    stride = fp + ip
    cp = stride + fp
    conn = conn_ref[...].astype(F32)
    eye = flat(iota((npc, npc), 0) == iota((npc, npc), 1))
    below = flat(iota((npc, npc), 0) < iota((npc, npc), 1))
    high, low = halves(conn)
    cols = 64.0 * turn(eye, high) + turn(eye, low)
    rows = [conn[c : c + 1] for c in range(cells)]
    ones = jnp.ones((cells, npc), BF16)
    same = [flat(cols[:, c : c + 1] == rows[c + 1]) for c in range(cells - 1)]
    ri = lax.broadcasted_iota(jnp.int32, (cells, npc), 0)
    top = jnp.where(conn >= float(nodes), 1.0, 0.0)
    for c in range(cells - 1):
        top = jnp.where(ri == c, turn(ones, same[c]), top)
    rank_top = mul(top.astype(BF16), below)
    rank_b = rank_top.astype(BF16)
    top_slot = jnp.where(ri == cells - 1, conn - float(nodes), rank_top)
    fhit = to_col(face_ref[...].astype(F32), face) == rows[0]
    bot = jnp.where(ri == 0, jnp.max(jnp.where(fhit, 1.0, 0.0), axis=0, keepdims=True), 0.0)
    bot_slot = jnp.where(ri == 0, jnp.sum(jnp.where(fhit, iota((face, npc), 0), 0.0), axis=0, keepdims=True), 0.0)
    for c in range(cells - 1):
        both = jnp.concatenate([ones, rank_b], axis=0)
        got = mul(both, same[c])
        bot = jnp.where(ri == c + 1, got[:1], bot)
        bot_slot = jnp.where(ri == c + 1, got[cells + c : cells + c + 1], bot_slot)
    mid_rank = mul((1.0 - top - bot).astype(BF16), below)
    slot = jnp.where(top > 0.5, top_slot + float(stride), jnp.where(bot > 0.5, bot_slot, mid_rank + float(fp)))
    high, low = halves(conn + 1.0)
    number = iota((8, nodes), 1)[:1]
    for c in range(cells):
        perm = flat(iota((cp, npc), 0) == slot[c : c + 1])
        half = mul(perm, h_ref[c]).astype(BF16)
        hcan_ref[c] = turn(half, perm).astype(BF16)
        lead = perm[:stride]
        node = 64.0 * turn(lead, high)[:, c : c + 1] + turn(lead, low)[:, c : c + 1] - 1.0
        node_ref[c] = 64.0 * turn(high, lead)[c : c + 1] + turn(low, lead)[c : c + 1] - 1.0
        at = slice(c * stride, (c + 1) * stride)
        hit = node == number
        v_ref[at] = mul(flat(hit), x_ref[...]).astype(BF16)
        potc_ref[at] = jnp.sum(jnp.where(hit, pot_ref[...], 0.0), axis=1, keepdims=True)


def advance(image, now, before):
    if before is None:
        return (image - CENTER * now) / HALF
    return 2.0 * (image - CENTER * now) / HALF - before


def split(a):
    high = a.astype(BF16)
    return high, (a - high.astype(F32)).astype(BF16)


def mul(a, b):
    return jnp.dot(a, b, preferred_element_type=F32)


def mul_r(a, b):
    high, low = split(b)
    return mul(a, high) + mul(a, low)


def sweep(h_ref, y_ref, fp, emit):
    cells, cp = h_ref.shape[:2]
    stride = cp - fp
    carry = None
    for c in range(cells):
        prod = mul(h_ref[c], y_ref[c * stride : c * stride + cp])
        rows = prod[:stride]
        if c > 0:
            rows = jnp.concatenate([rows[:fp] + carry, rows[fp:]], axis=0)
        emit(c, rows, prod[:fp], carry)
        carry = prod[stride:]
    return carry


def response(hc, hn, potc, fp, upper):
    cp = hc.shape[0]
    stride = cp - fp
    if upper:
        f, r, s, g = slice(stride, cp), slice(0, stride), slice(0, fp), slice(stride, cp)
        rest = slice(0, stride)
    else:
        f, r, s, g = slice(0, fp), slice(fp, cp), slice(stride - fp, stride), slice(0, fp)
        rest = slice(fp, cp)
    gain = 2.0 / HALF
    out = [hc[f, f].astype(F32)]
    one = gain * hc[r, f].astype(F32)
    out.append(mul_r(hc[f, r], one))

    def pad_next(face_rows):
        zero = jnp.zeros((stride, fp), F32)
        return jnp.concatenate([zero, face_rows] if upper else [face_rows, zero], axis=0)

    def near(value, next_value):
        got = mul_r(hc[r, r], value) + (potc - CENTER) * value
        add = mul_r(hn[g, :], next_value)
        if upper:
            return jnp.concatenate([got[:fp] + add, got[fp:]], axis=0)
        return jnp.concatenate([got[: stride - fp], got[stride - fp :] + add], axis=0)

    two = gain * near(one, pad_next(one[s]))
    out.append(mul_r(hc[f, r], two))
    two_next = gain * mul_r(hn, pad_next(one[s]))
    if upper:
        two_next = jnp.concatenate([two_next[:stride], two[s]], axis=0)
    else:
        two_next = jnp.concatenate([two[s], two_next[fp:]], axis=0)
    three = gain * near(two, two_next) - one
    out.append(mul_r(hc[f, r], three))
    return out


def store_matrices(mats, out_ref, at, fp, width):
    for part in range(2):
        for j, m in enumerate(mats):
            block, lane = divmod((part * len(mats) + j) * fp, width)
            out_ref[at + block, :, lane : lane + fp] = split(m)[part]


def load_matrices(ref, at, count, fp, width):
    out = []
    for j in range(count):
        pieces = []
        for part in range(2):
            block, lane = divmod((part * count + j) * fp, width)
            pieces.append(ref[at + block, :, lane : lane + fp].astype(F32))
        out.append(pieces[0] + pieces[1])
    return out


def free_kernel(
    fp, ip, conn_ref, face_ref, hraw_ref, raw_ref, potraw_ref, ghost_ref,
    h_ref, v_ref, pot_ref, node_ref, first_ref, own_ref, up_ref, down_ref, a_ref, b_ref,
):
    order(fp, ip, conn_ref, face_ref, hraw_ref, raw_ref, potraw_ref, h_ref, v_ref, pot_ref, node_ref)
    cells, cp = h_ref.shape[:2]
    stride = cp - fp
    total = cells * stride
    width = v_ref.shape[1]
    a_ref[:total] = v_ref[...]
    a_ref[total:] = ghost_ref[:fp]
    b_ref[total:] = jnp.zeros((fp, width), BF16)

    def keep(k, low, high):
        own_ref[0, k] = low
        own_ref[1, k] = high
        down_ref[k] = low.astype(BF16)
        up_ref[k] = high.astype(BF16)

    now_ref, other_ref = a_ref, b_ref
    for k in range(DEGREE):
        ends = {}

        def emit(c, rows, lower, carry, k=k, now_ref=now_ref, other_ref=other_ref, ends=ends):
            at = slice(c * stride, (c + 1) * stride)
            if c == 0:
                ends["low"] = rows[:fp]
            now = now_ref[at].astype(F32)
            before = None if k == 0 else other_ref[at].astype(F32)
            if k == 1:
                before = v_ref[at].astype(F32)
            value = advance(rows + pot_ref[at] * now, now, before).astype(BF16)
            if c == 0:
                value = jnp.concatenate([jnp.zeros((fp, width), BF16), value[fp:]], axis=0)
            if k == 0:
                first_ref[at] = value
            other_ref[at] = value

        high = sweep(h_ref, now_ref, fp, emit)
        keep(k, ends["low"], high)
        if k == 0:
            a_ref[total:] = jnp.zeros((fp, width), BF16)
        now_ref, other_ref = other_ref, now_ref
    keep(DEGREE, mul(h_ref[0, :fp], now_ref[:cp]), mul(h_ref[cells - 1, stride:], now_ref[total - stride :]))
    low = response(h_ref[0], h_ref[1], pot_ref[fp:cp], fp, False)
    high = response(h_ref[cells - 1], h_ref[cells - 2], pot_ref[total - stride :], fp, True)
    store_matrices(low, down_ref, DEGREE + 1, fp, width)
    store_matrices(high, up_ref, DEGREE + 1, fp, width)
    count = len(low)
    for side, mats in enumerate((low, high)):
        for j, m in enumerate(mats):
            own_ref_at = (DEGREE + 1) * 0
            block, lane = divmod(j * fp, width)
            own_ref[side, DEGREE + 1 + block + own_ref_at, :, lane : lane + fp] = m


def forced_kernel(
    fp, place_ref, v_ref, ghost_ref, first_ref, own_ref, fromleft_ref, fromright_ref, h_ref, pot_ref,
    x_ref, image_ref, w_ref, slab_ref, a_ref, b_ref, c_ref,
):
    cells, cp = h_ref.shape[:2]
    stride = cp - fp
    total = cells * stride
    width = v_ref.shape[1]
    half = cells // 2
    potg = to_col(jnp.sum(ghost_ref[fp:].astype(F32), axis=0, keepdims=True)[:, :fp], fp)
    histories = []
    last_image = None
    for side, (got_ref, pot, start) in enumerate(
        ((fromleft_ref, pot_ref[:fp], v_ref[:fp]), (fromright_ref, potg, ghost_ref[:fp]))
    ):
        mats = load_matrices(got_ref, DEGREE + 1, DEGREE, fp, width)
        for j in range(DEGREE):
            block, lane = divmod(j * fp, width)
            mats[j] = mats[j] + own_ref[side, DEGREE + 1 + block, :, lane : lane + fp]
        mats = [split(m) for m in mats]
        values = [start]
        for k in range(DEGREE + 1 if side == 0 else DEGREE):
            h = own_ref[side, k] + got_ref[k].astype(F32)
            for m in range(1, k + 1):
                h = h + mul(mats[k - m][0], values[m]) + mul(mats[k - m][1], values[m])
            now = values[k].astype(F32)
            h = h + pot * now
            if k == DEGREE:
                last_image = h
                break
            value = advance(h, now, None if k == 0 else values[k - 1].astype(F32))
            if side == 1:
                value = jnp.where(place_ref[0] == 1, 0.0, value)
            values.append(value.astype(BF16))
        histories.append(values)
    low, high = histories
    a_ref[:fp] = low[1]
    a_ref[fp:total] = first_ref[fp:]
    a_ref[total:] = high[1]
    refs = [None, a_ref, b_ref, c_ref, a_ref]
    for k in range(1, DEGREE + 1):
        now_ref = refs[k]

        def emit(c, rows, lower, carry, k=k, now_ref=now_ref):
            at = slice(c * stride, (c + 1) * stride)
            now = now_ref[at].astype(F32)
            image = rows + pot_ref[at] * now
            if k == DEGREE:
                out = image.astype(BF16)
                part, at_w = divmod(c, half)
                w_ref[part, at_w * stride : (at_w + 1) * stride] = out
                if c == half:
                    w_ref[0, half * stride :] = carry.astype(BF16)
                    w_ref[1, :fp] = (lower + pot_ref[c * stride : c * stride + fp] * now[:fp]).astype(BF16)
                if c == 0:
                    out = jnp.concatenate([last_image.astype(BF16), out[fp:]], axis=0)
                image_ref[at] = out
                return
            before = (v_ref if k == 1 else refs[k - 1])[at].astype(F32)
            value = advance(image, now, before).astype(BF16)
            if c == 0:
                value = jnp.concatenate([low[k + 1], value[fp:]], axis=0)
            refs[k + 1][at] = value
            if k + 1 == DEGREE:
                x_ref[at] = value

        end = sweep(h_ref, now_ref, fp, emit)
        if k < DEGREE:
            refs[k + 1][total:] = high[k + 1]
        else:
            w_ref[1, half * stride :] = end.astype(BF16)
    x_ref[total:] = high[DEGREE]

    @pl.when(place_ref[1] == 0)
    def _():
        slab_ref[...] = x_ref[half * stride :]

    @pl.when(place_ref[1] == 1)
    def _():
        slab_ref[...] = x_ref[: half * stride + fp]


def back_kernel(node_ref, x_ref, image_ref, out_ref):
    rows = out_ref.shape[1]
    width = x_ref.shape[1]
    want = (lax.broadcasted_iota(jnp.int32, (rows, 1), 0) + pl.program_id(0) * rows).astype(F32)
    hit = flat(want == node_ref[...])
    out_ref[0, :, :width] = mul(hit, x_ref[...]).astype(BF16)
    out_ref[0, :, width:] = mul(hit, image_ref[...]).astype(BF16)


def gram_kernel(scale, x_ref, y_ref, out_ref, rows_ref):
    parts, _, width = y_ref.shape

    @pl.when(pl.program_id(0) == 0)
    def _():
        for j in range(parts):
            rows_ref[:, j * width : (j + 1) * width] = y_ref[j]

    out_ref[0] = (
        lax.dot_general(x_ref[0], rows_ref[...], (((0,), (0,)), ((), ())), preferred_element_type=F32) * scale
    )


def residual_kernel(x_ref, y_ref, p_ref, out_ref):
    parts, _, width = x_ref.shape
    x = jnp.concatenate([x_ref[j] for j in range(parts)], axis=1)
    y = jnp.concatenate([y_ref[j] for j in range(parts)], axis=1)
    out_ref[...] = y.astype(F32) - jnp.dot(x, p_ref[...], preferred_element_type=F32)


def full(shape):
    return pl.BlockSpec(shape, lambda i: (0,) * len(shape))


def swap(block, axis, bit):
    return lax.ppermute(block, axis, [(i, i ^ bit) for i in range(lax.axis_size(axis))])


def shift(block, axis, distance):
    n = lax.axis_size(axis)
    return lax.ppermute(block, axis, [(i, i + distance) for i in range(n) if 0 <= i + distance < n])


def tmul(a, b):
    return lax.dot_general(a, b, (((0,), (0,)), ((), ())), preferred_element_type=F32)


def near_gram_kernel(scale, core_ref, x_ref, w_ref, other_ref, out_ref):
    slab, width = w_ref.shape[1:]
    at = (slice(0, slab), slice(x_ref.shape[0] - slab, x_ref.shape[0]))
    own = [x_ref[a] for a in at]
    out_ref[:width] = (tmul(own[0], w_ref[0]) + tmul(own[1], w_ref[1])) * scale
    half = width // 2

    @pl.when(core_ref[0] == 0)
    def _():
        out_ref[width:] = sum(tmul(own[i][:, :half], other_ref[i]) for i in range(2)) * scale

    @pl.when(core_ref[0] == 1)
    def _():
        out_ref[width:] = sum(tmul(other_ref[i, :, half:], own[i]) for i in range(2)) * scale


def far_gram_kernel(scale, place_ref, w_ref, other_ref, far_ref, near_ref, out_ref):
    width = w_ref.shape[2]
    near = near_ref.shape[0]
    side, core = place_ref[0], place_ref[1]
    out_ref[:near] = near_ref[...]
    far = far_ref[...]
    mine = pl.multiple_of(near + core * width, width // 2)
    other = pl.multiple_of(near + (1 - core) * width, width // 2)
    out_ref[pl.ds(mine, width)] = tmul(w_ref[side], far) * scale
    out_ref[pl.ds(other, width)] = tmul(other_ref[side], far) * scale


def paired_residual_kernel(place_ref, q0_ref, q1_ref, q2_ref, q3_ref, both_ref, out_ref, p_ref, q_ref):
    parts, _, width = both_ref.shape
    width = width // 2
    half = width // 2
    for k, ref in enumerate((q0_ref, q1_ref, q2_ref, q3_ref)):
        q_ref[k] = ref[...]
    me = place_ref[0]
    eye = (lax.broadcasted_iota(jnp.int32, (width, width), 0) == lax.broadcasted_iota(jnp.int32, (width, width), 1)).astype(
        F32
    ).astype(BF16)

    def turned(a):
        return lax.dot_general(eye, a, (((1,), (1,)), ((), ())), preferred_element_type=F32)

    def piece(i, lo, hi):
        return q_ref[jnp.bitwise_xor(me, i), lo:hi]

    def put(i, j, value):
        p_ref[i * width : (i + 1) * width, j * width : (j + 1) * width] = value

    near = width + half
    for i in range(parts):
        put(i, i, piece(i, 0, width))
    for i in range(0, parts, 2):
        block = jnp.concatenate([piece(i, width, near), piece(i + 1, width, near)], axis=0)
        put(i, i + 1, block)
        put(i + 1, i, turned(block).astype(BF16))
    for i in (0, 1):
        for j in (2, 3):
            one = piece(j ^ 2, near + i * width, near + (i + 1) * width)
            two = piece(i ^ 2, near + (j - 2) * width, near + (j - 1) * width)
            block = (one.astype(F32) + turned(two)).astype(BF16)
            put(i, j, block)
            put(j, i, turned(block).astype(BF16))
    x = jnp.concatenate([both_ref[j, :, :width] for j in range(parts)], axis=1)
    for j in range(parts):
        at = slice(j * width, (j + 1) * width)
        out_ref[:, at] = both_ref[j, :, width:].astype(F32) - mul(x, p_ref[:, at])


def paired_tail(x_own, w_own, give, cut, o, d, dom, nodes):
    slab, width = w_own.shape[1:]
    orb, rows = cut.shape[:2]
    side, core = o // 2, o % 2
    scale = 1.0 / (nodes * dom)
    sds = jax.ShapeDtypeStruct
    smem = pl.BlockSpec(memory_space=pltpu.SMEM)
    vmem = pl.BlockSpec(memory_space=pltpu.VMEM)
    far = swap(give, "orb", 2)
    cut, w_own = lax.optimization_barrier((cut, w_own))
    w_other = swap(w_own, "orb", 1)
    near_rows = width + width // 2
    near = pl.pallas_call(
        functools.partial(near_gram_kernel, scale),
        in_specs=[smem] + [vmem] * 3,
        out_shape=sds((near_rows, width), F32),
        compiler_params=params(),
        cost_estimate=pl.CostEstimate(flops=12 * slab * width * width, bytes_accessed=4 << 20, transcendentals=0),
    )(core.reshape(1), x_own, w_own, w_other)
    share = pl.pallas_call(
        functools.partial(far_gram_kernel, scale),
        in_specs=[smem] + [vmem] * 4,
        out_shape=sds((near_rows + 2 * width, width), F32),
        compiler_params=params(),
        cost_estimate=pl.CostEstimate(flops=8 * slab * width * width, bytes_accessed=4 << 20, transcendentals=0),
    )(jnp.stack([side, core]), w_own, w_other, far, near)

    bits = []
    bit = 1
    while bit < dom:
        mine = (d // bit) % 2
        share = share.reshape(2, share.shape[0] // 2, width)
        keep = lax.dynamic_index_in_dim(share, mine, 0, keepdims=False)
        give = lax.dynamic_index_in_dim(share, 1 - mine, 0, keepdims=False)
        give = give.astype(BF16)
        if bit == 1:
            cut, give = lax.optimization_barrier((cut, give))
            both = lax.all_to_all(cut, "orb", split_axis=0, concat_axis=0, tiled=True)
        share = keep + swap(give, "dom", bit).astype(F32)
        bits.append((bit, mine))
        bit *= 2
    share = share.astype(BF16)
    for bit, mine in reversed(bits):
        got = swap(share, "dom", bit)
        share = jnp.where(mine == 0, jnp.concatenate([share, got], axis=0), jnp.concatenate([got, share], axis=0))
    q2 = swap(share, "orb", 2)
    q1 = swap(share, "orb", 1)
    q3 = swap(q2, "orb", 1)
    cols = orb * width
    return pl.pallas_call(
        paired_residual_kernel,
        in_specs=[smem] + [vmem] * 5,
        out_shape=(sds((rows, cols), F32), sds((cols, cols), BF16)),
        scratch_shapes=[pltpu.VMEM((orb,) + share.shape, BF16)],
        compiler_params=params(),
    )(o.reshape(1), share, q1, q2, q3, both)


def body(orbitals, potential, cell_hamiltonian, connectivity, face_nodes):
    nodes, width = orbitals.shape
    cells, npc = connectivity.shape
    face = face_nodes.shape[0]
    fp, ip = up16(face), up16(npc - 2 * face)
    fp = (fp + 63) // 64 * 64
    stride = fp + ip
    cp = stride + fp
    total = cells * stride
    orb, dom = lax.axis_size("orb"), lax.axis_size("dom")
    d = lax.axis_index("dom")
    o = lax.axis_index("orb")
    sds = jax.ShapeDtypeStruct
    pot_row = potential.reshape(1, nodes)
    face_row = face_nodes.reshape(1, face)

    face_values = pl.pallas_call(
        face_kernel, out_shape=sds((fp + 16, width), BF16), compiler_params=params()
    )(face_row, orbitals, pot_row)
    ghost = shift(face_values, "dom", -1)

    extra = -(-DEGREE * fp // width)
    sent = DEGREE + 1 + -(-2 * DEGREE * fp // width)
    ext = pltpu.VMEM((total + fp, width), BF16)
    cost = pl.CostEstimate(
        flops=2 * DEGREE * cells * cp * cp * width, bytes_accessed=8 << 20, transcendentals=0
    )
    hcan, y, pot, node, first, own, up, down = pl.pallas_call(
        functools.partial(free_kernel, fp, ip),
        out_shape=[
            sds((cells, cp, cp), BF16),
            sds((total, width), BF16),
            sds((total, 1), F32),
            sds((cells, 1, stride), F32),
            sds((total, width), BF16),
            sds((2, DEGREE + 1 + extra, fp, width), F32),
            sds((sent, fp, width), BF16),
            sds((sent, fp, width), BF16),
        ],
        scratch_shapes=[ext, ext],
        compiler_params=params(),
        cost_estimate=cost,
    )(connectivity, face_row, cell_hamiltonian, orbitals, pot_row, ghost)
    node_row = node.reshape(1, total)
    from_left = shift(up, "dom", 1)
    from_right = shift(down, "dom", -1)
    vmem = pl.BlockSpec(memory_space=pltpu.VMEM)
    slab = cells // 2 * stride + fp
    place = jnp.stack([(d == dom - 1).astype(jnp.int32), (o // 2) % 2])
    x_own, image, w_own, give = pl.pallas_call(
        functools.partial(forced_kernel, fp),
        in_specs=[pl.BlockSpec(memory_space=pltpu.SMEM)] + [vmem] * 8,
        out_shape=[
            sds((total + fp, width), BF16),
            sds((total, width), BF16),
            sds((2, slab, width), BF16),
            sds((slab, width), BF16),
        ],
        scratch_shapes=[ext, ext, ext],
        compiler_params=params(),
        cost_estimate=cost,
    )(place, y, ghost, first, own, from_left, from_right, hcan, pot)

    cut = pl.pallas_call(
        back_kernel,
        grid=(orb,),
        in_specs=[full((1, total)), full((total, width)), full((total, width))],
        out_specs=pl.BlockSpec((1, nodes // orb, 2 * width), lambda i: (i, 0, 0)),
        out_shape=sds((orb, nodes // orb, 2 * width), BF16),
        compiler_params=params(),
        cost_estimate=pl.CostEstimate(flops=4 * total * nodes * width, bytes_accessed=4 << 20, transcendentals=0),
    )(node_row, x_own, image)
    if orb == 4 and dom % 8 == 0:
        return paired_tail(x_own, w_own, give, cut, o, d, dom, nodes)
    both = lax.all_to_all(cut, "orb", split_axis=0, concat_axis=0, tiled=True)
    x_rows, i_rows = both[:, :, :width], both[:, :, width:]

    rows = nodes // orb
    cols = orb * width
    share = pl.pallas_call(
        functools.partial(gram_kernel, 1.0 / (nodes * dom)),
        grid=(orb,),
        in_specs=[pl.BlockSpec((1, rows, width), lambda i: (i, 0, 0)), full((orb, rows, width))],
        out_specs=pl.BlockSpec((1, width, cols), lambda i: (i, 0, 0)),
        out_shape=sds((orb, width, cols), F32),
        scratch_shapes=[pltpu.VMEM((rows, cols), BF16)],
        compiler_params=params(),
    )(x_rows, i_rows)

    hops = []
    for axis, me, size in (("orb", o, orb), ("dom", d, dom)):
        if axis == "dom":
            share = share.reshape(dom, width // dom, cols)
        bit = 1
        while bit < size:
            share = share.reshape((share.shape[0] // 2, 2) + share.shape[1:])
            mine = (me // bit) % 2
            keep = lax.dynamic_index_in_dim(share, mine, 1, keepdims=False)
            give = lax.dynamic_index_in_dim(share, 1 - mine, 1, keepdims=False)
            got = swap(give.astype(BF16), axis, bit)
            share = keep + got.astype(F32)
            hops.append((axis, bit, mine))
            bit *= 2
    share = share.astype(BF16)
    for axis, bit, mine in reversed(hops):
        if axis == "orb" and share.shape[0] == dom and bit * 2 == orb:
            share = share.reshape(1, width, cols)
        got = swap(share, axis, bit)
        share = jnp.where(mine == 0, jnp.stack([share, got], axis=1), jnp.stack([got, share], axis=1))
        share = share.reshape((share.shape[0] * 2,) + share.shape[2:])
    projected = share.reshape(cols, cols)

    residual = pl.pallas_call(
        residual_kernel, out_shape=sds((rows, cols), F32), compiler_params=params()
    )(x_rows, i_rows, projected)
    return (residual, projected)


def solution(mesh):
    return jax.shard_map(
        body,
        mesh=mesh,
        in_specs=(P("dom", "orb"), P("dom"), P("dom", None, None), P("dom", None), P("dom")),
        out_specs=(P(("dom", "orb"), None), P()),
        check_vma=False,
    )
```

```python
import functools

import jax
import jax.numpy as jnp
from jax import lax
from jax.experimental import pallas as pl
from jax.experimental.pallas import tpu as pltpu
from jax.sharding import PartitionSpec as P

DEGREE = 4
CENTER = 1.5
HALF = 2.0
F32 = jnp.float32
BF16 = jnp.bfloat16
VMEM_LIMIT = 50 * 1024 * 1024


def up16(n):
    return (n + 15) // 16 * 16


def iota(shape, dim):
    return lax.broadcasted_iota(jnp.int32, shape, dim).astype(F32)


def to_col(row, rows):
    n = row.shape[1]
    return jnp.sum(jnp.where(iota((rows, n), 0) == iota((rows, n), 1), row, 0.0), axis=1, keepdims=True)


def to_row(col):
    n = col.shape[0]
    return jnp.sum(jnp.where(iota((n, n), 0) == iota((n, n), 1), col, 0.0), axis=0, keepdims=True)


def params():
    return pltpu.CompilerParams(vmem_limit_bytes=VMEM_LIMIT)


def thirds(a):
    one = a.astype(BF16)
    rest = a - one.astype(F32)
    two = rest.astype(BF16)
    return one, two, (rest - two.astype(F32)).astype(BF16)


def face_kernel(face_ref, x_ref, pot_ref, out_ref):
    width = x_ref.shape[1]
    fp = out_ref.shape[0] - 16
    nodes = x_ref.shape[0]
    col = to_col(face_ref[...].astype(F32) + 1.0, fp) - 1.0
    hit = jnp.where(col == iota((fp, nodes), 1), 1.0, 0.0).astype(BF16)
    out_ref[:fp] = mul(hit, x_ref[...]).astype(BF16)
    ri = lax.broadcasted_iota(jnp.int32, (16, nodes), 0)
    parts = [p.astype(F32) for p in thirds(pot_ref[...])]
    rows = jnp.where(ri == 0, parts[0], jnp.where(ri == 1, parts[1], jnp.where(ri == 2, parts[2], 0.0))).astype(BF16)
    got = lax.dot_general(rows, hit, (((1,), (1,)), ((), ())), preferred_element_type=F32).astype(BF16)
    if width > fp:
        got = jnp.concatenate([got, jnp.zeros((16, width - fp), BF16)], axis=1)
    out_ref[fp:] = got


def turn(a, b):
    return lax.dot_general(a, b, (((1,), (1,)), ((), ())), preferred_element_type=F32)


def halves(a):
    high = jnp.floor(a * (1.0 / 64.0))
    return high.astype(BF16), (a - 64.0 * high).astype(BF16)


def flat(mask):
    return jnp.where(mask, 1.0, 0.0).astype(BF16)


def order(fp, ip, conn_ref, face_ref, h_ref, x_ref, pot_ref, hcan_ref, v_ref, potc_ref, node_ref):
    cells, npc = conn_ref.shape
    nodes = x_ref.shape[0]
    face = face_ref.shape[1]
    stride = fp + ip
    cp = stride + fp
    conn = conn_ref[...].astype(F32)
    eye = flat(iota((npc, npc), 0) == iota((npc, npc), 1))
    below = flat(iota((npc, npc), 0) < iota((npc, npc), 1))
    high, low = halves(conn)
    cols = 64.0 * turn(eye, high) + turn(eye, low)
    rows = [conn[c : c + 1] for c in range(cells)]
    ones = jnp.ones((cells, npc), BF16)
    same = [flat(cols[:, c : c + 1] == rows[c + 1]) for c in range(cells - 1)]
    ri = lax.broadcasted_iota(jnp.int32, (cells, npc), 0)
    top = jnp.where(conn >= float(nodes), 1.0, 0.0)
    for c in range(cells - 1):
        top = jnp.where(ri == c, turn(ones, same[c]), top)
    rank_top = mul(top.astype(BF16), below)
    rank_b = rank_top.astype(BF16)
    top_slot = jnp.where(ri == cells - 1, conn - float(nodes), rank_top)
    fhit = to_col(face_ref[...].astype(F32), face) == rows[0]
    bot = jnp.where(ri == 0, jnp.max(jnp.where(fhit, 1.0, 0.0), axis=0, keepdims=True), 0.0)
    bot_slot = jnp.where(ri == 0, jnp.sum(jnp.where(fhit, iota((face, npc), 0), 0.0), axis=0, keepdims=True), 0.0)
    for c in range(cells - 1):
        both = jnp.concatenate([ones, rank_b], axis=0)
        got = mul(both, same[c])
        bot = jnp.where(ri == c + 1, got[:1], bot)
        bot_slot = jnp.where(ri == c + 1, got[cells + c : cells + c + 1], bot_slot)
    mid_rank = mul((1.0 - top - bot).astype(BF16), below)
    slot = jnp.where(top > 0.5, top_slot + float(stride), jnp.where(bot > 0.5, bot_slot, mid_rank + float(fp)))
    high, low = halves(conn + 1.0)
    number = iota((8, nodes), 1)[:1]
    for c in range(cells):
        perm = flat(iota((cp, npc), 0) == slot[c : c + 1])
        half = mul(perm, h_ref[c]).astype(BF16)
        hcan_ref[c] = turn(half, perm).astype(BF16)
        lead = perm[:stride]
        node = 64.0 * turn(lead, high)[:, c : c + 1] + turn(lead, low)[:, c : c + 1] - 1.0
        node_ref[c] = 64.0 * turn(high, lead)[c : c + 1] + turn(low, lead)[c : c + 1] - 1.0
        at = slice(c * stride, (c + 1) * stride)
        hit = node == number
        v_ref[at] = mul(flat(hit), x_ref[...]).astype(BF16)
        potc_ref[at] = jnp.sum(jnp.where(hit, pot_ref[...], 0.0), axis=1, keepdims=True)


def advance(image, now, before):
    if before is None:
        return (image - CENTER * now) / HALF
    return 2.0 * (image - CENTER * now) / HALF - before


def split(a):
    high = a.astype(BF16)
    return high, (a - high.astype(F32)).astype(BF16)


def mul(a, b):
    return jnp.dot(a, b, preferred_element_type=F32)


def mul_r(a, b):
    high, low = split(b)
    return mul(a, high) + mul(a, low)


def sweep(h_ref, y_ref, fp, emit):
    cells, cp = h_ref.shape[:2]
    stride = cp - fp
    carry = None
    for c in range(cells):
        prod = mul(h_ref[c], y_ref[c * stride : c * stride + cp])
        rows = prod[:stride]
        if c > 0:
            rows = jnp.concatenate([rows[:fp] + carry, rows[fp:]], axis=0)
        emit(c, rows, prod[:fp], carry)
        carry = prod[stride:]
    return carry


def response(hc, hn, potc, fp, upper):
    cp = hc.shape[0]
    stride = cp - fp
    if upper:
        f, r, s, g = slice(stride, cp), slice(0, stride), slice(0, fp), slice(stride, cp)
        rest = slice(0, stride)
    else:
        f, r, s, g = slice(0, fp), slice(fp, cp), slice(stride - fp, stride), slice(0, fp)
        rest = slice(fp, cp)
    gain = 2.0 / HALF
    out = [hc[f, f].astype(F32)]
    one = gain * hc[r, f].astype(F32)
    out.append(mul_r(hc[f, r], one))

    def pad_next(face_rows):
        zero = jnp.zeros((stride, fp), F32)
        return jnp.concatenate([zero, face_rows] if upper else [face_rows, zero], axis=0)

    def near(value, next_value):
        got = mul_r(hc[r, r], value) + (potc - CENTER) * value
        add = mul_r(hn[g, :], next_value)
        if upper:
            return jnp.concatenate([got[:fp] + add, got[fp:]], axis=0)
        return jnp.concatenate([got[: stride - fp], got[stride - fp :] + add], axis=0)

    two = gain * near(one, pad_next(one[s]))
    out.append(mul_r(hc[f, r], two))
    two_next = gain * mul_r(hn, pad_next(one[s]))
    if upper:
        two_next = jnp.concatenate([two_next[:stride], two[s]], axis=0)
    else:
        two_next = jnp.concatenate([two[s], two_next[fp:]], axis=0)
    three = gain * near(two, two_next) - one
    out.append(mul_r(hc[f, r], three))
    return out


def store_matrices(mats, out_ref, at, fp, width):
    for part in range(2):
        for j, m in enumerate(mats):
            block, lane = divmod((part * len(mats) + j) * fp, width)
            out_ref[at + block, :, lane : lane + fp] = split(m)[part]


def load_matrices(ref, at, count, fp, width):
    out = []
    for j in range(count):
        pieces = []
        for part in range(2):
            block, lane = divmod((part * count + j) * fp, width)
            pieces.append(ref[at + block, :, lane : lane + fp].astype(F32))
        out.append(pieces[0] + pieces[1])
    return out


def free_kernel(
    fp, ip, conn_ref, face_ref, hraw_ref, raw_ref, potraw_ref, ghost_ref,
    h_ref, v_ref, pot_ref, node_ref, first_ref, own_ref, up_ref, down_ref, a_ref, b_ref,
):
    order(fp, ip, conn_ref, face_ref, hraw_ref, raw_ref, potraw_ref, h_ref, v_ref, pot_ref, node_ref)
    cells, cp = h_ref.shape[:2]
    stride = cp - fp
    total = cells * stride
    width = v_ref.shape[1]
    a_ref[:total] = v_ref[...]
    a_ref[total:] = ghost_ref[:fp]
    b_ref[total:] = jnp.zeros((fp, width), BF16)

    def keep(k, low, high):
        own_ref[0, k] = low
        own_ref[1, k] = high
        down_ref[k] = low.astype(BF16)
        up_ref[k] = high.astype(BF16)

    now_ref, other_ref = a_ref, b_ref
    for k in range(DEGREE):
        ends = {}

        def emit(c, rows, lower, carry, k=k, now_ref=now_ref, other_ref=other_ref, ends=ends):
            at = slice(c * stride, (c + 1) * stride)
            if c == 0:
                ends["low"] = rows[:fp]
            now = now_ref[at].astype(F32)
            before = None if k == 0 else other_ref[at].astype(F32)
            if k == 1:
                before = v_ref[at].astype(F32)
            value = advance(rows + pot_ref[at] * now, now, before).astype(BF16)
            if c == 0:
                value = jnp.concatenate([jnp.zeros((fp, width), BF16), value[fp:]], axis=0)
            if k == 0:
                first_ref[at] = value
            other_ref[at] = value

        high = sweep(h_ref, now_ref, fp, emit)
        keep(k, ends["low"], high)
        if k == 0:
            a_ref[total:] = jnp.zeros((fp, width), BF16)
        now_ref, other_ref = other_ref, now_ref
    keep(DEGREE, mul(h_ref[0, :fp], now_ref[:cp]), mul(h_ref[cells - 1, stride:], now_ref[total - stride :]))
    low = response(h_ref[0], h_ref[1], pot_ref[fp:cp], fp, False)
    high = response(h_ref[cells - 1], h_ref[cells - 2], pot_ref[total - stride :], fp, True)
    store_matrices(low, down_ref, DEGREE + 1, fp, width)
    store_matrices(high, up_ref, DEGREE + 1, fp, width)
    count = len(low)
    for side, mats in enumerate((low, high)):
        for j, m in enumerate(mats):
            own_ref_at = (DEGREE + 1) * 0
            block, lane = divmod(j * fp, width)
            own_ref[side, DEGREE + 1 + block + own_ref_at, :, lane : lane + fp] = m


def forced_kernel(
    fp, place_ref, v_ref, ghost_ref, first_ref, own_ref, fromleft_ref, fromright_ref, h_ref, pot_ref,
    x_ref, image_ref, w_ref, slab_ref, a_ref, b_ref, c_ref,
):
    cells, cp = h_ref.shape[:2]
    stride = cp - fp
    total = cells * stride
    width = v_ref.shape[1]
    half = cells // 2
    potg = to_col(jnp.sum(ghost_ref[fp:].astype(F32), axis=0, keepdims=True)[:, :fp], fp)
    histories = []
    last_image = None
    for side, (got_ref, pot, start) in enumerate(
        ((fromleft_ref, pot_ref[:fp], v_ref[:fp]), (fromright_ref, potg, ghost_ref[:fp]))
    ):
        mats = load_matrices(got_ref, DEGREE + 1, DEGREE, fp, width)
        for j in range(DEGREE):
            block, lane = divmod(j * fp, width)
            mats[j] = mats[j] + own_ref[side, DEGREE + 1 + block, :, lane : lane + fp]
        mats = [split(m) for m in mats]
        values = [start]
        for k in range(DEGREE + 1 if side == 0 else DEGREE):
            h = own_ref[side, k] + got_ref[k].astype(F32)
            for m in range(1, k + 1):
                h = h + mul(mats[k - m][0], values[m]) + mul(mats[k - m][1], values[m])
            now = values[k].astype(F32)
            h = h + pot * now
            if k == DEGREE:
                last_image = h
                break
            value = advance(h, now, None if k == 0 else values[k - 1].astype(F32))
            if side == 1:
                value = jnp.where(place_ref[0] == 1, 0.0, value)
            values.append(value.astype(BF16))
        histories.append(values)
    low, high = histories
    a_ref[:fp] = low[1]
    a_ref[fp:total] = first_ref[fp:]
    a_ref[total:] = high[1]
    refs = [None, a_ref, b_ref, c_ref, a_ref]
    for k in range(1, DEGREE + 1):
        now_ref = refs[k]

        def emit(c, rows, lower, carry, k=k, now_ref=now_ref):
            at = slice(c * stride, (c + 1) * stride)
            now = now_ref[at].astype(F32)
            image = rows + pot_ref[at] * now
            if k == DEGREE:
                out = image.astype(BF16)
                part, at_w = divmod(c, half)
                w_ref[part, at_w * stride : (at_w + 1) * stride] = out
                if c == half:
                    w_ref[0, half * stride :] = carry.astype(BF16)
                    w_ref[1, :fp] = (lower + pot_ref[c * stride : c * stride + fp] * now[:fp]).astype(BF16)
                if c == 0:
                    out = jnp.concatenate([last_image.astype(BF16), out[fp:]], axis=0)
                image_ref[at] = out
                return
            before = (v_ref if k == 1 else refs[k - 1])[at].astype(F32)
            value = advance(image, now, before).astype(BF16)
            if c == 0:
                value = jnp.concatenate([low[k + 1], value[fp:]], axis=0)
            refs[k + 1][at] = value
            if k + 1 == DEGREE:
                x_ref[at] = value

        end = sweep(h_ref, now_ref, fp, emit)
        if k < DEGREE:
            refs[k + 1][total:] = high[k + 1]
        else:
            w_ref[1, half * stride :] = end.astype(BF16)
    x_ref[total:] = high[DEGREE]

    @pl.when(place_ref[1] == 0)
    def _():
        slab_ref[...] = x_ref[half * stride :]

    @pl.when(place_ref[1] == 1)
    def _():
        slab_ref[...] = x_ref[: half * stride + fp]


def back_kernel(node_ref, x_ref, image_ref, out_ref):
    rows = out_ref.shape[1]
    width = x_ref.shape[1]
    want = (lax.broadcasted_iota(jnp.int32, (rows, 1), 0) + pl.program_id(0) * rows).astype(F32)
    hit = flat(want == node_ref[...])
    out_ref[0, :, :width] = mul(hit, x_ref[...]).astype(BF16)
    out_ref[0, :, width:] = mul(hit, image_ref[...]).astype(BF16)


def back_pair_kernel(at_ref, node_ref, x_ref, image_ref, *out_refs):
    rows = out_refs[0].shape[0]
    for i in range(2):
        want = (lax.broadcasted_iota(jnp.int32, (rows, 1), 0) + at_ref[i] * rows).astype(F32)
        hit = flat(want == node_ref[...])
        out_refs[2 * i][...] = mul(hit, x_ref[...]).astype(BF16)
        out_refs[2 * i + 1][...] = mul(hit, image_ref[...]).astype(BF16)


def gram_kernel(scale, x_ref, y_ref, out_ref, rows_ref):
    parts, _, width = y_ref.shape

    @pl.when(pl.program_id(0) == 0)
    def _():
        for j in range(parts):
            rows_ref[:, j * width : (j + 1) * width] = y_ref[j]

    out_ref[0] = (
        lax.dot_general(x_ref[0], rows_ref[...], (((0,), (0,)), ((), ())), preferred_element_type=F32) * scale
    )


def residual_kernel(x_ref, y_ref, p_ref, out_ref):
    parts, _, width = x_ref.shape
    x = jnp.concatenate([x_ref[j] for j in range(parts)], axis=1)
    y = jnp.concatenate([y_ref[j] for j in range(parts)], axis=1)
    out_ref[...] = y.astype(F32) - jnp.dot(x, p_ref[...], preferred_element_type=F32)


def full(shape):
    return pl.BlockSpec(shape, lambda i: (0,) * len(shape))


def swap(block, axis, bit):
    return lax.ppermute(block, axis, [(i, i ^ bit) for i in range(lax.axis_size(axis))])


def shift(block, axis, distance):
    n = lax.axis_size(axis)
    return lax.ppermute(block, axis, [(i, i + distance) for i in range(n) if 0 <= i + distance < n])


def tmul(a, b):
    return lax.dot_general(a, b, (((0,), (0,)), ((), ())), preferred_element_type=F32)


def near_gram_kernel(scale, core_ref, x_ref, w_ref, other_ref, out_ref):
    slab, width = w_ref.shape[1:]
    at = (slice(0, slab), slice(x_ref.shape[0] - slab, x_ref.shape[0]))
    own = [x_ref[a] for a in at]
    out_ref[:width] = (tmul(own[0], w_ref[0]) + tmul(own[1], w_ref[1])) * scale
    half = width // 2

    @pl.when(core_ref[0] == 0)
    def _():
        out_ref[width:] = sum(tmul(own[i][:, :half], other_ref[i]) for i in range(2)) * scale

    @pl.when(core_ref[0] == 1)
    def _():
        out_ref[width:] = sum(tmul(other_ref[i, :, half:], own[i]) for i in range(2)) * scale


def far_gram_kernel(scale, place_ref, w_ref, other_ref, far_ref, near_ref, out_ref):
    width = w_ref.shape[2]
    near = near_ref.shape[0]
    side, core = place_ref[0], place_ref[1]
    out_ref[:near] = near_ref[...]
    far = far_ref[...]
    mine = pl.multiple_of(near + core * width, width // 2)
    other = pl.multiple_of(near + (1 - core) * width, width // 2)
    out_ref[pl.ds(mine, width)] = tmul(w_ref[side], far) * scale
    out_ref[pl.ds(other, width)] = tmul(other_ref[side], far) * scale


def paired_residual_kernel(place_ref, q0_ref, q1_ref, q2_ref, q3_ref, *refs):
    parts = 4
    x_refs, y_refs, (out_ref, p_ref, q_ref) = refs[: 2 * parts : 2], refs[1 : 2 * parts : 2], refs[2 * parts :]
    width = x_refs[0].shape[1]
    half = width // 2
    for k, ref in enumerate((q0_ref, q1_ref, q2_ref, q3_ref)):
        q_ref[k] = ref[...]
    me = place_ref[0]
    eye = (lax.broadcasted_iota(jnp.int32, (width, width), 0) == lax.broadcasted_iota(jnp.int32, (width, width), 1)).astype(
        F32
    ).astype(BF16)

    def turned(a):
        return lax.dot_general(eye, a, (((1,), (1,)), ((), ())), preferred_element_type=F32)

    def piece(i, lo, hi):
        return q_ref[jnp.bitwise_xor(me, i), lo:hi]

    def put(i, j, value):
        p_ref[i * width : (i + 1) * width, j * width : (j + 1) * width] = value

    near = width + half
    for i in range(parts):
        put(i, i, piece(i, 0, width))
    for i in range(0, parts, 2):
        block = jnp.concatenate([piece(i, width, near), piece(i + 1, width, near)], axis=0)
        put(i, i + 1, block)
        put(i + 1, i, turned(block).astype(BF16))
    for i in (0, 1):
        for j in (2, 3):
            one = piece(j ^ 2, near + i * width, near + (i + 1) * width)
            two = piece(i ^ 2, near + (j - 2) * width, near + (j - 1) * width)
            block = (one.astype(F32) + turned(two)).astype(BF16)
            put(i, j, block)
            put(j, i, turned(block).astype(BF16))
    x = jnp.concatenate([ref[...] for ref in x_refs], axis=1)
    spots = [pl.ds(pl.multiple_of(jnp.bitwise_xor(me, k) * width, width), width) for k in range(parts)]
    for k in range(parts):
        at = spots[k]
        p = jnp.concatenate([p_ref[spots[m], at] for m in range(parts)], axis=0)
        out_ref[:, at] = y_refs[k][...].astype(F32) - mul(x, p)


def paired_tail(x_own, image, w_own, give, node_row, o, d, dom, nodes):
    slab, width = w_own.shape[1:]
    orb = 4
    rows = nodes // orb
    side, core = o // 2, o % 2
    scale = 1.0 / (nodes * dom)
    sds = jax.ShapeDtypeStruct
    smem = pl.BlockSpec(memory_space=pltpu.SMEM)
    vmem = pl.BlockSpec(memory_space=pltpu.VMEM)
    far = swap(give, "orb", 2)
    total = image.shape[0]

    def back(first, second, x_own, image):
        whole = lambda *shape: pl.BlockSpec(shape, lambda i: (0,) * len(shape))
        return pl.pallas_call(
            back_pair_kernel,
            grid=(1,),
            in_specs=[smem, whole(1, total), whole(total, width), whole(total, width)],
            out_specs=[whole(rows, width)] * 4,
            out_shape=[sds((rows, width), BF16)] * 4,
            compiler_params=params(),
            cost_estimate=pl.CostEstimate(flops=1 << 20, bytes_accessed=1 << 10, transcendentals=0),
        )(jnp.stack([jnp.bitwise_xor(o, first), jnp.bitwise_xor(o, second)]), node_row, x_own, image)

    cuts = back(2, 3, x_own, image)
    w_other = swap(w_own, "orb", 1)
    top = width + width // 2
    near = pl.pallas_call(
        functools.partial(near_gram_kernel, scale),
        in_specs=[smem] + [vmem] * 3,
        out_shape=sds((top, width), F32),
        compiler_params=params(),
        cost_estimate=pl.CostEstimate(flops=1 << 20, bytes_accessed=1 << 10, transcendentals=0),
    )(core.reshape(1), x_own, w_own, w_other)
    far, near, *cuts = lax.optimization_barrier((far, near, *cuts))
    rows_far = [swap(cut, "orb", 2 + i // 2) for i, cut in enumerate(cuts)]
    share = pl.pallas_call(
        functools.partial(far_gram_kernel, scale),
        in_specs=[smem] + [vmem] * 4,
        out_shape=sds((top + 2 * width, width), F32),
        compiler_params=params(),
        cost_estimate=pl.CostEstimate(flops=8 * slab * width * width, bytes_accessed=4 << 20, transcendentals=0),
    )(jnp.stack([side, core]), w_own, w_other, far, near)

    bits = []
    pending, rows_got = list(rows_far), []
    bit = 1
    while bit < dom:
        mine = (d // bit) % 2
        share = share.reshape(2, share.shape[0] // 2, width)
        keep = lax.dynamic_index_in_dim(share, mine, 0, keepdims=False)
        give = lax.dynamic_index_in_dim(share, 1 - mine, 0, keepdims=False)
        give = give.astype(BF16)
        if bit == 1:
            x_own, image, give = lax.optimization_barrier((x_own, image, give))
            near_rows = back(0, 1, x_own, image)
            rows_near = list(near_rows[:2]) + [swap(cut, "orb", 1) for cut in near_rows[2:]]
        share = keep + swap(give, "dom", bit).astype(F32)
        if pending:
            share, got = lax.optimization_barrier((share, pending.pop(0)))
            rows_got.append(got)
        bits.append((bit, mine))
        bit *= 2
    share = share.astype(BF16)
    for bit, mine in reversed(bits):
        got = swap(share, "dom", bit)
        share = jnp.where(mine == 0, jnp.concatenate([share, got], axis=0), jnp.concatenate([got, share], axis=0))
        if pending:
            share, got = lax.optimization_barrier((share, pending.pop(0)))
            rows_got.append(got)
    rows_got += pending
    q2 = swap(share, "orb", 2)
    q1 = swap(share, "orb", 1)
    q3 = swap(q2, "orb", 1)
    cols = orb * width
    return pl.pallas_call(
        paired_residual_kernel,
        in_specs=[smem] + [vmem] * 12,
        out_shape=(sds((rows, cols), F32), sds((cols, cols), BF16)),
        scratch_shapes=[pltpu.VMEM((orb,) + share.shape, BF16)],
        compiler_params=params(),
    )(o.reshape(1), share, q1, q2, q3, *rows_near, *rows_got)


def body(orbitals, potential, cell_hamiltonian, connectivity, face_nodes):
    nodes, width = orbitals.shape
    cells, npc = connectivity.shape
    face = face_nodes.shape[0]
    fp, ip = up16(face), up16(npc - 2 * face)
    fp = (fp + 63) // 64 * 64
    stride = fp + ip
    cp = stride + fp
    total = cells * stride
    orb, dom = lax.axis_size("orb"), lax.axis_size("dom")
    d = lax.axis_index("dom")
    o = lax.axis_index("orb")
    sds = jax.ShapeDtypeStruct
    pot_row = potential.reshape(1, nodes)
    face_row = face_nodes.reshape(1, face)

    face_values = pl.pallas_call(
        face_kernel, out_shape=sds((fp + 16, width), BF16), compiler_params=params()
    )(face_row, orbitals, pot_row)
    ghost = shift(face_values, "dom", -1)

    extra = -(-DEGREE * fp // width)
    sent = DEGREE + 1 + -(-2 * DEGREE * fp // width)
    ext = pltpu.VMEM((total + fp, width), BF16)
    cost = pl.CostEstimate(
        flops=2 * DEGREE * cells * cp * cp * width, bytes_accessed=8 << 20, transcendentals=0
    )
    hcan, y, pot, node, first, own, up, down = pl.pallas_call(
        functools.partial(free_kernel, fp, ip),
        out_shape=[
            sds((cells, cp, cp), BF16),
            sds((total, width), BF16),
            sds((total, 1), F32),
            sds((cells, 1, stride), F32),
            sds((total, width), BF16),
            sds((2, DEGREE + 1 + extra, fp, width), F32),
            sds((sent, fp, width), BF16),
            sds((sent, fp, width), BF16),
        ],
        scratch_shapes=[ext, ext],
        compiler_params=params(),
        cost_estimate=cost,
    )(connectivity, face_row, cell_hamiltonian, orbitals, pot_row, ghost)
    node_row = node.reshape(1, total)
    from_left = shift(up, "dom", 1)
    from_right = shift(down, "dom", -1)
    vmem = pl.BlockSpec(memory_space=pltpu.VMEM)
    slab = cells // 2 * stride + fp
    place = jnp.stack([(d == dom - 1).astype(jnp.int32), (o // 2) % 2])
    x_own, image, w_own, give = pl.pallas_call(
        functools.partial(forced_kernel, fp),
        in_specs=[pl.BlockSpec(memory_space=pltpu.SMEM)] + [vmem] * 8,
        out_shape=[
            sds((total + fp, width), BF16),
            sds((total, width), BF16),
            sds((2, slab, width), BF16),
            sds((slab, width), BF16),
        ],
        scratch_shapes=[ext, ext, ext],
        compiler_params=params(),
        cost_estimate=cost,
    )(place, y, ghost, first, own, from_left, from_right, hcan, pot)

    if orb == 4 and dom % 8 == 0:
        return paired_tail(x_own, image, w_own, give, node_row, o, d, dom, nodes)
    cut = pl.pallas_call(
        back_kernel,
        grid=(orb,),
        in_specs=[full((1, total)), full((total, width)), full((total, width))],
        out_specs=pl.BlockSpec((1, nodes // orb, 2 * width), lambda i: (i, 0, 0)),
        out_shape=sds((orb, nodes // orb, 2 * width), BF16),
        compiler_params=params(),
        cost_estimate=pl.CostEstimate(flops=4 * total * nodes * width, bytes_accessed=4 << 20, transcendentals=0),
    )(node_row, x_own, image)
    both = lax.all_to_all(cut, "orb", split_axis=0, concat_axis=0, tiled=True)
    x_rows, i_rows = both[:, :, :width], both[:, :, width:]

    rows = nodes // orb
    cols = orb * width
    share = pl.pallas_call(
        functools.partial(gram_kernel, 1.0 / (nodes * dom)),
        grid=(orb,),
        in_specs=[pl.BlockSpec((1, rows, width), lambda i: (i, 0, 0)), full((orb, rows, width))],
        out_specs=pl.BlockSpec((1, width, cols), lambda i: (i, 0, 0)),
        out_shape=sds((orb, width, cols), F32),
        scratch_shapes=[pltpu.VMEM((rows, cols), BF16)],
        compiler_params=params(),
    )(x_rows, i_rows)

    hops = []
    for axis, me, size in (("orb", o, orb), ("dom", d, dom)):
        if axis == "dom":
            share = share.reshape(dom, width // dom, cols)
        bit = 1
        while bit < size:
            share = share.reshape((share.shape[0] // 2, 2) + share.shape[1:])
            mine = (me // bit) % 2
            keep = lax.dynamic_index_in_dim(share, mine, 1, keepdims=False)
            give = lax.dynamic_index_in_dim(share, 1 - mine, 1, keepdims=False)
            got = swap(give.astype(BF16), axis, bit)
            share = keep + got.astype(F32)
            hops.append((axis, bit, mine))
            bit *= 2
    share = share.astype(BF16)
    for axis, bit, mine in reversed(hops):
        if axis == "orb" and share.shape[0] == dom and bit * 2 == orb:
            share = share.reshape(1, width, cols)
        got = swap(share, axis, bit)
        share = jnp.where(mine == 0, jnp.stack([share, got], axis=1), jnp.stack([got, share], axis=1))
        share = share.reshape((share.shape[0] * 2,) + share.shape[2:])
    projected = share.reshape(cols, cols)

    residual = pl.pallas_call(
        residual_kernel, out_shape=sds((rows, cols), F32), compiler_params=params()
    )(x_rows, i_rows, projected)
    return (residual, projected)


def solution(mesh):
    return jax.shard_map(
        body,
        mesh=mesh,
        in_specs=(P("dom", "orb"), P("dom"), P("dom", None, None), P("dom", None), P("dom")),
        out_specs=(P(("dom", "orb"), None), P()),
        check_vma=False,
    )
```

```python
import functools

import jax
import jax.numpy as jnp
from jax import lax
from jax.experimental import pallas as pl
from jax.experimental.pallas import tpu as pltpu
from jax.sharding import PartitionSpec as P

DEGREE = 4
CENTER = 1.5
HALF = 2.0
F32 = jnp.float32
BF16 = jnp.bfloat16
VMEM_LIMIT = 50 * 1024 * 1024


def up16(n):
    return (n + 15) // 16 * 16


def iota(shape, dim):
    return lax.broadcasted_iota(jnp.int32, shape, dim).astype(F32)


def to_col(row, rows):
    n = row.shape[1]
    return jnp.sum(jnp.where(iota((rows, n), 0) == iota((rows, n), 1), row, 0.0), axis=1, keepdims=True)


def to_row(col):
    n = col.shape[0]
    return jnp.sum(jnp.where(iota((n, n), 0) == iota((n, n), 1), col, 0.0), axis=0, keepdims=True)


def params():
    return pltpu.CompilerParams(vmem_limit_bytes=VMEM_LIMIT)


def thirds(a):
    one = a.astype(BF16)
    rest = a - one.astype(F32)
    two = rest.astype(BF16)
    return one, two, (rest - two.astype(F32)).astype(BF16)


def face_kernel(face_ref, x_ref, pot_ref, out_ref):
    width = x_ref.shape[1]
    fp = out_ref.shape[0] - 16
    nodes = x_ref.shape[0]
    col = to_col(face_ref[...].astype(F32) + 1.0, fp) - 1.0
    hit = jnp.where(col == iota((fp, nodes), 1), 1.0, 0.0).astype(BF16)
    out_ref[:fp] = mul(hit, x_ref[...]).astype(BF16)
    ri = lax.broadcasted_iota(jnp.int32, (16, nodes), 0)
    parts = [p.astype(F32) for p in thirds(pot_ref[...])]
    rows = jnp.where(ri == 0, parts[0], jnp.where(ri == 1, parts[1], jnp.where(ri == 2, parts[2], 0.0))).astype(BF16)
    got = lax.dot_general(rows, hit, (((1,), (1,)), ((), ())), preferred_element_type=F32).astype(BF16)
    if width > fp:
        got = jnp.concatenate([got, jnp.zeros((16, width - fp), BF16)], axis=1)
    out_ref[fp:] = got


def turn(a, b):
    return lax.dot_general(a, b, (((1,), (1,)), ((), ())), preferred_element_type=F32)


def halves(a):
    high = jnp.floor(a * (1.0 / 64.0))
    return high.astype(BF16), (a - 64.0 * high).astype(BF16)


def flat(mask):
    return jnp.where(mask, 1.0, 0.0).astype(BF16)


def order(fp, ip, conn_ref, face_ref, h_ref, x_ref, pot_ref, hcan_ref, v_ref, potc_ref, node_ref):
    cells, npc = conn_ref.shape
    nodes = x_ref.shape[0]
    face = face_ref.shape[1]
    stride = fp + ip
    cp = stride + fp
    conn = conn_ref[...].astype(F32)
    eye = flat(iota((npc, npc), 0) == iota((npc, npc), 1))
    below = flat(iota((npc, npc), 0) < iota((npc, npc), 1))
    high, low = halves(conn)
    cols = 64.0 * turn(eye, high) + turn(eye, low)
    rows = [conn[c : c + 1] for c in range(cells)]
    ones = jnp.ones((cells, npc), BF16)
    same = [flat(cols[:, c : c + 1] == rows[c + 1]) for c in range(cells - 1)]
    ri = lax.broadcasted_iota(jnp.int32, (cells, npc), 0)
    top = jnp.where(conn >= float(nodes), 1.0, 0.0)
    for c in range(cells - 1):
        top = jnp.where(ri == c, turn(ones, same[c]), top)
    rank_top = mul(top.astype(BF16), below)
    rank_b = rank_top.astype(BF16)
    top_slot = jnp.where(ri == cells - 1, conn - float(nodes), rank_top)
    fhit = to_col(face_ref[...].astype(F32), face) == rows[0]
    bot = jnp.where(ri == 0, jnp.max(jnp.where(fhit, 1.0, 0.0), axis=0, keepdims=True), 0.0)
    bot_slot = jnp.where(ri == 0, jnp.sum(jnp.where(fhit, iota((face, npc), 0), 0.0), axis=0, keepdims=True), 0.0)
    for c in range(cells - 1):
        both = jnp.concatenate([ones, rank_b], axis=0)
        got = mul(both, same[c])
        bot = jnp.where(ri == c + 1, got[:1], bot)
        bot_slot = jnp.where(ri == c + 1, got[cells + c : cells + c + 1], bot_slot)
    mid_rank = mul((1.0 - top - bot).astype(BF16), below)
    slot = jnp.where(top > 0.5, top_slot + float(stride), jnp.where(bot > 0.5, bot_slot, mid_rank + float(fp)))
    high, low = halves(conn + 1.0)
    number = iota((8, nodes), 1)[:1]
    for c in range(cells):
        perm = flat(iota((cp, npc), 0) == slot[c : c + 1])
        half = mul(perm, h_ref[c]).astype(BF16)
        hcan_ref[c] = turn(half, perm).astype(BF16)
        lead = perm[:stride]
        node = 64.0 * turn(lead, high)[:, c : c + 1] + turn(lead, low)[:, c : c + 1] - 1.0
        node_ref[c] = 64.0 * turn(high, lead)[c : c + 1] + turn(low, lead)[c : c + 1] - 1.0
        at = slice(c * stride, (c + 1) * stride)
        hit = node == number
        v_ref[at] = mul(flat(hit), x_ref[...]).astype(BF16)
        potc_ref[at] = jnp.sum(jnp.where(hit, pot_ref[...], 0.0), axis=1, keepdims=True)


def advance(image, now, before):
    if before is None:
        return (image - CENTER * now) / HALF
    return 2.0 * (image - CENTER * now) / HALF - before


def split(a):
    high = a.astype(BF16)
    return high, (a - high.astype(F32)).astype(BF16)


def mul(a, b):
    return jnp.dot(a, b, preferred_element_type=F32)


def mul_r(a, b):
    high, low = split(b)
    return mul(a, high) + mul(a, low)


def sweep(h_ref, y_ref, fp, emit):
    cells, cp = h_ref.shape[:2]
    stride = cp - fp
    carry = None
    for c in range(cells):
        prod = mul(h_ref[c], y_ref[c * stride : c * stride + cp])
        rows = prod[:stride]
        if c > 0:
            rows = jnp.concatenate([rows[:fp] + carry, rows[fp:]], axis=0)
        emit(c, rows, prod[:fp], carry)
        carry = prod[stride:]
    return carry


def response(hc, hn, potc, fp, upper):
    cp = hc.shape[0]
    stride = cp - fp
    if upper:
        f, r, s, g = slice(stride, cp), slice(0, stride), slice(0, fp), slice(stride, cp)
        rest = slice(0, stride)
    else:
        f, r, s, g = slice(0, fp), slice(fp, cp), slice(stride - fp, stride), slice(0, fp)
        rest = slice(fp, cp)
    gain = 2.0 / HALF
    out = [hc[f, f].astype(F32)]
    one = gain * hc[r, f].astype(F32)
    out.append(mul_r(hc[f, r], one))

    def pad_next(face_rows):
        zero = jnp.zeros((stride, fp), F32)
        return jnp.concatenate([zero, face_rows] if upper else [face_rows, zero], axis=0)

    def near(value, next_value):
        got = mul_r(hc[r, r], value) + (potc - CENTER) * value
        add = mul_r(hn[g, :], next_value)
        if upper:
            return jnp.concatenate([got[:fp] + add, got[fp:]], axis=0)
        return jnp.concatenate([got[: stride - fp], got[stride - fp :] + add], axis=0)

    two = gain * near(one, pad_next(one[s]))
    out.append(mul_r(hc[f, r], two))
    two_next = gain * mul_r(hn, pad_next(one[s]))
    if upper:
        two_next = jnp.concatenate([two_next[:stride], two[s]], axis=0)
    else:
        two_next = jnp.concatenate([two[s], two_next[fp:]], axis=0)
    three = gain * near(two, two_next) - one
    out.append(mul_r(hc[f, r], three))
    return out


def store_matrices(mats, out_ref, at, fp, width):
    for j, m in enumerate(mats):
        block, lane = divmod(j * fp, width)
        out_ref[at + block, :, lane : lane + fp] = m.astype(out_ref.dtype)


def load_matrices(ref, at, count, fp, width):
    spots = [divmod(j * fp, width) for j in range(count)]
    return [ref[at + block, :, lane : lane + fp].astype(F32) for block, lane in spots]


def free_kernel(
    fp, ip, conn_ref, face_ref, hraw_ref, raw_ref, potraw_ref, ghost_ref,
    h_ref, v_ref, pot_ref, node_ref, first_ref, own_ref, up_ref, down_ref, a_ref, b_ref,
):
    order(fp, ip, conn_ref, face_ref, hraw_ref, raw_ref, potraw_ref, h_ref, v_ref, pot_ref, node_ref)
    cells, cp = h_ref.shape[:2]
    stride = cp - fp
    total = cells * stride
    width = v_ref.shape[1]
    a_ref[:total] = v_ref[...]
    a_ref[total:] = ghost_ref[:fp]
    b_ref[total:] = jnp.zeros((fp, width), BF16)

    def keep(k, low, high):
        own_ref[0, k] = low
        own_ref[1, k] = high
        if k < DEGREE:
            down_ref[k] = low.astype(BF16)
        up_ref[k] = high.astype(BF16)

    now_ref, other_ref = a_ref, b_ref
    for k in range(DEGREE):
        ends = {}

        def emit(c, rows, lower, carry, k=k, now_ref=now_ref, other_ref=other_ref, ends=ends):
            at = slice(c * stride, (c + 1) * stride)
            if c == 0:
                ends["low"] = rows[:fp]
            now = now_ref[at].astype(F32)
            before = None if k == 0 else other_ref[at].astype(F32)
            if k == 1:
                before = v_ref[at].astype(F32)
            value = advance(rows + pot_ref[at] * now, now, before).astype(BF16)
            if c == 0:
                value = jnp.concatenate([jnp.zeros((fp, width), BF16), value[fp:]], axis=0)
            if k == 0:
                first_ref[at] = value
            other_ref[at] = value

        high = sweep(h_ref, now_ref, fp, emit)
        keep(k, ends["low"], high)
        if k == 0:
            a_ref[total:] = jnp.zeros((fp, width), BF16)
        now_ref, other_ref = other_ref, now_ref
    keep(DEGREE, mul(h_ref[0, :fp], now_ref[:cp]), mul(h_ref[cells - 1, stride:], now_ref[total - stride :]))
    low = response(h_ref[0], h_ref[1], pot_ref[fp:cp], fp, False)
    high = response(h_ref[cells - 1], h_ref[cells - 2], pot_ref[total - stride :], fp, True)
    store_matrices(low, down_ref, DEGREE, fp, width)
    store_matrices(high, up_ref, DEGREE + 1, fp, width)
    for side, mats in enumerate((low, high)):
        store_matrices(mats, own_ref.at[side], DEGREE + 1, fp, width)


def forced_kernel(
    fp, place_ref, v_ref, ghost_ref, first_ref, own_ref, fromleft_ref, fromright_ref, h_ref, pot_ref,
    x_ref, image_ref, w_ref, slab_ref, a_ref, b_ref, c_ref,
):
    cells, cp = h_ref.shape[:2]
    stride = cp - fp
    total = cells * stride
    width = v_ref.shape[1]
    half = cells // 2
    extra = own_ref.shape[1] - DEGREE - 1
    potg = to_col(jnp.sum(ghost_ref[fp:].astype(F32), axis=0, keepdims=True)[:, :fp], fp)
    histories = []
    last_image = None
    for side, (got_ref, pot, start) in enumerate(
        ((fromleft_ref, pot_ref[:fp], v_ref[:fp]), (fromright_ref, potg, ghost_ref[:fp]))
    ):
        theirs = load_matrices(got_ref, got_ref.shape[0] - extra, DEGREE, fp, width)
        ours = load_matrices(own_ref.at[side], DEGREE + 1, DEGREE, fp, width)
        mats = [a + b for a, b in zip(theirs, ours)]
        mats = [split(m) for m in mats]
        values = [start]
        for k in range(DEGREE + 1 if side == 0 else DEGREE):
            h = own_ref[side, k] + got_ref[k].astype(F32)
            for m in range(1, k + 1):
                h = h + mul(mats[k - m][0], values[m]) + mul(mats[k - m][1], values[m])
            now = values[k].astype(F32)
            h = h + pot * now
            if k == DEGREE:
                last_image = h
                break
            value = advance(h, now, None if k == 0 else values[k - 1].astype(F32))
            if side == 1:
                value = jnp.where(place_ref[0] == 1, 0.0, value)
            values.append(value.astype(BF16))
        histories.append(values)
    low, high = histories
    a_ref[:fp] = low[1]
    a_ref[fp:total] = first_ref[fp:]
    a_ref[total:] = high[1]
    refs = [None, a_ref, b_ref, c_ref, a_ref]
    for k in range(1, DEGREE + 1):
        now_ref = refs[k]

        def emit(c, rows, lower, carry, k=k, now_ref=now_ref):
            at = slice(c * stride, (c + 1) * stride)
            now = now_ref[at].astype(F32)
            image = rows + pot_ref[at] * now
            if k == DEGREE:
                out = image.astype(BF16)
                part, at_w = divmod(c, half)
                w_ref[part, at_w * stride : (at_w + 1) * stride] = out
                if c == half:
                    w_ref[0, half * stride :] = carry.astype(BF16)
                    w_ref[1, :fp] = (lower + pot_ref[c * stride : c * stride + fp] * now[:fp]).astype(BF16)
                if c == 0:
                    out = jnp.concatenate([last_image.astype(BF16), out[fp:]], axis=0)
                image_ref[at] = out
                return
            before = (v_ref if k == 1 else refs[k - 1])[at].astype(F32)
            value = advance(image, now, before).astype(BF16)
            if c == 0:
                value = jnp.concatenate([low[k + 1], value[fp:]], axis=0)
            refs[k + 1][at] = value
            if k + 1 == DEGREE:
                x_ref[at] = value

        end = sweep(h_ref, now_ref, fp, emit)
        if k < DEGREE:
            refs[k + 1][total:] = high[k + 1]
        else:
            w_ref[1, half * stride :] = end.astype(BF16)
    x_ref[total:] = high[DEGREE]

    @pl.when(place_ref[1] == 0)
    def _():
        slab_ref[...] = x_ref[half * stride :]

    @pl.when(place_ref[1] == 1)
    def _():
        slab_ref[...] = x_ref[: half * stride + fp]


def back_kernel(node_ref, x_ref, image_ref, out_ref):
    rows = out_ref.shape[1]
    width = x_ref.shape[1]
    want = (lax.broadcasted_iota(jnp.int32, (rows, 1), 0) + pl.program_id(0) * rows).astype(F32)
    hit = flat(want == node_ref[...])
    out_ref[0, :, :width] = mul(hit, x_ref[...]).astype(BF16)
    out_ref[0, :, width:] = mul(hit, image_ref[...]).astype(BF16)


def back_pair_kernel(at_ref, node_ref, x_ref, image_ref, *out_refs):
    rows = out_refs[0].shape[0]
    width = x_ref.shape[1]
    for i, out_ref in enumerate(out_refs):
        want = (lax.broadcasted_iota(jnp.int32, (rows, 1), 0) + at_ref[i] * rows).astype(F32)
        hit = flat(want == node_ref[...])
        out_ref[:, :width] = mul(hit, x_ref[...]).astype(BF16)
        out_ref[:, width:] = mul(hit, image_ref[...]).astype(BF16)


def gram_kernel(scale, x_ref, y_ref, out_ref, rows_ref):
    parts, _, width = y_ref.shape

    @pl.when(pl.program_id(0) == 0)
    def _():
        for j in range(parts):
            rows_ref[:, j * width : (j + 1) * width] = y_ref[j]

    out_ref[0] = (
        lax.dot_general(x_ref[0], rows_ref[...], (((0,), (0,)), ((), ())), preferred_element_type=F32) * scale
    )


def residual_kernel(x_ref, y_ref, p_ref, out_ref):
    parts, _, width = x_ref.shape
    x = jnp.concatenate([x_ref[j] for j in range(parts)], axis=1)
    y = jnp.concatenate([y_ref[j] for j in range(parts)], axis=1)
    out_ref[...] = y.astype(F32) - jnp.dot(x, p_ref[...], preferred_element_type=F32)


def full(shape):
    return pl.BlockSpec(shape, lambda i: (0,) * len(shape))


def swap(block, axis, bit):
    return lax.ppermute(block, axis, [(i, i ^ bit) for i in range(lax.axis_size(axis))])


def shift(block, axis, distance):
    n = lax.axis_size(axis)
    return lax.ppermute(block, axis, [(i, i + distance) for i in range(n) if 0 <= i + distance < n])


def tmul(a, b):
    return lax.dot_general(a, b, (((0,), (0,)), ((), ())), preferred_element_type=F32)


def near_gram_kernel(scale, core_ref, x_ref, w_ref, other_ref, out_ref):
    slab, width = w_ref.shape[1:]
    at = (slice(0, slab), slice(x_ref.shape[0] - slab, x_ref.shape[0]))
    own = [x_ref[a] for a in at]
    out_ref[:width] = (tmul(own[0], w_ref[0]) + tmul(own[1], w_ref[1])) * scale
    half = width // 2

    @pl.when(core_ref[0] == 0)
    def _():
        out_ref[width:] = sum(tmul(own[i][:, :half], other_ref[i]) for i in range(2)) * scale

    @pl.when(core_ref[0] == 1)
    def _():
        out_ref[width:] = sum(tmul(other_ref[i, :, half:], own[i]) for i in range(2)) * scale


def far_gram_kernel(scale, place_ref, w_ref, other_ref, far_ref, near_ref, out_ref):
    width = w_ref.shape[2]
    near = near_ref.shape[0]
    side, core = place_ref[0], place_ref[1]
    out_ref[:near] = near_ref[...]
    far = far_ref[...]
    mine = pl.multiple_of(near + core * width, width // 2)
    other = pl.multiple_of(near + (1 - core) * width, width // 2)
    out_ref[pl.ds(mine, width)] = tmul(w_ref[side], far) * scale
    out_ref[pl.ds(other, width)] = tmul(other_ref[side], far) * scale


def paired_residual_kernel(place_ref, q0_ref, q1_ref, q2_ref, q3_ref, *refs):
    parts = 4
    row_refs, (out_ref, p_ref, q_ref) = refs[:parts], refs[parts:]
    width = row_refs[0].shape[1] // 2
    half = width // 2
    for k, ref in enumerate((q0_ref, q1_ref, q2_ref, q3_ref)):
        q_ref[k] = ref[...]
    me = place_ref[0]
    eye = (lax.broadcasted_iota(jnp.int32, (width, width), 0) == lax.broadcasted_iota(jnp.int32, (width, width), 1)).astype(
        F32
    ).astype(BF16)

    def turned(a):
        return lax.dot_general(eye, a, (((1,), (1,)), ((), ())), preferred_element_type=F32)

    def piece(i, lo, hi):
        return q_ref[jnp.bitwise_xor(me, i), lo:hi]

    def put(i, j, value):
        p_ref[i * width : (i + 1) * width, j * width : (j + 1) * width] = value

    near = width + half
    for i in range(parts):
        put(i, i, piece(i, 0, width))
    for i in range(0, parts, 2):
        block = jnp.concatenate([piece(i, width, near), piece(i + 1, width, near)], axis=0)
        put(i, i + 1, block)
        put(i + 1, i, turned(block).astype(BF16))
    for i in (0, 1):
        for j in (2, 3):
            one = piece(j ^ 2, near + i * width, near + (i + 1) * width)
            two = piece(i ^ 2, near + (j - 2) * width, near + (j - 1) * width)
            block = (one.astype(F32) + turned(two)).astype(BF16)
            put(i, j, block)
            put(j, i, turned(block).astype(BF16))
    x = jnp.concatenate([ref[:, :width] for ref in row_refs], axis=1)
    spots = [pl.ds(pl.multiple_of(jnp.bitwise_xor(me, k) * width, width), width) for k in range(parts)]
    for k in range(parts):
        at = spots[k]
        p = jnp.concatenate([p_ref[spots[m], at] for m in range(parts)], axis=0)
        out_ref[:, at] = row_refs[k][:, width:].astype(F32) - mul(x, p)


def paired_tail(x_own, image, w_own, give, node_row, o, d, dom, nodes):
    slab, width = w_own.shape[1:]
    orb = 4
    rows = nodes // orb
    side, core = o // 2, o % 2
    scale = 1.0 / (nodes * dom)
    sds = jax.ShapeDtypeStruct
    smem = pl.BlockSpec(memory_space=pltpu.SMEM)
    vmem = pl.BlockSpec(memory_space=pltpu.VMEM)
    far = swap(give, "orb", 2)
    total = image.shape[0]

    def back(first, second, x_own, image):
        whole = lambda *shape: pl.BlockSpec(shape, lambda i: (0,) * len(shape))
        return pl.pallas_call(
            back_pair_kernel,
            grid=(1,),
            in_specs=[smem, whole(1, total), whole(total, width), whole(total, width)],
            out_specs=[whole(rows, 2 * width)] * 2,
            out_shape=[sds((rows, 2 * width), BF16)] * 2,
            compiler_params=params(),
            cost_estimate=pl.CostEstimate(flops=1 << 20, bytes_accessed=1 << 10, transcendentals=0),
        )(jnp.stack([jnp.bitwise_xor(o, first), jnp.bitwise_xor(o, second)]), node_row, x_own, image)

    cuts = back(2, 3, x_own, image)
    w_other = swap(w_own, "orb", 1)
    top = width + width // 2
    near = pl.pallas_call(
        functools.partial(near_gram_kernel, scale),
        in_specs=[smem] + [vmem] * 3,
        out_shape=sds((top, width), F32),
        compiler_params=params(),
        cost_estimate=pl.CostEstimate(flops=1 << 20, bytes_accessed=1 << 10, transcendentals=0),
    )(core.reshape(1), x_own, w_own, w_other)
    far, near, *cuts = lax.optimization_barrier((far, near, *cuts))
    row2 = swap(cuts[0], "orb", 2)
    cut3 = cuts[1]
    share = pl.pallas_call(
        functools.partial(far_gram_kernel, scale),
        in_specs=[smem] + [vmem] * 4,
        out_shape=sds((top + 2 * width, width), F32),
        compiler_params=params(),
        cost_estimate=pl.CostEstimate(flops=8 * slab * width * width, bytes_accessed=4 << 20, transcendentals=0),
    )(jnp.stack([side, core]), w_own, w_other, far, near)

    bits = []
    bit = 1
    while bit < dom:
        mine = (d // bit) % 2
        share = share.reshape(2, share.shape[0] // 2, width)
        keep = lax.dynamic_index_in_dim(share, mine, 0, keepdims=False)
        give = lax.dynamic_index_in_dim(share, 1 - mine, 0, keepdims=False)
        give = give.astype(BF16)
        if bit == 1:
            x_own, image, give = lax.optimization_barrier((x_own, image, give))
            row0, cut1 = back(0, 1, x_own, image)
        share = keep + swap(give, "dom", bit).astype(F32)
        bits.append((bit, mine))
        bit *= 2
    share, row2, cut3 = lax.optimization_barrier((share.astype(BF16), row2, cut3))
    row3 = swap(cut3, "orb", 3)
    for bit, mine in reversed(bits):
        got = swap(share, "dom", bit)
        share = jnp.where(mine == 0, jnp.concatenate([share, got], axis=0), jnp.concatenate([got, share], axis=0))
    share, row2, row3 = lax.optimization_barrier((share, row2, row3))
    q2 = swap(share, "orb", 2)
    q1 = swap(share, "orb", 1)
    row1 = swap(cut1, "orb", 1)
    q2, row1 = lax.optimization_barrier((q2, row1))
    q3 = swap(q2, "orb", 1)
    cols = orb * width
    return pl.pallas_call(
        paired_residual_kernel,
        in_specs=[smem] + [vmem] * 8,
        out_shape=(sds((rows, cols), F32), sds((cols, cols), BF16)),
        scratch_shapes=[pltpu.VMEM((orb,) + share.shape, BF16)],
        compiler_params=params(),
    )(o.reshape(1), share, q1, q2, q3, row0, row1, row2, row3)


def body(orbitals, potential, cell_hamiltonian, connectivity, face_nodes):
    nodes, width = orbitals.shape
    cells, npc = connectivity.shape
    face = face_nodes.shape[0]
    fp, ip = up16(face), up16(npc - 2 * face)
    fp = (fp + 63) // 64 * 64
    stride = fp + ip
    cp = stride + fp
    total = cells * stride
    orb, dom = lax.axis_size("orb"), lax.axis_size("dom")
    d = lax.axis_index("dom")
    o = lax.axis_index("orb")
    sds = jax.ShapeDtypeStruct
    pot_row = potential.reshape(1, nodes)
    face_row = face_nodes.reshape(1, face)

    face_values = pl.pallas_call(
        face_kernel, out_shape=sds((fp + 16, width), BF16), compiler_params=params()
    )(face_row, orbitals, pot_row)
    ghost = shift(face_values, "dom", -1)

    extra = -(-DEGREE * fp // width)
    ext = pltpu.VMEM((total + fp, width), BF16)
    cost = pl.CostEstimate(
        flops=2 * DEGREE * cells * cp * cp * width, bytes_accessed=8 << 20, transcendentals=0
    )
    hcan, y, pot, node, first, own, up, down = pl.pallas_call(
        functools.partial(free_kernel, fp, ip),
        out_shape=[
            sds((cells, cp, cp), BF16),
            sds((total, width), BF16),
            sds((total, 1), F32),
            sds((cells, 1, stride), F32),
            sds((total, width), BF16),
            sds((2, DEGREE + 1 + extra, fp, width), F32),
            sds((DEGREE + 1 + extra, fp, width), BF16),
            sds((DEGREE + extra, fp, width), BF16),
        ],
        scratch_shapes=[ext, ext],
        compiler_params=params(),
        cost_estimate=cost,
    )(connectivity, face_row, cell_hamiltonian, orbitals, pot_row, ghost)
    node_row = node.reshape(1, total)
    from_left = shift(up, "dom", 1)
    from_right = shift(down, "dom", -1)
    vmem = pl.BlockSpec(memory_space=pltpu.VMEM)
    slab = cells // 2 * stride + fp
    place = jnp.stack([(d == dom - 1).astype(jnp.int32), (o // 2) % 2])
    x_own, image, w_own, give = pl.pallas_call(
        functools.partial(forced_kernel, fp),
        in_specs=[pl.BlockSpec(memory_space=pltpu.SMEM)] + [vmem] * 8,
        out_shape=[
            sds((total + fp, width), BF16),
            sds((total, width), BF16),
            sds((2, slab, width), BF16),
            sds((slab, width), BF16),
        ],
        scratch_shapes=[ext, ext, ext],
        compiler_params=params(),
        cost_estimate=cost,
    )(place, y, ghost, first, own, from_left, from_right, hcan, pot)

    if orb == 4 and dom % 8 == 0:
        return paired_tail(x_own, image, w_own, give, node_row, o, d, dom, nodes)
    cut = pl.pallas_call(
        back_kernel,
        grid=(orb,),
        in_specs=[full((1, total)), full((total, width)), full((total, width))],
        out_specs=pl.BlockSpec((1, nodes // orb, 2 * width), lambda i: (i, 0, 0)),
        out_shape=sds((orb, nodes // orb, 2 * width), BF16),
        compiler_params=params(),
        cost_estimate=pl.CostEstimate(flops=4 * total * nodes * width, bytes_accessed=4 << 20, transcendentals=0),
    )(node_row, x_own, image)
    both = lax.all_to_all(cut, "orb", split_axis=0, concat_axis=0, tiled=True)
    x_rows, i_rows = both[:, :, :width], both[:, :, width:]

    rows = nodes // orb
    cols = orb * width
    share = pl.pallas_call(
        functools.partial(gram_kernel, 1.0 / (nodes * dom)),
        grid=(orb,),
        in_specs=[pl.BlockSpec((1, rows, width), lambda i: (i, 0, 0)), full((orb, rows, width))],
        out_specs=pl.BlockSpec((1, width, cols), lambda i: (i, 0, 0)),
        out_shape=sds((orb, width, cols), F32),
        scratch_shapes=[pltpu.VMEM((rows, cols), BF16)],
        compiler_params=params(),
    )(x_rows, i_rows)

    hops = []
    for axis, me, size in (("orb", o, orb), ("dom", d, dom)):
        if axis == "dom":
            share = share.reshape(dom, width // dom, cols)
        bit = 1
        while bit < size:
            share = share.reshape((share.shape[0] // 2, 2) + share.shape[1:])
            mine = (me // bit) % 2
            keep = lax.dynamic_index_in_dim(share, mine, 1, keepdims=False)
            give = lax.dynamic_index_in_dim(share, 1 - mine, 1, keepdims=False)
            got = swap(give.astype(BF16), axis, bit)
            share = keep + got.astype(F32)
            hops.append((axis, bit, mine))
            bit *= 2
    share = share.astype(BF16)
    for axis, bit, mine in reversed(hops):
        if axis == "orb" and share.shape[0] == dom and bit * 2 == orb:
            share = share.reshape(1, width, cols)
        got = swap(share, axis, bit)
        share = jnp.where(mine == 0, jnp.stack([share, got], axis=1), jnp.stack([got, share], axis=1))
        share = share.reshape((share.shape[0] * 2,) + share.shape[2:])
    projected = share.reshape(cols, cols)

    residual = pl.pallas_call(
        residual_kernel, out_shape=sds((rows, cols), F32), compiler_params=params()
    )(x_rows, i_rows, projected)
    return (residual, projected)


def solution(mesh):
    return jax.shard_map(
        body,
        mesh=mesh,
        in_specs=(P("dom", "orb"), P("dom"), P("dom", None, None), P("dom", None), P("dom")),
        out_specs=(P(("dom", "orb"), None), P()),
        check_vma=False,
    )
```

```python
import functools

import jax
import jax.numpy as jnp
from jax import lax
from jax.experimental import pallas as pl
from jax.experimental.pallas import tpu as pltpu
from jax.sharding import PartitionSpec as P

DEGREE = 4
CENTER = 1.5
HALF = 2.0
F32 = jnp.float32
BF16 = jnp.bfloat16
VMEM_LIMIT = 50 * 1024 * 1024


def up16(n):
    return (n + 15) // 16 * 16


def iota(shape, dim):
    return lax.broadcasted_iota(jnp.int32, shape, dim).astype(F32)


def to_col(row, rows):
    n = row.shape[1]
    return jnp.sum(jnp.where(iota((rows, n), 0) == iota((rows, n), 1), row, 0.0), axis=1, keepdims=True)


def to_row(col):
    n = col.shape[0]
    return jnp.sum(jnp.where(iota((n, n), 0) == iota((n, n), 1), col, 0.0), axis=0, keepdims=True)


def params():
    return pltpu.CompilerParams(vmem_limit_bytes=VMEM_LIMIT)


def thirds(a):
    one = a.astype(BF16)
    rest = a - one.astype(F32)
    two = rest.astype(BF16)
    return one, two, (rest - two.astype(F32)).astype(BF16)


def face_kernel(face_ref, x_ref, pot_ref, out_ref):
    width = x_ref.shape[1]
    fp = out_ref.shape[0] - 16
    nodes = x_ref.shape[0]
    col = to_col(face_ref[...].astype(F32) + 1.0, fp) - 1.0
    hit = jnp.where(col == iota((fp, nodes), 1), 1.0, 0.0).astype(BF16)
    out_ref[:fp] = mul(hit, x_ref[...]).astype(BF16)
    ri = lax.broadcasted_iota(jnp.int32, (16, nodes), 0)
    parts = [p.astype(F32) for p in thirds(pot_ref[...])]
    rows = jnp.where(ri == 0, parts[0], jnp.where(ri == 1, parts[1], jnp.where(ri == 2, parts[2], 0.0))).astype(BF16)
    got = lax.dot_general(rows, hit, (((1,), (1,)), ((), ())), preferred_element_type=F32).astype(BF16)
    if width > fp:
        got = jnp.concatenate([got, jnp.zeros((16, width - fp), BF16)], axis=1)
    out_ref[fp:] = got


def turn(a, b):
    return lax.dot_general(a, b, (((1,), (1,)), ((), ())), preferred_element_type=F32)


def halves(a):
    high = jnp.floor(a * (1.0 / 64.0))
    return high.astype(BF16), (a - 64.0 * high).astype(BF16)


def flat(mask):
    return jnp.where(mask, 1.0, 0.0).astype(BF16)


def order(fp, ip, conn_ref, face_ref, h_ref, x_ref, pot_ref, hcan_ref, v_ref, potc_ref, node_ref):
    cells, npc = conn_ref.shape
    nodes = x_ref.shape[0]
    face = face_ref.shape[1]
    stride = fp + ip
    cp = stride + fp
    conn = conn_ref[...].astype(F32)
    eye = flat(iota((npc, npc), 0) == iota((npc, npc), 1))
    below = flat(iota((npc, npc), 0) < iota((npc, npc), 1))
    high, low = halves(conn)
    cols = 64.0 * turn(eye, high) + turn(eye, low)
    rows = [conn[c : c + 1] for c in range(cells)]
    ones = jnp.ones((cells, npc), BF16)
    same = [flat(cols[:, c : c + 1] == rows[c + 1]) for c in range(cells - 1)]
    ri = lax.broadcasted_iota(jnp.int32, (cells, npc), 0)
    top = jnp.where(conn >= float(nodes), 1.0, 0.0)
    for c in range(cells - 1):
        top = jnp.where(ri == c, turn(ones, same[c]), top)
    rank_top = mul(top.astype(BF16), below)
    rank_b = rank_top.astype(BF16)
    top_slot = jnp.where(ri == cells - 1, conn - float(nodes), rank_top)
    fhit = to_col(face_ref[...].astype(F32), face) == rows[0]
    bot = jnp.where(ri == 0, jnp.max(jnp.where(fhit, 1.0, 0.0), axis=0, keepdims=True), 0.0)
    bot_slot = jnp.where(ri == 0, jnp.sum(jnp.where(fhit, iota((face, npc), 0), 0.0), axis=0, keepdims=True), 0.0)
    for c in range(cells - 1):
        both = jnp.concatenate([ones, rank_b], axis=0)
        got = mul(both, same[c])
        bot = jnp.where(ri == c + 1, got[:1], bot)
        bot_slot = jnp.where(ri == c + 1, got[cells + c : cells + c + 1], bot_slot)
    mid_rank = mul((1.0 - top - bot).astype(BF16), below)
    slot = jnp.where(top > 0.5, top_slot + float(stride), jnp.where(bot > 0.5, bot_slot, mid_rank + float(fp)))
    high, low = halves(conn + 1.0)
    number = iota((8, nodes), 1)[:1]
    for c in range(cells):
        perm = flat(iota((cp, npc), 0) == slot[c : c + 1])
        half = mul(perm, h_ref[c]).astype(BF16)
        hcan_ref[c] = turn(half, perm).astype(BF16)
        lead = perm[:stride]
        node = 64.0 * turn(lead, high)[:, c : c + 1] + turn(lead, low)[:, c : c + 1] - 1.0
        node_ref[c] = 64.0 * turn(high, lead)[c : c + 1] + turn(low, lead)[c : c + 1] - 1.0
        at = slice(c * stride, (c + 1) * stride)
        hit = node == number
        v_ref[at] = mul(flat(hit), x_ref[...]).astype(BF16)
        potc_ref[at] = jnp.sum(jnp.where(hit, pot_ref[...], 0.0), axis=1, keepdims=True)


def advance(image, now, before):
    if before is None:
        return (image - CENTER * now) / HALF
    return 2.0 * (image - CENTER * now) / HALF - before


def split(a):
    high = a.astype(BF16)
    return high, (a - high.astype(F32)).astype(BF16)


def mul(a, b):
    return jnp.dot(a, b, preferred_element_type=F32)


def mul_r(a, b):
    high, low = split(b)
    return mul(a, high) + mul(a, low)


def sweep(h_ref, y_ref, fp, emit):
    cells, cp = h_ref.shape[:2]
    stride = cp - fp
    carry = None
    for c in range(cells):
        prod = mul(h_ref[c], y_ref[c * stride : c * stride + cp])
        rows = prod[:stride]
        if c > 0:
            rows = jnp.concatenate([rows[:fp] + carry, rows[fp:]], axis=0)
        emit(c, rows, prod[:fp], carry)
        carry = prod[stride:]
    return carry


def response(hc, hn, potc, fp, upper):
    cp = hc.shape[0]
    stride = cp - fp
    if upper:
        f, r, s, g = slice(stride, cp), slice(0, stride), slice(0, fp), slice(stride, cp)
        rest = slice(0, stride)
    else:
        f, r, s, g = slice(0, fp), slice(fp, cp), slice(stride - fp, stride), slice(0, fp)
        rest = slice(fp, cp)
    gain = 2.0 / HALF
    out = [hc[f, f].astype(F32)]
    one = gain * hc[r, f].astype(F32)
    out.append(mul_r(hc[f, r], one))

    def pad_next(face_rows):
        zero = jnp.zeros((stride, fp), F32)
        return jnp.concatenate([zero, face_rows] if upper else [face_rows, zero], axis=0)

    def near(value, next_value):
        got = mul_r(hc[r, r], value) + (potc - CENTER) * value
        add = mul_r(hn[g, :], next_value)
        if upper:
            return jnp.concatenate([got[:fp] + add, got[fp:]], axis=0)
        return jnp.concatenate([got[: stride - fp], got[stride - fp :] + add], axis=0)

    two = gain * near(one, pad_next(one[s]))
    out.append(mul_r(hc[f, r], two))
    two_next = gain * mul_r(hn, pad_next(one[s]))
    if upper:
        two_next = jnp.concatenate([two_next[:stride], two[s]], axis=0)
    else:
        two_next = jnp.concatenate([two[s], two_next[fp:]], axis=0)
    three = gain * near(two, two_next) - one
    out.append(mul_r(hc[f, r], three))
    return out


def store_matrices(mats, out_ref, at, fp, width):
    for j, m in enumerate(mats):
        block, lane = divmod(j * fp, width)
        out_ref[at + block, :, lane : lane + fp] = m.astype(out_ref.dtype)


def load_matrices(ref, at, count, fp, width):
    spots = [divmod(j * fp, width) for j in range(count)]
    return [ref[at + block, :, lane : lane + fp].astype(F32) for block, lane in spots]


def free_kernel(
    fp, ip, conn_ref, face_ref, hraw_ref, raw_ref, potraw_ref, ghost_ref,
    h_ref, v_ref, pot_ref, node_ref, first_ref, own_ref, up_ref, down_ref, a_ref, b_ref,
):
    order(fp, ip, conn_ref, face_ref, hraw_ref, raw_ref, potraw_ref, h_ref, v_ref, pot_ref, node_ref)
    cells, cp = h_ref.shape[:2]
    stride = cp - fp
    total = cells * stride
    width = v_ref.shape[1]
    a_ref[:total] = v_ref[...]
    a_ref[total:] = ghost_ref[:fp]
    b_ref[total:] = jnp.zeros((fp, width), BF16)

    def keep(k, low, high):
        own_ref[0, k] = low
        own_ref[1, k] = high
        if k < DEGREE:
            down_ref[k] = low.astype(BF16)
        up_ref[k] = high.astype(BF16)

    now_ref, other_ref = a_ref, b_ref
    for k in range(DEGREE):
        ends = {}

        def emit(c, rows, lower, carry, k=k, now_ref=now_ref, other_ref=other_ref, ends=ends):
            at = slice(c * stride, (c + 1) * stride)
            if c == 0:
                ends["low"] = rows[:fp]
            now = now_ref[at].astype(F32)
            before = None if k == 0 else other_ref[at].astype(F32)
            if k == 1:
                before = v_ref[at].astype(F32)
            value = advance(rows + pot_ref[at] * now, now, before).astype(BF16)
            if c == 0:
                value = jnp.concatenate([jnp.zeros((fp, width), BF16), value[fp:]], axis=0)
            if k == 0:
                first_ref[at] = value
            other_ref[at] = value

        high = sweep(h_ref, now_ref, fp, emit)
        keep(k, ends["low"], high)
        if k == 0:
            a_ref[total:] = jnp.zeros((fp, width), BF16)
        now_ref, other_ref = other_ref, now_ref
    keep(DEGREE, mul(h_ref[0, :fp], now_ref[:cp]), mul(h_ref[cells - 1, stride:], now_ref[total - stride :]))
    low = response(h_ref[0], h_ref[1], pot_ref[fp:cp], fp, False)
    high = response(h_ref[cells - 1], h_ref[cells - 2], pot_ref[total - stride :], fp, True)
    store_matrices(low, down_ref, DEGREE, fp, width)
    store_matrices(high, up_ref, DEGREE + 1, fp, width)
    for side, mats in enumerate((low, high)):
        store_matrices(mats, own_ref.at[side], DEGREE + 1, fp, width)


def forced_kernel(
    fp, place_ref, v_ref, ghost_ref, first_ref, own_ref, fromleft_ref, fromright_ref, h_ref, pot_ref,
    x_ref, face_image_ref, slab_ref, a_ref, b_ref, c_ref,
):
    cells, cp = h_ref.shape[:2]
    stride = cp - fp
    total = cells * stride
    width = v_ref.shape[1]
    half = cells // 2
    extra = own_ref.shape[1] - DEGREE - 1
    potg = to_col(jnp.sum(ghost_ref[fp:].astype(F32), axis=0, keepdims=True)[:, :fp], fp)
    nothing = jnp.zeros((fp, width), BF16)
    sides = []
    for side, (got_ref, pot, start) in enumerate(
        ((fromleft_ref, pot_ref[:fp], v_ref[:fp]), (fromright_ref, potg, ghost_ref[:fp]))
    ):
        theirs = load_matrices(got_ref, got_ref.shape[0] - extra, DEGREE, fp, width)
        ours = load_matrices(own_ref.at[side], DEGREE + 1, DEGREE, fp, width)
        mats = [a + b for a, b in zip(theirs, ours)]
        line = jnp.concatenate(mats[::-1], axis=1)
        sides.append((got_ref, pot, jnp.concatenate(split(line), axis=0), [start]))
    for k in range(DEGREE + 1):
        for side, (got_ref, pot, line, values) in enumerate(sides):
            if side == 1 and k == DEGREE:
                continue
            h = own_ref[side, k] + got_ref[k].astype(F32)
            if k > 0:
                past = [values[m] if m >= 1 else nothing for m in range(k - DEGREE + 1, k + 1)]
                both = mul(line, jnp.concatenate(past, axis=0))
                h = h + both[:fp] + both[fp:]
            now = values[k].astype(F32)
            h = h + pot * now
            if k == DEGREE:
                face_image_ref[...] = h
                continue
            value = advance(h, now, None if k == 0 else values[k - 1].astype(F32))
            if side == 1:
                value = jnp.where(place_ref[0] == 1, 0.0, value)
            values.append(value.astype(BF16))
    low, high = sides[0][3], sides[1][3]
    a_ref[:fp] = low[1]
    a_ref[fp:total] = first_ref[fp:]
    a_ref[total:] = high[1]
    refs = [v_ref, a_ref, b_ref, c_ref, x_ref]
    for k in range(1, DEGREE):
        now_ref = refs[k]

        def emit(c, rows, lower, carry, k=k, now_ref=now_ref):
            at = slice(c * stride, (c + 1) * stride)
            now = now_ref[at].astype(F32)
            value = advance(rows + pot_ref[at] * now, now, refs[k - 1][at].astype(F32)).astype(BF16)
            if c == 0:
                value = jnp.concatenate([low[k + 1], value[fp:]], axis=0)
            refs[k + 1][at] = value

        sweep(h_ref, now_ref, fp, emit)
        refs[k + 1][total:] = high[k + 1]

    @pl.when(place_ref[1] == 0)
    def _():
        slab_ref[...] = x_ref[half * stride :]

    @pl.when(place_ref[1] == 1)
    def _():
        slab_ref[...] = x_ref[: half * stride + fp]


def image_kernel(fp, place_ref, x_ref, face_image_ref, h_ref, pot_ref, image_ref, w_ref, first_ref, second_ref):
    cells, cp = h_ref.shape[:2]
    stride = cp - fp
    half = cells // 2

    def emit(c, rows, lower, carry):
        at = slice(c * stride, (c + 1) * stride)
        now = x_ref[at].astype(F32)
        out = (rows + pot_ref[at] * now).astype(BF16)
        part, at_w = divmod(c, half)
        w_ref[part, at_w * stride : (at_w + 1) * stride] = out
        if c == half:
            w_ref[0, half * stride :] = carry.astype(BF16)
            w_ref[1, :fp] = (lower + pot_ref[c * stride : c * stride + fp] * now[:fp]).astype(BF16)
        if c == 0:
            out = jnp.concatenate([face_image_ref[...].astype(BF16), out[fp:]], axis=0)
        image_ref[at] = out

    w_ref[1, half * stride :] = sweep(h_ref, x_ref, fp, emit).astype(BF16)
    n = first_ref.shape[0]
    first_ref[...] = w_ref[place_ref[1], :n]
    second_ref[...] = w_ref[place_ref[1], n:]


def back_kernel(node_ref, x_ref, image_ref, out_ref):
    rows = out_ref.shape[1]
    width = x_ref.shape[1]
    want = (lax.broadcasted_iota(jnp.int32, (rows, 1), 0) + pl.program_id(0) * rows).astype(F32)
    hit = flat(want == node_ref[...])
    out_ref[0, :, :width] = mul(hit, x_ref[...]).astype(BF16)
    out_ref[0, :, width:] = mul(hit, image_ref[...]).astype(BF16)


def back_pair_kernel(at_ref, node_ref, x_ref, image_ref, *out_refs):
    rows = out_refs[0].shape[0]
    width = x_ref.shape[1]
    for i, out_ref in enumerate(out_refs):
        want = (lax.broadcasted_iota(jnp.int32, (rows, 1), 0) + at_ref[i] * rows).astype(F32)
        hit = flat(want == node_ref[...])
        out_ref[:, :width] = mul(hit, x_ref[...]).astype(BF16)
        out_ref[:, width:] = mul(hit, image_ref[...]).astype(BF16)


def gram_kernel(scale, x_ref, y_ref, out_ref, rows_ref):
    parts, _, width = y_ref.shape

    @pl.when(pl.program_id(0) == 0)
    def _():
        for j in range(parts):
            rows_ref[:, j * width : (j + 1) * width] = y_ref[j]

    out_ref[0] = (
        lax.dot_general(x_ref[0], rows_ref[...], (((0,), (0,)), ((), ())), preferred_element_type=F32) * scale
    )


def residual_kernel(x_ref, y_ref, p_ref, out_ref):
    parts, _, width = x_ref.shape
    x = jnp.concatenate([x_ref[j] for j in range(parts)], axis=1)
    y = jnp.concatenate([y_ref[j] for j in range(parts)], axis=1)
    out_ref[...] = y.astype(F32) - jnp.dot(x, p_ref[...], preferred_element_type=F32)


def full(shape):
    return pl.BlockSpec(shape, lambda i: (0,) * len(shape))


def swap(block, axis, bit):
    return lax.ppermute(block, axis, [(i, i ^ bit) for i in range(lax.axis_size(axis))])


def shift(block, axis, distance):
    n = lax.axis_size(axis)
    return lax.ppermute(block, axis, [(i, i + distance) for i in range(n) if 0 <= i + distance < n])


def tmul(a, b):
    return lax.dot_general(a, b, (((0,), (0,)), ((), ())), preferred_element_type=F32)


def near_gram_kernel(scale, core_ref, x_ref, w_ref, other_ref, out_ref):
    slab, width = w_ref.shape[1:]
    at = (slice(0, slab), slice(x_ref.shape[0] - slab, x_ref.shape[0]))
    own = [x_ref[a] for a in at]
    out_ref[:width] = (tmul(own[0], w_ref[0]) + tmul(own[1], w_ref[1])) * scale
    half = width // 2

    @pl.when(core_ref[0] == 0)
    def _():
        out_ref[width:] = sum(tmul(w_ref[i, :, :half], other_ref[at[i]]) for i in range(2)) * scale

    @pl.when(core_ref[0] == 1)
    def _():
        out_ref[width:] = sum(tmul(other_ref[at[i], half:], w_ref[i]) for i in range(2)) * scale


def part_ways(sum_ref, mine, keep_ref, give_ref):
    n = keep_ref.shape[0]
    keep_ref[...] = sum_ref[pl.ds(pl.multiple_of(mine * n, 16), n)]
    give_ref[...] = sum_ref[pl.ds(pl.multiple_of((1 - mine) * n, 16), n)].astype(BF16)


def halve_kernel(step, bits_ref, keep_ref, got_ref, *refs):
    total = keep_ref[...] + got_ref[...].astype(F32)
    if len(refs) == 1:
        refs[0][...] = total.astype(BF16)
        return
    *outs, sum_ref = refs
    sum_ref[...] = total
    part_ways(sum_ref, bits_ref[step], *outs)


def join_kernel(step, bits_ref, own_ref, got_ref, out_ref):
    n = own_ref.shape[0]
    mine = bits_ref[step]
    out_ref[pl.ds(pl.multiple_of(mine * n, 16), n)] = own_ref[...]
    out_ref[pl.ds(pl.multiple_of((1 - mine) * n, 16), n)] = got_ref[...]


def far_gram_kernel(scale, bits_ref, place_ref, w_ref, first_ref, second_ref, far_ref, near_ref, keep_ref, give_ref, out_ref):
    width = w_ref.shape[2]
    near = near_ref.shape[0]
    side, core = place_ref[0], place_ref[1]
    out_ref[:near] = near_ref[...]
    far = far_ref[...]
    mine = pl.multiple_of(near + core * width, width // 2)
    other = pl.multiple_of(near + (1 - core) * width, width // 2)
    out_ref[pl.ds(mine, width)] = tmul(w_ref[side], far) * scale
    n = first_ref.shape[0]
    out_ref[pl.ds(other, width)] = (tmul(first_ref[...], far[:n]) + tmul(second_ref[...], far[n:])) * scale
    part_ways(out_ref, bits_ref[0], keep_ref, give_ref)


def paired_residual_kernel(place_ref, q0_ref, q1_ref, q2_ref, q3_ref, *refs):
    parts = 4
    row_refs, (out_ref, p_ref, q_ref) = refs[:parts], refs[parts:]
    width = row_refs[0].shape[1] // 2
    half = width // 2
    for k, ref in enumerate((q0_ref, q1_ref, q2_ref, q3_ref)):
        q_ref[k] = ref[...]
    me = place_ref[0]
    eye = (lax.broadcasted_iota(jnp.int32, (width, width), 0) == lax.broadcasted_iota(jnp.int32, (width, width), 1)).astype(
        F32
    ).astype(BF16)

    def turned(a):
        return lax.dot_general(eye, a, (((1,), (1,)), ((), ())), preferred_element_type=F32)

    def piece(i, lo, hi):
        return q_ref[jnp.bitwise_xor(me, i), lo:hi]

    def put(i, j, value):
        p_ref[i * width : (i + 1) * width, j * width : (j + 1) * width] = value

    near = width + half
    for i in range(parts):
        put(i, i, piece(i, 0, width))
    for i in range(0, parts, 2):
        block = jnp.concatenate([piece(i, width, near), piece(i + 1, width, near)], axis=0)
        put(i, i + 1, block)
        put(i + 1, i, turned(block).astype(BF16))
    for i in (0, 1):
        for j in (2, 3):
            one = piece(j ^ 2, near + i * width, near + (i + 1) * width)
            two = piece(i ^ 2, near + (j - 2) * width, near + (j - 1) * width)
            block = (one.astype(F32) + turned(two)).astype(BF16)
            put(i, j, block)
            put(j, i, turned(block).astype(BF16))
    x = jnp.concatenate([ref[:, :width] for ref in row_refs], axis=1)
    spots = [pl.ds(pl.multiple_of(jnp.bitwise_xor(me, k) * width, width), width) for k in range(parts)]
    for k in range(parts):
        at = spots[k]
        p = jnp.concatenate([p_ref[spots[m], at] for m in range(parts)], axis=0)
        out_ref[:, at] = row_refs[k][:, width:].astype(F32) - mul(x, p)


def paired_tail(x_own, image, w_own, w_side, give, node_row, o, d, dom, nodes):
    slab, width = w_own.shape[1:]
    orb = 4
    rows = nodes // orb
    side, core = o // 2, o % 2
    scale = 1.0 / (nodes * dom)
    sds = jax.ShapeDtypeStruct
    smem = pl.BlockSpec(memory_space=pltpu.SMEM)
    vmem = pl.BlockSpec(memory_space=pltpu.VMEM)
    far = swap(give, "orb", 2)
    total = image.shape[0]

    def back(first, second, x_own, image):
        whole = lambda *shape: pl.BlockSpec(shape, lambda i: (0,) * len(shape))
        return pl.pallas_call(
            back_pair_kernel,
            grid=(1,),
            in_specs=[smem, whole(1, total), whole(total, width), whole(total, width)],
            out_specs=[whole(rows, 2 * width)] * 2,
            out_shape=[sds((rows, 2 * width), BF16)] * 2,
            compiler_params=params(),
            cost_estimate=pl.CostEstimate(flops=1 << 20, bytes_accessed=1 << 10, transcendentals=0),
        )(jnp.stack([jnp.bitwise_xor(o, first), jnp.bitwise_xor(o, second)]), node_row, x_own, image)

    cuts = back(2, 3, x_own, image)
    x_other = swap(x_own, "orb", 1)
    w_other = [swap(w, "orb", 1) for w in w_side]
    top = width + width // 2
    near = pl.pallas_call(
        functools.partial(near_gram_kernel, scale),
        in_specs=[smem] + [vmem] * 3,
        out_shape=sds((top, width), F32),
        compiler_params=params(),
        cost_estimate=pl.CostEstimate(flops=1 << 20, bytes_accessed=1 << 10, transcendentals=0),
    )(core.reshape(1), x_own, w_own, x_other)
    far, near, *cuts, w_other[0], w_other[1] = lax.optimization_barrier((far, near, *cuts, *w_other))
    row2 = swap(cuts[0], "orb", 2)
    cut3 = cuts[1]
    steps = (dom - 1).bit_length()
    bits = jnp.stack([(d // (1 << i)) % 2 for i in range(steps)])
    little = pl.CostEstimate(flops=1 << 10, bytes_accessed=1 << 10, transcendentals=0)
    count = top + 2 * width
    keep, give = pl.pallas_call(
        functools.partial(far_gram_kernel, scale),
        in_specs=[smem] * 2 + [vmem] * 5,
        out_shape=[sds((count // 2, width), F32), sds((count // 2, width), BF16)],
        scratch_shapes=[pltpu.VMEM((count, width), F32)],
        compiler_params=params(),
        cost_estimate=pl.CostEstimate(flops=8 * slab * width * width, bytes_accessed=4 << 20, transcendentals=0),
    )(bits, jnp.stack([side, core]), w_own, *w_other, far, near)
    row0 = cut1 = row3 = None
    for i in range(steps):
        if i == 0:
            x_own, image, give = lax.optimization_barrier((x_own, image, give))
            row0, cut1 = back(0, 1, x_own, image)
        got = swap(give, "dom", 1 << i)
        n = keep.shape[0]
        last = i == steps - 1
        outs = pl.pallas_call(
            functools.partial(halve_kernel, i + 1),
            in_specs=[smem] + [vmem] * 2,
            out_shape=[sds((n, width), BF16)] if last else [sds((n // 2, width), F32), sds((n // 2, width), BF16)],
            scratch_shapes=[] if last else [pltpu.VMEM((n, width), F32)],
            compiler_params=params(),
            cost_estimate=little,
        )(bits, keep, got)
        outs = list(outs)
        if i == 1:
            outs[-1], row2, cut3 = lax.optimization_barrier((outs[-1], row2, cut3))
            row3 = swap(cut3, "orb", 3)
        if last:
            share = outs[0]
        else:
            keep, give = outs
    for i in reversed(range(steps)):
        got = swap(share, "dom", 1 << i)
        share = pl.pallas_call(
            functools.partial(join_kernel, i),
            in_specs=[smem] + [vmem] * 2,
            out_shape=sds((2 * share.shape[0], width), BF16),
            compiler_params=params(),
            cost_estimate=little,
        )(bits, share, got)
        if i == 1:
            share, row3 = lax.optimization_barrier((share, row3))
    q2 = swap(share, "orb", 2)
    q1 = swap(share, "orb", 1)
    row1 = swap(cut1, "orb", 1)
    q2, row1 = lax.optimization_barrier((q2, row1))
    q3 = swap(q2, "orb", 1)
    cols = orb * width
    return pl.pallas_call(
        paired_residual_kernel,
        in_specs=[smem] + [vmem] * 8,
        out_shape=(sds((rows, cols), F32), sds((cols, cols), BF16)),
        scratch_shapes=[pltpu.VMEM((orb,) + share.shape, BF16)],
        compiler_params=params(),
    )(o.reshape(1), share, q1, q2, q3, row0, row1, row2, row3)


def body(orbitals, potential, cell_hamiltonian, connectivity, face_nodes):
    nodes, width = orbitals.shape
    cells, npc = connectivity.shape
    face = face_nodes.shape[0]
    fp, ip = up16(face), up16(npc - 2 * face)
    fp = (fp + 63) // 64 * 64
    stride = fp + ip
    cp = stride + fp
    total = cells * stride
    orb, dom = lax.axis_size("orb"), lax.axis_size("dom")
    d = lax.axis_index("dom")
    o = lax.axis_index("orb")
    sds = jax.ShapeDtypeStruct
    pot_row = potential.reshape(1, nodes)
    face_row = face_nodes.reshape(1, face)

    face_values = pl.pallas_call(
        face_kernel, out_shape=sds((fp + 16, width), BF16), compiler_params=params()
    )(face_row, orbitals, pot_row)
    ghost = shift(face_values, "dom", -1)

    extra = -(-DEGREE * fp // width)
    ext = pltpu.VMEM((total + fp, width), BF16)
    cost = pl.CostEstimate(
        flops=2 * DEGREE * cells * cp * cp * width, bytes_accessed=8 << 20, transcendentals=0
    )
    hcan, y, pot, node, first, own, up, down = pl.pallas_call(
        functools.partial(free_kernel, fp, ip),
        out_shape=[
            sds((cells, cp, cp), BF16),
            sds((total, width), BF16),
            sds((total, 1), F32),
            sds((cells, 1, stride), F32),
            sds((total, width), BF16),
            sds((2, DEGREE + 1 + extra, fp, width), F32),
            sds((DEGREE + 1 + extra, fp, width), BF16),
            sds((DEGREE + extra, fp, width), BF16),
        ],
        scratch_shapes=[ext, ext],
        compiler_params=params(),
        cost_estimate=cost,
    )(connectivity, face_row, cell_hamiltonian, orbitals, pot_row, ghost)
    node_row = node.reshape(1, total)
    from_left = shift(up, "dom", 1)
    from_right = shift(down, "dom", -1)
    vmem = pl.BlockSpec(memory_space=pltpu.VMEM)
    slab = cells // 2 * stride + fp
    place = jnp.stack([(d == dom - 1).astype(jnp.int32), (o // 2) % 2])
    x_own, face_image, give = pl.pallas_call(
        functools.partial(forced_kernel, fp),
        in_specs=[pl.BlockSpec(memory_space=pltpu.SMEM)] + [vmem] * 8,
        out_shape=[
            sds((total + fp, width), BF16),
            sds((fp, width), F32),
            sds((slab, width), BF16),
        ],
        scratch_shapes=[ext, ext, ext],
        compiler_params=params(),
        cost_estimate=cost,
    )(place, y, ghost, first, own, from_left, from_right, hcan, pot)
    image, w_own, *w_side = pl.pallas_call(
        functools.partial(image_kernel, fp),
        in_specs=[pl.BlockSpec(memory_space=pltpu.SMEM)] + [vmem] * 4,
        out_shape=[sds((total, width), BF16), sds((2, slab, width), BF16)] + [sds((slab // 2, width), BF16)] * 2,
        compiler_params=params(),
        cost_estimate=pl.CostEstimate(flops=1 << 20, bytes_accessed=1 << 10, transcendentals=0),
    )(place, x_own, face_image, hcan, pot)

    if orb == 4 and dom % 8 == 0:
        return paired_tail(x_own, image, w_own, w_side, give, node_row, o, d, dom, nodes)
    cut = pl.pallas_call(
        back_kernel,
        grid=(orb,),
        in_specs=[full((1, total)), full((total, width)), full((total, width))],
        out_specs=pl.BlockSpec((1, nodes // orb, 2 * width), lambda i: (i, 0, 0)),
        out_shape=sds((orb, nodes // orb, 2 * width), BF16),
        compiler_params=params(),
        cost_estimate=pl.CostEstimate(flops=4 * total * nodes * width, bytes_accessed=4 << 20, transcendentals=0),
    )(node_row, x_own, image)
    both = lax.all_to_all(cut, "orb", split_axis=0, concat_axis=0, tiled=True)
    x_rows, i_rows = both[:, :, :width], both[:, :, width:]

    rows = nodes // orb
    cols = orb * width
    share = pl.pallas_call(
        functools.partial(gram_kernel, 1.0 / (nodes * dom)),
        grid=(orb,),
        in_specs=[pl.BlockSpec((1, rows, width), lambda i: (i, 0, 0)), full((orb, rows, width))],
        out_specs=pl.BlockSpec((1, width, cols), lambda i: (i, 0, 0)),
        out_shape=sds((orb, width, cols), F32),
        scratch_shapes=[pltpu.VMEM((rows, cols), BF16)],
        compiler_params=params(),
    )(x_rows, i_rows)

    hops = []
    for axis, me, size in (("orb", o, orb), ("dom", d, dom)):
        if axis == "dom":
            share = share.reshape(dom, width // dom, cols)
        bit = 1
        while bit < size:
            share = share.reshape((share.shape[0] // 2, 2) + share.shape[1:])
            mine = (me // bit) % 2
            keep = lax.dynamic_index_in_dim(share, mine, 1, keepdims=False)
            give = lax.dynamic_index_in_dim(share, 1 - mine, 1, keepdims=False)
            got = swap(give.astype(BF16), axis, bit)
            share = keep + got.astype(F32)
            hops.append((axis, bit, mine))
            bit *= 2
    share = share.astype(BF16)
    for axis, bit, mine in reversed(hops):
        if axis == "orb" and share.shape[0] == dom and bit * 2 == orb:
            share = share.reshape(1, width, cols)
        got = swap(share, axis, bit)
        share = jnp.where(mine == 0, jnp.stack([share, got], axis=1), jnp.stack([got, share], axis=1))
        share = share.reshape((share.shape[0] * 2,) + share.shape[2:])
    projected = share.reshape(cols, cols)

    residual = pl.pallas_call(
        residual_kernel, out_shape=sds((rows, cols), F32), compiler_params=params()
    )(x_rows, i_rows, projected)
    return (residual, projected)


def solution(mesh):
    return jax.shard_map(
        body,
        mesh=mesh,
        in_specs=(P("dom", "orb"), P("dom"), P("dom", None, None), P("dom", None), P("dom")),
        out_specs=(P(("dom", "orb"), None), P()),
        check_vma=False,
    )
```

```python
import functools

import jax
import jax.numpy as jnp
from jax import lax
from jax.experimental import pallas as pl
from jax.experimental.pallas import tpu as pltpu
from jax.sharding import PartitionSpec as P

DEGREE = 4
CENTER = 1.5
HALF = 2.0
F32 = jnp.float32
BF16 = jnp.bfloat16
VMEM_LIMIT = 50 * 1024 * 1024


def up16(n):
    return (n + 15) // 16 * 16


def iota(shape, dim):
    return lax.broadcasted_iota(jnp.int32, shape, dim).astype(F32)


def to_col(row, rows):
    n = row.shape[1]
    return jnp.sum(jnp.where(iota((rows, n), 0) == iota((rows, n), 1), row, 0.0), axis=1, keepdims=True)


def to_row(col):
    n = col.shape[0]
    return jnp.sum(jnp.where(iota((n, n), 0) == iota((n, n), 1), col, 0.0), axis=0, keepdims=True)


def params():
    return pltpu.CompilerParams(vmem_limit_bytes=VMEM_LIMIT)


def thirds(a):
    one = a.astype(BF16)
    rest = a - one.astype(F32)
    two = rest.astype(BF16)
    return one, two, (rest - two.astype(F32)).astype(BF16)


def face_kernel(face_ref, x_ref, pot_ref, out_ref):
    width = x_ref.shape[1]
    fp = out_ref.shape[0] - 16
    nodes = x_ref.shape[0]
    col = to_col(face_ref[...].astype(F32) + 1.0, fp) - 1.0
    hit = jnp.where(col == iota((fp, nodes), 1), 1.0, 0.0).astype(BF16)
    out_ref[:fp] = mul(hit, x_ref[...]).astype(BF16)
    ri = lax.broadcasted_iota(jnp.int32, (16, nodes), 0)
    parts = [p.astype(F32) for p in thirds(pot_ref[...])]
    rows = jnp.where(ri == 0, parts[0], jnp.where(ri == 1, parts[1], jnp.where(ri == 2, parts[2], 0.0))).astype(BF16)
    got = lax.dot_general(rows, hit, (((1,), (1,)), ((), ())), preferred_element_type=F32).astype(BF16)
    if width > fp:
        got = jnp.concatenate([got, jnp.zeros((16, width - fp), BF16)], axis=1)
    out_ref[fp:] = got


def turn(a, b):
    return lax.dot_general(a, b, (((1,), (1,)), ((), ())), preferred_element_type=F32)


def halves(a):
    high = jnp.floor(a * (1.0 / 64.0))
    return high.astype(BF16), (a - 64.0 * high).astype(BF16)


def flat(mask):
    return jnp.where(mask, 1.0, 0.0).astype(BF16)


def order(fp, ip, conn_ref, face_ref, h_ref, x_ref, pot_ref, hcan_ref, v_ref, potc_ref, node_ref):
    cells, npc = conn_ref.shape
    nodes = x_ref.shape[0]
    face = face_ref.shape[1]
    stride = fp + ip
    cp = stride + fp
    conn = conn_ref[...].astype(F32)
    eye = flat(iota((npc, npc), 0) == iota((npc, npc), 1))
    below = flat(iota((npc, npc), 0) < iota((npc, npc), 1))
    high, low = halves(conn)
    cols = 64.0 * turn(eye, high) + turn(eye, low)
    rows = [conn[c : c + 1] for c in range(cells)]
    ones = jnp.ones((cells, npc), BF16)
    same = [flat(cols[:, c : c + 1] == rows[c + 1]) for c in range(cells - 1)]
    ri = lax.broadcasted_iota(jnp.int32, (cells, npc), 0)
    top = jnp.where(conn >= float(nodes), 1.0, 0.0)
    for c in range(cells - 1):
        top = jnp.where(ri == c, turn(ones, same[c]), top)
    rank_top = mul(top.astype(BF16), below)
    rank_b = rank_top.astype(BF16)
    top_slot = jnp.where(ri == cells - 1, conn - float(nodes), rank_top)
    fhit = to_col(face_ref[...].astype(F32), face) == rows[0]
    bot = jnp.where(ri == 0, jnp.max(jnp.where(fhit, 1.0, 0.0), axis=0, keepdims=True), 0.0)
    bot_slot = jnp.where(ri == 0, jnp.sum(jnp.where(fhit, iota((face, npc), 0), 0.0), axis=0, keepdims=True), 0.0)
    for c in range(cells - 1):
        both = jnp.concatenate([ones, rank_b], axis=0)
        got = mul(both, same[c])
        bot = jnp.where(ri == c + 1, got[:1], bot)
        bot_slot = jnp.where(ri == c + 1, got[cells + c : cells + c + 1], bot_slot)
    mid_rank = mul((1.0 - top - bot).astype(BF16), below)
    slot = jnp.where(top > 0.5, top_slot + float(stride), jnp.where(bot > 0.5, bot_slot, mid_rank + float(fp)))
    high, low = halves(conn + 1.0)
    number = iota((8, nodes), 1)[:1]
    for c in range(cells):
        perm = flat(iota((cp, npc), 0) == slot[c : c + 1])
        half = mul(perm, h_ref[c]).astype(BF16)
        hcan_ref[c] = turn(half, perm).astype(BF16)
        lead = perm[:stride]
        node = 64.0 * turn(lead, high)[:, c : c + 1] + turn(lead, low)[:, c : c + 1] - 1.0
        node_ref[c] = 64.0 * turn(high, lead)[c : c + 1] + turn(low, lead)[c : c + 1] - 1.0
        at = slice(c * stride, (c + 1) * stride)
        hit = node == number
        v_ref[at] = mul(flat(hit), x_ref[...]).astype(BF16)
        potc_ref[at] = jnp.sum(jnp.where(hit, pot_ref[...], 0.0), axis=1, keepdims=True)


def advance(image, now, before):
    if before is None:
        return (image - CENTER * now) / HALF
    return 2.0 * (image - CENTER * now) / HALF - before


def split(a):
    high = a.astype(BF16)
    return high, (a - high.astype(F32)).astype(BF16)


def mul(a, b):
    return jnp.dot(a, b, preferred_element_type=F32)


def mul_r(a, b):
    n = b.shape[1]
    both = mul(a, jnp.concatenate(split(b), axis=1))
    return both[:, :n] + both[:, n:]


def sweep(h_ref, y_ref, fp, emit):
    cells, cp = h_ref.shape[:2]
    stride = cp - fp
    carry = None
    for c in range(cells):
        prod = mul(h_ref[c], y_ref[c * stride : c * stride + cp])
        rows = prod[:stride]
        if c > 0:
            rows = jnp.concatenate([rows[:fp] + carry, rows[fp:]], axis=0)
        emit(c, rows, prod[:fp], carry)
        carry = prod[stride:]
    return carry


def response(hc, hn, potc, fp, upper):
    cp = hc.shape[0]
    stride = cp - fp
    if upper:
        f, r, s, g = slice(stride, cp), slice(0, stride), slice(0, fp), slice(stride, cp)
        rest = slice(0, stride)
    else:
        f, r, s, g = slice(0, fp), slice(fp, cp), slice(stride - fp, stride), slice(0, fp)
        rest = slice(fp, cp)
    gain = 2.0 / HALF
    out = [hc[f, f].astype(F32)]
    one = gain * hc[r, f].astype(F32)
    out.append(mul_r(hc[f, r], one))

    def pad_next(face_rows):
        zero = jnp.zeros((stride, fp), F32)
        return jnp.concatenate([zero, face_rows] if upper else [face_rows, zero], axis=0)

    def near(value, next_value):
        got = mul_r(hc[r, r], value) + (potc - CENTER) * value
        add = mul_r(hn[g, :], next_value)
        if upper:
            return jnp.concatenate([got[:fp] + add, got[fp:]], axis=0)
        return jnp.concatenate([got[: stride - fp], got[stride - fp :] + add], axis=0)

    two = gain * near(one, pad_next(one[s]))
    out.append(mul_r(hc[f, r], two))
    two_next = gain * mul_r(hn, pad_next(one[s]))
    if upper:
        two_next = jnp.concatenate([two_next[:stride], two[s]], axis=0)
    else:
        two_next = jnp.concatenate([two[s], two_next[fp:]], axis=0)
    three = gain * near(two, two_next) - one
    out.append(mul_r(hc[f, r], three))
    return out


def store_matrices(mats, out_ref, at, fp, width):
    for j, m in enumerate(mats):
        block, lane = divmod(j * fp, width)
        out_ref[at + block, :, lane : lane + fp] = m.astype(out_ref.dtype)


def load_matrices(ref, at, count, fp, width):
    spots = [divmod(j * fp, width) for j in range(count)]
    return [ref[at + block, :, lane : lane + fp].astype(F32) for block, lane in spots]


def free_kernel(
    fp, ip, conn_ref, face_ref, hraw_ref, raw_ref, potraw_ref, ghost_ref,
    h_ref, v_ref, pot_ref, node_ref, first_ref, own_ref, up_ref, down_ref, a_ref, b_ref,
):
    order(fp, ip, conn_ref, face_ref, hraw_ref, raw_ref, potraw_ref, h_ref, v_ref, pot_ref, node_ref)
    cells, cp = h_ref.shape[:2]
    stride = cp - fp
    total = cells * stride
    width = v_ref.shape[1]
    a_ref[:total] = v_ref[...]
    a_ref[total:] = ghost_ref[:fp]
    b_ref[total:] = jnp.zeros((fp, width), BF16)

    def keep(k, low, high):
        own_ref[0, k] = low
        own_ref[1, k] = high
        if k < DEGREE:
            down_ref[k] = low.astype(BF16)
        up_ref[k] = high.astype(BF16)

    now_ref, other_ref = a_ref, b_ref
    for k in range(DEGREE):
        ends = {}

        def emit(c, rows, lower, carry, k=k, now_ref=now_ref, other_ref=other_ref, ends=ends):
            at = slice(c * stride, (c + 1) * stride)
            if c == 0:
                ends["low"] = rows[:fp]
            now = now_ref[at].astype(F32)
            before = None if k == 0 else other_ref[at].astype(F32)
            if k == 1:
                before = v_ref[at].astype(F32)
            value = advance(rows + pot_ref[at] * now, now, before).astype(BF16)
            if c == 0:
                value = jnp.concatenate([jnp.zeros((fp, width), BF16), value[fp:]], axis=0)
            if k == 0:
                first_ref[at] = value
            other_ref[at] = value

        high = sweep(h_ref, now_ref, fp, emit)
        keep(k, ends["low"], high)
        if k == 0:
            a_ref[total:] = jnp.zeros((fp, width), BF16)
        now_ref, other_ref = other_ref, now_ref
    keep(DEGREE, mul(h_ref[0, :fp], now_ref[:cp]), mul(h_ref[cells - 1, stride:], now_ref[total - stride :]))
    low = response(h_ref[0], h_ref[1], pot_ref[fp:cp], fp, False)
    high = response(h_ref[cells - 1], h_ref[cells - 2], pot_ref[total - stride :], fp, True)
    store_matrices(low, down_ref, DEGREE, fp, width)
    store_matrices(high, up_ref, DEGREE + 1, fp, width)
    for side, mats in enumerate((low, high)):
        store_matrices(mats, own_ref.at[side], DEGREE + 1, fp, width)


def forced_kernel(
    fp, place_ref, v_ref, ghost_ref, first_ref, own_ref, fromleft_ref, fromright_ref, h_ref, pot_ref,
    x_ref, face_image_ref, slab_ref, a_ref, b_ref, c_ref,
):
    cells, cp = h_ref.shape[:2]
    stride = cp - fp
    total = cells * stride
    width = v_ref.shape[1]
    half = cells // 2
    extra = own_ref.shape[1] - DEGREE - 1
    potg = to_col(jnp.sum(ghost_ref[fp:].astype(F32), axis=0, keepdims=True)[:, :fp], fp)
    nothing = jnp.zeros((fp, width), BF16)
    sides = []
    for side, (got_ref, pot, start) in enumerate(
        ((fromleft_ref, pot_ref[:fp], v_ref[:fp]), (fromright_ref, potg, ghost_ref[:fp]))
    ):
        theirs = load_matrices(got_ref, got_ref.shape[0] - extra, DEGREE, fp, width)
        ours = load_matrices(own_ref.at[side], DEGREE + 1, DEGREE, fp, width)
        mats = [a + b for a, b in zip(theirs, ours)]
        line = jnp.concatenate(mats[::-1], axis=1)
        sides.append((got_ref, pot, jnp.concatenate(split(line), axis=0), [start]))
    for k in range(DEGREE + 1):
        for side, (got_ref, pot, line, values) in enumerate(sides):
            if side == 1 and k == DEGREE:
                continue
            h = own_ref[side, k] + got_ref[k].astype(F32)
            if k > 0:
                past = [values[m] if m >= 1 else nothing for m in range(k - DEGREE + 1, k + 1)]
                both = mul(line, jnp.concatenate(past, axis=0))
                h = h + both[:fp] + both[fp:]
            now = values[k].astype(F32)
            h = h + pot * now
            if k == DEGREE:
                face_image_ref[...] = h
                continue
            value = advance(h, now, None if k == 0 else values[k - 1].astype(F32))
            if side == 1:
                value = jnp.where(place_ref[0] == 1, 0.0, value)
            values.append(value.astype(BF16))
    low, high = sides[0][3], sides[1][3]
    a_ref[:fp] = low[1]
    a_ref[fp:total] = first_ref[fp:]
    a_ref[total:] = high[1]
    refs = [v_ref, a_ref, b_ref, c_ref, x_ref]
    for k in range(1, DEGREE):
        now_ref = refs[k]

        def emit(c, rows, lower, carry, k=k, now_ref=now_ref):
            at = slice(c * stride, (c + 1) * stride)
            now = now_ref[at].astype(F32)
            value = advance(rows + pot_ref[at] * now, now, refs[k - 1][at].astype(F32)).astype(BF16)
            if c == 0:
                value = jnp.concatenate([low[k + 1], value[fp:]], axis=0)
            refs[k + 1][at] = value

        sweep(h_ref, now_ref, fp, emit)
        refs[k + 1][total:] = high[k + 1]

    @pl.when(place_ref[1] == 0)
    def _():
        slab_ref[...] = x_ref[half * stride :]

    @pl.when(place_ref[1] == 1)
    def _():
        slab_ref[...] = x_ref[: half * stride + fp]


def image_kernel(fp, place_ref, x_ref, face_image_ref, h_ref, pot_ref, image_ref, w_ref, first_ref, second_ref):
    cells, cp = h_ref.shape[:2]
    stride = cp - fp
    half = cells // 2

    def emit(c, rows, lower, carry):
        at = slice(c * stride, (c + 1) * stride)
        now = x_ref[at].astype(F32)
        out = (rows + pot_ref[at] * now).astype(BF16)
        part, at_w = divmod(c, half)
        w_ref[part, at_w * stride : (at_w + 1) * stride] = out
        if c == half:
            w_ref[0, half * stride :] = carry.astype(BF16)
            w_ref[1, :fp] = (lower + pot_ref[c * stride : c * stride + fp] * now[:fp]).astype(BF16)
        if c == 0:
            out = jnp.concatenate([face_image_ref[...].astype(BF16), out[fp:]], axis=0)
        image_ref[at] = out

    w_ref[1, half * stride :] = sweep(h_ref, x_ref, fp, emit).astype(BF16)
    n = first_ref.shape[0]
    first_ref[...] = w_ref[place_ref[1], :n]
    second_ref[...] = w_ref[place_ref[1], n:]


def back_kernel(node_ref, x_ref, image_ref, out_ref):
    rows = out_ref.shape[1]
    width = x_ref.shape[1]
    want = (lax.broadcasted_iota(jnp.int32, (rows, 1), 0) + pl.program_id(0) * rows).astype(F32)
    hit = flat(want == node_ref[...])
    out_ref[0, :, :width] = mul(hit, x_ref[...]).astype(BF16)
    out_ref[0, :, width:] = mul(hit, image_ref[...]).astype(BF16)


def back_pair_kernel(at_ref, node_ref, x_ref, image_ref, *out_refs):
    rows = out_refs[0].shape[0]
    width = x_ref.shape[1]
    for i, out_ref in enumerate(out_refs):
        want = (lax.broadcasted_iota(jnp.int32, (rows, 1), 0) + at_ref[i] * rows).astype(F32)
        hit = flat(want == node_ref[...])
        out_ref[:, :width] = mul(hit, x_ref[...]).astype(BF16)
        out_ref[:, width:] = mul(hit, image_ref[...]).astype(BF16)


def gram_kernel(scale, x_ref, y_ref, out_ref, rows_ref):
    parts, _, width = y_ref.shape

    @pl.when(pl.program_id(0) == 0)
    def _():
        for j in range(parts):
            rows_ref[:, j * width : (j + 1) * width] = y_ref[j]

    out_ref[0] = (
        lax.dot_general(x_ref[0], rows_ref[...], (((0,), (0,)), ((), ())), preferred_element_type=F32) * scale
    )


def residual_kernel(x_ref, y_ref, p_ref, out_ref):
    parts, _, width = x_ref.shape
    x = jnp.concatenate([x_ref[j] for j in range(parts)], axis=1)
    y = jnp.concatenate([y_ref[j] for j in range(parts)], axis=1)
    out_ref[...] = y.astype(F32) - jnp.dot(x, p_ref[...], preferred_element_type=F32)


def full(shape):
    return pl.BlockSpec(shape, lambda i: (0,) * len(shape))


def swap(block, axis, bit):
    return lax.ppermute(block, axis, [(i, i ^ bit) for i in range(lax.axis_size(axis))])


def shift(block, axis, distance):
    n = lax.axis_size(axis)
    return lax.ppermute(block, axis, [(i, i + distance) for i in range(n) if 0 <= i + distance < n])


def tmul(a, b):
    return lax.dot_general(a, b, (((0,), (0,)), ((), ())), preferred_element_type=F32)


def near_gram_kernel(scale, core_ref, x_ref, w_ref, other_ref, out_ref):
    slab, width = w_ref.shape[1:]
    at = (slice(0, slab), slice(x_ref.shape[0] - slab, x_ref.shape[0]))
    own = [x_ref[a] for a in at]
    out_ref[:width] = (tmul(own[0], w_ref[0]) + tmul(own[1], w_ref[1])) * scale
    half = width // 2

    @pl.when(core_ref[0] == 0)
    def _():
        out_ref[width:] = sum(tmul(w_ref[i, :, :half], other_ref[at[i]]) for i in range(2)) * scale

    @pl.when(core_ref[0] == 1)
    def _():
        out_ref[width:] = sum(tmul(other_ref[at[i], half:], w_ref[i]) for i in range(2)) * scale


def part_ways(sum_ref, mine, keep_ref, give_refs):
    n = keep_ref.shape[0]
    keep_ref[...] = sum_ref[pl.ds(pl.multiple_of(mine * n, 16), n)]
    for j, give_ref in enumerate(give_refs):
        give_ref[...] = sum_ref[pl.ds(pl.multiple_of(jnp.bitwise_xor(mine, j + 1) * n, 16), n)].astype(BF16)


def reduce_kernel(step, ways, bits_ref, keep_ref, *refs):
    total = keep_ref[...]
    for got_ref in refs[: ways - 1]:
        total = total + got_ref[...].astype(F32)
    refs = refs[ways - 1 :]
    if len(refs) == 1:
        refs[0][...] = total.astype(BF16)
        return
    keep_out, *gives, sum_ref = refs
    sum_ref[...] = total
    part_ways(sum_ref, bits_ref[step], keep_out, gives)


def join_kernel(step, bits_ref, own_ref, *refs):
    *got_refs, out_ref = refs
    n = own_ref.shape[0]
    mine = bits_ref[step]
    for j, ref in enumerate([own_ref] + got_refs):
        out_ref[pl.ds(pl.multiple_of(jnp.bitwise_xor(mine, j) * n, 16), n)] = ref[...]


def far_gram_kernel(scale, bits_ref, place_ref, w_ref, first_ref, second_ref, far_ref, near_ref, keep_ref, *refs):
    *give_refs, out_ref = refs
    width = w_ref.shape[2]
    near = near_ref.shape[0]
    side, core = place_ref[0], place_ref[1]
    out_ref[:near] = near_ref[...]
    far = far_ref[...]
    mine = pl.multiple_of(near + core * width, width // 2)
    other = pl.multiple_of(near + (1 - core) * width, width // 2)
    out_ref[pl.ds(mine, width)] = tmul(w_ref[side], far) * scale
    n = first_ref.shape[0]
    out_ref[pl.ds(other, width)] = (tmul(first_ref[...], far[:n]) + tmul(second_ref[...], far[n:])) * scale
    part_ways(out_ref, bits_ref[0], keep_ref, give_refs)


def paired_residual_kernel(place_ref, *refs):
    q_refs, refs = refs[:8], refs[8:]
    parts = 4
    row_refs, (out_ref, p_ref, q_ref) = refs[:parts], refs[parts:]
    width = row_refs[0].shape[1] // 2
    half = width // 2
    me, mine = place_ref[0], place_ref[1]
    n = q_refs[0].shape[0]
    for k in range(parts):
        for j in range(2):
            q_ref[k, pl.ds(pl.multiple_of(jnp.bitwise_xor(mine, j) * n, 16), n)] = q_refs[2 * k + j][...]
    eye = (lax.broadcasted_iota(jnp.int32, (width, width), 0) == lax.broadcasted_iota(jnp.int32, (width, width), 1)).astype(
        F32
    ).astype(BF16)

    def turned(a):
        return lax.dot_general(eye, a, (((1,), (1,)), ((), ())), preferred_element_type=F32)

    def piece(i, lo, hi):
        return q_ref[jnp.bitwise_xor(me, i), lo:hi]

    def put(i, j, value):
        p_ref[i * width : (i + 1) * width, j * width : (j + 1) * width] = value

    near = width + half
    for i in range(parts):
        put(i, i, piece(i, 0, width))
    for i in range(0, parts, 2):
        block = jnp.concatenate([piece(i, width, near), piece(i + 1, width, near)], axis=0)
        put(i, i + 1, block)
        put(i + 1, i, turned(block).astype(BF16))
    for i in (0, 1):
        for j in (2, 3):
            one = piece(j ^ 2, near + i * width, near + (i + 1) * width)
            two = piece(i ^ 2, near + (j - 2) * width, near + (j - 1) * width)
            block = (one.astype(F32) + turned(two)).astype(BF16)
            put(i, j, block)
            put(j, i, turned(block).astype(BF16))
    x = jnp.concatenate([ref[:, :width] for ref in row_refs], axis=1)
    spots = [pl.ds(pl.multiple_of(jnp.bitwise_xor(me, k) * width, width), width) for k in range(parts)]
    for k in range(parts):
        at = spots[k]
        p = jnp.concatenate([p_ref[spots[m], at] for m in range(parts)], axis=0)
        out_ref[:, at] = row_refs[k][:, width:].astype(F32) - mul(x, p)


def paired_tail(x_own, image, w_own, w_side, give, node_row, o, d, dom, nodes):
    slab, width = w_own.shape[1:]
    orb = 4
    rows = nodes // orb
    side, core = o // 2, o % 2
    scale = 1.0 / (nodes * dom)
    sds = jax.ShapeDtypeStruct
    smem = pl.BlockSpec(memory_space=pltpu.SMEM)
    vmem = pl.BlockSpec(memory_space=pltpu.VMEM)
    far = swap(give, "orb", 2)
    total = image.shape[0]

    def back(first, second, x_own, image):
        whole = lambda *shape: pl.BlockSpec(shape, lambda i: (0,) * len(shape))
        return pl.pallas_call(
            back_pair_kernel,
            grid=(1,),
            in_specs=[smem, whole(1, total), whole(total, width), whole(total, width)],
            out_specs=[whole(rows, 2 * width)] * 2,
            out_shape=[sds((rows, 2 * width), BF16)] * 2,
            compiler_params=params(),
            cost_estimate=pl.CostEstimate(flops=1 << 20, bytes_accessed=1 << 10, transcendentals=0),
        )(jnp.stack([jnp.bitwise_xor(o, first), jnp.bitwise_xor(o, second)]), node_row, x_own, image)

    cuts = back(2, 3, x_own, image)
    x_other = swap(x_own, "orb", 1)
    w_other = [swap(w, "orb", 1) for w in w_side]
    top = width + width // 2
    near = pl.pallas_call(
        functools.partial(near_gram_kernel, scale),
        in_specs=[smem] + [vmem] * 3,
        out_shape=sds((top, width), F32),
        compiler_params=params(),
        cost_estimate=pl.CostEstimate(flops=1 << 20, bytes_accessed=1 << 10, transcendentals=0),
    )(core.reshape(1), x_own, w_own, x_other)
    far, near, *cuts, w_other[0], w_other[1] = lax.optimization_barrier((far, near, *cuts, *w_other))
    row2, row3 = swap(cuts[0], "orb", 2), swap(cuts[1], "orb", 3)
    groups, base = [], 1
    while base < dom:
        ways = 2 if base == 1 or base * 4 > dom else 4
        groups.append((base, ways))
        base *= ways
    bits = jnp.stack([(d // base) % ways for base, ways in groups])
    little = pl.CostEstimate(flops=1 << 10, bytes_accessed=1 << 10, transcendentals=0)
    count = top + 2 * width

    def parts_of(n, ways):
        return [sds((n // ways, width), F32)] + [sds((n // ways, width), BF16)] * (ways - 1)

    keep, *gives = pl.pallas_call(
        functools.partial(far_gram_kernel, scale),
        in_specs=[smem] * 2 + [vmem] * 5,
        out_shape=parts_of(count, 2),
        scratch_shapes=[pltpu.VMEM((count, width), F32)],
        compiler_params=params(),
        cost_estimate=pl.CostEstimate(flops=8 * slab * width * width, bytes_accessed=4 << 20, transcendentals=0),
    )(bits, jnp.stack([side, core]), w_own, *w_other, far, near)
    row0 = cut1 = None
    for i, (base, ways) in enumerate(groups):
        if i == 0:
            x_own, image, gives[0] = lax.optimization_barrier((x_own, image, gives[0]))
            row0, cut1 = back(0, 1, x_own, image)
        gots = [swap(give, "dom", base * (j + 1)) for j, give in enumerate(gives)]
        n = keep.shape[0]
        last = i == len(groups) - 1
        outs = pl.pallas_call(
            functools.partial(reduce_kernel, i + 1, ways),
            in_specs=[smem] + [vmem] * ways,
            out_shape=[sds((n, width), BF16)] if last else parts_of(n, groups[i + 1][1]),
            scratch_shapes=[] if last else [pltpu.VMEM((n, width), F32)],
            compiler_params=params(),
            cost_estimate=little,
        )(bits, keep, *gots)
        outs = list(outs)
        if i == 0:
            outs[-1], row0, cut1 = lax.optimization_barrier((outs[-1], row0, cut1))
        if last:
            outs[-1], row2 = lax.optimization_barrier((outs[-1], row2))
            share = outs[0]
        else:
            keep, *gives = outs
    for i in reversed(range(1, len(groups))):
        base, ways = groups[i]
        gots = [swap(share, "dom", base * j) for j in range(1, ways)]
        share = pl.pallas_call(
            functools.partial(join_kernel, i),
            in_specs=[smem] + [vmem] * ways,
            out_shape=sds((ways * share.shape[0], width), BF16),
            compiler_params=params(),
            cost_estimate=little,
        )(bits, share, *gots)
    row1 = swap(cut1, "orb", 1)
    got = swap(share, "dom", 1)
    got, row3 = lax.optimization_barrier((got, row3))
    q2 = [swap(share, "orb", 2), swap(got, "orb", 2)]
    q1 = [swap(share, "orb", 1), swap(got, "orb", 1)]
    q3a = swap(q2[0], "orb", 1)
    q2[1], q1[0], q1[1], q3a, row1 = lax.optimization_barrier((q2[1], q1[0], q1[1], q3a, row1))
    q3 = [q3a, swap(q2[1], "orb", 1)]
    cols = orb * width
    return pl.pallas_call(
        paired_residual_kernel,
        in_specs=[smem] + [vmem] * 12,
        out_shape=(sds((rows, cols), F32), sds((cols, cols), BF16)),
        scratch_shapes=[pltpu.VMEM((orb, count, width), BF16)],
        compiler_params=params(),
    )(jnp.stack([o, d % 2]), share, got, *q1, *q2, *q3, row0, row1, row2, row3)


def body(orbitals, potential, cell_hamiltonian, connectivity, face_nodes):
    nodes, width = orbitals.shape
    cells, npc = connectivity.shape
    face = face_nodes.shape[0]
    fp, ip = up16(face), up16(npc - 2 * face)
    fp = (fp + 63) // 64 * 64
    stride = fp + ip
    cp = stride + fp
    total = cells * stride
    orb, dom = lax.axis_size("orb"), lax.axis_size("dom")
    d = lax.axis_index("dom")
    o = lax.axis_index("orb")
    sds = jax.ShapeDtypeStruct
    pot_row = potential.reshape(1, nodes)
    face_row = face_nodes.reshape(1, face)

    face_values = pl.pallas_call(
        face_kernel, out_shape=sds((fp + 16, width), BF16), compiler_params=params()
    )(face_row, orbitals, pot_row)
    ghost = shift(face_values, "dom", -1)

    extra = -(-DEGREE * fp // width)
    ext = pltpu.VMEM((total + fp, width), BF16)
    cost = pl.CostEstimate(
        flops=2 * DEGREE * cells * cp * cp * width, bytes_accessed=8 << 20, transcendentals=0
    )
    hcan, y, pot, node, first, own, up, down = pl.pallas_call(
        functools.partial(free_kernel, fp, ip),
        out_shape=[
            sds((cells, cp, cp), BF16),
            sds((total, width), BF16),
            sds((total, 1), F32),
            sds((cells, 1, stride), F32),
            sds((total, width), BF16),
            sds((2, DEGREE + 1 + extra, fp, width), F32),
            sds((DEGREE + 1 + extra, fp, width), BF16),
            sds((DEGREE + extra, fp, width), BF16),
        ],
        scratch_shapes=[ext, ext],
        compiler_params=params(),
        cost_estimate=cost,
    )(connectivity, face_row, cell_hamiltonian, orbitals, pot_row, ghost)
    node_row = node.reshape(1, total)
    from_left = shift(up, "dom", 1)
    from_right = shift(down, "dom", -1)
    vmem = pl.BlockSpec(memory_space=pltpu.VMEM)
    slab = cells // 2 * stride + fp
    place = jnp.stack([(d == dom - 1).astype(jnp.int32), (o // 2) % 2])
    x_own, face_image, give = pl.pallas_call(
        functools.partial(forced_kernel, fp),
        in_specs=[pl.BlockSpec(memory_space=pltpu.SMEM)] + [vmem] * 8,
        out_shape=[
            sds((total + fp, width), BF16),
            sds((fp, width), F32),
            sds((slab, width), BF16),
        ],
        scratch_shapes=[ext, ext, ext],
        compiler_params=params(),
        cost_estimate=cost,
    )(place, y, ghost, first, own, from_left, from_right, hcan, pot)
    image, w_own, *w_side = pl.pallas_call(
        functools.partial(image_kernel, fp),
        in_specs=[pl.BlockSpec(memory_space=pltpu.SMEM)] + [vmem] * 4,
        out_shape=[sds((total, width), BF16), sds((2, slab, width), BF16)] + [sds((slab // 2, width), BF16)] * 2,
        compiler_params=params(),
        cost_estimate=pl.CostEstimate(flops=1 << 20, bytes_accessed=1 << 10, transcendentals=0),
    )(place, x_own, face_image, hcan, pot)

    if orb == 4 and dom % 8 == 0:
        return paired_tail(x_own, image, w_own, w_side, give, node_row, o, d, dom, nodes)
    cut = pl.pallas_call(
        back_kernel,
        grid=(orb,),
        in_specs=[full((1, total)), full((total, width)), full((total, width))],
        out_specs=pl.BlockSpec((1, nodes // orb, 2 * width), lambda i: (i, 0, 0)),
        out_shape=sds((orb, nodes // orb, 2 * width), BF16),
        compiler_params=params(),
        cost_estimate=pl.CostEstimate(flops=4 * total * nodes * width, bytes_accessed=4 << 20, transcendentals=0),
    )(node_row, x_own, image)
    both = lax.all_to_all(cut, "orb", split_axis=0, concat_axis=0, tiled=True)
    x_rows, i_rows = both[:, :, :width], both[:, :, width:]

    rows = nodes // orb
    cols = orb * width
    share = pl.pallas_call(
        functools.partial(gram_kernel, 1.0 / (nodes * dom)),
        grid=(orb,),
        in_specs=[pl.BlockSpec((1, rows, width), lambda i: (i, 0, 0)), full((orb, rows, width))],
        out_specs=pl.BlockSpec((1, width, cols), lambda i: (i, 0, 0)),
        out_shape=sds((orb, width, cols), F32),
        scratch_shapes=[pltpu.VMEM((rows, cols), BF16)],
        compiler_params=params(),
    )(x_rows, i_rows)

    hops = []
    for axis, me, size in (("orb", o, orb), ("dom", d, dom)):
        if axis == "dom":
            share = share.reshape(dom, width // dom, cols)
        bit = 1
        while bit < size:
            share = share.reshape((share.shape[0] // 2, 2) + share.shape[1:])
            mine = (me // bit) % 2
            keep = lax.dynamic_index_in_dim(share, mine, 1, keepdims=False)
            give = lax.dynamic_index_in_dim(share, 1 - mine, 1, keepdims=False)
            got = swap(give.astype(BF16), axis, bit)
            share = keep + got.astype(F32)
            hops.append((axis, bit, mine))
            bit *= 2
    share = share.astype(BF16)
    for axis, bit, mine in reversed(hops):
        if axis == "orb" and share.shape[0] == dom and bit * 2 == orb:
            share = share.reshape(1, width, cols)
        got = swap(share, axis, bit)
        share = jnp.where(mine == 0, jnp.stack([share, got], axis=1), jnp.stack([got, share], axis=1))
        share = share.reshape((share.shape[0] * 2,) + share.shape[2:])
    projected = share.reshape(cols, cols)

    residual = pl.pallas_call(
        residual_kernel, out_shape=sds((rows, cols), F32), compiler_params=params()
    )(x_rows, i_rows, projected)
    return (residual, projected)


def solution(mesh):
    return jax.shard_map(
        body,
        mesh=mesh,
        in_specs=(P("dom", "orb"), P("dom"), P("dom", None, None), P("dom", None), P("dom")),
        out_specs=(P(("dom", "orb"), None), P()),
        check_vma=False,
    )
```

```python
import functools

import jax
import jax.numpy as jnp
from jax import lax
from jax.experimental import pallas as pl
from jax.experimental.pallas import tpu as pltpu
from jax.sharding import PartitionSpec as P

DEGREE = 4
CENTER = 1.5
HALF = 2.0
F32 = jnp.float32
BF16 = jnp.bfloat16
VMEM_LIMIT = 50 * 1024 * 1024


def up16(n):
    return (n + 15) // 16 * 16


def iota(shape, dim):
    return lax.broadcasted_iota(jnp.int32, shape, dim).astype(F32)


def to_col(row, rows):
    n = row.shape[1]
    return jnp.sum(jnp.where(iota((rows, n), 0) == iota((rows, n), 1), row, 0.0), axis=1, keepdims=True)


def to_row(col):
    n = col.shape[0]
    return jnp.sum(jnp.where(iota((n, n), 0) == iota((n, n), 1), col, 0.0), axis=0, keepdims=True)


def params():
    return pltpu.CompilerParams(vmem_limit_bytes=VMEM_LIMIT)


def thirds(a):
    one = a.astype(BF16)
    rest = a - one.astype(F32)
    two = rest.astype(BF16)
    return one, two, (rest - two.astype(F32)).astype(BF16)


def face_kernel(face_ref, x_ref, pot_ref, out_ref):
    width = x_ref.shape[1]
    fp = out_ref.shape[0] - 16
    nodes = x_ref.shape[0]
    col = to_col(face_ref[...].astype(F32) + 1.0, fp) - 1.0
    hit = jnp.where(col == iota((fp, nodes), 1), 1.0, 0.0).astype(BF16)
    out_ref[:fp] = mul(hit, x_ref[...]).astype(BF16)
    ri = lax.broadcasted_iota(jnp.int32, (16, nodes), 0)
    parts = [p.astype(F32) for p in thirds(pot_ref[...])]
    rows = jnp.where(ri == 0, parts[0], jnp.where(ri == 1, parts[1], jnp.where(ri == 2, parts[2], 0.0))).astype(BF16)
    got = lax.dot_general(rows, hit, (((1,), (1,)), ((), ())), preferred_element_type=F32).astype(BF16)
    if width > fp:
        got = jnp.concatenate([got, jnp.zeros((16, width - fp), BF16)], axis=1)
    out_ref[fp:] = got


def turn(a, b):
    return lax.dot_general(a, b, (((1,), (1,)), ((), ())), preferred_element_type=F32)


def halves(a):
    high = jnp.floor(a * (1.0 / 64.0))
    return high.astype(BF16), (a - 64.0 * high).astype(BF16)


def flat(mask):
    return jnp.where(mask, 1.0, 0.0).astype(BF16)


def order(fp, ip, arrived, conn_ref, face_ref, h_ref, x_ref, pot_ref, hcan_ref, v_ref, potc_ref, node_ref):
    cells, npc = conn_ref.shape
    nodes = x_ref.shape[0]
    face = face_ref.shape[1]
    stride = fp + ip
    cp = stride + fp
    conn = conn_ref[...].astype(F32)
    eye = flat(iota((npc, npc), 0) == iota((npc, npc), 1))
    below = flat(iota((npc, npc), 0) < iota((npc, npc), 1))
    high, low = halves(conn)
    cols = 64.0 * turn(eye, high) + turn(eye, low)
    rows = [conn[c : c + 1] for c in range(cells)]
    ones = jnp.ones((cells, npc), BF16)
    same = [flat(cols[:, c : c + 1] == rows[c + 1]) for c in range(cells - 1)]
    ri = lax.broadcasted_iota(jnp.int32, (cells, npc), 0)
    top = jnp.where(conn >= float(nodes), 1.0, 0.0)
    for c in range(cells - 1):
        top = jnp.where(ri == c, turn(ones, same[c]), top)
    rank_top = mul(top.astype(BF16), below)
    rank_b = rank_top.astype(BF16)
    top_slot = jnp.where(ri == cells - 1, conn - float(nodes), rank_top)
    fhit = to_col(face_ref[...].astype(F32), face) == rows[0]
    bot = jnp.where(ri == 0, jnp.max(jnp.where(fhit, 1.0, 0.0), axis=0, keepdims=True), 0.0)
    bot_slot = jnp.where(ri == 0, jnp.sum(jnp.where(fhit, iota((face, npc), 0), 0.0), axis=0, keepdims=True), 0.0)
    for c in range(cells - 1):
        both = jnp.concatenate([ones, rank_b], axis=0)
        got = mul(both, same[c])
        bot = jnp.where(ri == c + 1, got[:1], bot)
        bot_slot = jnp.where(ri == c + 1, got[cells + c : cells + c + 1], bot_slot)
    mid_rank = mul((1.0 - top - bot).astype(BF16), below)
    slot = jnp.where(top > 0.5, top_slot + float(stride), jnp.where(bot > 0.5, bot_slot, mid_rank + float(fp)))
    high, low = halves(conn + 1.0)
    number = iota((8, nodes), 1)[:1]
    arrived()
    for c in range(cells):
        perm = flat(iota((cp, npc), 0) == slot[c : c + 1])
        half = mul(perm, h_ref[c]).astype(BF16)
        hcan_ref[c] = turn(half, perm).astype(BF16)
        lead = perm[:stride]
        node = 64.0 * turn(lead, high)[:, c : c + 1] + turn(lead, low)[:, c : c + 1] - 1.0
        node_ref[c] = 64.0 * turn(high, lead)[c : c + 1] + turn(low, lead)[c : c + 1] - 1.0
        at = slice(c * stride, (c + 1) * stride)
        hit = node == number
        v_ref[at] = mul(flat(hit), x_ref[...]).astype(BF16)
        potc_ref[at] = jnp.sum(jnp.where(hit, pot_ref[...], 0.0), axis=1, keepdims=True)


def advance(image, now, before):
    if before is None:
        return (image - CENTER * now) / HALF
    return 2.0 * (image - CENTER * now) / HALF - before


def split(a):
    high = a.astype(BF16)
    return high, (a - high.astype(F32)).astype(BF16)


def mul(a, b):
    return jnp.dot(a, b, preferred_element_type=F32)


def mul_r(a, b):
    return mul(a, b.astype(BF16))


def sweep(h_ref, y_ref, fp, emit):
    cells, cp = h_ref.shape[:2]
    stride = cp - fp
    carry = None
    for c in range(cells):
        prod = mul(h_ref[c], y_ref[c * stride : c * stride + cp])
        rows = prod[:stride]
        if c > 0:
            rows = jnp.concatenate([rows[:fp] + carry, rows[fp:]], axis=0)
        emit(c, rows, prod[:fp], carry)
        carry = prod[stride:]
    return carry


def response(hc, hn, potc, fp, upper):
    cp = hc.shape[0]
    stride = cp - fp
    if upper:
        f, r, s, g = slice(stride, cp), slice(0, stride), slice(0, fp), slice(stride, cp)
        rest = slice(0, stride)
    else:
        f, r, s, g = slice(0, fp), slice(fp, cp), slice(stride - fp, stride), slice(0, fp)
        rest = slice(fp, cp)
    gain = 2.0 / HALF
    out = [hc[f, f].astype(F32)]
    one = gain * hc[r, f].astype(F32)
    out.append(mul_r(hc[f, r], one))

    def pad_next(face_rows):
        zero = jnp.zeros((stride, fp), F32)
        return jnp.concatenate([zero, face_rows] if upper else [face_rows, zero], axis=0)

    def near(value, next_value):
        got = mul_r(hc[r, r], value) + (potc - CENTER) * value
        add = mul_r(hn[g, :], next_value)
        if upper:
            return jnp.concatenate([got[:fp] + add, got[fp:]], axis=0)
        return jnp.concatenate([got[: stride - fp], got[stride - fp :] + add], axis=0)

    two = gain * near(one, pad_next(one[s]))
    out.append(mul_r(hc[f, r], two))
    two_next = gain * mul_r(hn, pad_next(one[s]))
    if upper:
        two_next = jnp.concatenate([two_next[:stride], two[s]], axis=0)
    else:
        two_next = jnp.concatenate([two[s], two_next[fp:]], axis=0)
    three = gain * near(two, two_next) - one
    out.append(mul_r(hc[f, r], three))
    return out


def store_matrices(mats, out_ref, at, fp, width):
    for j, m in enumerate(mats):
        block, lane = divmod(j * fp, width)
        out_ref[at + block, :, lane : lane + fp] = m.astype(out_ref.dtype)


def load_matrices(ref, at, count, fp, width):
    spots = [divmod(j * fp, width) for j in range(count)]
    return [ref[at + block, :, lane : lane + fp].astype(F32) for block, lane in spots]


def free_kernel(
    fp, ip, conn_ref, face_ref, hraw_ref, raw_ref, potraw_ref, ghost_ref,
    h_ref, v_ref, pot_ref, node_ref, first_ref, own_ref, up_ref, down_ref, a_ref, b_ref, hin_ref, sem,
):
    copy = pltpu.make_async_copy(hraw_ref, hin_ref, sem)
    copy.start()
    order(fp, ip, copy.wait, conn_ref, face_ref, hin_ref, raw_ref, potraw_ref, h_ref, v_ref, pot_ref, node_ref)
    cells, cp = h_ref.shape[:2]
    stride = cp - fp
    total = cells * stride
    width = v_ref.shape[1]
    a_ref[:total] = v_ref[...]
    a_ref[total:] = ghost_ref[:fp]
    b_ref[total:] = jnp.zeros((fp, width), BF16)

    def keep(k, low, high):
        own_ref[0, k] = low
        own_ref[1, k] = high
        if k < DEGREE:
            down_ref[k] = low.astype(BF16)
        up_ref[k] = high.astype(BF16)

    now_ref, other_ref = a_ref, b_ref
    for k in range(DEGREE):
        ends = {}

        def emit(c, rows, lower, carry, k=k, now_ref=now_ref, other_ref=other_ref, ends=ends):
            at = slice(c * stride, (c + 1) * stride)
            if c == 0:
                ends["low"] = rows[:fp]
            now = now_ref[at].astype(F32)
            before = None if k == 0 else other_ref[at].astype(F32)
            if k == 1:
                before = v_ref[at].astype(F32)
            value = advance(rows + pot_ref[at] * now, now, before).astype(BF16)
            if c == 0:
                value = jnp.concatenate([jnp.zeros((fp, width), BF16), value[fp:]], axis=0)
            if k == 0:
                first_ref[at] = value
            other_ref[at] = value

        high = sweep(h_ref, now_ref, fp, emit)
        keep(k, ends["low"], high)
        if k == 0:
            a_ref[total:] = jnp.zeros((fp, width), BF16)
        now_ref, other_ref = other_ref, now_ref
    keep(DEGREE, mul(h_ref[0, :fp], now_ref[:cp]), mul(h_ref[cells - 1, stride:], now_ref[total - stride :]))
    low = response(h_ref[0], h_ref[1], pot_ref[fp:cp], fp, False)
    high = response(h_ref[cells - 1], h_ref[cells - 2], pot_ref[total - stride :], fp, True)
    store_matrices(low, down_ref, DEGREE, fp, width)
    store_matrices(high, up_ref, DEGREE + 1, fp, width)
    for side, mats in enumerate((low, high)):
        store_matrices(mats, own_ref.at[side], DEGREE + 1, fp, width)


def forced_kernel(
    fp, place_ref, v_ref, ghost_ref, first_ref, own_ref, fromleft_ref, fromright_ref, h_ref, pot_ref,
    x_ref, face_image_ref, slab_ref, a_ref, b_ref, c_ref,
):
    cells, cp = h_ref.shape[:2]
    stride = cp - fp
    total = cells * stride
    width = v_ref.shape[1]
    half = cells // 2
    extra = own_ref.shape[1] - DEGREE - 1
    potg = to_col(jnp.sum(ghost_ref[fp:].astype(F32), axis=0, keepdims=True)[:, :fp], fp)
    nothing = jnp.zeros((fp, width), BF16)
    sides = []
    for side, (got_ref, pot, start) in enumerate(
        ((fromleft_ref, pot_ref[:fp], v_ref[:fp]), (fromright_ref, potg, ghost_ref[:fp]))
    ):
        theirs = load_matrices(got_ref, got_ref.shape[0] - extra, DEGREE, fp, width)
        ours = load_matrices(own_ref.at[side], DEGREE + 1, DEGREE, fp, width)
        mats = [a + b for a, b in zip(theirs, ours)]
        line = jnp.concatenate(mats[::-1], axis=1)
        sides.append((got_ref, pot, jnp.concatenate(split(line), axis=0), [start]))
    for k in range(DEGREE + 1):
        for side, (got_ref, pot, line, values) in enumerate(sides):
            if side == 1 and k == DEGREE:
                continue
            h = own_ref[side, k] + got_ref[k].astype(F32)
            if k > 0:
                past = [values[m] if m >= 1 else nothing for m in range(k - DEGREE + 1, k + 1)]
                both = mul(line, jnp.concatenate(past, axis=0))
                h = h + both[:fp] + both[fp:]
            now = values[k].astype(F32)
            h = h + pot * now
            if k == DEGREE:
                face_image_ref[...] = h
                continue
            value = advance(h, now, None if k == 0 else values[k - 1].astype(F32))
            if side == 1:
                value = jnp.where(place_ref[0] == 1, 0.0, value)
            values.append(value.astype(BF16))
    low, high = sides[0][3], sides[1][3]
    a_ref[:fp] = low[1]
    a_ref[fp:total] = first_ref[fp:]
    a_ref[total:] = high[1]
    refs = [v_ref, a_ref, b_ref, c_ref, x_ref]
    for k in range(1, DEGREE):
        now_ref = refs[k]

        def emit(c, rows, lower, carry, k=k, now_ref=now_ref):
            at = slice(c * stride, (c + 1) * stride)
            now = now_ref[at].astype(F32)
            value = advance(rows + pot_ref[at] * now, now, refs[k - 1][at].astype(F32)).astype(BF16)
            if c == 0:
                value = jnp.concatenate([low[k + 1], value[fp:]], axis=0)
            refs[k + 1][at] = value

        sweep(h_ref, now_ref, fp, emit)
        refs[k + 1][total:] = high[k + 1]

    @pl.when(place_ref[1] == 0)
    def _():
        slab_ref[...] = x_ref[half * stride :]

    @pl.when(place_ref[1] == 1)
    def _():
        slab_ref[...] = x_ref[: half * stride + fp]


def image_kernel(fp, place_ref, x_ref, face_image_ref, h_ref, pot_ref, image_ref, w_ref, first_ref, second_ref):
    cells, cp = h_ref.shape[:2]
    stride = cp - fp
    half = cells // 2

    def emit(c, rows, lower, carry):
        at = slice(c * stride, (c + 1) * stride)
        now = x_ref[at].astype(F32)
        out = (rows + pot_ref[at] * now).astype(BF16)
        part, at_w = divmod(c, half)
        w_ref[part, at_w * stride : (at_w + 1) * stride] = out
        if c == half:
            w_ref[0, half * stride :] = carry.astype(BF16)
            w_ref[1, :fp] = (lower + pot_ref[c * stride : c * stride + fp] * now[:fp]).astype(BF16)
        if c == 0:
            out = jnp.concatenate([face_image_ref[...].astype(BF16), out[fp:]], axis=0)
        image_ref[at] = out

    w_ref[1, half * stride :] = sweep(h_ref, x_ref, fp, emit).astype(BF16)
    n = first_ref.shape[0]
    first_ref[...] = w_ref[place_ref[1], :n]
    second_ref[...] = w_ref[place_ref[1], n:]


def back_kernel(node_ref, x_ref, image_ref, out_ref):
    rows = out_ref.shape[1]
    width = x_ref.shape[1]
    want = (lax.broadcasted_iota(jnp.int32, (rows, 1), 0) + pl.program_id(0) * rows).astype(F32)
    hit = flat(want == node_ref[...])
    out_ref[0, :, :width] = mul(hit, x_ref[...]).astype(BF16)
    out_ref[0, :, width:] = mul(hit, image_ref[...]).astype(BF16)


def back_pair_kernel(at_ref, node_ref, x_ref, image_ref, *out_refs):
    rows = out_refs[0].shape[0]
    width = x_ref.shape[1]
    for i, out_ref in enumerate(out_refs):
        want = (lax.broadcasted_iota(jnp.int32, (rows, 1), 0) + at_ref[i] * rows).astype(F32)
        hit = flat(want == node_ref[...])
        out_ref[:, :width] = mul(hit, x_ref[...]).astype(BF16)
        out_ref[:, width:] = mul(hit, image_ref[...]).astype(BF16)


def gram_kernel(scale, x_ref, y_ref, out_ref, rows_ref):
    parts, _, width = y_ref.shape

    @pl.when(pl.program_id(0) == 0)
    def _():
        for j in range(parts):
            rows_ref[:, j * width : (j + 1) * width] = y_ref[j]

    out_ref[0] = (
        lax.dot_general(x_ref[0], rows_ref[...], (((0,), (0,)), ((), ())), preferred_element_type=F32) * scale
    )


def residual_kernel(x_ref, y_ref, p_ref, out_ref):
    parts, _, width = x_ref.shape
    x = jnp.concatenate([x_ref[j] for j in range(parts)], axis=1)
    y = jnp.concatenate([y_ref[j] for j in range(parts)], axis=1)
    out_ref[...] = y.astype(F32) - jnp.dot(x, p_ref[...], preferred_element_type=F32)


def full(shape):
    return pl.BlockSpec(shape, lambda i: (0,) * len(shape))


def swap(block, axis, bit):
    return lax.ppermute(block, axis, [(i, i ^ bit) for i in range(lax.axis_size(axis))])


def shift(block, axis, distance):
    n = lax.axis_size(axis)
    return lax.ppermute(block, axis, [(i, i + distance) for i in range(n) if 0 <= i + distance < n])


def tmul(a, b):
    return lax.dot_general(a, b, (((0,), (0,)), ((), ())), preferred_element_type=F32)


def near_gram_kernel(scale, core_ref, x_ref, w_ref, other_ref, out_ref):
    slab, width = w_ref.shape[1:]
    at = (slice(0, slab), slice(x_ref.shape[0] - slab, x_ref.shape[0]))
    own = [x_ref[a] for a in at]
    out_ref[:width] = (tmul(own[0], w_ref[0]) + tmul(own[1], w_ref[1])) * scale
    half = width // 2

    @pl.when(core_ref[0] == 0)
    def _():
        out_ref[width:] = sum(tmul(w_ref[i, :, :half], other_ref[at[i]]) for i in range(2)) * scale

    @pl.when(core_ref[0] == 1)
    def _():
        out_ref[width:] = sum(tmul(other_ref[at[i], half:], w_ref[i]) for i in range(2)) * scale


def part_ways(sum_ref, mine, keep_ref, give_refs):
    n = keep_ref.shape[0]
    keep_ref[...] = sum_ref[pl.ds(pl.multiple_of(mine * n, 16), n)]
    for j, give_ref in enumerate(give_refs):
        give_ref[...] = sum_ref[pl.ds(pl.multiple_of(jnp.bitwise_xor(mine, j + 1) * n, 16), n)].astype(BF16)


def reduce_kernel(step, ways, bits_ref, keep_ref, *refs):
    total = keep_ref[...]
    for got_ref in refs[: ways - 1]:
        total = total + got_ref[...].astype(F32)
    refs = refs[ways - 1 :]
    if len(refs) == 1:
        refs[0][...] = total.astype(BF16)
        return
    keep_out, *gives, sum_ref = refs
    sum_ref[...] = total
    part_ways(sum_ref, bits_ref[step], keep_out, gives)


def join_kernel(step, bits_ref, own_ref, *refs):
    *got_refs, out_ref = refs
    n = own_ref.shape[0]
    mine = bits_ref[step]
    for j, ref in enumerate([own_ref] + got_refs):
        out_ref[pl.ds(pl.multiple_of(jnp.bitwise_xor(mine, j) * n, 16), n)] = ref[...]


def far_gram_kernel(scale, bits_ref, place_ref, w_ref, first_ref, second_ref, far_ref, near_ref, keep_ref, *refs):
    *give_refs, out_ref = refs
    width = w_ref.shape[2]
    near = near_ref.shape[0]
    side, core = place_ref[0], place_ref[1]
    out_ref[:near] = near_ref[...]
    far = far_ref[...]
    mine = pl.multiple_of(near + core * width, width // 2)
    other = pl.multiple_of(near + (1 - core) * width, width // 2)
    out_ref[pl.ds(mine, width)] = tmul(w_ref[side], far) * scale
    n = first_ref.shape[0]
    out_ref[pl.ds(other, width)] = (tmul(first_ref[...], far[:n]) + tmul(second_ref[...], far[n:])) * scale
    part_ways(out_ref, bits_ref[0], keep_ref, give_refs)


def paired_residual_kernel(place_ref, *refs):
    q_refs, refs = refs[:8], refs[8:]
    parts = 4
    row_refs, (out_hbm, p_hbm, out_ref, p_ref, q_ref, sems) = refs[:parts], refs[parts:]
    width = row_refs[0].shape[1] // 2
    half = width // 2
    me, mine = place_ref[0], place_ref[1]
    n = q_refs[0].shape[0]
    for k in range(parts):
        for j in range(2):
            q_ref[k, pl.ds(pl.multiple_of(jnp.bitwise_xor(mine, j) * n, 16), n)] = q_refs[2 * k + j][...]
    eye = (lax.broadcasted_iota(jnp.int32, (width, width), 0) == lax.broadcasted_iota(jnp.int32, (width, width), 1)).astype(
        F32
    ).astype(BF16)

    def turned(a):
        return lax.dot_general(eye, a, (((1,), (1,)), ((), ())), preferred_element_type=F32)

    def piece(i, lo, hi):
        return q_ref[jnp.bitwise_xor(me, i), lo:hi]

    def put(i, j, value):
        p_ref[i * width : (i + 1) * width, j * width : (j + 1) * width] = value

    near = width + half
    for i in range(parts):
        put(i, i, piece(i, 0, width))
    for i in range(0, parts, 2):
        block = jnp.concatenate([piece(i, width, near), piece(i + 1, width, near)], axis=0)
        put(i, i + 1, block)
        put(i + 1, i, turned(block).astype(BF16))
    for i in (0, 1):
        for j in (2, 3):
            one = piece(j ^ 2, near + i * width, near + (i + 1) * width)
            two = piece(i ^ 2, near + (j - 2) * width, near + (j - 1) * width)
            block = (one.astype(F32) + turned(two)).astype(BF16)
            put(i, j, block)
            put(j, i, turned(block).astype(BF16))
    copies = [pltpu.make_async_copy(p_ref, p_hbm, sems.at[parts])]
    copies[0].start()
    x = jnp.concatenate([ref[:, :width] for ref in row_refs], axis=1)
    spots = [pl.ds(pl.multiple_of(jnp.bitwise_xor(me, k) * width, width), width) for k in range(parts)]
    for k in range(parts):
        at = spots[k]
        p = jnp.concatenate([p_ref[spots[m], at] for m in range(parts)], axis=0)
        out_ref[k] = row_refs[k][:, width:].astype(F32) - mul(x, p)
        copies.append(pltpu.make_async_copy(out_ref.at[k], out_hbm.at[:, at], sems.at[k]))
        copies[-1].start()
    for copy in copies:
        copy.wait()


def paired_tail(x_own, image, w_own, w_side, give, node_row, o, d, dom, nodes):
    slab, width = w_own.shape[1:]
    orb = 4
    rows = nodes // orb
    side, core = o // 2, o % 2
    scale = 1.0 / (nodes * dom)
    sds = jax.ShapeDtypeStruct
    smem = pl.BlockSpec(memory_space=pltpu.SMEM)
    vmem = pl.BlockSpec(memory_space=pltpu.VMEM)
    far = swap(give, "orb", 2)
    total = image.shape[0]

    def back(first, second, x_own, image):
        whole = lambda *shape: pl.BlockSpec(shape, lambda i: (0,) * len(shape))
        return pl.pallas_call(
            back_pair_kernel,
            grid=(1,),
            in_specs=[smem, whole(1, total), whole(total, width), whole(total, width)],
            out_specs=[whole(rows, 2 * width)] * 2,
            out_shape=[sds((rows, 2 * width), BF16)] * 2,
            compiler_params=params(),
            cost_estimate=pl.CostEstimate(flops=1 << 20, bytes_accessed=1 << 10, transcendentals=0),
        )(jnp.stack([jnp.bitwise_xor(o, first), jnp.bitwise_xor(o, second)]), node_row, x_own, image)

    cuts = back(2, 3, x_own, image)
    x_other = swap(x_own, "orb", 1)
    w_other = [swap(w, "orb", 1) for w in w_side]
    top = width + width // 2
    near = pl.pallas_call(
        functools.partial(near_gram_kernel, scale),
        in_specs=[smem] + [vmem] * 3,
        out_shape=sds((top, width), F32),
        compiler_params=params(),
        cost_estimate=pl.CostEstimate(flops=1 << 20, bytes_accessed=1 << 10, transcendentals=0),
    )(core.reshape(1), x_own, w_own, x_other)
    far, near, *cuts, w_other[0], w_other[1] = lax.optimization_barrier((far, near, *cuts, *w_other))
    row2, row3 = swap(cuts[0], "orb", 2), swap(cuts[1], "orb", 3)
    groups, base = [], 1
    while base < dom:
        ways = 2 if base == 1 or base * 4 > dom else 4
        groups.append((base, ways))
        base *= ways
    bits = jnp.stack([(d // base) % ways for base, ways in groups])
    little = pl.CostEstimate(flops=1 << 10, bytes_accessed=1 << 10, transcendentals=0)
    count = top + 2 * width

    def parts_of(n, ways):
        return [sds((n // ways, width), F32)] + [sds((n // ways, width), BF16)] * (ways - 1)

    keep, *gives = pl.pallas_call(
        functools.partial(far_gram_kernel, scale),
        in_specs=[smem] * 2 + [vmem] * 5,
        out_shape=parts_of(count, 2),
        scratch_shapes=[pltpu.VMEM((count, width), F32)],
        compiler_params=params(),
        cost_estimate=pl.CostEstimate(flops=8 * slab * width * width, bytes_accessed=4 << 20, transcendentals=0),
    )(bits, jnp.stack([side, core]), w_own, *w_other, far, near)
    row0 = cut1 = None
    for i, (base, ways) in enumerate(groups):
        if i == 0:
            x_own, image, gives[0] = lax.optimization_barrier((x_own, image, gives[0]))
            row0, cut1 = back(0, 1, x_own, image)
        gots = [swap(give, "dom", base * (j + 1)) for j, give in enumerate(gives)]
        n = keep.shape[0]
        last = i == len(groups) - 1
        outs = pl.pallas_call(
            functools.partial(reduce_kernel, i + 1, ways),
            in_specs=[smem] + [vmem] * ways,
            out_shape=[sds((n, width), BF16)] if last else parts_of(n, groups[i + 1][1]),
            scratch_shapes=[] if last else [pltpu.VMEM((n, width), F32)],
            compiler_params=params(),
            cost_estimate=little,
        )(bits, keep, *gots)
        outs = list(outs)
        if i == 0:
            outs[-1], row0, cut1 = lax.optimization_barrier((outs[-1], row0, cut1))
        if last:
            outs[-1], row2 = lax.optimization_barrier((outs[-1], row2))
            share = outs[0]
        else:
            keep, *gives = outs
    for i in reversed(range(1, len(groups))):
        base, ways = groups[i]
        gots = [swap(share, "dom", base * j) for j in range(1, ways)]
        share = pl.pallas_call(
            functools.partial(join_kernel, i),
            in_specs=[smem] + [vmem] * ways,
            out_shape=sds((ways * share.shape[0], width), BF16),
            compiler_params=params(),
            cost_estimate=little,
        )(bits, share, *gots)
    row1 = swap(cut1, "orb", 1)
    got = swap(share, "dom", 1)
    got, row3 = lax.optimization_barrier((got, row3))
    q2 = [swap(share, "orb", 2), swap(got, "orb", 2)]
    q1 = [swap(share, "orb", 1), swap(got, "orb", 1)]
    q3a = swap(q2[0], "orb", 1)
    q2[1], row1 = lax.optimization_barrier((q2[1], row1))
    q3 = [q3a, swap(q2[1], "orb", 1)]
    cols = orb * width
    return pl.pallas_call(
        paired_residual_kernel,
        in_specs=[smem] + [vmem] * 12,
        out_shape=(sds((rows, cols), F32), sds((cols, cols), BF16)),
        out_specs=[pl.BlockSpec(memory_space=pl.ANY)] * 2,
        scratch_shapes=[
            pltpu.VMEM((orb, rows, width), F32),
            pltpu.VMEM((cols, cols), BF16),
            pltpu.VMEM((orb, count, width), BF16),
            pltpu.SemaphoreType.DMA((orb + 1,)),
        ],
        compiler_params=params(),
    )(jnp.stack([o, d % 2]), share, got, *q1, *q2, *q3, row0, row1, row2, row3)


def body(orbitals, potential, cell_hamiltonian, connectivity, face_nodes):
    nodes, width = orbitals.shape
    cells, npc = connectivity.shape
    face = face_nodes.shape[0]
    fp, ip = up16(face), up16(npc - 2 * face)
    fp = (fp + 63) // 64 * 64
    stride = fp + ip
    cp = stride + fp
    total = cells * stride
    orb, dom = lax.axis_size("orb"), lax.axis_size("dom")
    d = lax.axis_index("dom")
    o = lax.axis_index("orb")
    sds = jax.ShapeDtypeStruct
    pot_row = potential.reshape(1, nodes)
    face_row = face_nodes.reshape(1, face)

    face_values = pl.pallas_call(
        face_kernel, out_shape=sds((fp + 16, width), BF16), compiler_params=params()
    )(face_row, orbitals, pot_row)
    ghost = shift(face_values, "dom", -1)

    extra = -(-DEGREE * fp // width)
    ext = pltpu.VMEM((total + fp, width), BF16)
    cost = pl.CostEstimate(
        flops=2 * DEGREE * cells * cp * cp * width, bytes_accessed=8 << 20, transcendentals=0
    )
    vmem = pl.BlockSpec(memory_space=pltpu.VMEM)
    hcan, y, pot, node, first, own, up, down = pl.pallas_call(
        functools.partial(free_kernel, fp, ip),
        in_specs=[vmem] * 2 + [pl.BlockSpec(memory_space=pl.ANY)] + [vmem] * 3,
        out_shape=[
            sds((cells, cp, cp), BF16),
            sds((total, width), BF16),
            sds((total, 1), F32),
            sds((cells, 1, stride), F32),
            sds((total, width), BF16),
            sds((2, DEGREE + 1 + extra, fp, width), F32),
            sds((DEGREE + 1 + extra, fp, width), BF16),
            sds((DEGREE + extra, fp, width), BF16),
        ],
        scratch_shapes=[ext, ext, pltpu.VMEM((cells, npc, npc), BF16), pltpu.SemaphoreType.DMA],
        compiler_params=params(),
        cost_estimate=cost,
    )(connectivity, face_row, cell_hamiltonian, orbitals, pot_row, ghost)
    node_row = node.reshape(1, total)
    from_left = shift(up, "dom", 1)
    from_right = shift(down, "dom", -1)
    vmem = pl.BlockSpec(memory_space=pltpu.VMEM)
    slab = cells // 2 * stride + fp
    place = jnp.stack([(d == dom - 1).astype(jnp.int32), (o // 2) % 2])
    x_own, face_image, give = pl.pallas_call(
        functools.partial(forced_kernel, fp),
        in_specs=[pl.BlockSpec(memory_space=pltpu.SMEM)] + [vmem] * 8,
        out_shape=[
            sds((total + fp, width), BF16),
            sds((fp, width), F32),
            sds((slab, width), BF16),
        ],
        scratch_shapes=[ext, ext, ext],
        compiler_params=params(),
        cost_estimate=cost,
    )(place, y, ghost, first, own, from_left, from_right, hcan, pot)
    image, w_own, *w_side = pl.pallas_call(
        functools.partial(image_kernel, fp),
        in_specs=[pl.BlockSpec(memory_space=pltpu.SMEM)] + [vmem] * 4,
        out_shape=[sds((total, width), BF16), sds((2, slab, width), BF16)] + [sds((slab // 2, width), BF16)] * 2,
        compiler_params=params(),
        cost_estimate=pl.CostEstimate(flops=1 << 20, bytes_accessed=1 << 10, transcendentals=0),
    )(place, x_own, face_image, hcan, pot)

    if orb == 4 and dom % 8 == 0:
        return paired_tail(x_own, image, w_own, w_side, give, node_row, o, d, dom, nodes)
    cut = pl.pallas_call(
        back_kernel,
        grid=(orb,),
        in_specs=[full((1, total)), full((total, width)), full((total, width))],
        out_specs=pl.BlockSpec((1, nodes // orb, 2 * width), lambda i: (i, 0, 0)),
        out_shape=sds((orb, nodes // orb, 2 * width), BF16),
        compiler_params=params(),
        cost_estimate=pl.CostEstimate(flops=4 * total * nodes * width, bytes_accessed=4 << 20, transcendentals=0),
    )(node_row, x_own, image)
    both = lax.all_to_all(cut, "orb", split_axis=0, concat_axis=0, tiled=True)
    x_rows, i_rows = both[:, :, :width], both[:, :, width:]

    rows = nodes // orb
    cols = orb * width
    share = pl.pallas_call(
        functools.partial(gram_kernel, 1.0 / (nodes * dom)),
        grid=(orb,),
        in_specs=[pl.BlockSpec((1, rows, width), lambda i: (i, 0, 0)), full((orb, rows, width))],
        out_specs=pl.BlockSpec((1, width, cols), lambda i: (i, 0, 0)),
        out_shape=sds((orb, width, cols), F32),
        scratch_shapes=[pltpu.VMEM((rows, cols), BF16)],
        compiler_params=params(),
    )(x_rows, i_rows)

    hops = []
    for axis, me, size in (("orb", o, orb), ("dom", d, dom)):
        if axis == "dom":
            share = share.reshape(dom, width // dom, cols)
        bit = 1
        while bit < size:
            share = share.reshape((share.shape[0] // 2, 2) + share.shape[1:])
            mine = (me // bit) % 2
            keep = lax.dynamic_index_in_dim(share, mine, 1, keepdims=False)
            give = lax.dynamic_index_in_dim(share, 1 - mine, 1, keepdims=False)
            got = swap(give.astype(BF16), axis, bit)
            share = keep + got.astype(F32)
            hops.append((axis, bit, mine))
            bit *= 2
    share = share.astype(BF16)
    for axis, bit, mine in reversed(hops):
        if axis == "orb" and share.shape[0] == dom and bit * 2 == orb:
            share = share.reshape(1, width, cols)
        got = swap(share, axis, bit)
        share = jnp.where(mine == 0, jnp.stack([share, got], axis=1), jnp.stack([got, share], axis=1))
        share = share.reshape((share.shape[0] * 2,) + share.shape[2:])
    projected = share.reshape(cols, cols)

    residual = pl.pallas_call(
        residual_kernel, out_shape=sds((rows, cols), F32), compiler_params=params()
    )(x_rows, i_rows, projected)
    return (residual, projected)


def solution(mesh):
    return jax.shard_map(
        body,
        mesh=mesh,
        in_specs=(P("dom", "orb"), P("dom"), P("dom", None, None), P("dom", None), P("dom")),
        out_specs=(P(("dom", "orb"), None), P()),
        check_vma=False,
    )
```

```python
import functools

import jax
import jax.numpy as jnp
from jax import lax
from jax.experimental import pallas as pl
from jax.experimental.pallas import tpu as pltpu
from jax.sharding import PartitionSpec as P

DEGREE = 4
CENTER = 1.5
HALF = 2.0
F32 = jnp.float32
BF16 = jnp.bfloat16
VMEM_LIMIT = 50 * 1024 * 1024


def up16(n):
    return (n + 15) // 16 * 16


def iota(shape, dim):
    return lax.broadcasted_iota(jnp.int32, shape, dim).astype(F32)


def to_col(row, rows):
    n = row.shape[1]
    return jnp.sum(jnp.where(iota((rows, n), 0) == iota((rows, n), 1), row, 0.0), axis=1, keepdims=True)


def to_row(col):
    n = col.shape[0]
    return jnp.sum(jnp.where(iota((n, n), 0) == iota((n, n), 1), col, 0.0), axis=0, keepdims=True)


def params():
    return pltpu.CompilerParams(vmem_limit_bytes=VMEM_LIMIT)


def thirds(a):
    one = a.astype(BF16)
    rest = a - one.astype(F32)
    two = rest.astype(BF16)
    return one, two, (rest - two.astype(F32)).astype(BF16)


def face_kernel(face_ref, x_ref, pot_ref, out_ref):
    width = x_ref.shape[1]
    fp = out_ref.shape[0] - 16
    nodes = x_ref.shape[0]
    col = to_col(face_ref[...].astype(F32) + 1.0, fp) - 1.0
    hit = jnp.where(col == iota((fp, nodes), 1), 1.0, 0.0).astype(BF16)
    out_ref[:fp] = mul(hit, x_ref[...]).astype(BF16)
    ri = lax.broadcasted_iota(jnp.int32, (16, nodes), 0)
    parts = [p.astype(F32) for p in thirds(pot_ref[...])]
    rows = jnp.where(ri == 0, parts[0], jnp.where(ri == 1, parts[1], jnp.where(ri == 2, parts[2], 0.0))).astype(BF16)
    got = lax.dot_general(rows, hit, (((1,), (1,)), ((), ())), preferred_element_type=F32).astype(BF16)
    if width > fp:
        got = jnp.concatenate([got, jnp.zeros((16, width - fp), BF16)], axis=1)
    out_ref[fp:] = got


def turn(a, b):
    return lax.dot_general(a, b, (((1,), (1,)), ((), ())), preferred_element_type=F32)


def halves(a):
    high = jnp.floor(a * (1.0 / 64.0))
    return high.astype(BF16), (a - 64.0 * high).astype(BF16)


def flat(mask):
    return jnp.where(mask, 1.0, 0.0).astype(BF16)


def order(fp, ip, arrived, conn_ref, face_ref, h_ref, x_ref, pot_ref, hcan_ref, v_ref, potc_ref, node_ref):
    cells, npc = conn_ref.shape
    nodes = x_ref.shape[0]
    face = face_ref.shape[1]
    stride = fp + ip
    cp = stride + fp
    conn = conn_ref[...].astype(F32)
    eye = flat(iota((npc, npc), 0) == iota((npc, npc), 1))
    below = flat(iota((npc, npc), 0) < iota((npc, npc), 1))
    high, low = halves(conn)
    cols = 64.0 * turn(eye, high) + turn(eye, low)
    rows = [conn[c : c + 1] for c in range(cells)]
    ones = jnp.ones((cells, npc), BF16)
    same = [flat(cols[:, c : c + 1] == rows[c + 1]) for c in range(cells - 1)]
    ri = lax.broadcasted_iota(jnp.int32, (cells, npc), 0)
    top = jnp.where(conn >= float(nodes), 1.0, 0.0)
    for c in range(cells - 1):
        top = jnp.where(ri == c, turn(ones, same[c]), top)
    rank_top = mul(top.astype(BF16), below)
    rank_b = rank_top.astype(BF16)
    top_slot = jnp.where(ri == cells - 1, conn - float(nodes), rank_top)
    fhit = to_col(face_ref[...].astype(F32), face) == rows[0]
    bot = jnp.where(ri == 0, jnp.max(jnp.where(fhit, 1.0, 0.0), axis=0, keepdims=True), 0.0)
    bot_slot = jnp.where(ri == 0, jnp.sum(jnp.where(fhit, iota((face, npc), 0), 0.0), axis=0, keepdims=True), 0.0)
    for c in range(cells - 1):
        both = jnp.concatenate([ones, rank_b], axis=0)
        got = mul(both, same[c])
        bot = jnp.where(ri == c + 1, got[:1], bot)
        bot_slot = jnp.where(ri == c + 1, got[cells + c : cells + c + 1], bot_slot)
    mid_rank = mul((1.0 - top - bot).astype(BF16), below)
    slot = jnp.where(top > 0.5, top_slot + float(stride), jnp.where(bot > 0.5, bot_slot, mid_rank + float(fp)))
    high, low = halves(conn + 1.0)
    number = iota((8, nodes), 1)[:1]
    arrived()
    for c in range(cells):
        perm = flat(iota((cp, npc), 0) == slot[c : c + 1])
        half = mul(perm, h_ref[c]).astype(BF16)
        hcan_ref[c] = turn(half, perm).astype(BF16)
        lead = perm[:stride]
        node = 64.0 * turn(lead, high)[:, c : c + 1] + turn(lead, low)[:, c : c + 1] - 1.0
        node_ref[c] = 64.0 * turn(high, lead)[c : c + 1] + turn(low, lead)[c : c + 1] - 1.0
        at = slice(c * stride, (c + 1) * stride)
        hit = node == number
        v_ref[at] = mul(flat(hit), x_ref[...]).astype(BF16)
        potc_ref[at] = jnp.sum(jnp.where(hit, pot_ref[...], 0.0), axis=1, keepdims=True)


def advance(image, now, before):
    if before is None:
        return (image - CENTER * now) / HALF
    return 2.0 * (image - CENTER * now) / HALF - before


def split(a):
    high = a.astype(BF16)
    return high, (a - high.astype(F32)).astype(BF16)


def mul(a, b):
    return jnp.dot(a, b, preferred_element_type=F32)


def mul_r(a, b):
    return mul(a, b.astype(BF16))


def sweep(h_ref, y_ref, fp, emit):
    cells, cp = h_ref.shape[:2]
    stride = cp - fp
    carry = None
    for c in range(cells):
        prod = mul(h_ref[c], y_ref[c * stride : c * stride + cp])
        rows = prod[:stride]
        if c > 0:
            rows = jnp.concatenate([rows[:fp] + carry, rows[fp:]], axis=0)
        emit(c, rows, prod[:fp], carry)
        carry = prod[stride:]
    return carry


def response(hc, hn, potc, fp, upper):
    cp = hc.shape[0]
    stride = cp - fp
    if upper:
        f, r, s, g = slice(stride, cp), slice(0, stride), slice(0, fp), slice(stride, cp)
        rest = slice(0, stride)
    else:
        f, r, s, g = slice(0, fp), slice(fp, cp), slice(stride - fp, stride), slice(0, fp)
        rest = slice(fp, cp)
    gain = 2.0 / HALF
    out = [hc[f, f].astype(F32)]
    one = gain * hc[r, f].astype(F32)
    out.append(mul_r(hc[f, r], one))

    def pad_next(face_rows):
        zero = jnp.zeros((stride, fp), F32)
        return jnp.concatenate([zero, face_rows] if upper else [face_rows, zero], axis=0)

    def near(value, next_value):
        got = mul_r(hc[r, r], value) + (potc - CENTER) * value
        add = mul_r(hn[g, :], next_value)
        if upper:
            return jnp.concatenate([got[:fp] + add, got[fp:]], axis=0)
        return jnp.concatenate([got[: stride - fp], got[stride - fp :] + add], axis=0)

    two = gain * near(one, pad_next(one[s]))
    out.append(mul_r(hc[f, r], two))
    two_next = gain * mul_r(hn, pad_next(one[s]))
    if upper:
        two_next = jnp.concatenate([two_next[:stride], two[s]], axis=0)
    else:
        two_next = jnp.concatenate([two[s], two_next[fp:]], axis=0)
    three = gain * near(two, two_next) - one
    out.append(mul_r(hc[f, r], three))
    return out


def store_matrices(mats, out_ref, at, fp, width):
    for j, m in enumerate(mats):
        block, lane = divmod(j * fp, width)
        out_ref[at + block, :, lane : lane + fp] = m.astype(out_ref.dtype)


def load_matrices(ref, at, count, fp, width):
    spots = [divmod(j * fp, width) for j in range(count)]
    return [ref[at + block, :, lane : lane + fp].astype(F32) for block, lane in spots]


def free_kernel(
    fp, ip, conn_ref, face_ref, hraw_ref, raw_ref, potraw_ref, ghost_ref,
    h_hbm, v_ref, pot_hbm, node_ref, first_hbm, own_ref, up_ref, down_ref,
    h_ref, pot_ref, first_ref, a_ref, b_ref, hin_ref, sem, sems,
):
    copy = pltpu.make_async_copy(hraw_ref, hin_ref, sem)
    copy.start()
    order(fp, ip, copy.wait, conn_ref, face_ref, hin_ref, raw_ref, potraw_ref, h_ref, v_ref, pot_ref, node_ref)
    leaving = [
        pltpu.make_async_copy(src, dst, sems.at[i])
        for i, (src, dst) in enumerate(((h_ref, h_hbm), (pot_ref, pot_hbm), (first_ref, first_hbm)))
    ]
    leaving[0].start()
    leaving[1].start()
    cells, cp = h_ref.shape[:2]
    stride = cp - fp
    total = cells * stride
    width = v_ref.shape[1]
    a_ref[:total] = v_ref[...]
    a_ref[total:] = ghost_ref[:fp]
    b_ref[total:] = jnp.zeros((fp, width), BF16)

    def keep(k, low, high):
        own_ref[0, k] = low
        own_ref[1, k] = high
        if k < DEGREE:
            down_ref[k] = low.astype(BF16)
        up_ref[k] = high.astype(BF16)

    now_ref, other_ref = a_ref, b_ref
    for k in range(DEGREE):
        ends = {}

        def emit(c, rows, lower, carry, k=k, now_ref=now_ref, other_ref=other_ref, ends=ends):
            at = slice(c * stride, (c + 1) * stride)
            if c == 0:
                ends["low"] = rows[:fp]
            now = now_ref[at].astype(F32)
            before = None if k == 0 else other_ref[at].astype(F32)
            if k == 1:
                before = v_ref[at].astype(F32)
            value = advance(rows + pot_ref[at] * now, now, before).astype(BF16)
            if c == 0:
                value = jnp.concatenate([jnp.zeros((fp, width), BF16), value[fp:]], axis=0)
            if k == 0:
                first_ref[at] = value
            other_ref[at] = value

        high = sweep(h_ref, now_ref, fp, emit)
        keep(k, ends["low"], high)
        if k == 0:
            leaving[2].start()
            a_ref[total:] = jnp.zeros((fp, width), BF16)
        now_ref, other_ref = other_ref, now_ref
    keep(DEGREE, mul(h_ref[0, :fp], now_ref[:cp]), mul(h_ref[cells - 1, stride:], now_ref[total - stride :]))
    low = response(h_ref[0], h_ref[1], pot_ref[fp:cp], fp, False)
    high = response(h_ref[cells - 1], h_ref[cells - 2], pot_ref[total - stride :], fp, True)
    store_matrices(low, down_ref, DEGREE, fp, width)
    store_matrices(high, up_ref, DEGREE + 1, fp, width)
    for side, mats in enumerate((low, high)):
        store_matrices(mats, own_ref.at[side], DEGREE + 1, fp, width)
    for copy in leaving:
        copy.wait()


def forced_kernel(
    fp, place_ref, v_ref, ghost_ref, first_hbm, own_ref, fromleft_ref, fromright_ref, h_hbm, pot_hbm,
    x_ref, face_image_ref, slab_ref, a_ref, b_ref, c_ref, h_ref, pot_ref, sems,
):
    cells, cp = h_ref.shape[:2]
    stride = cp - fp
    total = cells * stride
    width = v_ref.shape[1]
    rest = pl.ds(fp, total - fp)
    coming = [
        pltpu.make_async_copy(src, dst, sems.at[i])
        for i, (src, dst) in enumerate(
            (
                (pot_hbm.at[pl.ds(0, fp)], pot_ref.at[pl.ds(0, fp)]),
                (first_hbm, a_ref.at[pl.ds(0, total)]),
                (pot_hbm.at[rest], pot_ref.at[rest]),
                (h_hbm, h_ref),
            )
        )
    ]
    for copy in coming:
        copy.start()
    coming[0].wait()
    half = cells // 2
    extra = own_ref.shape[1] - DEGREE - 1
    potg = to_col(jnp.sum(ghost_ref[fp:].astype(F32), axis=0, keepdims=True)[:, :fp], fp)
    nothing = jnp.zeros((fp, width), BF16)
    sides = []
    for side, (got_ref, pot, start) in enumerate(
        ((fromleft_ref, pot_ref[:fp], v_ref[:fp]), (fromright_ref, potg, ghost_ref[:fp]))
    ):
        theirs = load_matrices(got_ref, got_ref.shape[0] - extra, DEGREE, fp, width)
        ours = load_matrices(own_ref.at[side], DEGREE + 1, DEGREE, fp, width)
        mats = [a + b for a, b in zip(theirs, ours)]
        line = jnp.concatenate(mats[::-1], axis=1)
        sides.append((got_ref, pot, jnp.concatenate(split(line), axis=0), [start]))
    for k in range(DEGREE + 1):
        for side, (got_ref, pot, line, values) in enumerate(sides):
            if side == 1 and k == DEGREE:
                continue
            h = own_ref[side, k] + got_ref[k].astype(F32)
            if k > 0:
                past = [values[m] if m >= 1 else nothing for m in range(k - DEGREE + 1, k + 1)]
                both = mul(line, jnp.concatenate(past, axis=0))
                h = h + both[:fp] + both[fp:]
            now = values[k].astype(F32)
            h = h + pot * now
            if k == DEGREE:
                face_image_ref[...] = h
                continue
            value = advance(h, now, None if k == 0 else values[k - 1].astype(F32))
            if side == 1:
                value = jnp.where(place_ref[0] == 1, 0.0, value)
            values.append(value.astype(BF16))
    low, high = sides[0][3], sides[1][3]
    for copy in coming[1:]:
        copy.wait()
    a_ref[:fp] = low[1]
    a_ref[total:] = high[1]
    refs = [v_ref, a_ref, b_ref, c_ref, x_ref]
    for k in range(1, DEGREE):
        now_ref = refs[k]

        def emit(c, rows, lower, carry, k=k, now_ref=now_ref):
            at = slice(c * stride, (c + 1) * stride)
            now = now_ref[at].astype(F32)
            value = advance(rows + pot_ref[at] * now, now, refs[k - 1][at].astype(F32)).astype(BF16)
            if c == 0:
                value = jnp.concatenate([low[k + 1], value[fp:]], axis=0)
            refs[k + 1][at] = value

        sweep(h_ref, now_ref, fp, emit)
        refs[k + 1][total:] = high[k + 1]

    @pl.when(place_ref[1] == 0)
    def _():
        slab_ref[...] = x_ref[half * stride :]

    @pl.when(place_ref[1] == 1)
    def _():
        slab_ref[...] = x_ref[: half * stride + fp]


def image_kernel(fp, place_ref, x_ref, face_image_ref, h_ref, pot_ref, image_ref, w_ref, first_ref, second_ref):
    cells, cp = h_ref.shape[:2]
    stride = cp - fp
    half = cells // 2

    def emit(c, rows, lower, carry):
        at = slice(c * stride, (c + 1) * stride)
        now = x_ref[at].astype(F32)
        out = (rows + pot_ref[at] * now).astype(BF16)
        part, at_w = divmod(c, half)
        w_ref[part, at_w * stride : (at_w + 1) * stride] = out
        if c == half:
            w_ref[0, half * stride :] = carry.astype(BF16)
            w_ref[1, :fp] = (lower + pot_ref[c * stride : c * stride + fp] * now[:fp]).astype(BF16)
        if c == 0:
            out = jnp.concatenate([face_image_ref[...].astype(BF16), out[fp:]], axis=0)
        image_ref[at] = out

    w_ref[1, half * stride :] = sweep(h_ref, x_ref, fp, emit).astype(BF16)
    n = first_ref.shape[0]
    first_ref[...] = w_ref[place_ref[1], :n]
    second_ref[...] = w_ref[place_ref[1], n:]


def back_kernel(node_ref, x_ref, image_ref, out_ref):
    rows = out_ref.shape[1]
    width = x_ref.shape[1]
    want = (lax.broadcasted_iota(jnp.int32, (rows, 1), 0) + pl.program_id(0) * rows).astype(F32)
    hit = flat(want == node_ref[...])
    out_ref[0, :, :width] = mul(hit, x_ref[...]).astype(BF16)
    out_ref[0, :, width:] = mul(hit, image_ref[...]).astype(BF16)


def back_pair_kernel(at_ref, node_ref, x_ref, image_ref, *out_refs):
    rows = out_refs[0].shape[0]
    width = x_ref.shape[1]
    for i, out_ref in enumerate(out_refs):
        want = (lax.broadcasted_iota(jnp.int32, (rows, 1), 0) + at_ref[i] * rows).astype(F32)
        hit = flat(want == node_ref[...])
        out_ref[:, :width] = mul(hit, x_ref[...]).astype(BF16)
        out_ref[:, width:] = mul(hit, image_ref[...]).astype(BF16)


def gram_kernel(scale, x_ref, y_ref, out_ref, rows_ref):
    parts, _, width = y_ref.shape

    @pl.when(pl.program_id(0) == 0)
    def _():
        for j in range(parts):
            rows_ref[:, j * width : (j + 1) * width] = y_ref[j]

    out_ref[0] = (
        lax.dot_general(x_ref[0], rows_ref[...], (((0,), (0,)), ((), ())), preferred_element_type=F32) * scale
    )


def residual_kernel(x_ref, y_ref, p_ref, out_ref):
    parts, _, width = x_ref.shape
    x = jnp.concatenate([x_ref[j] for j in range(parts)], axis=1)
    y = jnp.concatenate([y_ref[j] for j in range(parts)], axis=1)
    out_ref[...] = y.astype(F32) - jnp.dot(x, p_ref[...], preferred_element_type=F32)


def full(shape):
    return pl.BlockSpec(shape, lambda i: (0,) * len(shape))


def swap(block, axis, bit):
    return lax.ppermute(block, axis, [(i, i ^ bit) for i in range(lax.axis_size(axis))])


def shift(block, axis, distance):
    n = lax.axis_size(axis)
    return lax.ppermute(block, axis, [(i, i + distance) for i in range(n) if 0 <= i + distance < n])


def tmul(a, b):
    return lax.dot_general(a, b, (((0,), (0,)), ((), ())), preferred_element_type=F32)


def near_gram_kernel(scale, core_ref, x_ref, w_ref, other_ref, out_ref):
    slab, width = w_ref.shape[1:]
    at = (slice(0, slab), slice(x_ref.shape[0] - slab, x_ref.shape[0]))
    own = [x_ref[a] for a in at]
    out_ref[:width] = (tmul(own[0], w_ref[0]) + tmul(own[1], w_ref[1])) * scale
    half = width // 2

    @pl.when(core_ref[0] == 0)
    def _():
        out_ref[width:] = sum(tmul(w_ref[i, :, :half], other_ref[at[i]]) for i in range(2)) * scale

    @pl.when(core_ref[0] == 1)
    def _():
        out_ref[width:] = sum(tmul(other_ref[at[i], half:], w_ref[i]) for i in range(2)) * scale


def part_ways(sum_ref, mine, keep_ref, give_refs):
    n = keep_ref.shape[0]
    keep_ref[...] = sum_ref[pl.ds(pl.multiple_of(mine * n, 16), n)]
    for j, give_ref in enumerate(give_refs):
        give_ref[...] = sum_ref[pl.ds(pl.multiple_of(jnp.bitwise_xor(mine, j + 1) * n, 16), n)].astype(BF16)


def reduce_kernel(step, ways, bits_ref, keep_ref, *refs):
    total = keep_ref[...]
    for got_ref in refs[: ways - 1]:
        total = total + got_ref[...].astype(F32)
    refs = refs[ways - 1 :]
    if len(refs) == 1:
        refs[0][...] = total.astype(BF16)
        return
    keep_out, *gives, sum_ref = refs
    sum_ref[...] = total
    part_ways(sum_ref, bits_ref[step], keep_out, gives)


def join_kernel(step, bits_ref, own_ref, *refs):
    *got_refs, out_ref = refs
    n = own_ref.shape[0]
    mine = bits_ref[step]
    for j, ref in enumerate([own_ref] + got_refs):
        out_ref[pl.ds(pl.multiple_of(jnp.bitwise_xor(mine, j) * n, 16), n)] = ref[...]


def far_gram_kernel(scale, bits_ref, place_ref, w_ref, first_ref, second_ref, far_ref, near_ref, keep_ref, *refs):
    *give_refs, out_ref = refs
    width = w_ref.shape[2]
    near = near_ref.shape[0]
    side, core = place_ref[0], place_ref[1]
    out_ref[:near] = near_ref[...]
    far = far_ref[...]
    mine = pl.multiple_of(near + core * width, width // 2)
    other = pl.multiple_of(near + (1 - core) * width, width // 2)
    out_ref[pl.ds(mine, width)] = tmul(w_ref[side], far) * scale
    n = first_ref.shape[0]
    out_ref[pl.ds(other, width)] = (tmul(first_ref[...], far[:n]) + tmul(second_ref[...], far[n:])) * scale
    part_ways(out_ref, bits_ref[0], keep_ref, give_refs)


def paired_residual_kernel(place_ref, *refs):
    q_refs, refs = refs[:8], refs[8:]
    parts = 4
    row_refs, (out_hbm, p_hbm, out_ref, p_ref, q_ref, sems) = refs[:parts], refs[parts:]
    width = row_refs[0].shape[1] // 2
    half = width // 2
    me, mine = place_ref[0], place_ref[1]
    n = q_refs[0].shape[0]
    for k in range(parts):
        for j in range(2):
            q_ref[k, pl.ds(pl.multiple_of(jnp.bitwise_xor(mine, j) * n, 16), n)] = q_refs[2 * k + j][...]
    eye = (lax.broadcasted_iota(jnp.int32, (width, width), 0) == lax.broadcasted_iota(jnp.int32, (width, width), 1)).astype(
        F32
    ).astype(BF16)

    def turned(a):
        return lax.dot_general(eye, a, (((1,), (1,)), ((), ())), preferred_element_type=F32)

    def piece(i, lo, hi):
        return q_ref[jnp.bitwise_xor(me, i), lo:hi]

    def put(i, j, value):
        p_ref[i * width : (i + 1) * width, j * width : (j + 1) * width] = value

    near = width + half
    for i in range(parts):
        put(i, i, piece(i, 0, width))
    for i in range(0, parts, 2):
        block = jnp.concatenate([piece(i, width, near), piece(i + 1, width, near)], axis=0)
        put(i, i + 1, block)
        put(i + 1, i, turned(block).astype(BF16))
    for i in (0, 1):
        for j in (2, 3):
            one = piece(j ^ 2, near + i * width, near + (i + 1) * width)
            two = piece(i ^ 2, near + (j - 2) * width, near + (j - 1) * width)
            block = (one.astype(F32) + turned(two)).astype(BF16)
            put(i, j, block)
            put(j, i, turned(block).astype(BF16))
    copies = [pltpu.make_async_copy(p_ref, p_hbm, sems.at[parts])]
    copies[0].start()
    x = jnp.concatenate([ref[:, :width] for ref in row_refs], axis=1)
    spots = [pl.ds(pl.multiple_of(jnp.bitwise_xor(me, k) * width, width), width) for k in range(parts)]
    for k in range(parts):
        at = spots[k]
        p = jnp.concatenate([p_ref[spots[m], at] for m in range(parts)], axis=0)
        out_ref[k] = row_refs[k][:, width:].astype(F32) - mul(x, p)
        copies.append(pltpu.make_async_copy(out_ref.at[k], out_hbm.at[:, at], sems.at[k]))
        copies[-1].start()
    for copy in copies:
        copy.wait()


def paired_tail(x_own, image, w_own, w_side, give, node_row, o, d, dom, nodes):
    slab, width = w_own.shape[1:]
    orb = 4
    rows = nodes // orb
    side, core = o // 2, o % 2
    scale = 1.0 / (nodes * dom)
    sds = jax.ShapeDtypeStruct
    smem = pl.BlockSpec(memory_space=pltpu.SMEM)
    vmem = pl.BlockSpec(memory_space=pltpu.VMEM)
    far = swap(give, "orb", 2)
    total = image.shape[0]

    def back(first, second, x_own, image):
        whole = lambda *shape: pl.BlockSpec(shape, lambda i: (0,) * len(shape))
        return pl.pallas_call(
            back_pair_kernel,
            grid=(1,),
            in_specs=[smem, whole(1, total), whole(total, width), whole(total, width)],
            out_specs=[whole(rows, 2 * width)] * 2,
            out_shape=[sds((rows, 2 * width), BF16)] * 2,
            compiler_params=params(),
            cost_estimate=pl.CostEstimate(flops=1 << 20, bytes_accessed=1 << 10, transcendentals=0),
        )(jnp.stack([jnp.bitwise_xor(o, first), jnp.bitwise_xor(o, second)]), node_row, x_own, image)

    cuts = back(2, 3, x_own, image)
    x_other = swap(x_own, "orb", 1)
    w_other = [swap(w, "orb", 1) for w in w_side]
    top = width + width // 2
    near = pl.pallas_call(
        functools.partial(near_gram_kernel, scale),
        in_specs=[smem] + [vmem] * 3,
        out_shape=sds((top, width), F32),
        compiler_params=params(),
        cost_estimate=pl.CostEstimate(flops=1 << 20, bytes_accessed=1 << 10, transcendentals=0),
    )(core.reshape(1), x_own, w_own, x_other)
    far, near, *cuts, w_other[0], w_other[1] = lax.optimization_barrier((far, near, *cuts, *w_other))
    row2, row3 = swap(cuts[0], "orb", 2), swap(cuts[1], "orb", 3)
    groups, base = [], 1
    while base < dom:
        ways = 2 if base == 1 or base * 4 > dom else 4
        groups.append((base, ways))
        base *= ways
    bits = jnp.stack([(d // base) % ways for base, ways in groups])
    little = pl.CostEstimate(flops=1 << 10, bytes_accessed=1 << 10, transcendentals=0)
    count = top + 2 * width

    def parts_of(n, ways):
        return [sds((n // ways, width), F32)] + [sds((n // ways, width), BF16)] * (ways - 1)

    keep, *gives = pl.pallas_call(
        functools.partial(far_gram_kernel, scale),
        in_specs=[smem] * 2 + [vmem] * 5,
        out_shape=parts_of(count, 2),
        scratch_shapes=[pltpu.VMEM((count, width), F32)],
        compiler_params=params(),
        cost_estimate=pl.CostEstimate(flops=8 * slab * width * width, bytes_accessed=4 << 20, transcendentals=0),
    )(bits, jnp.stack([side, core]), w_own, *w_other, far, near)
    row0 = cut1 = None
    for i, (base, ways) in enumerate(groups):
        if i == 0:
            x_own, image, gives[0] = lax.optimization_barrier((x_own, image, gives[0]))
            row0, cut1 = back(0, 1, x_own, image)
        gots = [swap(give, "dom", base * (j + 1)) for j, give in enumerate(gives)]
        n = keep.shape[0]
        last = i == len(groups) - 1
        outs = pl.pallas_call(
            functools.partial(reduce_kernel, i + 1, ways),
            in_specs=[smem] + [vmem] * ways,
            out_shape=[sds((n, width), BF16)] if last else parts_of(n, groups[i + 1][1]),
            scratch_shapes=[] if last else [pltpu.VMEM((n, width), F32)],
            compiler_params=params(),
            cost_estimate=little,
        )(bits, keep, *gots)
        outs = list(outs)
        if i == 0:
            outs[-1], row0, cut1 = lax.optimization_barrier((outs[-1], row0, cut1))
        if last:
            outs[-1], row2 = lax.optimization_barrier((outs[-1], row2))
            share = outs[0]
        else:
            keep, *gives = outs
    for i in reversed(range(1, len(groups))):
        base, ways = groups[i]
        gots = [swap(share, "dom", base * j) for j in range(1, ways)]
        share = pl.pallas_call(
            functools.partial(join_kernel, i),
            in_specs=[smem] + [vmem] * ways,
            out_shape=sds((ways * share.shape[0], width), BF16),
            compiler_params=params(),
            cost_estimate=little,
        )(bits, share, *gots)
    row1 = swap(cut1, "orb", 1)
    got = swap(share, "dom", 1)
    got, row3 = lax.optimization_barrier((got, row3))
    q2 = [swap(share, "orb", 2), swap(got, "orb", 2)]
    q1 = [swap(share, "orb", 1), swap(got, "orb", 1)]
    q3a = swap(q2[0], "orb", 1)
    q2[1], row1 = lax.optimization_barrier((q2[1], row1))
    q3 = [q3a, swap(q2[1], "orb", 1)]
    cols = orb * width
    return pl.pallas_call(
        paired_residual_kernel,
        in_specs=[smem] + [vmem] * 12,
        out_shape=(sds((rows, cols), F32), sds((cols, cols), BF16)),
        out_specs=[pl.BlockSpec(memory_space=pl.ANY)] * 2,
        scratch_shapes=[
            pltpu.VMEM((orb, rows, width), F32),
            pltpu.VMEM((cols, cols), BF16),
            pltpu.VMEM((orb, count, width), BF16),
            pltpu.SemaphoreType.DMA((orb + 1,)),
        ],
        compiler_params=params(),
    )(jnp.stack([o, d % 2]), share, got, *q1, *q2, *q3, row0, row1, row2, row3)


def body(orbitals, potential, cell_hamiltonian, connectivity, face_nodes):
    nodes, width = orbitals.shape
    cells, npc = connectivity.shape
    face = face_nodes.shape[0]
    fp, ip = up16(face), up16(npc - 2 * face)
    fp = (fp + 63) // 64 * 64
    stride = fp + ip
    cp = stride + fp
    total = cells * stride
    orb, dom = lax.axis_size("orb"), lax.axis_size("dom")
    d = lax.axis_index("dom")
    o = lax.axis_index("orb")
    sds = jax.ShapeDtypeStruct
    pot_row = potential.reshape(1, nodes)
    face_row = face_nodes.reshape(1, face)

    face_values = pl.pallas_call(
        face_kernel, out_shape=sds((fp + 16, width), BF16), compiler_params=params()
    )(face_row, orbitals, pot_row)
    ghost = shift(face_values, "dom", -1)

    extra = -(-DEGREE * fp // width)
    ext = pltpu.VMEM((total + fp, width), BF16)
    cost = pl.CostEstimate(
        flops=2 * DEGREE * cells * cp * cp * width, bytes_accessed=8 << 20, transcendentals=0
    )
    vmem, hbm = pl.BlockSpec(memory_space=pltpu.VMEM), pl.BlockSpec(memory_space=pl.ANY)
    hcan, y, pot, node, first, own, up, down = pl.pallas_call(
        functools.partial(free_kernel, fp, ip),
        in_specs=[vmem] * 2 + [pl.BlockSpec(memory_space=pl.ANY)] + [vmem] * 3,
        out_shape=[
            sds((cells, cp, cp), BF16),
            sds((total, width), BF16),
            sds((total, 1), F32),
            sds((cells, 1, stride), F32),
            sds((total, width), BF16),
            sds((2, DEGREE + 1 + extra, fp, width), F32),
            sds((DEGREE + 1 + extra, fp, width), BF16),
            sds((DEGREE + extra, fp, width), BF16),
        ],
        out_specs=[hbm, vmem, hbm, vmem, hbm, vmem, vmem, vmem],
        scratch_shapes=[
            pltpu.VMEM((cells, cp, cp), BF16),
            pltpu.VMEM((total, 1), F32),
            pltpu.VMEM((total, width), BF16),
            ext,
            ext,
            pltpu.VMEM((cells, npc, npc), BF16),
            pltpu.SemaphoreType.DMA,
            pltpu.SemaphoreType.DMA((3,)),
        ],
        compiler_params=params(),
        cost_estimate=cost,
    )(connectivity, face_row, cell_hamiltonian, orbitals, pot_row, ghost)
    node_row = node.reshape(1, total)
    from_left = shift(up, "dom", 1)
    from_right = shift(down, "dom", -1)
    slab = cells // 2 * stride + fp
    place = jnp.stack([(d == dom - 1).astype(jnp.int32), (o // 2) % 2])
    x_own, face_image, give = pl.pallas_call(
        functools.partial(forced_kernel, fp),
        in_specs=[pl.BlockSpec(memory_space=pltpu.SMEM), vmem, vmem, hbm, vmem, vmem, vmem, hbm, hbm],
        out_shape=[
            sds((total + fp, width), BF16),
            sds((fp, width), F32),
            sds((slab, width), BF16),
        ],
        scratch_shapes=[
            ext,
            ext,
            ext,
            pltpu.VMEM((cells, cp, cp), BF16),
            pltpu.VMEM((total, 1), F32),
            pltpu.SemaphoreType.DMA((4,)),
        ],
        compiler_params=params(),
        cost_estimate=cost,
    )(place, y, ghost, first, own, from_left, from_right, hcan, pot)
    image, w_own, *w_side = pl.pallas_call(
        functools.partial(image_kernel, fp),
        in_specs=[pl.BlockSpec(memory_space=pltpu.SMEM)] + [vmem] * 4,
        out_shape=[sds((total, width), BF16), sds((2, slab, width), BF16)] + [sds((slab // 2, width), BF16)] * 2,
        compiler_params=params(),
        cost_estimate=pl.CostEstimate(flops=1 << 20, bytes_accessed=1 << 10, transcendentals=0),
    )(place, x_own, face_image, hcan, pot)

    if orb == 4 and dom % 8 == 0:
        return paired_tail(x_own, image, w_own, w_side, give, node_row, o, d, dom, nodes)
    cut = pl.pallas_call(
        back_kernel,
        grid=(orb,),
        in_specs=[full((1, total)), full((total, width)), full((total, width))],
        out_specs=pl.BlockSpec((1, nodes // orb, 2 * width), lambda i: (i, 0, 0)),
        out_shape=sds((orb, nodes // orb, 2 * width), BF16),
        compiler_params=params(),
        cost_estimate=pl.CostEstimate(flops=4 * total * nodes * width, bytes_accessed=4 << 20, transcendentals=0),
    )(node_row, x_own, image)
    both = lax.all_to_all(cut, "orb", split_axis=0, concat_axis=0, tiled=True)
    x_rows, i_rows = both[:, :, :width], both[:, :, width:]

    rows = nodes // orb
    cols = orb * width
    share = pl.pallas_call(
        functools.partial(gram_kernel, 1.0 / (nodes * dom)),
        grid=(orb,),
        in_specs=[pl.BlockSpec((1, rows, width), lambda i: (i, 0, 0)), full((orb, rows, width))],
        out_specs=pl.BlockSpec((1, width, cols), lambda i: (i, 0, 0)),
        out_shape=sds((orb, width, cols), F32),
        scratch_shapes=[pltpu.VMEM((rows, cols), BF16)],
        compiler_params=params(),
    )(x_rows, i_rows)

    hops = []
    for axis, me, size in (("orb", o, orb), ("dom", d, dom)):
        if axis == "dom":
            share = share.reshape(dom, width // dom, cols)
        bit = 1
        while bit < size:
            share = share.reshape((share.shape[0] // 2, 2) + share.shape[1:])
            mine = (me // bit) % 2
            keep = lax.dynamic_index_in_dim(share, mine, 1, keepdims=False)
            give = lax.dynamic_index_in_dim(share, 1 - mine, 1, keepdims=False)
            got = swap(give.astype(BF16), axis, bit)
            share = keep + got.astype(F32)
            hops.append((axis, bit, mine))
            bit *= 2
    share = share.astype(BF16)
    for axis, bit, mine in reversed(hops):
        if axis == "orb" and share.shape[0] == dom and bit * 2 == orb:
            share = share.reshape(1, width, cols)
        got = swap(share, axis, bit)
        share = jnp.where(mine == 0, jnp.stack([share, got], axis=1), jnp.stack([got, share], axis=1))
        share = share.reshape((share.shape[0] * 2,) + share.shape[2:])
    projected = share.reshape(cols, cols)

    residual = pl.pallas_call(
        residual_kernel, out_shape=sds((rows, cols), F32), compiler_params=params()
    )(x_rows, i_rows, projected)
    return (residual, projected)


def solution(mesh):
    return jax.shard_map(
        body,
        mesh=mesh,
        in_specs=(P("dom", "orb"), P("dom"), P("dom", None, None), P("dom", None), P("dom")),
        out_specs=(P(("dom", "orb"), None), P()),
        check_vma=False,
    )
```

```python
import functools

import jax
import jax.numpy as jnp
from jax import lax
from jax.experimental import pallas as pl
from jax.experimental.pallas import tpu as pltpu
from jax.sharding import PartitionSpec as P

DEGREE = 4
CENTER = 1.5
HALF = 2.0
F32 = jnp.float32
BF16 = jnp.bfloat16
LANES = 128
VMEM_LIMIT = 50 * 1024 * 1024


def up16(n):
    return (n + 15) // 16 * 16


def iota(shape, dim):
    return lax.broadcasted_iota(jnp.int32, shape, dim).astype(F32)


def to_col(row, rows):
    n = row.shape[1]
    return jnp.sum(jnp.where(iota((rows, n), 0) == iota((rows, n), 1), row, 0.0), axis=1, keepdims=True)


def to_row(col):
    n = col.shape[0]
    return jnp.sum(jnp.where(iota((n, n), 0) == iota((n, n), 1), col, 0.0), axis=0, keepdims=True)


def params():
    return pltpu.CompilerParams(vmem_limit_bytes=VMEM_LIMIT)


def thirds(a):
    one = a.astype(BF16)
    rest = a - one.astype(F32)
    two = rest.astype(BF16)
    return one, two, (rest - two.astype(F32)).astype(BF16)


def face_kernel(face_ref, x_ref, pot_ref, out_ref):
    width = x_ref.shape[1]
    fp = out_ref.shape[0] - 16
    nodes = x_ref.shape[0]
    col = to_col(face_ref[...].astype(F32) + 1.0, fp) - 1.0
    hit = jnp.where(col == iota((fp, nodes), 1), 1.0, 0.0).astype(BF16)
    out_ref[:fp] = mul(hit, x_ref[...]).astype(BF16)
    ri = lax.broadcasted_iota(jnp.int32, (16, nodes), 0)
    parts = [p.astype(F32) for p in thirds(pot_ref[...])]
    rows = jnp.where(ri == 0, parts[0], jnp.where(ri == 1, parts[1], jnp.where(ri == 2, parts[2], 0.0))).astype(BF16)
    got = lax.dot_general(rows, hit, (((1,), (1,)), ((), ())), preferred_element_type=F32).astype(BF16)
    if width > fp:
        got = jnp.concatenate([got, jnp.zeros((16, width - fp), BF16)], axis=1)
    out_ref[fp:] = got


def turn(a, b):
    return lax.dot_general(a, b, (((1,), (1,)), ((), ())), preferred_element_type=F32)


def halves(a):
    high = jnp.floor(a * (1.0 / 64.0))
    return high.astype(BF16), (a - 64.0 * high).astype(BF16)


def flat(mask):
    return jnp.where(mask, 1.0, 0.0).astype(BF16)


def order(fp, ip, arrived, conn_ref, face_ref, h_ref, x_ref, pot_ref, hcan_ref, v_ref, potc_ref, node_ref):
    cells, npc = conn_ref.shape
    nodes = x_ref.shape[0]
    face = face_ref.shape[1]
    stride = fp + ip
    cp = stride + fp
    conn = conn_ref[...].astype(F32)
    eye = flat(iota((npc, npc), 0) == iota((npc, npc), 1))
    below = flat(iota((npc, npc), 0) < iota((npc, npc), 1))
    high, low = halves(conn)
    cols = 64.0 * turn(eye, high) + turn(eye, low)
    rows = [conn[c : c + 1] for c in range(cells)]
    ones = jnp.ones((cells, npc), BF16)
    same = [flat(cols[:, c : c + 1] == rows[c + 1]) for c in range(cells - 1)]
    ri = lax.broadcasted_iota(jnp.int32, (cells, npc), 0)
    top = jnp.where(conn >= float(nodes), 1.0, 0.0)
    for c in range(cells - 1):
        top = jnp.where(ri == c, turn(ones, same[c]), top)
    rank_top = mul(top.astype(BF16), below)
    rank_b = rank_top.astype(BF16)
    top_slot = jnp.where(ri == cells - 1, conn - float(nodes), rank_top)
    fhit = to_col(face_ref[...].astype(F32), face) == rows[0]
    bot = jnp.where(ri == 0, jnp.max(jnp.where(fhit, 1.0, 0.0), axis=0, keepdims=True), 0.0)
    bot_slot = jnp.where(ri == 0, jnp.sum(jnp.where(fhit, iota((face, npc), 0), 0.0), axis=0, keepdims=True), 0.0)
    for c in range(cells - 1):
        both = jnp.concatenate([ones, rank_b], axis=0)
        got = mul(both, same[c])
        bot = jnp.where(ri == c + 1, got[:1], bot)
        bot_slot = jnp.where(ri == c + 1, got[cells + c : cells + c + 1], bot_slot)
    mid_rank = mul((1.0 - top - bot).astype(BF16), below)
    slot = jnp.where(top > 0.5, top_slot + float(stride), jnp.where(bot > 0.5, bot_slot, mid_rank + float(fp)))
    high, low = halves(conn + 1.0)
    number = iota((8, nodes), 1)[:1]
    arrived()
    for c in range(cells):
        perm = flat(iota((cp, npc), 0) == slot[c : c + 1])
        half = mul(perm, h_ref[c]).astype(BF16)
        hcan_ref[c] = turn(half, perm).astype(BF16)
        lead = perm[:stride]
        node = 64.0 * turn(lead, high)[:, c : c + 1] + turn(lead, low)[:, c : c + 1] - 1.0
        node_ref[c] = 64.0 * turn(high, lead)[c : c + 1] + turn(low, lead)[c : c + 1] - 1.0
        at = slice(c * stride, (c + 1) * stride)
        hit = node == number
        v_ref[at] = mul(flat(hit), x_ref[...]).astype(BF16)
        column = jnp.sum(jnp.where(hit, pot_ref[...], 0.0), axis=1, keepdims=True)
        potc_ref[at] = jnp.broadcast_to(column, (stride, LANES))


def spread(column, width):
    if width <= LANES:
        return column[:, :width]
    return jnp.concatenate([column] * (width // LANES), axis=1)


def advance(image, now, before):
    if before is None:
        return (image - CENTER * now) / HALF
    return 2.0 * (image - CENTER * now) / HALF - before


def split(a):
    high = a.astype(BF16)
    return high, (a - high.astype(F32)).astype(BF16)


def mul(a, b):
    return jnp.dot(a, b, preferred_element_type=F32)


def mul_r(a, b):
    return mul(a, b.astype(BF16))


def sweep(h_ref, y_ref, fp, emit):
    cells, cp = h_ref.shape[:2]
    stride = cp - fp
    carry = None
    for c in range(cells):
        prod = mul(h_ref[c], y_ref[c * stride : c * stride + cp])
        rows = prod[:stride]
        if c > 0:
            rows = jnp.concatenate([rows[:fp] + carry, rows[fp:]], axis=0)
        emit(c, rows, prod[:fp], carry)
        carry = prod[stride:]
    return carry


def response(hc, hn, potc, fp, upper):
    cp = hc.shape[0]
    stride = cp - fp
    if upper:
        f, r, s, g = slice(stride, cp), slice(0, stride), slice(0, fp), slice(stride, cp)
        rest = slice(0, stride)
    else:
        f, r, s, g = slice(0, fp), slice(fp, cp), slice(stride - fp, stride), slice(0, fp)
        rest = slice(fp, cp)
    potc = spread(potc, fp)
    gain = 2.0 / HALF
    out = [hc[f, f].astype(F32)]
    one = gain * hc[r, f].astype(F32)
    out.append(mul_r(hc[f, r], one))

    def pad_next(face_rows):
        zero = jnp.zeros((stride, fp), F32)
        return jnp.concatenate([zero, face_rows] if upper else [face_rows, zero], axis=0)

    def near(value, next_value):
        got = mul_r(hc[r, r], value) + (potc - CENTER) * value
        add = mul_r(hn[g, :], next_value)
        if upper:
            return jnp.concatenate([got[:fp] + add, got[fp:]], axis=0)
        return jnp.concatenate([got[: stride - fp], got[stride - fp :] + add], axis=0)

    two = gain * near(one, pad_next(one[s]))
    out.append(mul_r(hc[f, r], two))
    two_next = gain * mul_r(hn, pad_next(one[s]))
    if upper:
        two_next = jnp.concatenate([two_next[:stride], two[s]], axis=0)
    else:
        two_next = jnp.concatenate([two[s], two_next[fp:]], axis=0)
    three = gain * near(two, two_next) - one
    out.append(mul_r(hc[f, r], three))
    return out


def store_matrices(mats, out_ref, at, fp, width):
    for j, m in enumerate(mats):
        block, lane = divmod(j * fp, width)
        out_ref[at + block, :, lane : lane + fp] = m.astype(out_ref.dtype)


def load_matrices(ref, at, count, fp, width):
    spots = [divmod(j * fp, width) for j in range(count)]
    return [ref[at + block, :, lane : lane + fp].astype(F32) for block, lane in spots]


def free_kernel(
    fp, ip, conn_ref, face_ref, hraw_ref, raw_ref, potraw_ref, ghost_ref,
    h_hbm, v_ref, pot_hbm, node_ref, first_hbm, own_ref, up_ref, down_ref,
    h_ref, pot_ref, first_ref, a_ref, b_ref, hin_ref, sem, sems,
):
    copy = pltpu.make_async_copy(hraw_ref, hin_ref, sem)
    copy.start()
    order(fp, ip, copy.wait, conn_ref, face_ref, hin_ref, raw_ref, potraw_ref, h_ref, v_ref, pot_ref, node_ref)
    leaving = [
        pltpu.make_async_copy(src, dst, sems.at[i])
        for i, (src, dst) in enumerate(((h_ref, h_hbm), (pot_ref, pot_hbm), (first_ref, first_hbm)))
    ]
    leaving[0].start()
    leaving[1].start()
    cells, cp = h_ref.shape[:2]
    stride = cp - fp
    total = cells * stride
    width = v_ref.shape[1]
    a_ref[:total] = v_ref[...]
    a_ref[total:] = ghost_ref[:fp]
    b_ref[total:] = jnp.zeros((fp, width), BF16)

    def keep(k, low, high):
        own_ref[0, k] = low
        own_ref[1, k] = high
        if k < DEGREE:
            down_ref[k] = low.astype(BF16)
        up_ref[k] = high.astype(BF16)

    now_ref, other_ref = a_ref, b_ref
    for k in range(DEGREE):
        ends = {}

        def emit(c, rows, lower, carry, k=k, now_ref=now_ref, other_ref=other_ref, ends=ends):
            at = slice(c * stride, (c + 1) * stride)
            if c == 0:
                ends["low"] = rows[:fp]
            now = now_ref[at].astype(F32)
            before = None if k == 0 else other_ref[at].astype(F32)
            if k == 1:
                before = v_ref[at].astype(F32)
            value = advance(rows + spread(pot_ref[at], now.shape[1]) * now, now, before).astype(BF16)
            if c == 0:
                value = jnp.concatenate([jnp.zeros((fp, width), BF16), value[fp:]], axis=0)
            if k == 0:
                first_ref[at] = value
            other_ref[at] = value

        high = sweep(h_ref, now_ref, fp, emit)
        keep(k, ends["low"], high)
        if k == 0:
            leaving[2].start()
            a_ref[total:] = jnp.zeros((fp, width), BF16)
        now_ref, other_ref = other_ref, now_ref
    keep(DEGREE, mul(h_ref[0, :fp], now_ref[:cp]), mul(h_ref[cells - 1, stride:], now_ref[total - stride :]))
    low = response(h_ref[0], h_ref[1], pot_ref[fp:cp], fp, False)
    high = response(h_ref[cells - 1], h_ref[cells - 2], pot_ref[total - stride :], fp, True)
    store_matrices(low, down_ref, DEGREE, fp, width)
    store_matrices(high, up_ref, DEGREE + 1, fp, width)
    for side, mats in enumerate((low, high)):
        store_matrices(mats, own_ref.at[side], DEGREE + 1, fp, width)
    for copy in leaving:
        copy.wait()


def forced_kernel(
    fp, place_ref, v_ref, ghost_ref, first_hbm, own_ref, fromleft_ref, fromright_ref, h_hbm, pot_hbm,
    x_ref, face_image_ref, slab_ref, a_ref, b_ref, c_ref, h_ref, pot_ref, sems,
):
    cells, cp = h_ref.shape[:2]
    stride = cp - fp
    total = cells * stride
    width = v_ref.shape[1]
    rest = pl.ds(fp, total - fp)
    coming = [
        pltpu.make_async_copy(src, dst, sems.at[i])
        for i, (src, dst) in enumerate(
            (
                (pot_hbm.at[pl.ds(0, fp)], pot_ref.at[pl.ds(0, fp)]),
                (first_hbm, a_ref.at[pl.ds(0, total)]),
                (pot_hbm.at[rest], pot_ref.at[rest]),
                (h_hbm, h_ref),
            )
        )
    ]
    for copy in coming:
        copy.start()
    coming[0].wait()
    half = cells // 2
    extra = own_ref.shape[1] - DEGREE - 1
    potg = to_col(jnp.sum(ghost_ref[fp:].astype(F32), axis=0, keepdims=True)[:, :fp], fp)
    nothing = jnp.zeros((fp, width), BF16)
    sides = []
    for side, (got_ref, pot, start) in enumerate(
        ((fromleft_ref, spread(pot_ref[:fp], width), v_ref[:fp]), (fromright_ref, potg, ghost_ref[:fp]))
    ):
        theirs = load_matrices(got_ref, got_ref.shape[0] - extra, DEGREE, fp, width)
        ours = load_matrices(own_ref.at[side], DEGREE + 1, DEGREE, fp, width)
        mats = [a + b for a, b in zip(theirs, ours)]
        line = jnp.concatenate(mats[::-1], axis=1)
        sides.append((got_ref, pot, jnp.concatenate(split(line), axis=0), [start]))
    for k in range(DEGREE + 1):
        for side, (got_ref, pot, line, values) in enumerate(sides):
            if side == 1 and k == DEGREE:
                continue
            h = own_ref[side, k] + got_ref[k].astype(F32)
            if k > 0:
                past = [values[m] if m >= 1 else nothing for m in range(k - DEGREE + 1, k + 1)]
                both = mul(line, jnp.concatenate(past, axis=0))
                h = h + both[:fp] + both[fp:]
            now = values[k].astype(F32)
            h = h + pot * now
            if k == DEGREE:
                face_image_ref[...] = h
                continue
            value = advance(h, now, None if k == 0 else values[k - 1].astype(F32))
            if side == 1:
                value = jnp.where(place_ref[0] == 1, 0.0, value)
            values.append(value.astype(BF16))
    low, high = sides[0][3], sides[1][3]
    for copy in coming[1:]:
        copy.wait()
    a_ref[:fp] = low[1]
    a_ref[total:] = high[1]
    refs = [v_ref, a_ref, b_ref, c_ref, x_ref]
    for k in range(1, DEGREE):
        now_ref = refs[k]

        def emit(c, rows, lower, carry, k=k, now_ref=now_ref):
            at = slice(c * stride, (c + 1) * stride)
            now = now_ref[at].astype(F32)
            value = advance(rows + spread(pot_ref[at], now.shape[1]) * now, now, refs[k - 1][at].astype(F32)).astype(BF16)
            if c == 0:
                value = jnp.concatenate([low[k + 1], value[fp:]], axis=0)
            refs[k + 1][at] = value

        sweep(h_ref, now_ref, fp, emit)
        refs[k + 1][total:] = high[k + 1]

    @pl.when(place_ref[1] == 0)
    def _():
        slab_ref[...] = x_ref[half * stride :]

    @pl.when(place_ref[1] == 1)
    def _():
        slab_ref[...] = x_ref[: half * stride + fp]


def image_kernel(fp, place_ref, x_ref, face_image_ref, h_ref, pot_ref, image_ref, w_ref, first_ref, second_ref):
    cells, cp = h_ref.shape[:2]
    stride = cp - fp
    half = cells // 2

    def emit(c, rows, lower, carry):
        at = slice(c * stride, (c + 1) * stride)
        now = x_ref[at].astype(F32)
        out = (rows + spread(pot_ref[at], now.shape[1]) * now).astype(BF16)
        part, at_w = divmod(c, half)
        w_ref[part, at_w * stride : (at_w + 1) * stride] = out
        if c == half:
            w_ref[0, half * stride :] = carry.astype(BF16)
            w_ref[1, :fp] = (lower + spread(pot_ref[c * stride : c * stride + fp], now.shape[1]) * now[:fp]).astype(BF16)
        if c == 0:
            out = jnp.concatenate([face_image_ref[...].astype(BF16), out[fp:]], axis=0)
        image_ref[at] = out

    w_ref[1, half * stride :] = sweep(h_ref, x_ref, fp, emit).astype(BF16)
    n = first_ref.shape[0]
    first_ref[...] = w_ref[place_ref[1], :n]
    second_ref[...] = w_ref[place_ref[1], n:]


def back_kernel(node_ref, x_ref, image_ref, out_ref):
    rows = out_ref.shape[1]
    width = x_ref.shape[1]
    want = (lax.broadcasted_iota(jnp.int32, (rows, 1), 0) + pl.program_id(0) * rows).astype(F32)
    hit = flat(want == node_ref[...])
    out_ref[0, :, :width] = mul(hit, x_ref[...]).astype(BF16)
    out_ref[0, :, width:] = mul(hit, image_ref[...]).astype(BF16)


def back_pair_kernel(at_ref, node_ref, x_ref, image_ref, *out_refs):
    rows = out_refs[0].shape[0]
    width = x_ref.shape[1]
    for i, out_ref in enumerate(out_refs):
        want = (lax.broadcasted_iota(jnp.int32, (rows, 1), 0) + at_ref[i] * rows).astype(F32)
        hit = flat(want == node_ref[...])
        out_ref[:, :width] = mul(hit, x_ref[...]).astype(BF16)
        out_ref[:, width:] = mul(hit, image_ref[...]).astype(BF16)


def gram_kernel(scale, x_ref, y_ref, out_ref, rows_ref):
    parts, _, width = y_ref.shape

    @pl.when(pl.program_id(0) == 0)
    def _():
        for j in range(parts):
            rows_ref[:, j * width : (j + 1) * width] = y_ref[j]

    out_ref[0] = (
        lax.dot_general(x_ref[0], rows_ref[...], (((0,), (0,)), ((), ())), preferred_element_type=F32) * scale
    )


def residual_kernel(x_ref, y_ref, p_ref, out_ref):
    parts, _, width = x_ref.shape
    x = jnp.concatenate([x_ref[j] for j in range(parts)], axis=1)
    y = jnp.concatenate([y_ref[j] for j in range(parts)], axis=1)
    out_ref[...] = y.astype(F32) - jnp.dot(x, p_ref[...], preferred_element_type=F32)


def full(shape):
    return pl.BlockSpec(shape, lambda i: (0,) * len(shape))


def swap(block, axis, bit):
    return lax.ppermute(block, axis, [(i, i ^ bit) for i in range(lax.axis_size(axis))])


def shift(block, axis, distance):
    n = lax.axis_size(axis)
    return lax.ppermute(block, axis, [(i, i + distance) for i in range(n) if 0 <= i + distance < n])


def tmul(a, b):
    return lax.dot_general(a, b, (((0,), (0,)), ((), ())), preferred_element_type=F32)


def near_gram_kernel(scale, core_ref, x_ref, w_ref, other_ref, out_ref):
    slab, width = w_ref.shape[1:]
    at = (slice(0, slab), slice(x_ref.shape[0] - slab, x_ref.shape[0]))
    own = [x_ref[a] for a in at]
    out_ref[:width] = (tmul(own[0], w_ref[0]) + tmul(own[1], w_ref[1])) * scale
    half = width // 2

    @pl.when(core_ref[0] == 0)
    def _():
        out_ref[width:] = sum(tmul(w_ref[i, :, :half], other_ref[at[i]]) for i in range(2)) * scale

    @pl.when(core_ref[0] == 1)
    def _():
        out_ref[width:] = sum(tmul(other_ref[at[i], half:], w_ref[i]) for i in range(2)) * scale


def part_ways(sum_ref, mine, keep_ref, give_refs):
    n = keep_ref.shape[0]
    keep_ref[...] = sum_ref[pl.ds(pl.multiple_of(mine * n, 16), n)]
    for j, give_ref in enumerate(give_refs):
        give_ref[...] = sum_ref[pl.ds(pl.multiple_of(jnp.bitwise_xor(mine, j + 1) * n, 16), n)].astype(BF16)


def reduce_kernel(step, ways, bits_ref, keep_ref, *refs):
    total = keep_ref[...]
    for got_ref in refs[: ways - 1]:
        total = total + got_ref[...].astype(F32)
    refs = refs[ways - 1 :]
    if len(refs) == 1:
        refs[0][...] = total.astype(BF16)
        return
    keep_out, *gives, sum_ref = refs
    sum_ref[...] = total
    part_ways(sum_ref, bits_ref[step], keep_out, gives)


def join_kernel(step, bits_ref, own_ref, *refs):
    *got_refs, out_ref = refs
    n = own_ref.shape[0]
    mine = bits_ref[step]
    for j, ref in enumerate([own_ref] + got_refs):
        out_ref[pl.ds(pl.multiple_of(jnp.bitwise_xor(mine, j) * n, 16), n)] = ref[...]


def far_gram_kernel(scale, bits_ref, place_ref, w_ref, first_ref, second_ref, far_ref, near_ref, keep_ref, *refs):
    *give_refs, out_ref = refs
    width = w_ref.shape[2]
    near = near_ref.shape[0]
    side, core = place_ref[0], place_ref[1]
    out_ref[:near] = near_ref[...]
    far = far_ref[...]
    mine = pl.multiple_of(near + core * width, width // 2)
    other = pl.multiple_of(near + (1 - core) * width, width // 2)
    out_ref[pl.ds(mine, width)] = tmul(w_ref[side], far) * scale
    n = first_ref.shape[0]
    out_ref[pl.ds(other, width)] = (tmul(first_ref[...], far[:n]) + tmul(second_ref[...], far[n:])) * scale
    part_ways(out_ref, bits_ref[0], keep_ref, give_refs)


def paired_residual_kernel(place_ref, *refs):
    q_refs, refs = refs[:8], refs[8:]
    parts = 4
    row_refs, (out_hbm, p_hbm, out_ref, p_ref, q_ref, sems) = refs[:parts], refs[parts:]
    width = row_refs[0].shape[1] // 2
    half = width // 2
    me, mine = place_ref[0], place_ref[1]
    n = q_refs[0].shape[0]
    for k in range(parts):
        for j in range(2):
            q_ref[k, pl.ds(pl.multiple_of(jnp.bitwise_xor(mine, j) * n, 16), n)] = q_refs[2 * k + j][...]
    eye = (lax.broadcasted_iota(jnp.int32, (width, width), 0) == lax.broadcasted_iota(jnp.int32, (width, width), 1)).astype(
        F32
    ).astype(BF16)

    def turned(a):
        return lax.dot_general(eye, a, (((1,), (1,)), ((), ())), preferred_element_type=F32)

    def piece(i, lo, hi):
        return q_ref[jnp.bitwise_xor(me, i), lo:hi]

    def put(i, j, value):
        p_ref[i * width : (i + 1) * width, j * width : (j + 1) * width] = value

    near = width + half
    for i in range(parts):
        put(i, i, piece(i, 0, width))
    for i in range(0, parts, 2):
        block = jnp.concatenate([piece(i, width, near), piece(i + 1, width, near)], axis=0)
        put(i, i + 1, block)
        put(i + 1, i, turned(block).astype(BF16))
    for i in (0, 1):
        for j in (2, 3):
            one = piece(j ^ 2, near + i * width, near + (i + 1) * width)
            two = piece(i ^ 2, near + (j - 2) * width, near + (j - 1) * width)
            block = (one.astype(F32) + turned(two)).astype(BF16)
            put(i, j, block)
            put(j, i, turned(block).astype(BF16))
    copies = [pltpu.make_async_copy(p_ref, p_hbm, sems.at[parts])]
    copies[0].start()
    x = jnp.concatenate([ref[:, :width] for ref in row_refs], axis=1)
    spots = [pl.ds(pl.multiple_of(jnp.bitwise_xor(me, k) * width, width), width) for k in range(parts)]
    for k in range(parts):
        at = spots[k]
        p = jnp.concatenate([p_ref[spots[m], at] for m in range(parts)], axis=0)
        out_ref[k] = row_refs[k][:, width:].astype(F32) - mul(x, p)
        copies.append(pltpu.make_async_copy(out_ref.at[k], out_hbm.at[:, at], sems.at[k]))
        copies[-1].start()
    for copy in copies:
        copy.wait()


def paired_tail(x_own, image, w_own, w_side, give, node_row, o, d, dom, nodes):
    slab, width = w_own.shape[1:]
    orb = 4
    rows = nodes // orb
    side, core = o // 2, o % 2
    scale = 1.0 / (nodes * dom)
    sds = jax.ShapeDtypeStruct
    smem = pl.BlockSpec(memory_space=pltpu.SMEM)
    vmem = pl.BlockSpec(memory_space=pltpu.VMEM)
    far = swap(give, "orb", 2)
    total = image.shape[0]

    def back(first, second, x_own, image):
        whole = lambda *shape: pl.BlockSpec(shape, lambda i: (0,) * len(shape))
        return pl.pallas_call(
            back_pair_kernel,
            grid=(1,),
            in_specs=[smem, whole(1, total), whole(total, width), whole(total, width)],
            out_specs=[whole(rows, 2 * width)] * 2,
            out_shape=[sds((rows, 2 * width), BF16)] * 2,
            compiler_params=params(),
            cost_estimate=pl.CostEstimate(flops=1 << 20, bytes_accessed=1 << 10, transcendentals=0),
        )(jnp.stack([jnp.bitwise_xor(o, first), jnp.bitwise_xor(o, second)]), node_row, x_own, image)

    cuts = back(2, 3, x_own, image)
    x_other = swap(x_own, "orb", 1)
    w_other = [swap(w, "orb", 1) for w in w_side]
    top = width + width // 2
    near = pl.pallas_call(
        functools.partial(near_gram_kernel, scale),
        in_specs=[smem] + [vmem] * 3,
        out_shape=sds((top, width), F32),
        compiler_params=params(),
        cost_estimate=pl.CostEstimate(flops=1 << 20, bytes_accessed=1 << 10, transcendentals=0),
    )(core.reshape(1), x_own, w_own, x_other)
    far, near, *cuts, w_other[0], w_other[1] = lax.optimization_barrier((far, near, *cuts, *w_other))
    row2, row3 = swap(cuts[0], "orb", 2), swap(cuts[1], "orb", 3)
    groups, base = [], 1
    while base < dom:
        ways = 2 if base == 1 or base * 4 > dom else 4
        groups.append((base, ways))
        base *= ways
    bits = jnp.stack([(d // base) % ways for base, ways in groups])
    little = pl.CostEstimate(flops=1 << 10, bytes_accessed=1 << 10, transcendentals=0)
    count = top + 2 * width

    def parts_of(n, ways):
        return [sds((n // ways, width), F32)] + [sds((n // ways, width), BF16)] * (ways - 1)

    keep, *gives = pl.pallas_call(
        functools.partial(far_gram_kernel, scale),
        in_specs=[smem] * 2 + [vmem] * 5,
        out_shape=parts_of(count, 2),
        scratch_shapes=[pltpu.VMEM((count, width), F32)],
        compiler_params=params(),
        cost_estimate=pl.CostEstimate(flops=8 * slab * width * width, bytes_accessed=4 << 20, transcendentals=0),
    )(bits, jnp.stack([side, core]), w_own, *w_other, far, near)
    row0 = cut1 = None
    for i, (base, ways) in enumerate(groups):
        if i == 0:
            x_own, image, gives[0] = lax.optimization_barrier((x_own, image, gives[0]))
            row0, cut1 = back(0, 1, x_own, image)
        gots = [swap(give, "dom", base * (j + 1)) for j, give in enumerate(gives)]
        n = keep.shape[0]
        last = i == len(groups) - 1
        outs = pl.pallas_call(
            functools.partial(reduce_kernel, i + 1, ways),
            in_specs=[smem] + [vmem] * ways,
            out_shape=[sds((n, width), BF16)] if last else parts_of(n, groups[i + 1][1]),
            scratch_shapes=[] if last else [pltpu.VMEM((n, width), F32)],
            compiler_params=params(),
            cost_estimate=little,
        )(bits, keep, *gots)
        outs = list(outs)
        if i == 0:
            outs[-1], row0, cut1 = lax.optimization_barrier((outs[-1], row0, cut1))
        if last:
            outs[-1], row2 = lax.optimization_barrier((outs[-1], row2))
            share = outs[0]
        else:
            keep, *gives = outs
    for i in reversed(range(1, len(groups))):
        base, ways = groups[i]
        gots = [swap(share, "dom", base * j) for j in range(1, ways)]
        share = pl.pallas_call(
            functools.partial(join_kernel, i),
            in_specs=[smem] + [vmem] * ways,
            out_shape=sds((ways * share.shape[0], width), BF16),
            compiler_params=params(),
            cost_estimate=little,
        )(bits, share, *gots)
    row1 = swap(cut1, "orb", 1)
    got = swap(share, "dom", 1)
    got, row3 = lax.optimization_barrier((got, row3))
    q2 = [swap(share, "orb", 2), swap(got, "orb", 2)]
    q1 = [swap(share, "orb", 1), swap(got, "orb", 1)]
    q3a = swap(q2[0], "orb", 1)
    q2[1], row1 = lax.optimization_barrier((q2[1], row1))
    q3 = [q3a, swap(q2[1], "orb", 1)]
    cols = orb * width
    return pl.pallas_call(
        paired_residual_kernel,
        in_specs=[smem] + [vmem] * 12,
        out_shape=(sds((rows, cols), F32), sds((cols, cols), BF16)),
        out_specs=[pl.BlockSpec(memory_space=pl.ANY)] * 2,
        scratch_shapes=[
            pltpu.VMEM((orb, rows, width), F32),
            pltpu.VMEM((cols, cols), BF16),
            pltpu.VMEM((orb, count, width), BF16),
            pltpu.SemaphoreType.DMA((orb + 1,)),
        ],
        compiler_params=params(),
    )(jnp.stack([o, d % 2]), share, got, *q1, *q2, *q3, row0, row1, row2, row3)


def body(orbitals, potential, cell_hamiltonian, connectivity, face_nodes):
    nodes, width = orbitals.shape
    cells, npc = connectivity.shape
    face = face_nodes.shape[0]
    fp, ip = up16(face), up16(npc - 2 * face)
    fp = (fp + 63) // 64 * 64
    stride = fp + ip
    cp = stride + fp
    total = cells * stride
    orb, dom = lax.axis_size("orb"), lax.axis_size("dom")
    d = lax.axis_index("dom")
    o = lax.axis_index("orb")
    sds = jax.ShapeDtypeStruct
    pot_row = potential.reshape(1, nodes)
    face_row = face_nodes.reshape(1, face)

    face_values = pl.pallas_call(
        face_kernel, out_shape=sds((fp + 16, width), BF16), compiler_params=params()
    )(face_row, orbitals, pot_row)
    ghost = shift(face_values, "dom", -1)

    extra = -(-DEGREE * fp // width)
    ext = pltpu.VMEM((total + fp, width), BF16)
    cost = pl.CostEstimate(
        flops=2 * DEGREE * cells * cp * cp * width, bytes_accessed=8 << 20, transcendentals=0
    )
    vmem, hbm = pl.BlockSpec(memory_space=pltpu.VMEM), pl.BlockSpec(memory_space=pl.ANY)
    hcan, y, pot, node, first, own, up, down = pl.pallas_call(
        functools.partial(free_kernel, fp, ip),
        in_specs=[vmem] * 2 + [pl.BlockSpec(memory_space=pl.ANY)] + [vmem] * 3,
        out_shape=[
            sds((cells, cp, cp), BF16),
            sds((total, width), BF16),
            sds((total, LANES), F32),
            sds((cells, 1, stride), F32),
            sds((total, width), BF16),
            sds((2, DEGREE + 1 + extra, fp, width), F32),
            sds((DEGREE + 1 + extra, fp, width), BF16),
            sds((DEGREE + extra, fp, width), BF16),
        ],
        out_specs=[hbm, vmem, hbm, vmem, hbm, vmem, vmem, vmem],
        scratch_shapes=[
            pltpu.VMEM((cells, cp, cp), BF16),
            pltpu.VMEM((total, LANES), F32),
            pltpu.VMEM((total, width), BF16),
            ext,
            ext,
            pltpu.VMEM((cells, npc, npc), BF16),
            pltpu.SemaphoreType.DMA,
            pltpu.SemaphoreType.DMA((3,)),
        ],
        compiler_params=params(),
        cost_estimate=cost,
    )(connectivity, face_row, cell_hamiltonian, orbitals, pot_row, ghost)
    node_row = node.reshape(1, total)
    from_left = shift(up, "dom", 1)
    from_right = shift(down, "dom", -1)
    slab = cells // 2 * stride + fp
    place = jnp.stack([(d == dom - 1).astype(jnp.int32), (o // 2) % 2])
    x_own, face_image, give = pl.pallas_call(
        functools.partial(forced_kernel, fp),
        in_specs=[pl.BlockSpec(memory_space=pltpu.SMEM), vmem, vmem, hbm, vmem, vmem, vmem, hbm, hbm],
        out_shape=[
            sds((total + fp, width), BF16),
            sds((fp, width), F32),
            sds((slab, width), BF16),
        ],
        scratch_shapes=[
            ext,
            ext,
            ext,
            pltpu.VMEM((cells, cp, cp), BF16),
            pltpu.VMEM((total, LANES), F32),
            pltpu.SemaphoreType.DMA((4,)),
        ],
        compiler_params=params(),
        cost_estimate=cost,
    )(place, y, ghost, first, own, from_left, from_right, hcan, pot)
    image, w_own, *w_side = pl.pallas_call(
        functools.partial(image_kernel, fp),
        in_specs=[pl.BlockSpec(memory_space=pltpu.SMEM)] + [vmem] * 4,
        out_shape=[sds((total, width), BF16), sds((2, slab, width), BF16)] + [sds((slab // 2, width), BF16)] * 2,
        compiler_params=params(),
        cost_estimate=pl.CostEstimate(flops=1 << 20, bytes_accessed=1 << 10, transcendentals=0),
    )(place, x_own, face_image, hcan, pot)

    if orb == 4 and dom % 8 == 0:
        return paired_tail(x_own, image, w_own, w_side, give, node_row, o, d, dom, nodes)
    cut = pl.pallas_call(
        back_kernel,
        grid=(orb,),
        in_specs=[full((1, total)), full((total, width)), full((total, width))],
        out_specs=pl.BlockSpec((1, nodes // orb, 2 * width), lambda i: (i, 0, 0)),
        out_shape=sds((orb, nodes // orb, 2 * width), BF16),
        compiler_params=params(),
        cost_estimate=pl.CostEstimate(flops=4 * total * nodes * width, bytes_accessed=4 << 20, transcendentals=0),
    )(node_row, x_own, image)
    both = lax.all_to_all(cut, "orb", split_axis=0, concat_axis=0, tiled=True)
    x_rows, i_rows = both[:, :, :width], both[:, :, width:]

    rows = nodes // orb
    cols = orb * width
    share = pl.pallas_call(
        functools.partial(gram_kernel, 1.0 / (nodes * dom)),
        grid=(orb,),
        in_specs=[pl.BlockSpec((1, rows, width), lambda i: (i, 0, 0)), full((orb, rows, width))],
        out_specs=pl.BlockSpec((1, width, cols), lambda i: (i, 0, 0)),
        out_shape=sds((orb, width, cols), F32),
        scratch_shapes=[pltpu.VMEM((rows, cols), BF16)],
        compiler_params=params(),
    )(x_rows, i_rows)

    hops = []
    for axis, me, size in (("orb", o, orb), ("dom", d, dom)):
        if axis == "dom":
            share = share.reshape(dom, width // dom, cols)
        bit = 1
        while bit < size:
            share = share.reshape((share.shape[0] // 2, 2) + share.shape[1:])
            mine = (me // bit) % 2
            keep = lax.dynamic_index_in_dim(share, mine, 1, keepdims=False)
            give = lax.dynamic_index_in_dim(share, 1 - mine, 1, keepdims=False)
            got = swap(give.astype(BF16), axis, bit)
            share = keep + got.astype(F32)
            hops.append((axis, bit, mine))
            bit *= 2
    share = share.astype(BF16)
    for axis, bit, mine in reversed(hops):
        if axis == "orb" and share.shape[0] == dom and bit * 2 == orb:
            share = share.reshape(1, width, cols)
        got = swap(share, axis, bit)
        share = jnp.where(mine == 0, jnp.stack([share, got], axis=1), jnp.stack([got, share], axis=1))
        share = share.reshape((share.shape[0] * 2,) + share.shape[2:])
    projected = share.reshape(cols, cols)

    residual = pl.pallas_call(
        residual_kernel, out_shape=sds((rows, cols), F32), compiler_params=params()
    )(x_rows, i_rows, projected)
    return (residual, projected)


def solution(mesh):
    return jax.shard_map(
        body,
        mesh=mesh,
        in_specs=(P("dom", "orb"), P("dom"), P("dom", None, None), P("dom", None), P("dom")),
        out_specs=(P(("dom", "orb"), None), P()),
        check_vma=False,
    )
```

```python
import functools

import jax
import jax.numpy as jnp
from jax import lax
from jax.experimental import pallas as pl
from jax.experimental.pallas import tpu as pltpu
from jax.sharding import PartitionSpec as P

DEGREE = 4
CENTER = 1.5
HALF = 2.0
F32 = jnp.float32
BF16 = jnp.bfloat16
LANES = 128
VMEM_LIMIT = 50 * 1024 * 1024


def up16(n):
    return (n + 15) // 16 * 16


def iota(shape, dim):
    return lax.broadcasted_iota(jnp.int32, shape, dim).astype(F32)


def to_col(row, rows):
    n = row.shape[1]
    return jnp.sum(jnp.where(iota((rows, n), 0) == iota((rows, n), 1), row, 0.0), axis=1, keepdims=True)


def to_row(col):
    n = col.shape[0]
    return jnp.sum(jnp.where(iota((n, n), 0) == iota((n, n), 1), col, 0.0), axis=0, keepdims=True)


def params():
    return pltpu.CompilerParams(vmem_limit_bytes=VMEM_LIMIT)


def thirds(a):
    one = a.astype(BF16)
    rest = a - one.astype(F32)
    two = rest.astype(BF16)
    return one, two, (rest - two.astype(F32)).astype(BF16)


def face_kernel(face_ref, x_ref, pot_ref, out_ref):
    width = x_ref.shape[1]
    fp = out_ref.shape[0] - 16
    nodes = x_ref.shape[0]
    col = to_col(face_ref[...].astype(F32) + 1.0, fp) - 1.0
    hit = jnp.where(col == iota((fp, nodes), 1), 1.0, 0.0).astype(BF16)
    out_ref[:fp] = mul(hit, x_ref[...]).astype(BF16)
    ri = lax.broadcasted_iota(jnp.int32, (16, nodes), 0)
    parts = [p.astype(F32) for p in thirds(pot_ref[...])]
    rows = jnp.where(ri == 0, parts[0], jnp.where(ri == 1, parts[1], jnp.where(ri == 2, parts[2], 0.0))).astype(BF16)
    got = lax.dot_general(rows, hit, (((1,), (1,)), ((), ())), preferred_element_type=F32).astype(BF16)
    if width > fp:
        got = jnp.concatenate([got, jnp.zeros((16, width - fp), BF16)], axis=1)
    out_ref[fp:] = got


def turn(a, b):
    return lax.dot_general(a, b, (((1,), (1,)), ((), ())), preferred_element_type=F32)


def halves(a):
    high = jnp.floor(a * (1.0 / 64.0))
    return high.astype(BF16), (a - 64.0 * high).astype(BF16)


def flat(mask):
    return jnp.where(mask, 1.0, 0.0).astype(BF16)


def order(fp, ip, arrived, conn_ref, face_ref, h_ref, x_ref, pot_ref, hcan_ref, v_ref, potc_ref, node_ref):
    cells, npc = conn_ref.shape
    nodes = x_ref.shape[0]
    face = face_ref.shape[1]
    stride = fp + ip
    cp = stride + fp
    conn = conn_ref[...].astype(F32)
    eye = flat(iota((npc, npc), 0) == iota((npc, npc), 1))
    below = flat(iota((npc, npc), 0) < iota((npc, npc), 1))
    high, low = halves(conn)
    cols = 64.0 * turn(eye, high) + turn(eye, low)
    rows = [conn[c : c + 1] for c in range(cells)]
    ones = jnp.ones((cells, npc), BF16)
    same = [flat(cols[:, c : c + 1] == rows[c + 1]) for c in range(cells - 1)]
    ri = lax.broadcasted_iota(jnp.int32, (cells, npc), 0)
    top = jnp.where(conn >= float(nodes), 1.0, 0.0)
    for c in range(cells - 1):
        top = jnp.where(ri == c, turn(ones, same[c]), top)
    rank_top = mul(top.astype(BF16), below)
    rank_b = rank_top.astype(BF16)
    top_slot = jnp.where(ri == cells - 1, conn - float(nodes), rank_top)
    fhit = to_col(face_ref[...].astype(F32), face) == rows[0]
    bot = jnp.where(ri == 0, jnp.max(jnp.where(fhit, 1.0, 0.0), axis=0, keepdims=True), 0.0)
    bot_slot = jnp.where(ri == 0, jnp.sum(jnp.where(fhit, iota((face, npc), 0), 0.0), axis=0, keepdims=True), 0.0)
    for c in range(cells - 1):
        both = jnp.concatenate([ones, rank_b], axis=0)
        got = mul(both, same[c])
        bot = jnp.where(ri == c + 1, got[:1], bot)
        bot_slot = jnp.where(ri == c + 1, got[cells + c : cells + c + 1], bot_slot)
    mid_rank = mul((1.0 - top - bot).astype(BF16), below)
    slot = jnp.where(top > 0.5, top_slot + float(stride), jnp.where(bot > 0.5, bot_slot, mid_rank + float(fp)))
    high, low = halves(conn + 1.0)
    number = iota((8, nodes), 1)[:1]
    arrived()
    for c in range(cells):
        perm = flat(iota((cp, npc), 0) == slot[c : c + 1])
        half = mul(perm, h_ref[c]).astype(BF16)
        hcan_ref[c] = turn(half, perm).astype(BF16)
        lead = perm[:stride]
        node = 64.0 * turn(lead, high)[:, c : c + 1] + turn(lead, low)[:, c : c + 1] - 1.0
        node_ref[c] = 64.0 * turn(high, lead)[c : c + 1] + turn(low, lead)[c : c + 1] - 1.0
        at = slice(c * stride, (c + 1) * stride)
        hit = node == number
        v_ref[at] = mul(flat(hit), x_ref[...]).astype(BF16)
        column = jnp.sum(jnp.where(hit, pot_ref[...], 0.0), axis=1, keepdims=True)
        potc_ref[at] = jnp.broadcast_to(column, (stride, LANES))


def spread(column, width):
    if width <= LANES:
        return column[:, :width]
    return jnp.concatenate([column] * (width // LANES), axis=1)


def advance(image, now, before):
    if before is None:
        return (image - CENTER * now) / HALF
    return 2.0 * (image - CENTER * now) / HALF - before


def split(a):
    high = a.astype(BF16)
    return high, (a - high.astype(F32)).astype(BF16)


def mul(a, b):
    return jnp.dot(a, b, preferred_element_type=F32)


def mul_r(a, b):
    return mul(a, b.astype(BF16))


def sweep(h_ref, y_ref, fp, emit):
    cells, cp = h_ref.shape[:2]
    stride = cp - fp
    carry = None
    for c in range(cells):
        prod = mul(h_ref[c], y_ref[c * stride : c * stride + cp])
        rows = prod[:stride]
        if c > 0:
            rows = jnp.concatenate([rows[:fp] + carry, rows[fp:]], axis=0)
        emit(c, rows, prod[:fp], carry)
        carry = prod[stride:]
    return carry


def response(hc, hn, potc, fp, upper):
    cp = hc.shape[0]
    stride = cp - fp
    if upper:
        f, r, s, g = slice(stride, cp), slice(0, stride), slice(0, fp), slice(stride, cp)
        rest = slice(0, stride)
    else:
        f, r, s, g = slice(0, fp), slice(fp, cp), slice(stride - fp, stride), slice(0, fp)
        rest = slice(fp, cp)
    potc = spread(potc, fp)
    gain = 2.0 / HALF
    out = [hc[f, f].astype(F32)]
    one = gain * hc[r, f].astype(F32)
    out.append(mul_r(hc[f, r], one))

    def pad_next(face_rows):
        zero = jnp.zeros((stride, fp), F32)
        return jnp.concatenate([zero, face_rows] if upper else [face_rows, zero], axis=0)

    def near(value, next_value):
        got = mul_r(hc[r, r], value) + (potc - CENTER) * value
        add = mul_r(hn[g, :], next_value)
        if upper:
            return jnp.concatenate([got[:fp] + add, got[fp:]], axis=0)
        return jnp.concatenate([got[: stride - fp], got[stride - fp :] + add], axis=0)

    two = gain * near(one, pad_next(one[s]))
    out.append(mul_r(hc[f, r], two))
    two_next = gain * mul_r(hn, pad_next(one[s]))
    if upper:
        two_next = jnp.concatenate([two_next[:stride], two[s]], axis=0)
    else:
        two_next = jnp.concatenate([two[s], two_next[fp:]], axis=0)
    three = gain * near(two, two_next) - one
    out.append(mul_r(hc[f, r], three))
    return out


def store_matrices(mats, out_ref, at, fp, width):
    for j, m in enumerate(mats):
        block, lane = divmod(j * fp, width)
        out_ref[at + block, :, lane : lane + fp] = m.astype(out_ref.dtype)


def load_matrices(ref, at, count, fp, width):
    spots = [divmod(j * fp, width) for j in range(count)]
    return [ref[at + block, :, lane : lane + fp].astype(F32) for block, lane in spots]


def free_kernel(
    fp, ip, conn_ref, face_ref, hraw_ref, raw_ref, potraw_ref, ghost_ref,
    h_hbm, v_ref, pot_hbm, node_ref, first_hbm, own_ref, up_ref, down_ref,
    h_ref, pot_ref, first_ref, a_ref, b_ref, hin_ref, sem, sems,
):
    copy = pltpu.make_async_copy(hraw_ref, hin_ref, sem)
    copy.start()
    order(fp, ip, copy.wait, conn_ref, face_ref, hin_ref, raw_ref, potraw_ref, h_ref, v_ref, pot_ref, node_ref)
    leaving = [
        pltpu.make_async_copy(src, dst, sems.at[i])
        for i, (src, dst) in enumerate(((h_ref, h_hbm), (pot_ref, pot_hbm), (first_ref, first_hbm)))
    ]
    leaving[0].start()
    leaving[1].start()
    cells, cp = h_ref.shape[:2]
    stride = cp - fp
    total = cells * stride
    width = v_ref.shape[1]
    a_ref[:total] = v_ref[...]
    a_ref[total:] = ghost_ref[:fp]
    b_ref[total:] = jnp.zeros((fp, width), BF16)

    def keep(k, low, high):
        own_ref[0, k] = low
        own_ref[1, k] = high
        if k < DEGREE:
            down_ref[k] = low.astype(BF16)
        up_ref[k] = high.astype(BF16)

    now_ref, other_ref = a_ref, b_ref
    for k in range(DEGREE):
        ends = {}

        def emit(c, rows, lower, carry, k=k, now_ref=now_ref, other_ref=other_ref, ends=ends):
            at = slice(c * stride, (c + 1) * stride)
            if c == 0:
                ends["low"] = rows[:fp]
            now = now_ref[at].astype(F32)
            before = None if k == 0 else other_ref[at].astype(F32)
            if k == 1:
                before = v_ref[at].astype(F32)
            value = advance(rows + spread(pot_ref[at], now.shape[1]) * now, now, before).astype(BF16)
            if c == 0:
                value = jnp.concatenate([jnp.zeros((fp, width), BF16), value[fp:]], axis=0)
            if k == 0:
                first_ref[at] = value
            other_ref[at] = value

        high = sweep(h_ref, now_ref, fp, emit)
        keep(k, ends["low"], high)
        if k == 0:
            leaving[2].start()
            a_ref[total:] = jnp.zeros((fp, width), BF16)
        now_ref, other_ref = other_ref, now_ref
    keep(DEGREE, mul(h_ref[0, :fp], now_ref[:cp]), mul(h_ref[cells - 1, stride:], now_ref[total - stride :]))
    low = response(h_ref[0], h_ref[1], pot_ref[fp:cp], fp, False)
    high = response(h_ref[cells - 1], h_ref[cells - 2], pot_ref[total - stride :], fp, True)
    store_matrices(low, down_ref, DEGREE, fp, width)
    store_matrices(high, up_ref, DEGREE + 1, fp, width)
    for side, mats in enumerate((low, high)):
        store_matrices(mats, own_ref.at[side], DEGREE + 1, fp, width)
    for copy in leaving:
        copy.wait()


def forced_kernel(
    fp, place_ref, v_ref, ghost_ref, first_hbm, own_ref, fromleft_ref, fromright_ref, h_hbm, pot_hbm,
    x_ref, face_image_ref, slab_ref, a_ref, b_ref, c_ref, h_ref, pot_ref, sems,
):
    cells, cp = h_ref.shape[:2]
    stride = cp - fp
    total = cells * stride
    width = v_ref.shape[1]
    rest = pl.ds(fp, total - fp)
    coming = [
        pltpu.make_async_copy(src, dst, sems.at[i])
        for i, (src, dst) in enumerate(
            (
                (pot_hbm.at[pl.ds(0, fp)], pot_ref.at[pl.ds(0, fp)]),
                (first_hbm, a_ref.at[pl.ds(0, total)]),
                (pot_hbm.at[rest], pot_ref.at[rest]),
                (h_hbm, h_ref),
            )
        )
    ]
    for copy in coming:
        copy.start()
    coming[0].wait()
    half = cells // 2
    extra = own_ref.shape[1] - DEGREE - 1
    potg = to_col(jnp.sum(ghost_ref[fp:].astype(F32), axis=0, keepdims=True)[:, :fp], fp)
    nothing = jnp.zeros((fp, width), BF16)
    sides = []
    for side, (got_ref, pot, start) in enumerate(
        ((fromleft_ref, spread(pot_ref[:fp], width), v_ref[:fp]), (fromright_ref, potg, ghost_ref[:fp]))
    ):
        theirs = load_matrices(got_ref, got_ref.shape[0] - extra, DEGREE, fp, width)
        ours = load_matrices(own_ref.at[side], DEGREE + 1, DEGREE, fp, width)
        mats = [a + b for a, b in zip(theirs, ours)]
        line = jnp.concatenate(mats[::-1], axis=1)
        sides.append((got_ref, pot, jnp.concatenate(split(line), axis=0), [start]))
    for k in range(DEGREE + 1):
        for side, (got_ref, pot, line, values) in enumerate(sides):
            if side == 1 and k == DEGREE:
                continue
            h = own_ref[side, k] + got_ref[k].astype(F32)
            if k > 0:
                past = [values[m] if m >= 1 else nothing for m in range(k - DEGREE + 1, k + 1)]
                both = mul(line, jnp.concatenate(past, axis=0))
                h = h + both[:fp] + both[fp:]
            now = values[k].astype(F32)
            h = h + pot * now
            if k == DEGREE:
                face_image_ref[...] = h
                continue
            value = advance(h, now, None if k == 0 else values[k - 1].astype(F32))
            if side == 1:
                value = jnp.where(place_ref[0] == 1, 0.0, value)
            values.append(value.astype(BF16))
    low, high = sides[0][3], sides[1][3]
    for copy in coming[1:]:
        copy.wait()
    a_ref[:fp] = low[1]
    a_ref[total:] = high[1]
    refs = [v_ref, a_ref, b_ref, c_ref, x_ref]
    for k in range(1, DEGREE):
        now_ref = refs[k]

        def emit(c, rows, lower, carry, k=k, now_ref=now_ref):
            at = slice(c * stride, (c + 1) * stride)
            now = now_ref[at].astype(F32)
            value = advance(rows + spread(pot_ref[at], now.shape[1]) * now, now, refs[k - 1][at].astype(F32)).astype(BF16)
            if c == 0:
                value = jnp.concatenate([low[k + 1], value[fp:]], axis=0)
            refs[k + 1][at] = value

        sweep(h_ref, now_ref, fp, emit)
        refs[k + 1][total:] = high[k + 1]

    @pl.when(place_ref[1] == 0)
    def _():
        slab_ref[...] = x_ref[half * stride :]

    @pl.when(place_ref[1] == 1)
    def _():
        slab_ref[...] = x_ref[: half * stride + fp]


def image_kernel(fp, place_ref, x_ref, face_image_ref, h_ref, pot_ref, image_ref, w_ref, first_ref, second_ref):
    cells, cp = h_ref.shape[:2]
    stride = cp - fp
    half = cells // 2

    def emit(c, rows, lower, carry):
        at = slice(c * stride, (c + 1) * stride)
        now = x_ref[at].astype(F32)
        out = (rows + spread(pot_ref[at], now.shape[1]) * now).astype(BF16)
        part, at_w = divmod(c, half)
        w_ref[part, at_w * stride : (at_w + 1) * stride] = out
        if c == half:
            w_ref[0, half * stride :] = carry.astype(BF16)
            w_ref[1, :fp] = (lower + spread(pot_ref[c * stride : c * stride + fp], now.shape[1]) * now[:fp]).astype(BF16)
        if c == 0:
            out = jnp.concatenate([face_image_ref[...].astype(BF16), out[fp:]], axis=0)
        image_ref[at] = out

    w_ref[1, half * stride :] = sweep(h_ref, x_ref, fp, emit).astype(BF16)
    n = first_ref.shape[0]
    first_ref[...] = w_ref[place_ref[1], :n]
    second_ref[...] = w_ref[place_ref[1], n:]


def back_kernel(node_ref, x_ref, image_ref, out_ref):
    rows = out_ref.shape[1]
    width = x_ref.shape[1]
    want = (lax.broadcasted_iota(jnp.int32, (rows, 1), 0) + pl.program_id(0) * rows).astype(F32)
    hit = flat(want == node_ref[...])
    out_ref[0, :, :width] = mul(hit, x_ref[...]).astype(BF16)
    out_ref[0, :, width:] = mul(hit, image_ref[...]).astype(BF16)


def back_pair_kernel(at_ref, node_ref, x_ref, image_ref, *out_refs):
    rows = out_refs[0].shape[0]
    width = x_ref.shape[1]
    for i, out_ref in enumerate(out_refs):
        want = (lax.broadcasted_iota(jnp.int32, (rows, 1), 0) + at_ref[i] * rows).astype(F32)
        hit = flat(want == node_ref[...])
        out_ref[:, :width] = mul(hit, x_ref[...]).astype(BF16)
        out_ref[:, width:] = mul(hit, image_ref[...]).astype(BF16)


def gram_kernel(scale, x_ref, y_ref, out_ref, rows_ref):
    parts, _, width = y_ref.shape

    @pl.when(pl.program_id(0) == 0)
    def _():
        for j in range(parts):
            rows_ref[:, j * width : (j + 1) * width] = y_ref[j]

    out_ref[0] = (
        lax.dot_general(x_ref[0], rows_ref[...], (((0,), (0,)), ((), ())), preferred_element_type=F32) * scale
    )


def residual_kernel(x_ref, y_ref, p_ref, out_ref):
    parts, _, width = x_ref.shape
    x = jnp.concatenate([x_ref[j] for j in range(parts)], axis=1)
    y = jnp.concatenate([y_ref[j] for j in range(parts)], axis=1)
    out_ref[...] = y.astype(F32) - jnp.dot(x, p_ref[...], preferred_element_type=F32)


def full(shape):
    return pl.BlockSpec(shape, lambda i: (0,) * len(shape))


def swap(block, axis, bit):
    return lax.ppermute(block, axis, [(i, i ^ bit) for i in range(lax.axis_size(axis))])


def shift(block, axis, distance):
    n = lax.axis_size(axis)
    return lax.ppermute(block, axis, [(i, i + distance) for i in range(n) if 0 <= i + distance < n])


def tmul(a, b):
    return lax.dot_general(a, b, (((0,), (0,)), ((), ())), preferred_element_type=F32)


def near_gram_kernel(scale, core_ref, x_ref, w_ref, other_ref, out_ref):
    slab, width = w_ref.shape[1:]
    at = (slice(0, slab), slice(x_ref.shape[0] - slab, x_ref.shape[0]))
    own = [x_ref[a] for a in at]
    out_ref[:width] = (tmul(own[0], w_ref[0]) + tmul(own[1], w_ref[1])) * scale
    half = width // 2

    @pl.when(core_ref[0] == 0)
    def _():
        out_ref[width:] = sum(tmul(w_ref[i, :, :half], other_ref[at[i]]) for i in range(2)) * scale

    @pl.when(core_ref[0] == 1)
    def _():
        out_ref[width:] = sum(tmul(other_ref[at[i], half:], w_ref[i]) for i in range(2)) * scale


def part_ways(sum_ref, mine, keep_ref, give_refs):
    n = keep_ref.shape[0]
    keep_ref[...] = sum_ref[pl.ds(pl.multiple_of(mine * n, 16), n)]
    for j, give_ref in enumerate(give_refs):
        give_ref[...] = sum_ref[pl.ds(pl.multiple_of(jnp.bitwise_xor(mine, j + 1) * n, 16), n)].astype(BF16)


def reduce_kernel(step, ways, bits_ref, keep_ref, *refs):
    total = keep_ref[...]
    for got_ref in refs[: ways - 1]:
        total = total + got_ref[...].astype(F32)
    refs = refs[ways - 1 :]
    if len(refs) == 1:
        refs[0][...] = total.astype(BF16)
        return
    keep_out, *gives, sum_ref = refs
    sum_ref[...] = total
    part_ways(sum_ref, bits_ref[step], keep_out, gives)


def join_kernel(step, bits_ref, own_ref, *refs):
    *got_refs, out_ref = refs
    n = own_ref.shape[0]
    mine = bits_ref[step]
    for j, ref in enumerate([own_ref] + got_refs):
        out_ref[pl.ds(pl.multiple_of(jnp.bitwise_xor(mine, j) * n, 16), n)] = ref[...]


def far_gram_kernel(scale, bits_ref, place_ref, *refs):
    *pair_refs, far_ref, near_ref, keep_ref = refs[:7]
    refs = refs[7:]
    *give_refs, out_ref = refs
    n, width = pair_refs[0].shape
    near = near_ref.shape[0]
    core = place_ref[1]
    out_ref[:near] = near_ref[...]
    far = far_ref[...]
    for i, at in enumerate((core, 1 - core)):
        first_ref, second_ref = pair_refs[2 * i : 2 * i + 2]
        block = (tmul(first_ref[...], far[:n]) + tmul(second_ref[...], far[n:])) * scale
        out_ref[pl.ds(pl.multiple_of(near + at * width, width // 2), width)] = block
    part_ways(out_ref, bits_ref[0], keep_ref, give_refs)


def paired_residual_kernel(place_ref, *refs):
    q_refs, refs = refs[:8], refs[8:]
    parts = 4
    row_refs, (out_hbm, p_hbm, out_ref, p_ref, q_ref, sems) = refs[:parts], refs[parts:]
    width = row_refs[0].shape[1] // 2
    half = width // 2
    me, mine = place_ref[0], place_ref[1]
    n = q_refs[0].shape[0]
    for k in range(parts):
        for j in range(2):
            q_ref[k, pl.ds(pl.multiple_of(jnp.bitwise_xor(mine, j) * n, 16), n)] = q_refs[2 * k + j][...]
    eye = (lax.broadcasted_iota(jnp.int32, (width, width), 0) == lax.broadcasted_iota(jnp.int32, (width, width), 1)).astype(
        F32
    ).astype(BF16)

    def turned(a):
        return lax.dot_general(eye, a, (((1,), (1,)), ((), ())), preferred_element_type=F32)

    def piece(i, lo, hi):
        return q_ref[jnp.bitwise_xor(me, i), lo:hi]

    def put(i, j, value):
        p_ref[i * width : (i + 1) * width, j * width : (j + 1) * width] = value

    near = width + half
    for i in range(parts):
        put(i, i, piece(i, 0, width))
    for i in range(0, parts, 2):
        block = jnp.concatenate([piece(i, width, near), piece(i + 1, width, near)], axis=0)
        put(i, i + 1, block)
        put(i + 1, i, turned(block).astype(BF16))
    for i in (0, 1):
        for j in (2, 3):
            one = piece(j ^ 2, near + i * width, near + (i + 1) * width)
            two = piece(i ^ 2, near + (j - 2) * width, near + (j - 1) * width)
            block = (one.astype(F32) + turned(two)).astype(BF16)
            put(i, j, block)
            put(j, i, turned(block).astype(BF16))
    copies = [pltpu.make_async_copy(p_ref, p_hbm, sems.at[parts])]
    copies[0].start()
    x = jnp.concatenate([ref[:, :width] for ref in row_refs], axis=1)
    spots = [pl.ds(pl.multiple_of(jnp.bitwise_xor(me, k) * width, width), width) for k in range(parts)]
    for k in range(parts):
        at = spots[k]
        p = jnp.concatenate([p_ref[spots[m], at] for m in range(parts)], axis=0)
        out_ref[k] = row_refs[k][:, width:].astype(F32) - mul(x, p)
        copies.append(pltpu.make_async_copy(out_ref.at[k], out_hbm.at[:, at], sems.at[k]))
        copies[-1].start()
    for copy in copies:
        copy.wait()


def paired_tail(x_own, image, w_own, w_side, give, node_row, o, d, dom, nodes):
    slab, width = w_own.shape[1:]
    orb = 4
    rows = nodes // orb
    side, core = o // 2, o % 2
    scale = 1.0 / (nodes * dom)
    sds = jax.ShapeDtypeStruct
    smem = pl.BlockSpec(memory_space=pltpu.SMEM)
    vmem = pl.BlockSpec(memory_space=pltpu.VMEM)
    far = swap(give, "orb", 2)
    total = image.shape[0]

    def back(first, second, x_own, image):
        whole = lambda *shape: pl.BlockSpec(shape, lambda i: (0,) * len(shape))
        return pl.pallas_call(
            back_pair_kernel,
            grid=(1,),
            in_specs=[smem, whole(1, total), whole(total, width), whole(total, width)],
            out_specs=[whole(rows, 2 * width)] * 2,
            out_shape=[sds((rows, 2 * width), BF16)] * 2,
            compiler_params=params(),
            cost_estimate=pl.CostEstimate(flops=1 << 20, bytes_accessed=1 << 10, transcendentals=0),
        )(jnp.stack([jnp.bitwise_xor(o, first), jnp.bitwise_xor(o, second)]), node_row, x_own, image)

    cuts = back(2, 3, x_own, image)
    x_other = swap(x_own, "orb", 1)
    w_other = [swap(w, "orb", 1) for w in w_side]
    top = width + width // 2
    near = pl.pallas_call(
        functools.partial(near_gram_kernel, scale),
        in_specs=[smem] + [vmem] * 3,
        out_shape=sds((top, width), F32),
        compiler_params=params(),
        cost_estimate=pl.CostEstimate(flops=1 << 20, bytes_accessed=1 << 10, transcendentals=0),
    )(core.reshape(1), x_own, w_own, x_other)
    far, near, *cuts, w_other[0], w_other[1] = lax.optimization_barrier((far, near, *cuts, *w_other))
    row2, row3 = swap(cuts[0], "orb", 2), swap(cuts[1], "orb", 3)
    groups, base = [], 1
    while base < dom:
        ways = 2 if base == 1 or base * 4 > dom else 4
        groups.append((base, ways))
        base *= ways
    bits = jnp.stack([(d // base) % ways for base, ways in groups])
    little = pl.CostEstimate(flops=1 << 10, bytes_accessed=1 << 10, transcendentals=0)
    count = top + 2 * width

    def parts_of(n, ways):
        return [sds((n // ways, width), F32)] + [sds((n // ways, width), BF16)] * (ways - 1)

    keep, *gives = pl.pallas_call(
        functools.partial(far_gram_kernel, scale),
        in_specs=[smem] * 2 + [vmem] * 6,
        out_shape=parts_of(count, 2),
        scratch_shapes=[pltpu.VMEM((count, width), F32)],
        compiler_params=params(),
        cost_estimate=pl.CostEstimate(flops=8 * slab * width * width, bytes_accessed=4 << 20, transcendentals=0),
    )(bits, jnp.stack([side, core]), *w_side, *w_other, far, near)
    row0 = cut1 = None
    for i, (base, ways) in enumerate(groups):
        if i == 0:
            x_own, image, gives[0] = lax.optimization_barrier((x_own, image, gives[0]))
            row0, cut1 = back(0, 1, x_own, image)
        gots = [swap(give, "dom", base * (j + 1)) for j, give in enumerate(gives)]
        n = keep.shape[0]
        last = i == len(groups) - 1
        outs = pl.pallas_call(
            functools.partial(reduce_kernel, i + 1, ways),
            in_specs=[smem] + [vmem] * ways,
            out_shape=[sds((n, width), BF16)] if last else parts_of(n, groups[i + 1][1]),
            scratch_shapes=[] if last else [pltpu.VMEM((n, width), F32)],
            compiler_params=params(),
            cost_estimate=little,
        )(bits, keep, *gots)
        outs = list(outs)
        if i == 0:
            outs[-1], row0, cut1 = lax.optimization_barrier((outs[-1], row0, cut1))
        if last:
            share = outs[0]
        else:
            keep, *gives = outs
    for i in reversed(range(1, len(groups))):
        base, ways = groups[i]
        gots = [swap(share, "dom", base * j) for j in range(1, ways)]
        share = pl.pallas_call(
            functools.partial(join_kernel, i),
            in_specs=[smem] + [vmem] * ways,
            out_shape=sds((ways * share.shape[0], width), BF16),
            compiler_params=params(),
            cost_estimate=little,
        )(bits, share, *gots)
    share, row2 = lax.optimization_barrier((share, row2))
    row1 = swap(cut1, "orb", 1)
    got = swap(share, "dom", 1)
    got, row3 = lax.optimization_barrier((got, row3))
    q2 = [swap(share, "orb", 2), swap(got, "orb", 2)]
    q1 = [swap(share, "orb", 1), swap(got, "orb", 1)]
    q3a = swap(q2[0], "orb", 1)
    q2[1], row1 = lax.optimization_barrier((q2[1], row1))
    q3 = [q3a, swap(q2[1], "orb", 1)]
    cols = orb * width
    return pl.pallas_call(
        paired_residual_kernel,
        in_specs=[smem] + [vmem] * 12,
        out_shape=(sds((rows, cols), F32), sds((cols, cols), BF16)),
        out_specs=[pl.BlockSpec(memory_space=pl.ANY)] * 2,
        scratch_shapes=[
            pltpu.VMEM((orb, rows, width), F32),
            pltpu.VMEM((cols, cols), BF16),
            pltpu.VMEM((orb, count, width), BF16),
            pltpu.SemaphoreType.DMA((orb + 1,)),
        ],
        compiler_params=params(),
    )(jnp.stack([o, d % 2]), share, got, *q1, *q2, *q3, row0, row1, row2, row3)


def body(orbitals, potential, cell_hamiltonian, connectivity, face_nodes):
    nodes, width = orbitals.shape
    cells, npc = connectivity.shape
    face = face_nodes.shape[0]
    fp, ip = up16(face), up16(npc - 2 * face)
    fp = (fp + 63) // 64 * 64
    stride = fp + ip
    cp = stride + fp
    total = cells * stride
    orb, dom = lax.axis_size("orb"), lax.axis_size("dom")
    d = lax.axis_index("dom")
    o = lax.axis_index("orb")
    sds = jax.ShapeDtypeStruct
    pot_row = potential.reshape(1, nodes)
    face_row = face_nodes.reshape(1, face)

    face_values = pl.pallas_call(
        face_kernel, out_shape=sds((fp + 16, width), BF16), compiler_params=params()
    )(face_row, orbitals, pot_row)
    ghost = shift(face_values, "dom", -1)

    extra = -(-DEGREE * fp // width)
    ext = pltpu.VMEM((total + fp, width), BF16)
    cost = pl.CostEstimate(
        flops=2 * DEGREE * cells * cp * cp * width, bytes_accessed=8 << 20, transcendentals=0
    )
    vmem, hbm = pl.BlockSpec(memory_space=pltpu.VMEM), pl.BlockSpec(memory_space=pl.ANY)
    hcan, y, pot, node, first, own, up, down = pl.pallas_call(
        functools.partial(free_kernel, fp, ip),
        in_specs=[vmem] * 2 + [pl.BlockSpec(memory_space=pl.ANY)] + [vmem] * 3,
        out_shape=[
            sds((cells, cp, cp), BF16),
            sds((total, width), BF16),
            sds((total, LANES), F32),
            sds((cells, 1, stride), F32),
            sds((total, width), BF16),
            sds((2, DEGREE + 1 + extra, fp, width), F32),
            sds((DEGREE + 1 + extra, fp, width), BF16),
            sds((DEGREE + extra, fp, width), BF16),
        ],
        out_specs=[hbm, vmem, hbm, vmem, hbm, vmem, vmem, vmem],
        scratch_shapes=[
            pltpu.VMEM((cells, cp, cp), BF16),
            pltpu.VMEM((total, LANES), F32),
            pltpu.VMEM((total, width), BF16),
            ext,
            ext,
            pltpu.VMEM((cells, npc, npc), BF16),
            pltpu.SemaphoreType.DMA,
            pltpu.SemaphoreType.DMA((3,)),
        ],
        compiler_params=params(),
        cost_estimate=cost,
    )(connectivity, face_row, cell_hamiltonian, orbitals, pot_row, ghost)
    node_row = node.reshape(1, total)
    from_left = shift(up, "dom", 1)
    from_right = shift(down, "dom", -1)
    slab = cells // 2 * stride + fp
    place = jnp.stack([(d == dom - 1).astype(jnp.int32), (o // 2) % 2])
    x_own, face_image, give = pl.pallas_call(
        functools.partial(forced_kernel, fp),
        in_specs=[pl.BlockSpec(memory_space=pltpu.SMEM), vmem, vmem, hbm, vmem, vmem, vmem, hbm, hbm],
        out_shape=[
            sds((total + fp, width), BF16),
            sds((fp, width), F32),
            sds((slab, width), BF16),
        ],
        scratch_shapes=[
            ext,
            ext,
            ext,
            pltpu.VMEM((cells, cp, cp), BF16),
            pltpu.VMEM((total, LANES), F32),
            pltpu.SemaphoreType.DMA((4,)),
        ],
        compiler_params=params(),
        cost_estimate=cost,
    )(place, y, ghost, first, own, from_left, from_right, hcan, pot)
    image, w_own, *w_side = pl.pallas_call(
        functools.partial(image_kernel, fp),
        in_specs=[pl.BlockSpec(memory_space=pltpu.SMEM)] + [vmem] * 4,
        out_shape=[sds((total, width), BF16), sds((2, slab, width), BF16)] + [sds((slab // 2, width), BF16)] * 2,
        compiler_params=params(),
        cost_estimate=pl.CostEstimate(flops=1 << 20, bytes_accessed=1 << 10, transcendentals=0),
    )(place, x_own, face_image, hcan, pot)

    if orb == 4 and dom % 8 == 0:
        return paired_tail(x_own, image, w_own, w_side, give, node_row, o, d, dom, nodes)
    cut = pl.pallas_call(
        back_kernel,
        grid=(orb,),
        in_specs=[full((1, total)), full((total, width)), full((total, width))],
        out_specs=pl.BlockSpec((1, nodes // orb, 2 * width), lambda i: (i, 0, 0)),
        out_shape=sds((orb, nodes // orb, 2 * width), BF16),
        compiler_params=params(),
        cost_estimate=pl.CostEstimate(flops=4 * total * nodes * width, bytes_accessed=4 << 20, transcendentals=0),
    )(node_row, x_own, image)
    both = lax.all_to_all(cut, "orb", split_axis=0, concat_axis=0, tiled=True)
    x_rows, i_rows = both[:, :, :width], both[:, :, width:]

    rows = nodes // orb
    cols = orb * width
    share = pl.pallas_call(
        functools.partial(gram_kernel, 1.0 / (nodes * dom)),
        grid=(orb,),
        in_specs=[pl.BlockSpec((1, rows, width), lambda i: (i, 0, 0)), full((orb, rows, width))],
        out_specs=pl.BlockSpec((1, width, cols), lambda i: (i, 0, 0)),
        out_shape=sds((orb, width, cols), F32),
        scratch_shapes=[pltpu.VMEM((rows, cols), BF16)],
        compiler_params=params(),
    )(x_rows, i_rows)

    hops = []
    for axis, me, size in (("orb", o, orb), ("dom", d, dom)):
        if axis == "dom":
            share = share.reshape(dom, width // dom, cols)
        bit = 1
        while bit < size:
            share = share.reshape((share.shape[0] // 2, 2) + share.shape[1:])
            mine = (me // bit) % 2
            keep = lax.dynamic_index_in_dim(share, mine, 1, keepdims=False)
            give = lax.dynamic_index_in_dim(share, 1 - mine, 1, keepdims=False)
            got = swap(give.astype(BF16), axis, bit)
            share = keep + got.astype(F32)
            hops.append((axis, bit, mine))
            bit *= 2
    share = share.astype(BF16)
    for axis, bit, mine in reversed(hops):
        if axis == "orb" and share.shape[0] == dom and bit * 2 == orb:
            share = share.reshape(1, width, cols)
        got = swap(share, axis, bit)
        share = jnp.where(mine == 0, jnp.stack([share, got], axis=1), jnp.stack([got, share], axis=1))
        share = share.reshape((share.shape[0] * 2,) + share.shape[2:])
    projected = share.reshape(cols, cols)

    residual = pl.pallas_call(
        residual_kernel, out_shape=sds((rows, cols), F32), compiler_params=params()
    )(x_rows, i_rows, projected)
    return (residual, projected)


def solution(mesh):
    return jax.shard_map(
        body,
        mesh=mesh,
        in_specs=(P("dom", "orb"), P("dom"), P("dom", None, None), P("dom", None), P("dom")),
        out_specs=(P(("dom", "orb"), None), P()),
        check_vma=False,
    )
```

```python
import functools

import jax
import jax.numpy as jnp
from jax import lax
from jax.experimental import pallas as pl
from jax.experimental.pallas import tpu as pltpu
from jax.sharding import PartitionSpec as P

DEGREE = 4
CENTER = 1.5
HALF = 2.0
F32 = jnp.float32
BF16 = jnp.bfloat16
LANES = 128
VMEM_LIMIT = 50 * 1024 * 1024


def up16(n):
    return (n + 15) // 16 * 16


def iota(shape, dim):
    return lax.broadcasted_iota(jnp.int32, shape, dim).astype(F32)


def to_col(row, rows):
    n = row.shape[1]
    return jnp.sum(jnp.where(iota((rows, n), 0) == iota((rows, n), 1), row, 0.0), axis=1, keepdims=True)


def to_row(col):
    n = col.shape[0]
    return jnp.sum(jnp.where(iota((n, n), 0) == iota((n, n), 1), col, 0.0), axis=0, keepdims=True)


def params():
    return pltpu.CompilerParams(vmem_limit_bytes=VMEM_LIMIT)


def thirds(a):
    one = a.astype(BF16)
    rest = a - one.astype(F32)
    two = rest.astype(BF16)
    return one, two, (rest - two.astype(F32)).astype(BF16)


def face_kernel(face_ref, x_ref, pot_ref, out_ref):
    width = x_ref.shape[1]
    fp = out_ref.shape[0] - 16
    nodes = x_ref.shape[0]
    col = to_col(face_ref[...].astype(F32) + 1.0, fp) - 1.0
    hit = jnp.where(col == iota((fp, nodes), 1), 1.0, 0.0).astype(BF16)
    out_ref[:fp] = mul(hit, x_ref[...]).astype(BF16)
    ri = lax.broadcasted_iota(jnp.int32, (16, nodes), 0)
    parts = [p.astype(F32) for p in thirds(pot_ref[...])]
    rows = jnp.where(ri == 0, parts[0], jnp.where(ri == 1, parts[1], jnp.where(ri == 2, parts[2], 0.0))).astype(BF16)
    got = lax.dot_general(rows, hit, (((1,), (1,)), ((), ())), preferred_element_type=F32).astype(BF16)
    if width > fp:
        got = jnp.concatenate([got, jnp.zeros((16, width - fp), BF16)], axis=1)
    out_ref[fp:] = got


def turn(a, b):
    return lax.dot_general(a, b, (((1,), (1,)), ((), ())), preferred_element_type=F32)


def halves(a):
    high = jnp.floor(a * (1.0 / 64.0))
    return high.astype(BF16), (a - 64.0 * high).astype(BF16)


def flat(mask):
    return jnp.where(mask, 1.0, 0.0).astype(BF16)


def order(fp, ip, arrived, conn_ref, face_ref, h_ref, x_ref, pot_ref, hcan_ref, v_ref, potc_ref, node_ref):
    cells, npc = conn_ref.shape
    nodes = x_ref.shape[0]
    face = face_ref.shape[1]
    stride = fp + ip
    cp = stride + fp
    conn = conn_ref[...].astype(F32)
    eye = flat(iota((npc, npc), 0) == iota((npc, npc), 1))
    below = flat(iota((npc, npc), 0) < iota((npc, npc), 1))
    high, low = halves(conn)
    cols = 64.0 * turn(eye, high) + turn(eye, low)
    rows = [conn[c : c + 1] for c in range(cells)]
    ones = jnp.ones((cells, npc), BF16)
    same = [flat(cols[:, c : c + 1] == rows[c + 1]) for c in range(cells - 1)]
    ri = lax.broadcasted_iota(jnp.int32, (cells, npc), 0)
    top = jnp.where(conn >= float(nodes), 1.0, 0.0)
    for c in range(cells - 1):
        top = jnp.where(ri == c, turn(ones, same[c]), top)
    rank_top = mul(top.astype(BF16), below)
    rank_b = rank_top.astype(BF16)
    top_slot = jnp.where(ri == cells - 1, conn - float(nodes), rank_top)
    fhit = to_col(face_ref[...].astype(F32), face) == rows[0]
    bot = jnp.where(ri == 0, jnp.max(jnp.where(fhit, 1.0, 0.0), axis=0, keepdims=True), 0.0)
    bot_slot = jnp.where(ri == 0, jnp.sum(jnp.where(fhit, iota((face, npc), 0), 0.0), axis=0, keepdims=True), 0.0)
    for c in range(cells - 1):
        both = jnp.concatenate([ones, rank_b], axis=0)
        got = mul(both, same[c])
        bot = jnp.where(ri == c + 1, got[:1], bot)
        bot_slot = jnp.where(ri == c + 1, got[cells + c : cells + c + 1], bot_slot)
    mid_rank = mul((1.0 - top - bot).astype(BF16), below)
    slot = jnp.where(top > 0.5, top_slot + float(stride), jnp.where(bot > 0.5, bot_slot, mid_rank + float(fp)))
    high, low = halves(conn + 1.0)
    number = iota((8, nodes), 1)[:1]
    arrived()
    for c in range(cells):
        perm = flat(iota((cp, npc), 0) == slot[c : c + 1])
        half = mul(perm, h_ref[c]).astype(BF16)
        hcan_ref[c] = turn(half, perm).astype(BF16)
        lead = perm[:stride]
        node = 64.0 * turn(lead, high)[:, c : c + 1] + turn(lead, low)[:, c : c + 1] - 1.0
        node_ref[c] = 64.0 * turn(high, lead)[c : c + 1] + turn(low, lead)[c : c + 1] - 1.0
        at = slice(c * stride, (c + 1) * stride)
        hit = node == number
        v_ref[at] = mul(flat(hit), x_ref[...]).astype(BF16)
        column = jnp.sum(jnp.where(hit, pot_ref[...], 0.0), axis=1, keepdims=True)
        potc_ref[at] = jnp.broadcast_to(column, (stride, LANES))


def spread(column, width):
    if width <= LANES:
        return column[:, :width]
    return jnp.concatenate([column] * (width // LANES), axis=1)


def advance(image, now, before):
    if before is None:
        return (image - CENTER * now) / HALF
    return 2.0 * (image - CENTER * now) / HALF - before


def split(a):
    high = a.astype(BF16)
    return high, (a - high.astype(F32)).astype(BF16)


def mul(a, b):
    return jnp.dot(a, b, preferred_element_type=F32)


def mul_r(a, b):
    return mul(a, b.astype(BF16))


def sweep(h_ref, y_ref, fp, emit):
    cells, cp = h_ref.shape[:2]
    stride = cp - fp
    carry = None
    for c in range(cells):
        prod = mul(h_ref[c], y_ref[c * stride : c * stride + cp])
        rows = prod[:stride]
        if c > 0:
            rows = jnp.concatenate([rows[:fp] + carry, rows[fp:]], axis=0)
        emit(c, rows, prod[:fp], carry)
        carry = prod[stride:]
    return carry


def response(hc, hn, potc, fp, upper):
    cp = hc.shape[0]
    stride = cp - fp
    if upper:
        f, r, s, g = slice(stride, cp), slice(0, stride), slice(0, fp), slice(stride, cp)
        rest = slice(0, stride)
    else:
        f, r, s, g = slice(0, fp), slice(fp, cp), slice(stride - fp, stride), slice(0, fp)
        rest = slice(fp, cp)
    potc = spread(potc, fp)
    gain = 2.0 / HALF
    out = [hc[f, f].astype(F32)]
    one = gain * hc[r, f].astype(F32)
    out.append(mul_r(hc[f, r], one))

    def pad_next(face_rows):
        zero = jnp.zeros((stride, fp), F32)
        return jnp.concatenate([zero, face_rows] if upper else [face_rows, zero], axis=0)

    def near(value, next_value):
        got = mul_r(hc[r, r], value) + (potc - CENTER) * value
        add = mul_r(hn[g, :], next_value)
        if upper:
            return jnp.concatenate([got[:fp] + add, got[fp:]], axis=0)
        return jnp.concatenate([got[: stride - fp], got[stride - fp :] + add], axis=0)

    two = gain * near(one, pad_next(one[s]))
    out.append(mul_r(hc[f, r], two))
    two_next = gain * mul_r(hn, pad_next(one[s]))
    if upper:
        two_next = jnp.concatenate([two_next[:stride], two[s]], axis=0)
    else:
        two_next = jnp.concatenate([two[s], two_next[fp:]], axis=0)
    three = gain * near(two, two_next) - one
    out.append(mul_r(hc[f, r], three))
    return out


def store_matrices(mats, out_ref, at, fp, width):
    for j, m in enumerate(mats):
        block, lane = divmod(j * fp, width)
        out_ref[at + block, :, lane : lane + fp] = m.astype(out_ref.dtype)


def load_matrices(ref, at, count, fp, width):
    spots = [divmod(j * fp, width) for j in range(count)]
    return [ref[at + block, :, lane : lane + fp].astype(F32) for block, lane in spots]


def free_kernel(
    fp, ip, conn_ref, face_ref, hraw_ref, raw_ref, potraw_ref, ghost_ref,
    h_hbm, v_ref, pot_hbm, node_ref, first_hbm, own_ref, up_ref, down_ref,
    h_ref, pot_ref, first_ref, a_ref, b_ref, hin_ref, sem, sems,
):
    copy = pltpu.make_async_copy(hraw_ref, hin_ref, sem)
    copy.start()
    order(fp, ip, copy.wait, conn_ref, face_ref, hin_ref, raw_ref, potraw_ref, h_ref, v_ref, pot_ref, node_ref)
    leaving = [
        pltpu.make_async_copy(src, dst, sems.at[i])
        for i, (src, dst) in enumerate(((h_ref, h_hbm), (pot_ref, pot_hbm), (first_ref, first_hbm)))
    ]
    leaving[0].start()
    leaving[1].start()
    cells, cp = h_ref.shape[:2]
    stride = cp - fp
    total = cells * stride
    width = v_ref.shape[1]
    a_ref[:total] = v_ref[...]
    a_ref[total:] = ghost_ref[:fp]
    b_ref[total:] = jnp.zeros((fp, width), BF16)

    def keep(k, low, high):
        own_ref[0, k] = low
        own_ref[1, k] = high
        if k < DEGREE:
            down_ref[k] = low.astype(BF16)
        up_ref[k] = high.astype(BF16)

    now_ref, other_ref = a_ref, b_ref
    for k in range(DEGREE):
        ends = {}

        def emit(c, rows, lower, carry, k=k, now_ref=now_ref, other_ref=other_ref, ends=ends):
            at = slice(c * stride, (c + 1) * stride)
            if c == 0:
                ends["low"] = rows[:fp]
            now = now_ref[at].astype(F32)
            before = None if k == 0 else other_ref[at].astype(F32)
            if k == 1:
                before = v_ref[at].astype(F32)
            value = advance(rows + spread(pot_ref[at], now.shape[1]) * now, now, before).astype(BF16)
            if c == 0:
                value = jnp.concatenate([jnp.zeros((fp, width), BF16), value[fp:]], axis=0)
            if k == 0:
                first_ref[at] = value
            other_ref[at] = value

        high = sweep(h_ref, now_ref, fp, emit)
        keep(k, ends["low"], high)
        if k == 0:
            leaving[2].start()
            a_ref[total:] = jnp.zeros((fp, width), BF16)
        now_ref, other_ref = other_ref, now_ref
    keep(DEGREE, mul(h_ref[0, :fp], now_ref[:cp]), mul(h_ref[cells - 1, stride:], now_ref[total - stride :]))
    low = response(h_ref[0], h_ref[1], pot_ref[fp:cp], fp, False)
    high = response(h_ref[cells - 1], h_ref[cells - 2], pot_ref[total - stride :], fp, True)
    store_matrices(low, down_ref, DEGREE, fp, width)
    store_matrices(high, up_ref, DEGREE + 1, fp, width)
    for side, mats in enumerate((low, high)):
        store_matrices(mats, own_ref.at[side], DEGREE + 1, fp, width)
    for copy in leaving:
        copy.wait()


def forced_kernel(
    fp, place_ref, v_ref, ghost_ref, first_hbm, own_ref, fromleft_ref, fromright_ref, h_hbm, pot_hbm,
    x_ref, face_image_ref, slab_ref, a_ref, b_ref, c_ref, h_ref, pot_ref, sems,
):
    cells, cp = h_ref.shape[:2]
    stride = cp - fp
    total = cells * stride
    width = v_ref.shape[1]
    rest = pl.ds(fp, total - fp)
    coming = [
        pltpu.make_async_copy(src, dst, sems.at[i])
        for i, (src, dst) in enumerate(
            (
                (pot_hbm.at[pl.ds(0, fp)], pot_ref.at[pl.ds(0, fp)]),
                (first_hbm, a_ref.at[pl.ds(0, total)]),
                (pot_hbm.at[rest], pot_ref.at[rest]),
                (h_hbm, h_ref),
            )
        )
    ]
    for copy in coming:
        copy.start()
    coming[0].wait()
    half = cells // 2
    extra = own_ref.shape[1] - DEGREE - 1
    potg = to_col(jnp.sum(ghost_ref[fp:].astype(F32), axis=0, keepdims=True)[:, :fp], fp)
    nothing = jnp.zeros((fp, width), BF16)
    sides = []
    for side, (got_ref, pot, start) in enumerate(
        ((fromleft_ref, spread(pot_ref[:fp], width), v_ref[:fp]), (fromright_ref, potg, ghost_ref[:fp]))
    ):
        theirs = load_matrices(got_ref, got_ref.shape[0] - extra, DEGREE, fp, width)
        ours = load_matrices(own_ref.at[side], DEGREE + 1, DEGREE, fp, width)
        mats = [a + b for a, b in zip(theirs, ours)]
        line = jnp.concatenate(mats[::-1], axis=1)
        sides.append((got_ref, pot, jnp.concatenate(split(line), axis=0), [start]))
    for k in range(DEGREE + 1):
        for side, (got_ref, pot, line, values) in enumerate(sides):
            if side == 1 and k == DEGREE:
                continue
            h = own_ref[side, k] + got_ref[k].astype(F32)
            if k > 0:
                past = [values[m] if m >= 1 else nothing for m in range(k - DEGREE + 1, k + 1)]
                both = mul(line, jnp.concatenate(past, axis=0))
                h = h + both[:fp] + both[fp:]
            now = values[k].astype(F32)
            h = h + pot * now
            if k == DEGREE:
                face_image_ref[...] = h
                continue
            value = advance(h, now, None if k == 0 else values[k - 1].astype(F32))
            if side == 1:
                value = jnp.where(place_ref[0] == 1, 0.0, value)
            values.append(value.astype(BF16))
    low, high = sides[0][3], sides[1][3]
    for copy in coming[1:]:
        copy.wait()
    a_ref[:fp] = low[1]
    a_ref[total:] = high[1]
    refs = [v_ref, a_ref, b_ref, c_ref, x_ref]
    for k in range(1, DEGREE):
        now_ref = refs[k]

        def emit(c, rows, lower, carry, k=k, now_ref=now_ref):
            at = slice(c * stride, (c + 1) * stride)
            now = now_ref[at].astype(F32)
            value = advance(rows + spread(pot_ref[at], now.shape[1]) * now, now, refs[k - 1][at].astype(F32)).astype(BF16)
            if c == 0:
                value = jnp.concatenate([low[k + 1], value[fp:]], axis=0)
            refs[k + 1][at] = value

        sweep(h_ref, now_ref, fp, emit)
        refs[k + 1][total:] = high[k + 1]

    @pl.when(place_ref[1] == 0)
    def _():
        slab_ref[...] = x_ref[half * stride :]

    @pl.when(place_ref[1] == 1)
    def _():
        slab_ref[...] = x_ref[: half * stride + fp]


def image_kernel(fp, place_ref, x_ref, face_image_ref, h_ref, pot_ref, image_ref, w_ref, first_ref, second_ref):
    cells, cp = h_ref.shape[:2]
    stride = cp - fp
    half = cells // 2

    def emit(c, rows, lower, carry):
        at = slice(c * stride, (c + 1) * stride)
        now = x_ref[at].astype(F32)
        out = (rows + spread(pot_ref[at], now.shape[1]) * now).astype(BF16)
        part, at_w = divmod(c, half)
        w_ref[part, at_w * stride : (at_w + 1) * stride] = out
        if c == half:
            w_ref[0, half * stride :] = carry.astype(BF16)
            w_ref[1, :fp] = (lower + spread(pot_ref[c * stride : c * stride + fp], now.shape[1]) * now[:fp]).astype(BF16)
        if c == 0:
            out = jnp.concatenate([face_image_ref[...].astype(BF16), out[fp:]], axis=0)
        image_ref[at] = out

    w_ref[1, half * stride :] = sweep(h_ref, x_ref, fp, emit).astype(BF16)
    n = first_ref.shape[0]
    first_ref[...] = w_ref[place_ref[1], :n]
    second_ref[...] = w_ref[place_ref[1], n:]


def back_kernel(node_ref, x_ref, image_ref, out_ref):
    rows = out_ref.shape[1]
    width = x_ref.shape[1]
    want = (lax.broadcasted_iota(jnp.int32, (rows, 1), 0) + pl.program_id(0) * rows).astype(F32)
    hit = flat(want == node_ref[...])
    out_ref[0, :, :width] = mul(hit, x_ref[...]).astype(BF16)
    out_ref[0, :, width:] = mul(hit, image_ref[...]).astype(BF16)


def back_pair_kernel(at_ref, node_ref, x_ref, image_ref, *out_refs):
    rows = out_refs[0].shape[0]
    width = x_ref.shape[1]
    for i, out_ref in enumerate(out_refs):
        want = (lax.broadcasted_iota(jnp.int32, (rows, 1), 0) + at_ref[i] * rows).astype(F32)
        hit = flat(want == node_ref[...])
        out_ref[:, :width] = mul(hit, x_ref[...]).astype(BF16)
        out_ref[:, width:] = mul(hit, image_ref[...]).astype(BF16)


def gram_kernel(scale, x_ref, y_ref, out_ref, rows_ref):
    parts, _, width = y_ref.shape

    @pl.when(pl.program_id(0) == 0)
    def _():
        for j in range(parts):
            rows_ref[:, j * width : (j + 1) * width] = y_ref[j]

    out_ref[0] = (
        lax.dot_general(x_ref[0], rows_ref[...], (((0,), (0,)), ((), ())), preferred_element_type=F32) * scale
    )


def residual_kernel(x_ref, y_ref, p_ref, out_ref):
    parts, _, width = x_ref.shape
    x = jnp.concatenate([x_ref[j] for j in range(parts)], axis=1)
    y = jnp.concatenate([y_ref[j] for j in range(parts)], axis=1)
    out_ref[...] = y.astype(F32) - jnp.dot(x, p_ref[...], preferred_element_type=F32)


def full(shape):
    return pl.BlockSpec(shape, lambda i: (0,) * len(shape))


def swap(block, axis, bit):
    return lax.ppermute(block, axis, [(i, i ^ bit) for i in range(lax.axis_size(axis))])


def shift(block, axis, distance):
    n = lax.axis_size(axis)
    return lax.ppermute(block, axis, [(i, i + distance) for i in range(n) if 0 <= i + distance < n])


def tmul(a, b):
    return lax.dot_general(a, b, (((0,), (0,)), ((), ())), preferred_element_type=F32)


def near_gram_kernel(scale, core_ref, x_ref, w_ref, other_ref, out_ref):
    slab, width = w_ref.shape[1:]
    at = (slice(0, slab), slice(x_ref.shape[0] - slab, x_ref.shape[0]))
    own = [x_ref[a] for a in at]
    out_ref[:width] = (tmul(own[0], w_ref[0]) + tmul(own[1], w_ref[1])) * scale
    half = width // 2

    @pl.when(core_ref[0] == 0)
    def _():
        out_ref[width:] = sum(tmul(w_ref[i, :, :half], other_ref[at[i]]) for i in range(2)) * scale

    @pl.when(core_ref[0] == 1)
    def _():
        out_ref[width:] = sum(tmul(other_ref[at[i], half:], w_ref[i]) for i in range(2)) * scale


def part_ways(sum_ref, mine, keep_ref, give_refs):
    n = keep_ref.shape[0]
    keep_ref[...] = sum_ref[pl.ds(pl.multiple_of(mine * n, 16), n)]
    for j, give_ref in enumerate(give_refs):
        give_ref[...] = sum_ref[pl.ds(pl.multiple_of(jnp.bitwise_xor(mine, j + 1) * n, 16), n)].astype(BF16)


def reduce_kernel(step, ways, bits_ref, keep_ref, *refs):
    total = keep_ref[...]
    for got_ref in refs[: ways - 1]:
        total = total + got_ref[...].astype(F32)
    refs = refs[ways - 1 :]
    if len(refs) == 1:
        refs[0][...] = total.astype(BF16)
        return
    keep_out, *gives, sum_ref = refs
    sum_ref[...] = total
    part_ways(sum_ref, bits_ref[step], keep_out, gives)


def join_kernel(step, bits_ref, own_ref, *refs):
    *got_refs, out_ref = refs
    n = own_ref.shape[0]
    mine = bits_ref[step]
    for j, ref in enumerate([own_ref] + got_refs):
        out_ref[pl.ds(pl.multiple_of(jnp.bitwise_xor(mine, j) * n, 16), n)] = ref[...]


def far_gram_kernel(scale, bits_ref, place_ref, *refs):
    *pair_refs, far_ref, near_ref, keep_ref = refs[:7]
    refs = refs[7:]
    *give_refs, out_ref = refs
    n, width = pair_refs[0].shape
    near = near_ref.shape[0]
    core = place_ref[1]
    out_ref[:near] = near_ref[...]
    far = far_ref[...]
    for i, at in enumerate((core, 1 - core)):
        first_ref, second_ref = pair_refs[2 * i : 2 * i + 2]
        block = (tmul(first_ref[...], far[:n]) + tmul(second_ref[...], far[n:])) * scale
        out_ref[pl.ds(pl.multiple_of(near + at * width, width // 2), width)] = block
    part_ways(out_ref, bits_ref[0], keep_ref, give_refs)


def paired_residual_kernel(place_ref, *refs):
    q_refs, refs = refs[:8], refs[8:]
    parts = 4
    row_refs, (out_hbm, p_hbm, out_ref, p_ref, q_ref, sems) = refs[:parts], refs[parts:]
    width = row_refs[0].shape[1] // 2
    half = width // 2
    me, mine = place_ref[0], place_ref[1]
    n = q_refs[0].shape[0]
    for k in range(parts):
        for j in range(2):
            q_ref[k, pl.ds(pl.multiple_of(jnp.bitwise_xor(mine, j) * n, 16), n)] = q_refs[2 * k + j][...]
    eye = (lax.broadcasted_iota(jnp.int32, (width, width), 0) == lax.broadcasted_iota(jnp.int32, (width, width), 1)).astype(
        F32
    ).astype(BF16)

    def turned(a):
        return lax.dot_general(eye, a, (((1,), (1,)), ((), ())), preferred_element_type=F32)

    def piece(i, lo, hi):
        return q_ref[jnp.bitwise_xor(me, i), lo:hi]

    def put(i, j, value):
        p_ref[i * width : (i + 1) * width, j * width : (j + 1) * width] = value

    near = width + half
    for i in range(parts):
        put(i, i, piece(i, 0, width))
    for i in range(0, parts, 2):
        block = jnp.concatenate([piece(i, width, near), piece(i + 1, width, near)], axis=0)
        put(i, i + 1, block)
        put(i + 1, i, turned(block).astype(BF16))
    for i in (0, 1):
        for j in (2, 3):
            one = piece(j ^ 2, near + i * width, near + (i + 1) * width)
            two = piece(i ^ 2, near + (j - 2) * width, near + (j - 1) * width)
            block = (one.astype(F32) + turned(two)).astype(BF16)
            put(i, j, block)
            put(j, i, turned(block).astype(BF16))
    copies = [pltpu.make_async_copy(p_ref, p_hbm, sems.at[parts])]
    copies[0].start()
    x = jnp.concatenate([ref[:, :width] for ref in row_refs], axis=1)
    spots = [pl.ds(pl.multiple_of(jnp.bitwise_xor(me, k) * width, width), width) for k in range(parts)]
    for k in range(parts):
        at = spots[k]
        p = jnp.concatenate([p_ref[spots[m], at] for m in range(parts)], axis=0)
        out_ref[k] = row_refs[k][:, width:].astype(F32) - mul(x, p)
        copies.append(pltpu.make_async_copy(out_ref.at[k], out_hbm.at[:, at], sems.at[k]))
        copies[-1].start()
    for copy in copies:
        copy.wait()


def paired_tail(x_own, image, w_own, w_side, give, node_row, o, d, dom, nodes):
    slab, width = w_own.shape[1:]
    orb = 4
    rows = nodes // orb
    side, core = o // 2, o % 2
    scale = 1.0 / (nodes * dom)
    sds = jax.ShapeDtypeStruct
    smem = pl.BlockSpec(memory_space=pltpu.SMEM)
    vmem = pl.BlockSpec(memory_space=pltpu.VMEM)
    far = swap(give, "orb", 2)
    total = image.shape[0]

    def back(first, second, x_own, image):
        whole = lambda *shape: pl.BlockSpec(shape, lambda i: (0,) * len(shape))
        return pl.pallas_call(
            back_pair_kernel,
            grid=(1,),
            in_specs=[smem, whole(1, total), whole(total, width), whole(total, width)],
            out_specs=[whole(rows, 2 * width)] * 2,
            out_shape=[sds((rows, 2 * width), BF16)] * 2,
            compiler_params=params(),
            cost_estimate=pl.CostEstimate(flops=1 << 20, bytes_accessed=1 << 10, transcendentals=0),
        )(jnp.stack([jnp.bitwise_xor(o, first), jnp.bitwise_xor(o, second)]), node_row, x_own, image)

    cuts = back(2, 3, x_own, image)
    x_other = swap(x_own, "orb", 1)
    w_other = [swap(w, "orb", 1) for w in w_side]
    top = width + width // 2
    near = pl.pallas_call(
        functools.partial(near_gram_kernel, scale),
        in_specs=[smem] + [vmem] * 3,
        out_shape=sds((top, width), F32),
        compiler_params=params(),
        cost_estimate=pl.CostEstimate(flops=1 << 20, bytes_accessed=1 << 10, transcendentals=0),
    )(core.reshape(1), x_own, w_own, x_other)
    far, near, *cuts, w_other[0], w_other[1] = lax.optimization_barrier((far, near, *cuts, *w_other))
    row2, row3 = swap(cuts[0], "orb", 2), swap(cuts[1], "orb", 3)
    groups, base = [], 1
    while base < dom:
        ways = 2 if base == 1 or base * 4 > dom else 4
        groups.append((base, ways))
        base *= ways
    bits = jnp.stack([(d // base) % ways for base, ways in groups])
    little = pl.CostEstimate(flops=1 << 10, bytes_accessed=1 << 10, transcendentals=0)
    count = top + 2 * width

    def parts_of(n, ways):
        return [sds((n // ways, width), F32)] + [sds((n // ways, width), BF16)] * (ways - 1)

    keep, *gives = pl.pallas_call(
        functools.partial(far_gram_kernel, scale),
        in_specs=[smem] * 2 + [vmem] * 6,
        out_shape=parts_of(count, 2),
        scratch_shapes=[pltpu.VMEM((count, width), F32)],
        compiler_params=params(),
        cost_estimate=pl.CostEstimate(flops=8 * slab * width * width, bytes_accessed=4 << 20, transcendentals=0),
    )(bits, jnp.stack([side, core]), *w_side, *w_other, far, near)
    row0 = cut1 = None
    for i, (base, ways) in enumerate(groups):
        if i == 0:
            x_own, image, gives[0] = lax.optimization_barrier((x_own, image, gives[0]))
            row0, cut1 = back(0, 1, x_own, image)
        gots = [swap(give, "dom", base * (j + 1)) for j, give in enumerate(gives)]
        n = keep.shape[0]
        last = i == len(groups) - 1
        outs = pl.pallas_call(
            functools.partial(reduce_kernel, i + 1, ways),
            in_specs=[smem] + [vmem] * ways,
            out_shape=[sds((n, width), BF16)] if last else parts_of(n, groups[i + 1][1]),
            scratch_shapes=[] if last else [pltpu.VMEM((n, width), F32)],
            compiler_params=params(),
            cost_estimate=little,
        )(bits, keep, *gots)
        outs = list(outs)
        if i == 0:
            outs[-1], row0, cut1 = lax.optimization_barrier((outs[-1], row0, cut1))
        if last:
            share = outs[0]
        else:
            keep, *gives = outs
    for i in reversed(range(1, len(groups))):
        base, ways = groups[i]
        gots = [swap(share, "dom", base * j) for j in range(1, ways)]
        share = pl.pallas_call(
            functools.partial(join_kernel, i),
            in_specs=[smem] + [vmem] * ways,
            out_shape=sds((ways * share.shape[0], width), BF16),
            compiler_params=params(),
            cost_estimate=little,
        )(bits, share, *gots)
    share, row2 = lax.optimization_barrier((share, row2))
    row1 = swap(cut1, "orb", 1)
    got = swap(share, "dom", 1)
    got, row3 = lax.optimization_barrier((got, row3))
    q2 = [swap(share, "orb", 2), swap(got, "orb", 2)]
    q1 = [swap(share, "orb", 1), swap(got, "orb", 1)]
    q3a = swap(q2[0], "orb", 1)
    q3 = [q3a, swap(q2[1], "orb", 1)]
    cols = orb * width
    return pl.pallas_call(
        paired_residual_kernel,
        in_specs=[smem] + [vmem] * 12,
        out_shape=(sds((rows, cols), F32), sds((cols, cols), BF16)),
        out_specs=[pl.BlockSpec(memory_space=pl.ANY)] * 2,
        scratch_shapes=[
            pltpu.VMEM((orb, rows, width), F32),
            pltpu.VMEM((cols, cols), BF16),
            pltpu.VMEM((orb, count, width), BF16),
            pltpu.SemaphoreType.DMA((orb + 1,)),
        ],
        compiler_params=params(),
    )(jnp.stack([o, d % 2]), share, got, *q1, *q2, *q3, row0, row1, row2, row3)


def body(orbitals, potential, cell_hamiltonian, connectivity, face_nodes):
    nodes, width = orbitals.shape
    cells, npc = connectivity.shape
    face = face_nodes.shape[0]
    fp, ip = up16(face), up16(npc - 2 * face)
    fp = (fp + 63) // 64 * 64
    stride = fp + ip
    cp = stride + fp
    total = cells * stride
    orb, dom = lax.axis_size("orb"), lax.axis_size("dom")
    d = lax.axis_index("dom")
    o = lax.axis_index("orb")
    sds = jax.ShapeDtypeStruct
    pot_row = potential.reshape(1, nodes)
    face_row = face_nodes.reshape(1, face)

    face_values = pl.pallas_call(
        face_kernel, out_shape=sds((fp + 16, width), BF16), compiler_params=params()
    )(face_row, orbitals, pot_row)
    ghost = shift(face_values, "dom", -1)

    extra = -(-DEGREE * fp // width)
    ext = pltpu.VMEM((total + fp, width), BF16)
    cost = pl.CostEstimate(
        flops=2 * DEGREE * cells * cp * cp * width, bytes_accessed=8 << 20, transcendentals=0
    )
    vmem, hbm = pl.BlockSpec(memory_space=pltpu.VMEM), pl.BlockSpec(memory_space=pl.ANY)
    hcan, y, pot, node, first, own, up, down = pl.pallas_call(
        functools.partial(free_kernel, fp, ip),
        in_specs=[vmem] * 2 + [pl.BlockSpec(memory_space=pl.ANY)] + [vmem] * 3,
        out_shape=[
            sds((cells, cp, cp), BF16),
            sds((total, width), BF16),
            sds((total, LANES), F32),
            sds((cells, 1, stride), F32),
            sds((total, width), BF16),
            sds((2, DEGREE + 1 + extra, fp, width), F32),
            sds((DEGREE + 1 + extra, fp, width), BF16),
            sds((DEGREE + extra, fp, width), BF16),
        ],
        out_specs=[hbm, vmem, hbm, vmem, hbm, vmem, vmem, vmem],
        scratch_shapes=[
            pltpu.VMEM((cells, cp, cp), BF16),
            pltpu.VMEM((total, LANES), F32),
            pltpu.VMEM((total, width), BF16),
            ext,
            ext,
            pltpu.VMEM((cells, npc, npc), BF16),
            pltpu.SemaphoreType.DMA,
            pltpu.SemaphoreType.DMA((3,)),
        ],
        compiler_params=params(),
        cost_estimate=cost,
    )(connectivity, face_row, cell_hamiltonian, orbitals, pot_row, ghost)
    node_row = node.reshape(1, total)
    from_left = shift(up, "dom", 1)
    from_right = shift(down, "dom", -1)
    slab = cells // 2 * stride + fp
    place = jnp.stack([(d == dom - 1).astype(jnp.int32), (o // 2) % 2])
    x_own, face_image, give = pl.pallas_call(
        functools.partial(forced_kernel, fp),
        in_specs=[pl.BlockSpec(memory_space=pltpu.SMEM), vmem, vmem, hbm, vmem, vmem, vmem, hbm, hbm],
        out_shape=[
            sds((total + fp, width), BF16),
            sds((fp, width), F32),
            sds((slab, width), BF16),
        ],
        scratch_shapes=[
            ext,
            ext,
            ext,
            pltpu.VMEM((cells, cp, cp), BF16),
            pltpu.VMEM((total, LANES), F32),
            pltpu.SemaphoreType.DMA((4,)),
        ],
        compiler_params=params(),
        cost_estimate=cost,
    )(place, y, ghost, first, own, from_left, from_right, hcan, pot)
    image, w_own, *w_side = pl.pallas_call(
        functools.partial(image_kernel, fp),
        in_specs=[pl.BlockSpec(memory_space=pltpu.SMEM)] + [vmem] * 4,
        out_shape=[sds((total, width), BF16), sds((2, slab, width), BF16)] + [sds((slab // 2, width), BF16)] * 2,
        compiler_params=params(),
        cost_estimate=pl.CostEstimate(flops=1 << 20, bytes_accessed=1 << 10, transcendentals=0),
    )(place, x_own, face_image, hcan, pot)

    if orb == 4 and dom % 8 == 0:
        return paired_tail(x_own, image, w_own, w_side, give, node_row, o, d, dom, nodes)
    cut = pl.pallas_call(
        back_kernel,
        grid=(orb,),
        in_specs=[full((1, total)), full((total, width)), full((total, width))],
        out_specs=pl.BlockSpec((1, nodes // orb, 2 * width), lambda i: (i, 0, 0)),
        out_shape=sds((orb, nodes // orb, 2 * width), BF16),
        compiler_params=params(),
        cost_estimate=pl.CostEstimate(flops=4 * total * nodes * width, bytes_accessed=4 << 20, transcendentals=0),
    )(node_row, x_own, image)
    both = lax.all_to_all(cut, "orb", split_axis=0, concat_axis=0, tiled=True)
    x_rows, i_rows = both[:, :, :width], both[:, :, width:]

    rows = nodes // orb
    cols = orb * width
    share = pl.pallas_call(
        functools.partial(gram_kernel, 1.0 / (nodes * dom)),
        grid=(orb,),
        in_specs=[pl.BlockSpec((1, rows, width), lambda i: (i, 0, 0)), full((orb, rows, width))],
        out_specs=pl.BlockSpec((1, width, cols), lambda i: (i, 0, 0)),
        out_shape=sds((orb, width, cols), F32),
        scratch_shapes=[pltpu.VMEM((rows, cols), BF16)],
        compiler_params=params(),
    )(x_rows, i_rows)

    hops = []
    for axis, me, size in (("orb", o, orb), ("dom", d, dom)):
        if axis == "dom":
            share = share.reshape(dom, width // dom, cols)
        bit = 1
        while bit < size:
            share = share.reshape((share.shape[0] // 2, 2) + share.shape[1:])
            mine = (me // bit) % 2
            keep = lax.dynamic_index_in_dim(share, mine, 1, keepdims=False)
            give = lax.dynamic_index_in_dim(share, 1 - mine, 1, keepdims=False)
            got = swap(give.astype(BF16), axis, bit)
            share = keep + got.astype(F32)
            hops.append((axis, bit, mine))
            bit *= 2
    share = share.astype(BF16)
    for axis, bit, mine in reversed(hops):
        if axis == "orb" and share.shape[0] == dom and bit * 2 == orb:
            share = share.reshape(1, width, cols)
        got = swap(share, axis, bit)
        share = jnp.where(mine == 0, jnp.stack([share, got], axis=1), jnp.stack([got, share], axis=1))
        share = share.reshape((share.shape[0] * 2,) + share.shape[2:])
    projected = share.reshape(cols, cols)

    residual = pl.pallas_call(
        residual_kernel, out_shape=sds((rows, cols), F32), compiler_params=params()
    )(x_rows, i_rows, projected)
    return (residual, projected)


def solution(mesh):
    return jax.shard_map(
        body,
        mesh=mesh,
        in_specs=(P("dom", "orb"), P("dom"), P("dom", None, None), P("dom", None), P("dom")),
        out_specs=(P(("dom", "orb"), None), P()),
        check_vma=False,
    )
```
